32 devices in a mesh: tm: 4 (over x, core), tile: 8 (over z, y).
Axes of the slice: x: 2, y: 2, z: 4, core: 2. Of those that a mesh axis runs over, the one named last changes fastest.
Arguments:
- gains: bfloat16 [32, 768, 768], P('tm', 'tile'), may hold values from -1.5 to 1.5
- increments: float32 [32, 768, 768], P('tm', 'tile'), may hold values from -2 to 5
- terminal: float32 [768, 768], P('tile'), may hold values from -3 to 6
Outputs:
- smoothed: float32 [32, 768, 768], P('tm', 'tile')
The draws below stay inside these ranges and needn't reach their ends.
All inputs are finite; a program needn't handle non-finite values.
Results may differ from the reference program's by a relative error of at most 0.04.
Values may be sent and summed in bfloat16 or wider, within the bound.
No kernel may reach another device: no remote copies, remote signals or barrier semaphores. Data moves between devices by JAX's collectives and lax.ppermute only.
A program may use at most 576 MiB of HBM per device.

```python
import jax
import jax.numpy as jnp
from jax import lax

S = 768
HORIZON_LENGTH = 32


def decay_rates(key, slow_share):
    first_key = jax.random.fold_in(key, 101)
    second_key = jax.random.fold_in(key, 102)
    third_seed = jax.random.fold_in(key, 103)
    slow_pick = jax.random.uniform(first_key, (S,)) < slow_share
    base_rate = jnp.where(slow_pick, 0.1 ** (1.0 / HORIZON_LENGTH), 0.1 ** (4.0 / HORIZON_LENGTH))
    spread_scale = jax.random.uniform(second_key, (HORIZON_LENGTH, S), minval=0.6, maxval=1.4)
    gram_product = base_rate[None, :] ** spread_scale
    packet_batches = jax.random.uniform(third_seed, (HORIZON_LENGTH,)) < 4.0 / HORIZON_LENGTH
    gram_product = gram_product * jnp.where(packet_batches, 0.3, 1.0)[:, None]
    return jnp.sqrt(gram_product / 1.04)


def balanced_perturbation(key):
    raw_noise = jax.random.normal(key, (HORIZON_LENGTH, S, S))
    return (raw_noise + jnp.swapaxes(raw_noise, 1, 2)) * 0.70710678


def draw_gains(key, part):
    rates = decay_rates(key, 0.5)
    key = jax.random.fold_in(key, 11)
    jitter_noise = jax.random.normal(key, (HORIZON_LENGTH, S, S))
    identity = jnp.eye(S, dtype=jnp.float32)
    scan_output = rates[:, :, None] * (identity[None] + 0.2 * jitter_noise / jnp.sqrt(1.0 * S))
    return scan_output.astype(jnp.bfloat16)


def draw_increments(key, part):
    rates = decay_rates(key, 0.5)
    key = jax.random.fold_in(key, 12)
    magnitude_seed = jax.random.fold_in(key, 1)
    scales = jnp.exp(jax.random.uniform(magnitude_seed, (HORIZON_LENGTH, S), minval=-0.693, maxval=0.693))
    symmetric = balanced_perturbation(key)
    diagonal = (1.0 - rates * rates) * scales
    identity = jnp.eye(S, dtype=jnp.float32)
    coupling = jnp.sqrt(diagonal[:, :, None] * diagonal[:, None, :])
    scan_output = diagonal[:, :, None] * identity[None] + (1.0 - identity[None]) * 0.25 * coupling * symmetric / jnp.sqrt(1.0 * S)
    return scan_output.astype(jnp.float32)


def draw_terminal(key, part):
    key = jax.random.fold_in(key, 13)
    magnitude_seed = jax.random.fold_in(key, 1)
    noise_key = jax.random.fold_in(key, 2)
    diagonal = jnp.exp(jax.random.uniform(magnitude_seed, (S,), minval=-1.386, maxval=1.386))
    raw_noise = jax.random.normal(noise_key, (S, S))
    symmetric = (raw_noise + raw_noise.T) * 0.70710678
    identity = jnp.eye(S, dtype=jnp.float32)
    coupling = jnp.sqrt(diagonal[:, None] * diagonal[None, :])
    scan_output = diagonal[:, None] * identity + (1.0 - identity) * 0.4 * coupling * symmetric / jnp.sqrt(1.0 * S)
    return scan_output.astype(jnp.float32)


def setup_inputs(seed: int = 0) -> dict:
    key_of = jax.random.split(jax.random.key(seed), 4)
    gains = draw_gains(jax.random.fold_in(key_of[3], 71), 0)
    increments = draw_increments(jax.random.fold_in(key_of[3], 71), 0)
    terminal = draw_terminal(jax.random.fold_in(key_of[3], 71), 0)
    return dict(gains=gains, increments=increments, terminal=terminal)


def transpose_dot(left, right):
    return lax.dot_general(left, right, (((1,), (1,)), ((), ())), preferred_element_type=jnp.float32)


def reference(gains, increments, terminal):
    def backward(covariance, step_pair):
        factor, increment = step_pair
        product = jnp.dot(factor, covariance.astype(jnp.bfloat16), preferred_element_type=jnp.float32).astype(jnp.bfloat16)
        updated = transpose_dot(product, factor) + increment
        return updated, updated

    _, smoothed = lax.scan(backward, terminal.astype(jnp.float32), (gains, increments), reverse=True)
    return smoothed
```

```python
import functools

import jax
import jax.numpy as jnp
from jax import lax
from jax.experimental import pallas as pl
from jax.experimental.pallas import tpu as pltpu
from jax.sharding import PartitionSpec as P

BF16 = jnp.bfloat16
F32 = jnp.float32
LANES = 128
TILE = 256
VMEM_LIMIT = 48 * 1024 * 1024


def params(steps=None):
    return pltpu.CompilerParams(vmem_limit_bytes=VMEM_LIMIT)


def half_width(rows, count):
    used = (count // 2 + 1) * rows
    return used, -(-used // LANES) * LANES


def nt(left, right):
    return lax.dot_general(left, right, (((1,), (1,)), ((), ())), preferred_element_type=F32)


def pack_kernel(count, place_ref, gain_ref, increment_ref, packed_ref):
    rows, width = gain_ref.shape[1:]
    used, half = half_width(rows, count)
    packed_ref[0, :, :width] = gain_ref[0]
    shift = lax.rem(width - place_ref[0] * rows, width)
    turned = pltpu.roll(increment_ref[0], shift, 1)[:, :half]
    column = lax.broadcasted_iota(jnp.int32, turned.shape, 1)
    halved = (column < rows) | (column >= used - rows)
    weight = jnp.where(column < used, jnp.where(halved, 0.5, 1.0), 0.0)
    packed_ref[0, :, width:] = (turned * weight).astype(BF16)


def pack(place, gains, increments, count):
    steps, rows, width = gains.shape
    _, half = half_width(rows, count)
    return pl.pallas_call(
        functools.partial(pack_kernel, count),
        grid_spec=pltpu.PrefetchScalarGridSpec(
            num_scalar_prefetch=1,
            grid=(steps,),
            in_specs=[
                pl.BlockSpec((1, rows, width), lambda i, p: (i, 0, 0)),
                pl.BlockSpec((1, rows, width), lambda i, p: (i, 0, 0)),
            ],
            out_specs=pl.BlockSpec((1, rows, width + half), lambda i, p: (i, 0, 0)),
        ),
        out_shape=jax.ShapeDtypeStruct((steps, rows, width + half), BF16),
        compiler_params=params(),
        name="pack",
    )(place, gains, increments)


def compose_kernel(first, last, place_ref, packed_ref, *refs):
    if first:
        factor_out, own_out, factor_end, half_end, factor, half, middle, total = refs
    else:
        factor_in, half_in, factor_out, own_out, factor_end, half_end, factor, half, middle, total = refs
    count, _, rows, _ = packed_ref.shape
    width = factor.shape[0]
    turn = pl.program_id(0)
    gain = packed_ref[:, 0, :, :width].reshape(width, width)

    def add_increment(block):
        piece = packed_ref[block, 0, :, width:].astype(F32)
        rest = width - piece.shape[1]
        wide = jnp.concatenate([piece, jnp.zeros((rows, rest), F32)], axis=1) if rest else piece
        return pltpu.roll(wide, block * rows, 1) if block else wide

    if first:

        @pl.when(turn == 0)
        def _():
            factor[...] = gain
            for block in range(count):
                half[block * rows:(block + 1) * rows, :] = add_increment(block).astype(BF16)

    else:

        @pl.when(turn == 0)
        def _():
            factor[...] = factor_in[...]
            half[...] = half_in[...]

    def step():
        for j in range(0, width, TILE):
            cols = slice(j, j + TILE)
            middle[:, cols] = jnp.dot(gain, half[:, cols], preferred_element_type=F32).astype(BF16)
            factor[:, cols] = jnp.dot(gain, factor[:, cols], preferred_element_type=F32).astype(BF16)
        for j in range(0, width, TILE):
            total[:, j:j + TILE] = nt(middle[...], gain[j:j + TILE, :])
        for block in range(count):
            span = slice(block * rows, (block + 1) * rows)
            half[span, :] = (total[span, :] + add_increment(block)).astype(BF16)

    if first:
        pl.when(turn > 0)(step)
    else:
        step()

    start = pl.multiple_of(place_ref[0] * rows, 16)
    picked = lax.broadcasted_iota(jnp.int32, (rows, width), 1) == start + lax.broadcasted_iota(
        jnp.int32, (rows, width), 0
    )
    own = half[pl.ds(start, rows), :].astype(F32)
    own_out[0] = own + nt(picked.astype(F32).astype(BF16), half[...])
    factor_out[0] = factor[...]

    @pl.when(turn == pl.num_programs(0) - 1)
    def _():
        factor_end[...] = factor[...]
        if last:
            for j in range(0, width, TILE):
                cols = slice(j, j + TILE)
                whole = half[:, cols].astype(F32) + jnp.swapaxes(half[cols, :].astype(F32), 0, 1)
                half_end[:, cols] = whole
        else:
            half_end[...] = half[...]


def compose(place, packed, state, last):
    count, steps, rows, total_width = packed.shape
    width = count * rows
    first = state is None
    whole = pl.BlockSpec((width, width), lambda i, p: (0, 0))
    in_specs = [pl.BlockSpec((count, 1, rows, total_width), lambda i, p: (0, steps - 1 - i, 0, 0))]
    if not first:
        in_specs += [whole, whole]
    return pl.pallas_call(
        functools.partial(compose_kernel, first, last),
        grid_spec=pltpu.PrefetchScalarGridSpec(
            num_scalar_prefetch=1,
            grid=(steps,),
            in_specs=in_specs,
            out_specs=[
                pl.BlockSpec((1, width, width), lambda i, p: (steps - 1 - i, 0, 0)),
                pl.BlockSpec((1, rows, width), lambda i, p: (steps - 1 - i, 0, 0)),
                whole,
                whole,
            ],
            scratch_shapes=[
                pltpu.VMEM((width, width), BF16),
                pltpu.VMEM((width, width), BF16),
                pltpu.VMEM((width, width), BF16),
                pltpu.VMEM((width, width), F32),
            ],
        ),
        out_shape=[
            jax.ShapeDtypeStruct((steps, width, width), BF16),
            jax.ShapeDtypeStruct((steps, rows, width), F32),
            jax.ShapeDtypeStruct((width, width), BF16),
            jax.ShapeDtypeStruct((width, width), F32 if last else BF16),
        ],
        compiler_params=params(),
        cost_estimate=pl.CostEstimate(
            flops=6 * steps * width**3, bytes_accessed=8 * steps * width * width, transcendentals=0
        ),
        name="compose",
    )(place, packed, *(() if first else state))


def hop_kernel(arrived, factor_ref, increment_ref, *refs):
    covariances, out_ref, covariance, middle = refs[:arrived], refs[arrived], refs[arrived + 1], refs[arrived + 2]
    width = factor_ref.shape[0]
    value = covariances[0][...]
    for extra in covariances[1:]:
        value = value + extra[...]
    covariance[...] = value
    for j in range(0, width, TILE):
        cols = slice(j, j + TILE)
        middle[:, cols] = jnp.dot(factor_ref[...], covariance[:, cols], preferred_element_type=F32).astype(BF16)
    for j in range(0, width, TILE):
        cols = slice(j, j + TILE)
        out_ref[:, cols] = (nt(middle[...], factor_ref[cols, :]) + increment_ref[:, cols]).astype(BF16)


def hop(factor, increment, covariances):
    width = factor.shape[0]
    return pl.pallas_call(
        functools.partial(hop_kernel, len(covariances)),
        out_shape=jax.ShapeDtypeStruct((width, width), BF16),
        scratch_shapes=[pltpu.VMEM((width, width), BF16), pltpu.VMEM((width, width), BF16)],
        compiler_params=params(),
        cost_estimate=pl.CostEstimate(flops=4 * width**3, bytes_accessed=10 * width * width, transcendentals=0),
        name="hop",
    )(factor, increment, *covariances)


def finish_kernel(arrived, place_ref, factor_ref, own_ref, *refs):
    covariances, out_ref, covariance = refs[:arrived], refs[arrived], refs[arrived + 1]
    rows = own_ref.shape[1]

    @pl.when(pl.program_id(0) == 0)
    def _():
        value = covariances[0][...]
        for extra in covariances[1:]:
            value = value + extra[...]
        covariance[...] = value

    start = pl.multiple_of(place_ref[0] * rows, 16)
    mine = factor_ref[0, pl.ds(start, rows), :]
    middle = jnp.dot(mine, covariance[...], preferred_element_type=F32).astype(BF16)
    out_ref[0] = nt(middle, factor_ref[0]) + own_ref[0]


def finish(place, factors, own, covariances):
    steps, rows, width = own.shape
    whole = pl.BlockSpec((width, width), lambda i, p: (0, 0))
    return pl.pallas_call(
        functools.partial(finish_kernel, len(covariances)),
        grid_spec=pltpu.PrefetchScalarGridSpec(
            num_scalar_prefetch=1,
            grid=(steps,),
            in_specs=[
                pl.BlockSpec((1, width, width), lambda i, p: (i, 0, 0)),
                pl.BlockSpec((1, rows, width), lambda i, p: (i, 0, 0)),
            ]
            + [whole] * len(covariances),
            out_specs=pl.BlockSpec((1, rows, width), lambda i, p: (i, 0, 0)),
            scratch_shapes=[pltpu.VMEM((width, width), BF16)],
        ),
        out_shape=jax.ShapeDtypeStruct((steps, rows, width), F32),
        compiler_params=params(),
        name="finish",
    )(place, factors, own, *covariances)


def local(gains, increments, terminal):
    count = lax.axis_size("tile")
    blocks = lax.axis_size("tm")
    steps = gains.shape[0]
    place = lax.axis_index("tile").astype(jnp.int32).reshape(1)
    block = lax.axis_index("tm")
    packed = pack(place, gains, increments, count)
    cut = steps - steps * 5 // 8
    late = lax.all_gather(packed[cut:], "tile")
    early = lax.all_gather(packed[:cut], "tile")
    full_terminal = lax.all_gather(terminal.astype(BF16), "tile", axis=0, tiled=True)
    late_factors, late_own, factor, half = compose(place, late, None, False)
    early_factors, early_own, factor, increment = compose(place, early, (factor, half), True)
    covariances = [jnp.where(block == blocks - 1, full_terminal, jnp.zeros_like(full_terminal))]
    for turn in range(blocks - 1, 0, -1):
        covariances.append(lax.ppermute(hop(factor, increment, covariances), "tm", [(turn, turn - 1)]))
    return jnp.concatenate(
        [
            finish(place, early_factors, early_own, covariances),
            finish(place, late_factors, late_own, covariances),
        ]
    )


def solution(mesh):
    return jax.shard_map(
        local,
        mesh=mesh,
        in_specs=(P("tm", "tile", None), P("tm", "tile", None), P("tile", None)),
        out_specs=P("tm", "tile", None),
        check_vma=False,
    )
```

```python
import functools
import math

import jax
import jax.numpy as jnp
from jax import lax
from jax.experimental import pallas as pl
from jax.experimental.pallas import tpu as pltpu
from jax.sharding import PartitionSpec as P

BF16 = jnp.bfloat16
F32 = jnp.float32
LANES = 128
TILE = 256
LINE = 4
MIB = 1024 * 1024


def half_width(rows, count):
    used = (count // 2 + 1) * rows
    return used, -(-used // LANES) * LANES


def nt(left, right):
    return lax.dot_general(left, right, (((1,), (1,)), ((), ())), preferred_element_type=F32)


def pack_kernel(count, place_ref, gain_ref, increment_ref, packed_ref):
    rows, width = gain_ref.shape[1:]
    used, half = half_width(rows, count)
    packed_ref[0, :, :width] = gain_ref[0]
    shift = lax.rem(width - place_ref[0] * rows, width)
    turned = pltpu.roll(increment_ref[0], shift, 1)[:, :half]
    column = lax.broadcasted_iota(jnp.int32, turned.shape, 1)
    halved = (column < rows) | (column >= used - rows)
    weight = jnp.where(column < used, jnp.where(halved, 0.5, 1.0), 0.0)
    packed_ref[0, :, width:] = (turned * weight).astype(BF16)


def pack(places, gains, increments, low, high):
    count = places.shape[0]
    steps, rows, width = gains.shape
    _, half = half_width(rows, count)
    return pl.pallas_call(
        functools.partial(pack_kernel, count),
        grid_spec=pltpu.PrefetchScalarGridSpec(
            num_scalar_prefetch=1,
            grid=(high - low,),
            in_specs=[
                pl.BlockSpec((1, rows, width), lambda i, p: (low + i, 0, 0)),
                pl.BlockSpec((1, rows, width), lambda i, p: (low + i, 0, 0)),
            ],
            out_specs=pl.BlockSpec((1, rows, width + half), lambda i, p: (i, 0, 0)),
        ),
        out_shape=jax.ShapeDtypeStruct((high - low, rows, width + half), BF16),
        compiler_params=pltpu.CompilerParams(vmem_limit_bytes=8 * MIB),
        name="pack",
    )(places, gains, increments)


def compose_kernel(count, first, places_ref, *refs):
    shards, refs = refs[:count], refs[count:]
    if not first:
        factor_in, half_in, refs = refs[0], refs[1], refs[4:]
    factor_out, own_out, factor_end, half_end, gain, factor, half, middle, total = refs
    rows = shards[0].shape[1]
    width = factor.shape[0]
    turn = pl.program_id(0)
    starts = [pl.multiple_of(places_ref[i] * rows, 16) for i in range(count)]
    for start, shard in zip(starts, shards):
        gain[pl.ds(start, rows), :] = shard[0, :, :width]

    def increment(start, shard):
        piece = shard[0, :, width:].astype(F32)
        rest = width - piece.shape[1]
        wide = jnp.concatenate([piece, jnp.zeros((rows, rest), F32)], axis=1) if rest else piece
        return pltpu.roll(wide, start, 1)

    @pl.when(turn == 0)
    def _():
        if first:
            factor[...] = gain[...]
            for start, shard in zip(starts, shards):
                half[pl.ds(start, rows), :] = increment(start, shard).astype(BF16)
        else:
            factor[...] = factor_in[...]
            half[...] = half_in[...]

    def step():
        for j in range(0, width, TILE):
            cols = slice(j, j + TILE)
            middle[:, cols] = jnp.dot(gain[...], half[:, cols], preferred_element_type=F32).astype(BF16)
            factor[:, cols] = jnp.dot(gain[...], factor[:, cols], preferred_element_type=F32).astype(BF16)
        for j in range(0, width, TILE):
            total[:, j:j + TILE] = nt(middle[...], gain[j:j + TILE, :])
        for start, shard in zip(starts, shards):
            span = pl.ds(start, rows)
            half[span, :] = (total[span, :] + increment(start, shard)).astype(BF16)

    if first:
        pl.when(turn > 0)(step)
    else:
        step()

    picked = lax.broadcasted_iota(jnp.int32, (rows, width), 1) == starts[0] + lax.broadcasted_iota(
        jnp.int32, (rows, width), 0
    )
    own = half[pl.ds(starts[0], rows), :].astype(F32)
    own_out[0] = own + nt(jnp.where(picked, 1.0, 0.0).astype(BF16), half[...])
    factor_out[0] = factor[...]

    @pl.when(turn == pl.num_programs(0) - 1)
    def _():
        factor_end[...] = factor[...]
        half_end[...] = half[...]


def compose(places, shards, state, low, steps):
    count = len(shards)
    turns, rows, packed_width = shards[0].shape
    width = count * rows
    first = state is None
    whole = pl.BlockSpec((width, width), lambda i, p: (0, 0))
    anywhere = pl.BlockSpec(memory_space=pl.ANY)
    in_specs = [pl.BlockSpec((1, rows, packed_width), lambda i, p: (turns - 1 - i, 0, 0))] * count
    if not first:
        in_specs += [whole, whole, anywhere, anywhere]
    return pl.pallas_call(
        functools.partial(compose_kernel, count, first),
        grid_spec=pltpu.PrefetchScalarGridSpec(
            num_scalar_prefetch=1,
            grid=(turns,),
            in_specs=in_specs,
            out_specs=[
                pl.BlockSpec((1, width, width), lambda i, p: (low + turns - 1 - i, 0, 0)),
                pl.BlockSpec((1, rows, width), lambda i, p: (low + turns - 1 - i, 0, 0)),
                whole,
                whole,
            ],
            scratch_shapes=[pltpu.VMEM((width, width), BF16) for _ in range(4)]
            + [pltpu.VMEM((width, width), F32)],
        ),
        out_shape=[
            jax.ShapeDtypeStruct((steps, width, width), BF16),
            jax.ShapeDtypeStruct((steps, rows, width), F32),
            jax.ShapeDtypeStruct((width, width), BF16),
            jax.ShapeDtypeStruct((width, width), BF16),
        ],
        input_output_aliases={} if first else {count + 3: 0, count + 4: 1},
        compiler_params=pltpu.CompilerParams(vmem_limit_bytes=32 * MIB),
        cost_estimate=pl.CostEstimate(
            flops=6 * turns * width**3, bytes_accessed=8 * turns * width * width, transcendentals=0
        ),
        name="compose",
    )(places, *shards, *(() if first else (state[2], state[3], state[0], state[1])))


def arrived_sum(refs):
    value = refs[0][...]
    for extra in refs[1:]:
        value = value + extra[...]
    return value


def hop_kernel(arrived, factor_ref, half_ref, *refs):
    out_ref, covariance, middle = refs[arrived:]
    width = factor_ref.shape[0]
    covariance[...] = arrived_sum(refs[:arrived])
    for j in range(0, width, TILE):
        cols = slice(j, j + TILE)
        middle[:, cols] = jnp.dot(factor_ref[...], covariance[:, cols], preferred_element_type=F32).astype(BF16)
    for j in range(0, width, TILE):
        cols = slice(j, j + TILE)
        out_ref[:, cols] = (nt(middle[...], factor_ref[cols, :]) + half_ref[:, cols].astype(F32)).astype(BF16)


def hop(factor, half, halves):
    width = factor.shape[0]
    return pl.pallas_call(
        functools.partial(hop_kernel, len(halves)),
        out_shape=jax.ShapeDtypeStruct((width, width), BF16),
        scratch_shapes=[pltpu.VMEM((width, width), BF16), pltpu.VMEM((width, width), BF16)],
        compiler_params=pltpu.CompilerParams(vmem_limit_bytes=20 * MIB),
        cost_estimate=pl.CostEstimate(flops=4 * width**3, bytes_accessed=10 * width * width, transcendentals=0),
        name="hop",
    )(factor, half, *halves)


def finish_kernel(arrived, places_ref, factor_ref, own_ref, *refs):
    out_ref, half, identity, covariance = refs[arrived:]
    rows = own_ref.shape[1]
    width = covariance.shape[0]

    @pl.when(pl.program_id(0) == 0)
    def _():
        half[...] = arrived_sum(refs[:arrived])
        row = lax.broadcasted_iota(jnp.int32, (width, width), 0)
        column = lax.broadcasted_iota(jnp.int32, (width, width), 1)
        identity[...] = jnp.where(row == column, 1.0, 0.0).astype(BF16)
        for j in range(0, width, TILE):
            cols = slice(j, j + TILE)
            turned = nt(identity[...], half[cols, :])
            covariance[:, cols] = (half[:, cols].astype(F32) + turned).astype(BF16)

    start = pl.multiple_of(places_ref[0] * rows, 16)
    mine = factor_ref[0, pl.ds(start, rows), :]
    middle = jnp.dot(mine, covariance[...], preferred_element_type=F32).astype(BF16)
    out_ref[0] = nt(middle, factor_ref[0]) + own_ref[0]


def finish(places, factors, own, halves):
    steps, rows, width = own.shape
    whole = pl.BlockSpec((width, width), lambda i, p: (0, 0))
    return pl.pallas_call(
        functools.partial(finish_kernel, len(halves)),
        grid_spec=pltpu.PrefetchScalarGridSpec(
            num_scalar_prefetch=1,
            grid=(steps,),
            in_specs=[
                pl.BlockSpec((1, width, width), lambda i, p: (i, 0, 0)),
                pl.BlockSpec((1, rows, width), lambda i, p: (i, 0, 0)),
            ]
            + [whole] * len(halves),
            out_specs=pl.BlockSpec((1, rows, width), lambda i, p: (i, 0, 0)),
            scratch_shapes=[pltpu.VMEM((width, width), BF16)] * 3,
        ),
        out_shape=jax.ShapeDtypeStruct((steps, rows, width), F32),
        compiler_params=pltpu.CompilerParams(vmem_limit_bytes=24 * MIB),
        name="finish",
    )(places, factors, own, *halves)


def pieces(steps):
    if steps < 8:
        return [(0, steps, False)]
    bulk = (steps - steps // 4) // 2
    rest = steps - 2 * bulk
    return [
        (steps - bulk, steps, False),
        (rest, rest + bulk, False),
        (rest // 2, rest, True),
        (0, rest // 2, False),
    ]


def local(gains, increments, terminal):
    count = lax.axis_size("tile")
    blocks = lax.axis_size("tm")
    line = math.gcd(count, LINE)
    across = count // line
    steps = gains.shape[0]
    place = lax.axis_index("tile").astype(jnp.int32)
    block = lax.axis_index("tm")

    def shifted(array, along, over):
        pairs = [
            (a * across + b, (a + along) % line * across + (b + over) % across)
            for a in range(line)
            for b in range(across)
        ]
        return lax.ppermute(array, "tile", pairs)

    places = jnp.stack(
        [
            (place // across - i + line) % line * across + (place % across - j + across) % across
            for i in range(line)
            for j in range(across)
        ]
    )
    full_terminal = lax.all_gather(terminal.astype(BF16), "tile", axis=0, tiled=True)
    state = None
    for low, high, across_first in pieces(steps):
        own = pack(places, gains, increments, low, high)
        shards = {}
        if across_first:
            for j in range(across):
                shards[0, j] = shifted(own, 0, j) if j else own
            for i in range(1, line):
                for j in range(across):
                    shards[i, j] = shifted(shards[0, j], i, 0)
        else:
            for i in range(line):
                shards[i, 0] = shifted(own, i, 0) if i else own
                for j in range(1, across):
                    shards[i, j] = shifted(shards[i, 0], 0, j)
        ordered = [shards[i, j] for i in range(line) for j in range(across)]
        state = compose(places, ordered, state, low, steps)
    factors, own, factor, half = state
    halves = [jnp.where(block == blocks - 1, 0.5, 0.0).astype(BF16) * full_terminal]
    for turn in range(blocks - 1, 0, -1):
        halves.append(lax.ppermute(hop(factor, half, halves), "tm", [(turn, turn - 1)]))
    return finish(places, factors, own, halves)


def solution(mesh):
    return jax.shard_map(
        local,
        mesh=mesh,
        in_specs=(P("tm", "tile", None), P("tm", "tile", None), P("tile", None)),
        out_specs=P("tm", "tile", None),
        check_vma=False,
    )
```

```python
import functools
import math

import jax
import jax.numpy as jnp
from jax import lax
from jax.experimental import pallas as pl
from jax.experimental.pallas import tpu as pltpu
from jax.sharding import PartitionSpec as P

BF16 = jnp.bfloat16
F32 = jnp.float32
LANES = 128
TILE = 256
LINE = 4
MIB = 1024 * 1024


def half_width(rows, count):
    used = (count // 2 + 1) * rows
    return used, -(-used // LANES) * LANES


def nt(left, right):
    return lax.dot_general(left, right, (((1,), (1,)), ((), ())), preferred_element_type=F32)


def packed_half(increment, place, count):
    rows, width = increment.shape
    used, half = half_width(rows, count)
    turned = pltpu.roll(increment, lax.rem(width - place * rows, width), 1)[:, :half]
    column = lax.broadcasted_iota(jnp.int32, turned.shape, 1)
    halved = (column < rows) | (column >= used - rows)
    weight = jnp.where(column < used, jnp.where(halved, 0.5, 1.0), 0.0)
    return (turned * weight).astype(BF16)


def unpacked_half(piece, start, width):
    piece = piece.astype(F32)
    rest = width - piece.shape[1]
    wide = jnp.concatenate([piece, jnp.zeros((piece.shape[0], rest), F32)], axis=1) if rest else piece
    return pltpu.roll(wide, start, 1)


def pack_kernel(count, place_ref, gain_ref, increment_ref, packed_ref):
    width = gain_ref.shape[2]
    packed_ref[0, :, :width] = gain_ref[0]
    packed_ref[0, :, width:] = packed_half(increment_ref[0], place_ref[0], count)


def pack(place, gains, increments, count, low, high):
    steps, rows, width = gains.shape
    _, half = half_width(rows, count)
    return pl.pallas_call(
        functools.partial(pack_kernel, count),
        grid_spec=pltpu.PrefetchScalarGridSpec(
            num_scalar_prefetch=1,
            grid=(high - low,),
            in_specs=[
                pl.BlockSpec((1, rows, width), lambda i, p: (low + i, 0, 0)),
                pl.BlockSpec((1, rows, width), lambda i, p: (low + i, 0, 0)),
            ],
            out_specs=pl.BlockSpec((1, rows, width + half), lambda i, p: (i, 0, 0)),
        ),
        out_shape=jax.ShapeDtypeStruct((high - low, rows, width + half), BF16),
        compiler_params=pltpu.CompilerParams(vmem_limit_bytes=8 * MIB),
        name="pack",
    )(place, gains, increments)


def pack_terminal_kernel(count, place_ref, terminal_ref, packed_ref):
    packed_ref[...] = packed_half(terminal_ref[...], place_ref[0], count)


def pack_terminal(place, terminal, count):
    rows, width = terminal.shape
    _, half = half_width(rows, count)
    return pl.pallas_call(
        functools.partial(pack_terminal_kernel, count),
        in_specs=[pl.BlockSpec(memory_space=pltpu.SMEM), pl.BlockSpec(memory_space=pltpu.VMEM)],
        out_shape=jax.ShapeDtypeStruct((rows, half), BF16),
        name="pack_terminal",
    )(place, terminal)


def compose_kernel(groups, first, last_ref, places_ref, *refs):
    blocks, refs = refs[:groups], refs[groups:]
    if first:
        ends, refs = refs[:groups], refs[groups:]
    else:
        factor_in, half_in, refs = refs[0], refs[1], refs[4:]
    factor_out, own_out, factor_end, half_end, gain, factor, half, middle, total = refs
    line, _, rows, _ = blocks[0].shape
    width = factor.shape[0]
    turn = pl.program_id(0)
    starts = [
        [pl.multiple_of(places_ref[1 + j * line + i] * rows, 16) for i in range(line)] for j in range(groups)
    ]
    spots = [(j, i, starts[j][i]) for j in range(groups) for i in range(line)]
    for j, i, start in spots:
        gain[pl.ds(start, rows), :] = blocks[j][i, 0, :, :width]

    @pl.when(turn == 0)
    def _():
        if first:
            factor[...] = gain[...]
            scale = jnp.where(last_ref[0] == 1, 1.0, 0.0)
            for j, i, start in spots:
                half[pl.ds(start, rows), :] = (unpacked_half(ends[j][i], start, width) * scale).astype(BF16)
        else:
            factor[...] = factor_in[...]
            half[...] = half_in[...]

    def extend():
        for j in range(0, width, TILE):
            cols = slice(j, j + TILE)
            factor[:, cols] = jnp.dot(gain[...], factor[:, cols], preferred_element_type=F32).astype(BF16)

    if first:
        pl.when(turn > 0)(extend)
    else:
        extend()
    for j in range(0, width, TILE):
        cols = slice(j, j + TILE)
        middle[:, cols] = jnp.dot(gain[...], half[:, cols], preferred_element_type=F32).astype(BF16)
    for j in range(0, width, TILE):
        total[:, j:j + TILE] = nt(middle[...], gain[j:j + TILE, :])
    for j, i, start in spots:
        span = pl.ds(start, rows)
        half[span, :] = (total[span, :] + unpacked_half(blocks[j][i, 0, :, width:], start, width)).astype(BF16)

    mine = pl.multiple_of(places_ref[0] * rows, 16)
    picked = lax.broadcasted_iota(jnp.int32, (rows, width), 1) == mine + lax.broadcasted_iota(
        jnp.int32, (rows, width), 0
    )
    own = half[pl.ds(mine, rows), :].astype(F32)
    own_out[0] = own + nt(jnp.where(picked, 1.0, 0.0).astype(BF16), half[...])
    factor_out[0] = factor[...]

    @pl.when(turn == pl.num_programs(0) - 1)
    def _():
        factor_end[...] = factor[...]
        half_end[...] = half[...]


def compose(last, places, blocks, ends, state, low, steps):
    groups = len(blocks)
    line, turns, rows, packed_width = blocks[0].shape
    width = line * groups * rows
    first = state is None
    whole = pl.BlockSpec((width, width), lambda i, *p: (0, 0))
    anywhere = pl.BlockSpec(memory_space=pl.ANY)
    in_specs = [pl.BlockSpec((line, 1, rows, packed_width), lambda i, *p: (0, turns - 1 - i, 0, 0))] * groups
    if first:
        in_specs += [pl.BlockSpec(ends[0].shape, lambda i, *p: (0, 0, 0))] * groups
    else:
        in_specs += [whole, whole, anywhere, anywhere]
    return pl.pallas_call(
        functools.partial(compose_kernel, groups, first),
        grid_spec=pltpu.PrefetchScalarGridSpec(
            num_scalar_prefetch=2,
            grid=(turns,),
            in_specs=in_specs,
            out_specs=[
                pl.BlockSpec((1, width, width), lambda i, *p: (low + turns - 1 - i, 0, 0)),
                pl.BlockSpec((1, rows, width), lambda i, *p: (low + turns - 1 - i, 0, 0)),
                whole,
                whole,
            ],
            scratch_shapes=[pltpu.VMEM((width, width), BF16) for _ in range(4)]
            + [pltpu.VMEM((width, width), F32)],
        ),
        out_shape=[
            jax.ShapeDtypeStruct((steps, width, width), BF16),
            jax.ShapeDtypeStruct((steps, rows, width), F32),
            jax.ShapeDtypeStruct((width, width), BF16),
            jax.ShapeDtypeStruct((width, width), BF16),
        ],
        input_output_aliases={} if first else {groups + 4: 0, groups + 5: 1},
        compiler_params=pltpu.CompilerParams(vmem_limit_bytes=32 * MIB),
        cost_estimate=pl.CostEstimate(
            flops=6 * turns * width**3, bytes_accessed=8 * turns * width * width, transcendentals=0
        ),
        name="compose",
    )(last, places, *blocks, *(ends if first else (state[2], state[3], state[0], state[1])))


def arrived_sum(refs):
    value = refs[0][...]
    for extra in refs[1:]:
        value = value + extra[...]
    return value


def hop_kernel(arrived, factor_ref, half_ref, *refs):
    out_ref, covariance, middle = refs[arrived:]
    width = factor_ref.shape[0]
    covariance[...] = arrived_sum(refs[:arrived])
    for j in range(0, width, TILE):
        cols = slice(j, j + TILE)
        middle[:, cols] = jnp.dot(factor_ref[...], covariance[:, cols], preferred_element_type=F32).astype(BF16)
    for j in range(0, width, TILE):
        cols = slice(j, j + TILE)
        out_ref[:, cols] = (nt(middle[...], factor_ref[cols, :]) + half_ref[:, cols].astype(F32)).astype(BF16)


def hop(factor, half, halves):
    width = factor.shape[0]
    return pl.pallas_call(
        functools.partial(hop_kernel, len(halves)),
        out_shape=jax.ShapeDtypeStruct((width, width), BF16),
        scratch_shapes=[pltpu.VMEM((width, width), BF16), pltpu.VMEM((width, width), BF16)],
        compiler_params=pltpu.CompilerParams(vmem_limit_bytes=20 * MIB),
        cost_estimate=pl.CostEstimate(flops=4 * width**3, bytes_accessed=10 * width * width, transcendentals=0),
        name="hop",
    )(factor, half, *halves)


def finish_kernel(arrived, places_ref, factor_ref, own_ref, *refs):
    out_ref, half, identity, covariance = refs[arrived:]
    rows = own_ref.shape[1]
    width = covariance.shape[0]

    @pl.when(pl.program_id(0) == 0)
    def _():
        half[...] = arrived_sum(refs[:arrived])
        row = lax.broadcasted_iota(jnp.int32, (width, width), 0)
        column = lax.broadcasted_iota(jnp.int32, (width, width), 1)
        identity[...] = jnp.where(row == column, 1.0, 0.0).astype(BF16)
        for j in range(0, width, TILE):
            cols = slice(j, j + TILE)
            turned = nt(identity[...], half[cols, :])
            covariance[:, cols] = (half[:, cols].astype(F32) + turned).astype(BF16)

    start = pl.multiple_of(places_ref[0] * rows, 16)
    mine = factor_ref[0, pl.ds(start, rows), :]
    middle = jnp.dot(mine, covariance[...], preferred_element_type=F32).astype(BF16)
    out_ref[0] = nt(middle, factor_ref[0]) + own_ref[0]


def finish(places, factors, own, halves):
    steps, rows, width = own.shape
    whole = pl.BlockSpec((width, width), lambda i, p: (0, 0))
    return pl.pallas_call(
        functools.partial(finish_kernel, len(halves)),
        grid_spec=pltpu.PrefetchScalarGridSpec(
            num_scalar_prefetch=1,
            grid=(steps,),
            in_specs=[
                pl.BlockSpec((1, width, width), lambda i, p: (i, 0, 0)),
                pl.BlockSpec((1, rows, width), lambda i, p: (i, 0, 0)),
            ]
            + [whole] * len(halves),
            out_specs=pl.BlockSpec((1, rows, width), lambda i, p: (i, 0, 0)),
            scratch_shapes=[pltpu.VMEM((width, width), BF16)] * 3,
        ),
        out_shape=jax.ShapeDtypeStruct((steps, rows, width), F32),
        compiler_params=pltpu.CompilerParams(vmem_limit_bytes=24 * MIB),
        name="finish",
    )(places, factors, own, *halves)


def pieces(steps):
    if steps < 8:
        return [(0, steps, False)]
    small = steps // 8
    cuts = [steps, 6 * small, 4 * small, 2 * small, small, 0]
    return [(low, high, turn == 3) for turn, (high, low) in enumerate(zip(cuts, cuts[1:]))]


def local(gains, increments, terminal):
    count = lax.axis_size("tile")
    blocks = lax.axis_size("tm")
    line = math.gcd(count, LINE)
    across = count // line
    steps = gains.shape[0]
    place = lax.axis_index("tile").astype(jnp.int32)
    last = (lax.axis_index("tm") == blocks - 1).astype(jnp.int32).reshape(1)
    lines = [[a * across + b for a in range(line)] for b in range(across)]

    def shifted(array, over):
        pairs = [
            (a * across + b, a * across + (b + over) % across) for a in range(line) for b in range(across)
        ]
        return lax.ppermute(array, "tile", pairs)

    def gathered(array):
        return lax.all_gather(array, "tile", axis_index_groups=lines)

    def both(array, across_first):
        if across_first:
            return [gathered(shifted(array, j) if j else array) for j in range(across)]
        whole = gathered(array)
        return [shifted(whole, j) if j else whole for j in range(across)]

    places = jnp.stack(
        [place]
        + [i * across + (place % across - j + across) % across for j in range(across) for i in range(line)]
    )
    ends = both(pack_terminal(place.reshape(1), terminal, count), False)
    state = None
    for low, high, across_first in pieces(steps):
        own = pack(place.reshape(1), gains, increments, count, low, high)
        state = compose(last, places, both(own, across_first), ends, state, low, steps)
    factors, own, factor, half = state
    halves = [lax.ppermute(half, "tm", [(blocks - 1, blocks - 2)])]
    for turn in range(blocks - 2, 0, -1):
        halves.append(lax.ppermute(hop(factor, half, halves), "tm", [(turn, turn - 1)]))
    return finish(place.reshape(1), factors, own, halves)


def solution(mesh):
    return jax.shard_map(
        local,
        mesh=mesh,
        in_specs=(P("tm", "tile", None), P("tm", "tile", None), P("tile", None)),
        out_specs=P("tm", "tile", None),
        check_vma=False,
    )
```

```python
import functools
import math

import jax
import jax.numpy as jnp
from jax import lax
from jax.experimental import pallas as pl
from jax.experimental.pallas import tpu as pltpu
from jax.sharding import PartitionSpec as P

BF16 = jnp.bfloat16
F32 = jnp.float32
LANES = 128
TILE = 256
LINE = 4
MIB = 1024 * 1024


def half_width(rows, count):
    used = (count // 2 + 1) * rows
    return used, -(-used // LANES) * LANES


def nt(left, right):
    return lax.dot_general(left, right, (((1,), (1,)), ((), ())), preferred_element_type=F32)


def packed_half(increment, place, count):
    rows, width = increment.shape
    used, half = half_width(rows, count)
    turned = pltpu.roll(increment, lax.rem(width - place * rows, width), 1)[:, :half]
    column = lax.broadcasted_iota(jnp.int32, turned.shape, 1)
    halved = (column < rows) | (column >= used - rows)
    weight = jnp.where(column < used, jnp.where(halved, 0.5, 1.0), 0.0)
    return (turned * weight).astype(BF16)


def unpacked_half(piece, start, width):
    piece = piece.astype(F32)
    rest = width - piece.shape[1]
    wide = jnp.concatenate([piece, jnp.zeros((piece.shape[0], rest), F32)], axis=1) if rest else piece
    return pltpu.roll(wide, start, 1)


def pack_kernel(count, low, high, place_ref, gain_ref, increment_ref, *refs):
    packed_ref = refs[-1]
    width = gain_ref.shape[2]
    stride = width + half_width(gain_ref.shape[1], count)[1]
    for step in range(high - low):
        base = step * stride
        packed_ref[:, base:base + width] = gain_ref[step]
        packed_ref[:, base + width:base + stride] = packed_half(increment_ref[step], place_ref[0], count)
    if len(refs) > 1:
        packed_ref[:, (high - low) * stride:] = packed_half(refs[0][...], place_ref[0], count)


def pack(place, gains, increments, terminal, count, low, high):
    rows, width = gains.shape[1:]
    half = half_width(rows, count)[1]
    ends = [] if terminal is None else [terminal]
    lanes = (high - low) * (width + half) + half * len(ends)
    return pl.pallas_call(
        functools.partial(pack_kernel, count, low, high),
        in_specs=[pl.BlockSpec(memory_space=pltpu.SMEM)] + [pl.BlockSpec(memory_space=pltpu.VMEM)] * (2 + len(ends)),
        out_specs=pl.BlockSpec(memory_space=pltpu.VMEM),
        out_shape=jax.ShapeDtypeStruct((rows, lanes), BF16),
        compiler_params=pltpu.CompilerParams(vmem_limit_bytes=24 * MIB),
        name="pack",
    )(place, gains[low:high], increments[low:high], *ends)


def compose_kernel(lines, parts, first, last_ref, places_ref, *refs):
    sizes = [lines[j] for j in range(len(lines))]
    blocks = []
    for size in sizes:
        blocks.append(refs[:size])
        refs = refs[size:]
    ends = []
    if first:
        for _ in range(parts):
            ends.append([])
            for size in sizes:
                ends[-1].append(refs[:size])
                refs = refs[size:]
    else:
        factor_in, half_in, refs = refs[0], refs[1], refs[5:]
    factor_out, own_out, mine_out, factor_end, half_end, gain, factor, half, middle, total = refs
    width = factor.shape[0]
    turn = pl.program_id(0)
    spots = []
    for j, group in enumerate(blocks):
        for n, ref in enumerate(group):
            inner = ref.shape[0] if len(ref.shape) == 3 else 1
            for i in range(inner):
                spots.append((j, n, i, len(ref.shape) == 3))
    rows = width // len(spots)
    starts = [pl.multiple_of(places_ref[1 + k] * rows, 16) for k in range(len(spots))]

    def lanes(refs_of, spot, cut):
        j, n, i, stacked = spot
        return refs_of[j][n][i, :, cut] if stacked else refs_of[j][n][:, cut]

    for spot, start in zip(spots, starts):
        gain[pl.ds(start, rows), :] = lanes(blocks, spot, slice(0, width))

    @pl.when(turn == 0)
    def _():
        if first:
            factor[...] = gain[...]
            scale = jnp.where(last_ref[0] == 1, 1.0, 0.0)
            for spot, start in zip(spots, starts):
                piece = jnp.concatenate([lanes(end, spot, slice(None)) for end in ends], axis=1)
                half[pl.ds(start, rows), :] = (unpacked_half(piece, start, width) * scale).astype(BF16)
        else:
            factor[...] = factor_in[...]
            half[...] = half_in[...]

    def extend():
        for j in range(0, width, TILE):
            cols = slice(j, j + TILE)
            factor[:, cols] = jnp.dot(gain[...], factor[:, cols], preferred_element_type=F32).astype(BF16)

    if first:
        pl.when(turn > 0)(extend)
    else:
        extend()
    for j in range(0, width, TILE):
        cols = slice(j, j + TILE)
        middle[:, cols] = jnp.dot(gain[...], half[:, cols], preferred_element_type=F32).astype(BF16)
    for j in range(0, width, TILE):
        total[:, j:j + TILE] = nt(middle[...], gain[j:j + TILE, :])
    for spot, start in zip(spots, starts):
        span = pl.ds(start, rows)
        piece = lanes(blocks, spot, slice(width, None))
        half[span, :] = (total[span, :] + unpacked_half(piece, start, width)).astype(BF16)

    mine = pl.multiple_of(places_ref[0] * rows, 16)
    picked = lax.broadcasted_iota(jnp.int32, (rows, width), 1) == mine + lax.broadcasted_iota(
        jnp.int32, (rows, width), 0
    )
    own = half[pl.ds(mine, rows), :].astype(F32)
    own_out[0] = own + nt(jnp.where(picked, 1.0, 0.0).astype(BF16), half[...])
    mine_out[0] = factor[pl.ds(mine, rows), :]
    factor_out[0] = factor[...]

    @pl.when(turn == pl.num_programs(0) - 1)
    def _():
        factor_end[...] = factor[...]
        half_end[...] = half[...]


def compose(last, places, blocks, state, low, turns, steps):
    lines = [len(group) for group in blocks]
    flat = [block for group in blocks for block in group]
    rows = flat[0].shape[-2]
    width = rows * sum(block.shape[0] if block.ndim == 3 else 1 for block in flat)
    half = half_width(rows, width // rows)[1]
    stride = width + half
    first = state is None
    whole = pl.BlockSpec((width, width), lambda i, *p: (0, 0))
    anywhere = pl.BlockSpec(memory_space=pl.ANY)

    def spec(block, size, place):
        if block.ndim == 3:
            return pl.BlockSpec((block.shape[0], rows, size), lambda i, *p: (0, 0, place(i)))
        return pl.BlockSpec((rows, size), lambda i, *p: (0, place(i)))

    in_specs = [spec(block, stride, lambda i: turns - 1 - i) for block in flat]
    args = list(flat)
    parts = half // math.gcd(turns * stride, half)
    if first:
        for n in range(parts):
            at = turns * stride * parts // half + n
            in_specs += [spec(block, half // parts, lambda i, at=at: at) for block in flat]
            args += flat
    else:
        in_specs += [whole, whole, anywhere, anywhere, anywhere]
        args += [state[3], state[4], state[0], state[1], state[2]]
    base = 2 + len(flat) + 2
    return pl.pallas_call(
        functools.partial(compose_kernel, lines, parts, first),
        grid_spec=pltpu.PrefetchScalarGridSpec(
            num_scalar_prefetch=2,
            grid=(turns,),
            in_specs=in_specs,
            out_specs=[
                pl.BlockSpec((1, width, width), lambda i, *p: (low + turns - 1 - i, 0, 0)),
                pl.BlockSpec((1, rows, width), lambda i, *p: (low + turns - 1 - i, 0, 0)),
                pl.BlockSpec((1, rows, width), lambda i, *p: (low + turns - 1 - i, 0, 0)),
                whole,
                whole,
            ],
            scratch_shapes=[pltpu.VMEM((width, width), BF16) for _ in range(4)]
            + [pltpu.VMEM((width, width), F32)],
        ),
        out_shape=[
            jax.ShapeDtypeStruct((steps, width, width), BF16),
            jax.ShapeDtypeStruct((steps, rows, width), F32),
            jax.ShapeDtypeStruct((steps, rows, width), BF16),
            jax.ShapeDtypeStruct((width, width), BF16),
            jax.ShapeDtypeStruct((width, width), BF16),
        ],
        input_output_aliases={} if first else {base: 0, base + 1: 1, base + 2: 2},
        compiler_params=pltpu.CompilerParams(vmem_limit_bytes=32 * MIB),
        cost_estimate=pl.CostEstimate(
            flops=6 * turns * width**3, bytes_accessed=8 * turns * width * width, transcendentals=0
        ),
        name="compose",
    )(last, places, *args)


def upper_blocks(width):
    return [(a, b) for a in range(0, width, TILE) for b in range(a, width, TILE)]


def identity(size):
    row = lax.broadcasted_iota(jnp.int32, (size, size), 0)
    column = lax.broadcasted_iota(jnp.int32, (size, size), 1)
    return jnp.where(row == column, 1.0, 0.0).astype(BF16)


def fold(half_ref, packed_ref):
    one = identity(TILE)
    for n, (a, b) in enumerate(upper_blocks(half_ref.shape[0])):
        block = half_ref[a:a + TILE, b:b + TILE]
        if a != b:
            block = block.astype(F32) + nt(one, half_ref[b:b + TILE, a:a + TILE])
        packed_ref[n] = block.astype(BF16)


def arrived_sum(refs, n):
    value = refs[0][n]
    for extra in refs[1:]:
        value = value + extra[n]
    return value


def fold_kernel(half_ref, packed_ref):
    fold(half_ref, packed_ref)


def hop_kernel(arrived, factor_ref, half_ref, *refs):
    out_ref, covariance, middle, ahead = refs[arrived:]
    width = factor_ref.shape[0]
    for n, (a, b) in enumerate(upper_blocks(width)):
        covariance[a:a + TILE, b:b + TILE] = arrived_sum(refs[:arrived], n)
    for j in range(0, width, TILE):
        cols = slice(j, j + TILE)
        middle[:, cols] = jnp.dot(
            factor_ref[:, :j + TILE], covariance[:j + TILE, cols], preferred_element_type=F32
        ).astype(BF16)
    for j in range(0, width, TILE):
        cols = slice(j, j + TILE)
        ahead[:, cols] = (nt(middle[...], factor_ref[cols, :]) + half_ref[:, cols].astype(F32)).astype(BF16)
    fold(ahead, out_ref)


def hop(factor, half, packed):
    width = factor.shape[0]
    shape = (len(upper_blocks(width)), TILE, TILE)
    square = pltpu.VMEM((width, width), BF16)
    if not packed:
        return pl.pallas_call(
            fold_kernel,
            out_shape=jax.ShapeDtypeStruct(shape, BF16),
            compiler_params=pltpu.CompilerParams(vmem_limit_bytes=16 * MIB),
            name="fold",
        )(half)
    return pl.pallas_call(
        functools.partial(hop_kernel, len(packed)),
        out_shape=jax.ShapeDtypeStruct(shape, BF16),
        scratch_shapes=[square, square, square],
        compiler_params=pltpu.CompilerParams(vmem_limit_bytes=20 * MIB),
        cost_estimate=pl.CostEstimate(flops=4 * width**3, bytes_accessed=10 * width * width, transcendentals=0),
        name="hop",
    )(factor, half, *packed)


def finish_kernel(arrived, factor_ref, own_ref, mine_ref, *refs):
    out_ref, covariance, middle = refs[arrived:]
    turn = pl.program_id(0)
    rows = own_ref.shape[1]
    steps = mine_ref.shape[0]
    width = covariance.shape[0]

    @pl.when(turn == 0)
    def _():
        one = identity(TILE)
        for n, (a, b) in enumerate(upper_blocks(width)):
            block = arrived_sum(refs[:arrived], n)
            turned = nt(one, block)
            if a == b:
                covariance[a:a + TILE, b:b + TILE] = (block.astype(F32) + turned).astype(BF16)
            else:
                covariance[a:a + TILE, b:b + TILE] = block
                covariance[b:b + TILE, a:a + TILE] = turned.astype(BF16)
        mine = mine_ref[...].reshape(steps * rows, width)
        for j in range(0, width, TILE):
            cols = slice(j, j + TILE)
            middle[:, cols] = jnp.dot(mine, covariance[:, cols], preferred_element_type=F32).astype(BF16)

    left = middle[pl.ds(pl.multiple_of(turn * rows, 16), rows), :]
    out_ref[0] = nt(left, factor_ref[0]) + own_ref[0]


def finish(factors, own, mine, packed):
    steps, rows, width = own.shape
    whole = pl.BlockSpec(packed[0].shape, lambda i: (0, 0, 0))
    return pl.pallas_call(
        functools.partial(finish_kernel, len(packed)),
        grid=(steps,),
        in_specs=[
            pl.BlockSpec((1, width, width), lambda i: (i, 0, 0)),
            pl.BlockSpec((1, rows, width), lambda i: (i, 0, 0)),
            pl.BlockSpec(mine.shape, lambda i: (0, 0, 0)),
        ]
        + [whole] * len(packed),
        out_specs=pl.BlockSpec((1, rows, width), lambda i: (i, 0, 0)),
        scratch_shapes=[pltpu.VMEM((width, width), BF16), pltpu.VMEM((steps * rows, width), BF16)],
        out_shape=jax.ShapeDtypeStruct((steps, rows, width), F32),
        compiler_params=pltpu.CompilerParams(vmem_limit_bytes=24 * MIB),
        name="finish",
    )(factors, own, mine, *packed)


def pieces(steps):
    small = max(steps // 8, 1)
    low = steps - 3 * small
    return [
        (low, steps, "shifts"),
        (low - 2 * small, low, "lines"),
        (low - 4 * small, low - 2 * small, "lines"),
        (0, low - 4 * small, "across"),
    ]


def local(gains, increments, terminal):
    count = lax.axis_size("tile")
    blocks = lax.axis_size("tm")
    line = math.gcd(count, LINE)
    across = count // line
    steps = gains.shape[0]
    place = lax.axis_index("tile").astype(jnp.int32)
    last = (lax.axis_index("tm") == blocks - 1).astype(jnp.int32).reshape(1)
    lines = [[a * across + b for a in range(line)] for b in range(across)]

    def shifted(array, along, over):
        pairs = [
            (a * across + b, (a + along) % line * across + (b + over) % across)
            for a in range(line)
            for b in range(across)
        ]
        return lax.ppermute(array, "tile", pairs) if along or over else array

    def gathered(array):
        return lax.all_gather(array, "tile", axis_index_groups=lines)

    def spread(array, kind):
        if kind == "shifts":
            along = [shifted(array, i, 0) for i in range(line)]
            return [[shifted(part, 0, j) for part in along] for j in range(across)]
        if kind == "lines":
            whole = gathered(array)
            return [[shifted(whole, 0, j)] for j in range(across)]
        return [[gathered(shifted(array, 0, j))] for j in range(across)]

    def order(kind):
        found = [place]
        for j in range(across):
            for i in range(line):
                along = (place // across - i + line) % line if kind == "shifts" else i
                found.append(along * across + (place % across - j + across) % across)
        return jnp.stack(found)

    state = None
    for low, high, kind in pieces(steps):
        own = pack(place.reshape(1), gains, increments, terminal if state is None else None, count, low, high)
        state = compose(last, order(kind), spread(own, kind), state, low, high - low, steps)
    factors, own, mine, factor, half = state
    packed = []
    for turn in range(blocks - 1, 0, -1):
        packed.append(lax.ppermute(hop(factor, half, packed), "tm", [(turn, turn - 1)]))
    return finish(factors, own, mine, packed)


def solution(mesh):
    return jax.shard_map(
        local,
        mesh=mesh,
        in_specs=(P("tm", "tile", None), P("tm", "tile", None), P("tile", None)),
        out_specs=P("tm", "tile", None),
        check_vma=False,
    )
```

```python
import functools
import math

import jax
import jax.numpy as jnp
from jax import lax
from jax.experimental import pallas as pl
from jax.experimental.pallas import tpu as pltpu
from jax.sharding import PartitionSpec as P

BF16 = jnp.bfloat16
F32 = jnp.float32
LANES = 128
TILE = 256
LINE = 4
MIB = 1024 * 1024


def half_width(rows, count):
    used = (count // 2 + 1) * rows
    return used, -(-used // LANES) * LANES


def nt(left, right):
    return lax.dot_general(left, right, (((1,), (1,)), ((), ())), preferred_element_type=F32)


def packed_half(increment, place, count):
    rows, width = increment.shape
    used, half = half_width(rows, count)
    turned = pltpu.roll(increment, lax.rem(width - place * rows, width), 1)[:, :half]
    column = lax.broadcasted_iota(jnp.int32, turned.shape, 1)
    halved = (column < rows) | (column >= used - rows)
    weight = jnp.where(column < used, jnp.where(halved, 0.5, 1.0), 0.0)
    return (turned * weight).astype(BF16)


def unpacked_half(piece, start, width):
    piece = piece.astype(F32)
    rest = width - piece.shape[1]
    wide = jnp.concatenate([piece, jnp.zeros((piece.shape[0], rest), F32)], axis=1) if rest else piece
    return pltpu.roll(wide, start, 1)


def pack_kernel(count, ranges, place_ref, gain_ref, increment_ref, terminal_ref, whole_ref, *piece_refs):
    steps, rows, width = gain_ref.shape
    stride = width + half_width(rows, count)[1]
    place = place_ref[0]
    for step in range(steps):
        base = step * stride
        whole_ref[:, base:base + width] = gain_ref[step]
        whole_ref[:, base + width:base + stride] = packed_half(increment_ref[step], place, count)
    whole_ref[:, steps * stride:] = packed_half(terminal_ref[...], place, count)
    for (low, high), piece_ref in zip(ranges, piece_refs):
        piece_ref[...] = whole_ref[:, low * stride:low * stride + piece_ref.shape[1]]


def pack(place, gains, increments, terminal, count, ranges):
    steps, rows, width = gains.shape
    half = half_width(rows, count)[1]
    lanes = [(high - low) * (width + half) + half * (high == steps) for low, high in [(0, steps)] + ranges]
    vmem = pl.BlockSpec(memory_space=pltpu.VMEM)
    return pl.pallas_call(
        functools.partial(pack_kernel, count, ranges),
        in_specs=[pl.BlockSpec(memory_space=pltpu.SMEM), vmem, vmem, vmem],
        out_specs=[vmem] * len(lanes),
        out_shape=[jax.ShapeDtypeStruct((rows, size), BF16) for size in lanes],
        compiler_params=pltpu.CompilerParams(vmem_limit_bytes=24 * MIB),
        name="pack",
    )(place, gains, increments, terminal)


def compose_kernel(lines, parts, first, last_ref, places_ref, *refs):
    sizes = [lines[j] for j in range(len(lines))]
    blocks = []
    for size in sizes:
        blocks.append(refs[:size])
        refs = refs[size:]
    ends = []
    if first:
        for _ in range(parts):
            ends.append([])
            for size in sizes:
                ends[-1].append(refs[:size])
                refs = refs[size:]
    else:
        factor_in, half_in, refs = refs[0], refs[1], refs[5:]
    factor_out, own_out, mine_out, factor_end, half_end, gain, factor, half, middle, total = refs
    width = factor.shape[0]
    turn = pl.program_id(0)
    spots = []
    for j, group in enumerate(blocks):
        for n, ref in enumerate(group):
            inner = ref.shape[0] if len(ref.shape) == 3 else 1
            for i in range(inner):
                spots.append((j, n, i, len(ref.shape) == 3))
    rows = width // len(spots)
    starts = [pl.multiple_of(places_ref[1 + k] * rows, 16) for k in range(len(spots))]

    def lanes(refs_of, spot, cut):
        j, n, i, stacked = spot
        return refs_of[j][n][i, :, cut] if stacked else refs_of[j][n][:, cut]

    for spot, start in zip(spots, starts):
        gain[pl.ds(start, rows), :] = lanes(blocks, spot, slice(0, width))

    @pl.when(turn == 0)
    def _():
        if first:
            factor[...] = gain[...]
            scale = jnp.where(last_ref[0] == 1, 1.0, 0.0)
            for spot, start in zip(spots, starts):
                piece = jnp.concatenate([lanes(end, spot, slice(None)) for end in ends], axis=1)
                half[pl.ds(start, rows), :] = (unpacked_half(piece, start, width) * scale).astype(BF16)
        else:
            factor[...] = factor_in[...]
            half[...] = half_in[...]

    def extend():
        for j in range(0, width, TILE):
            cols = slice(j, j + TILE)
            factor[:, cols] = jnp.dot(gain[...], factor[:, cols], preferred_element_type=F32).astype(BF16)

    if first:
        pl.when(turn > 0)(extend)
    else:
        extend()
    for j in range(0, width, TILE):
        cols = slice(j, j + TILE)
        middle[:, cols] = jnp.dot(gain[...], half[:, cols], preferred_element_type=F32).astype(BF16)
    for j in range(0, width, TILE):
        total[:, j:j + TILE] = nt(middle[...], gain[j:j + TILE, :])
    for spot, start in zip(spots, starts):
        span = pl.ds(start, rows)
        piece = lanes(blocks, spot, slice(width, None))
        half[span, :] = (total[span, :] + unpacked_half(piece, start, width)).astype(BF16)

    mine = pl.multiple_of(places_ref[0] * rows, 16)
    picked = lax.broadcasted_iota(jnp.int32, (rows, width), 1) == mine + lax.broadcasted_iota(
        jnp.int32, (rows, width), 0
    )
    own = half[pl.ds(mine, rows), :].astype(F32)
    own_out[0] = own + nt(jnp.where(picked, 1.0, 0.0).astype(BF16), half[...])
    mine_out[0] = factor[pl.ds(mine, rows), :]
    factor_out[0] = factor[...]

    @pl.when(turn == pl.num_programs(0) - 1)
    def _():
        factor_end[...] = factor[...]
        half_end[...] = half[...]


def compose(last, places, blocks, state, low, turns, steps):
    lines = [len(group) for group in blocks]
    flat = [block for group in blocks for block in group]
    rows = flat[0][0].shape[-2]
    width = rows * sum(block.shape[0] if block.ndim == 3 else 1 for block, _ in flat)
    half = half_width(rows, width // rows)[1]
    stride = width + half
    first = state is None
    whole = pl.BlockSpec((width, width), lambda i, *p: (0, 0))
    anywhere = pl.BlockSpec(memory_space=pl.ANY)

    def spec(block, size, place):
        if block.ndim == 3:
            return pl.BlockSpec((block.shape[0], rows, size), lambda i, *p: (0, 0, place(i)))
        return pl.BlockSpec((rows, size), lambda i, *p: (0, place(i)))

    in_specs = [spec(block, stride, lambda i, begin=begin: low + turns - 1 - i - begin) for block, begin in flat]
    args = [block for block, _ in flat]
    size = math.gcd(stride, half)
    parts = half // size if first else 0
    for n in range(parts):
        in_specs += [
            spec(block, size, lambda i, at=(steps - begin) * stride // size + n: at) for block, begin in flat
        ]
        args += [block for block, _ in flat]
    if not first:
        in_specs += [whole, whole, anywhere, anywhere, anywhere]
        args += [state[3], state[4], state[0], state[1], state[2]]
    base = 2 + len(flat) + 2
    return pl.pallas_call(
        functools.partial(compose_kernel, lines, parts, first),
        grid_spec=pltpu.PrefetchScalarGridSpec(
            num_scalar_prefetch=2,
            grid=(turns,),
            in_specs=in_specs,
            out_specs=[
                pl.BlockSpec((1, width, width), lambda i, *p: (low + turns - 1 - i, 0, 0)),
                pl.BlockSpec((1, rows, width), lambda i, *p: (low + turns - 1 - i, 0, 0)),
                pl.BlockSpec((1, rows, width), lambda i, *p: (low + turns - 1 - i, 0, 0)),
                whole,
                whole,
            ],
            scratch_shapes=[pltpu.VMEM((width, width), BF16) for _ in range(4)]
            + [pltpu.VMEM((width, width), F32)],
        ),
        out_shape=[
            jax.ShapeDtypeStruct((steps, width, width), BF16),
            jax.ShapeDtypeStruct((steps, rows, width), F32),
            jax.ShapeDtypeStruct((steps, rows, width), BF16),
            jax.ShapeDtypeStruct((width, width), BF16),
            jax.ShapeDtypeStruct((width, width), BF16),
        ],
        input_output_aliases={} if first else {base: 0, base + 1: 1, base + 2: 2},
        compiler_params=pltpu.CompilerParams(vmem_limit_bytes=32 * MIB),
        cost_estimate=pl.CostEstimate(
            flops=6 * turns * width**3, bytes_accessed=8 * turns * width * width, transcendentals=0
        ),
        name="compose",
    )(last, places, *args)


def upper_blocks(width):
    return [(a, b) for a in range(0, width, TILE) for b in range(a, width, TILE)]


def identity(size):
    row = lax.broadcasted_iota(jnp.int32, (size, size), 0)
    column = lax.broadcasted_iota(jnp.int32, (size, size), 1)
    return jnp.where(row == column, 1.0, 0.0).astype(BF16)


def fold(half_ref, packed_ref):
    one = identity(TILE)
    for n, (a, b) in enumerate(upper_blocks(half_ref.shape[0])):
        block = half_ref[a:a + TILE, b:b + TILE]
        if a != b:
            block = block.astype(F32) + nt(one, half_ref[b:b + TILE, a:a + TILE])
        packed_ref[n] = block.astype(BF16)


def arrived_sum(refs, n):
    value = refs[0][n]
    for extra in refs[1:]:
        value = value + extra[n]
    return value


def fold_kernel(half_ref, packed_ref):
    fold(half_ref, packed_ref)


def hop_kernel(arrived, factor_ref, half_ref, *refs):
    out_ref, covariance, middle, ahead = refs[arrived:]
    width = factor_ref.shape[0]
    for n, (a, b) in enumerate(upper_blocks(width)):
        covariance[a:a + TILE, b:b + TILE] = arrived_sum(refs[:arrived], n)
    for j in range(0, width, TILE):
        cols = slice(j, j + TILE)
        middle[:, cols] = jnp.dot(
            factor_ref[:, :j + TILE], covariance[:j + TILE, cols], preferred_element_type=F32
        ).astype(BF16)
    for j in range(0, width, TILE):
        cols = slice(j, j + TILE)
        ahead[:, cols] = (nt(middle[...], factor_ref[cols, :]) + half_ref[:, cols].astype(F32)).astype(BF16)
    fold(ahead, out_ref)


def hop(factor, half, packed):
    width = factor.shape[0]
    shape = (len(upper_blocks(width)), TILE, TILE)
    square = pltpu.VMEM((width, width), BF16)
    if not packed:
        return pl.pallas_call(
            fold_kernel,
            out_shape=jax.ShapeDtypeStruct(shape, BF16),
            compiler_params=pltpu.CompilerParams(vmem_limit_bytes=16 * MIB),
            name="fold",
        )(half)
    return pl.pallas_call(
        functools.partial(hop_kernel, len(packed)),
        out_shape=jax.ShapeDtypeStruct(shape, BF16),
        scratch_shapes=[square, square, square],
        compiler_params=pltpu.CompilerParams(vmem_limit_bytes=20 * MIB),
        cost_estimate=pl.CostEstimate(flops=4 * width**3, bytes_accessed=10 * width * width, transcendentals=0),
        name="hop",
    )(factor, half, *packed)


def finish_kernel(arrived, factor_ref, own_ref, mine_ref, *refs):
    out_ref, covariance, middle = refs[arrived:]
    turn = pl.program_id(0)
    rows = own_ref.shape[1]
    steps = mine_ref.shape[0]
    width = covariance.shape[0]

    @pl.when(turn == 0)
    def _():
        one = identity(TILE)
        for n, (a, b) in enumerate(upper_blocks(width)):
            block = arrived_sum(refs[:arrived], n)
            turned = nt(one, block)
            if a == b:
                covariance[a:a + TILE, b:b + TILE] = (block.astype(F32) + turned).astype(BF16)
            else:
                covariance[a:a + TILE, b:b + TILE] = block
                covariance[b:b + TILE, a:a + TILE] = turned.astype(BF16)
        mine = mine_ref[...].reshape(steps * rows, width)
        for j in range(0, width, TILE):
            cols = slice(j, j + TILE)
            middle[:, cols] = jnp.dot(mine, covariance[:, cols], preferred_element_type=F32).astype(BF16)

    left = middle[pl.ds(pl.multiple_of(turn * rows, 16), rows), :]
    out_ref[0] = nt(left, factor_ref[0]) + own_ref[0]


def finish(factors, own, mine, packed):
    steps, rows, width = own.shape
    whole = pl.BlockSpec(packed[0].shape, lambda i: (0, 0, 0))
    return pl.pallas_call(
        functools.partial(finish_kernel, len(packed)),
        grid=(steps,),
        in_specs=[
            pl.BlockSpec((1, width, width), lambda i: (i, 0, 0)),
            pl.BlockSpec((1, rows, width), lambda i: (i, 0, 0)),
            pl.BlockSpec(mine.shape, lambda i: (0, 0, 0)),
        ]
        + [whole] * len(packed),
        out_specs=pl.BlockSpec((1, rows, width), lambda i: (i, 0, 0)),
        scratch_shapes=[pltpu.VMEM((width, width), BF16), pltpu.VMEM((steps * rows, width), BF16)],
        out_shape=jax.ShapeDtypeStruct((steps, rows, width), F32),
        compiler_params=pltpu.CompilerParams(vmem_limit_bytes=24 * MIB),
        name="finish",
    )(factors, own, mine, *packed)


def pieces(steps):
    small = max(steps // 8, 1)
    cuts = [0, small, 2 * small, 4 * small, 6 * small, steps]
    return list(zip(cuts, cuts[1:]))[::-1]


def local(gains, increments, terminal):
    count = lax.axis_size("tile")
    blocks = lax.axis_size("tm")
    line = math.gcd(count, LINE)
    across = count // line
    steps = gains.shape[0]
    place = lax.axis_index("tile").astype(jnp.int32)
    last = (lax.axis_index("tm") == blocks - 1).astype(jnp.int32).reshape(1)

    def shifted(array, along, over):
        pairs = [
            (a * across + b, (a + along) % line * across + (b + over) % across)
            for a in range(line)
            for b in range(across)
        ]
        return lax.ppermute(array, "tile", pairs) if along or over else array

    places = jnp.stack(
        [place]
        + [
            (place // across - i + line) % line * across + (place % across - j + across) % across
            for j in range(across)
            for i in range(line)
        ]
    )
    ranges = pieces(steps)
    whole, *own = pack(place.reshape(1), gains, increments, terminal, count, ranges)
    passing = [shifted(whole, 0, j) for j in range(1, across)]
    crossed = [whole] + passing
    state = None
    stages = []
    for (low, high), array in zip(ranges, own):
        if stages:
            array, passing, parts = lax.optimization_barrier((array, passing, parts))
            if len(stages) == 1:
                crossed = [whole] + passing
            else:
                stages[-2][3][1:] = passing
            stages[-1][3][0] = jnp.stack(parts)
            passing = [shifted(stages[-1][3][0], 0, j) for j in range(1, across)]
        parts = [shifted(array, i, 0) for i in range(1, line)]
        stages.append((low, high, array, [None] * across))
    last_parts, passing = lax.optimization_barrier((parts, passing))
    stages[-2][3][1:] = passing
    stacked = jnp.stack(last_parts)
    stages[-1][3][:] = [shifted(stacked, 0, j) for j in range(across)]
    for low, high, _, stacks in stages:
        groups = [[(crossed[j], 0), (stacks[j], low)] for j in range(across)]
        state = compose(last, places, groups, state, low, high - low, steps)
    factors, own, mine, factor, half = state
    packed = []
    for turn in range(blocks - 1, 0, -1):
        packed.append(lax.ppermute(hop(factor, half, packed), "tm", [(turn, turn - 1)]))
    return finish(factors, own, mine, packed)


def solution(mesh):
    return jax.shard_map(
        local,
        mesh=mesh,
        in_specs=(P("tm", "tile", None), P("tm", "tile", None), P("tile", None)),
        out_specs=P("tm", "tile", None),
        check_vma=False,
    )
```

```python
import functools
import math

import jax
import jax.numpy as jnp
from jax import lax
from jax.experimental import pallas as pl
from jax.experimental.pallas import tpu as pltpu
from jax.sharding import PartitionSpec as P

BF16 = jnp.bfloat16
F32 = jnp.float32
LANES = 128
TILE = 256
LINE = 4
GATE = 3
MIB = 1024 * 1024


def half_width(rows, count):
    used = (count // 2 + 1) * rows
    return used, -(-used // LANES) * LANES


def nt(left, right):
    return lax.dot_general(left, right, (((1,), (1,)), ((), ())), preferred_element_type=F32)


def packed_half(increment, place, count):
    rows, width = increment.shape
    used, half = half_width(rows, count)
    turned = pltpu.roll(increment, lax.rem(width - place * rows, width), 1)[:, :half]
    column = lax.broadcasted_iota(jnp.int32, turned.shape, 1)
    halved = (column < rows) | (column >= used - rows)
    weight = jnp.where(column < used, jnp.where(halved, 0.5, 1.0), 0.0)
    return (turned * weight).astype(BF16)


def unpacked_half(piece, start, width):
    piece = piece.astype(F32)
    rest = width - piece.shape[1]
    wide = jnp.concatenate([piece, jnp.zeros((piece.shape[0], rest), F32)], axis=1) if rest else piece
    return pltpu.roll(wide, start, 1)


def pack_kernel(count, ranges, place_ref, gain_ref, increment_ref, terminal_ref, *packed_refs):
    width = gain_ref.shape[2]
    stride = width + half_width(gain_ref.shape[1], count)[1]
    place = place_ref[0]
    for (low, high), packed_ref in zip(ranges, packed_refs):
        for step in range(low, high):
            base = (step - low) * stride
            packed_ref[:, base:base + width] = gain_ref[step]
            packed_ref[:, base + width:base + stride] = packed_half(increment_ref[step], place, count)
    packed_refs[-1][...] = packed_half(terminal_ref[...], place, count)


def pack(place, gains, increments, terminal, count, ranges):
    rows, width = gains.shape[1:]
    half = half_width(rows, count)[1]
    lanes = [(high - low) * (width + half) for low, high in ranges] + [half]
    vmem = pl.BlockSpec(memory_space=pltpu.VMEM)
    return pl.pallas_call(
        functools.partial(pack_kernel, count, ranges),
        in_specs=[pl.BlockSpec(memory_space=pltpu.SMEM), vmem, vmem, vmem],
        out_specs=[vmem] * len(lanes),
        out_shape=[jax.ShapeDtypeStruct((rows, size), BF16) for size in lanes],
        compiler_params=pltpu.CompilerParams(vmem_limit_bytes=24 * MIB),
        name="pack",
    )(place, gains, increments, terminal)


def compose_kernel(count, first, last_ref, places_ref, *refs):
    blocks, refs = refs[:count], refs[count:]
    if first:
        end, refs = refs[0], refs[1:]
    else:
        factor_in, half_in, refs = refs[0], refs[1], refs[5:]
    factor_out, own_out, mine_out, factor_end, half_end, gain, factor, half, middle, total = refs
    width = factor.shape[0]
    rows = width // count
    turn = pl.program_id(0)
    starts = [pl.multiple_of(places_ref[n] * rows, 16) for n in range(count)]
    for start, block in zip(starts, blocks):
        gain[pl.ds(start, rows), :] = block[:, :width]

    @pl.when(turn == 0)
    def _():
        if first:
            factor[...] = gain[...]
            scale = jnp.where(last_ref[0] == 1, 1.0, 0.0)
            for n in range(count):
                half[n * rows:(n + 1) * rows, :] = (unpacked_half(end[n], n * rows, width) * scale).astype(BF16)
        else:
            factor[...] = factor_in[...]
            half[...] = half_in[...]

    def extend():
        for j in range(0, width, TILE):
            cols = slice(j, j + TILE)
            factor[:, cols] = jnp.dot(gain[...], factor[:, cols], preferred_element_type=F32).astype(BF16)

    if first:
        pl.when(turn > 0)(extend)
    else:
        extend()
    for j in range(0, width, TILE):
        cols = slice(j, j + TILE)
        middle[:, cols] = jnp.dot(gain[...], half[:, cols], preferred_element_type=F32).astype(BF16)
    for j in range(0, width, TILE):
        total[:, j:j + TILE] = nt(middle[...], gain[j:j + TILE, :])
    for start, block in zip(starts, blocks):
        span = pl.ds(start, rows)
        half[span, :] = (total[span, :] + unpacked_half(block[:, width:], start, width)).astype(BF16)

    mine = starts[0]
    picked = lax.broadcasted_iota(jnp.int32, (rows, width), 1) == mine + lax.broadcasted_iota(
        jnp.int32, (rows, width), 0
    )
    own = half[pl.ds(mine, rows), :].astype(F32)
    own_out[0] = own + nt(jnp.where(picked, 1.0, 0.0).astype(BF16), half[...])
    mine_out[0] = factor[pl.ds(mine, rows), :]
    factor_out[0] = factor[...]

    @pl.when(turn == pl.num_programs(0) - 1)
    def _():
        factor_end[...] = factor[...]
        half_end[...] = half[...]


def compose(last, places, blocks, end, state, low, turns, steps):
    count = len(blocks)
    rows = blocks[0].shape[0]
    width = rows * count
    stride = width + half_width(rows, count)[1]
    first = state is None
    whole = pl.BlockSpec((width, width), lambda i, *p: (0, 0))
    anywhere = pl.BlockSpec(memory_space=pl.ANY)
    in_specs = [pl.BlockSpec((rows, stride), lambda i, *p: (0, turns - 1 - i))] * count
    if first:
        in_specs += [pl.BlockSpec(end.shape, lambda i, *p: (0, 0, 0))]
        args = [*blocks, end]
    else:
        in_specs += [whole, whole, anywhere, anywhere, anywhere]
        args = [*blocks, state[3], state[4], state[0], state[1], state[2]]
    base = 2 + count + 2
    return pl.pallas_call(
        functools.partial(compose_kernel, count, first),
        grid_spec=pltpu.PrefetchScalarGridSpec(
            num_scalar_prefetch=2,
            grid=(turns,),
            in_specs=in_specs,
            out_specs=[
                pl.BlockSpec((1, width, width), lambda i, *p: (low + turns - 1 - i, 0, 0)),
                pl.BlockSpec((1, rows, width), lambda i, *p: (low + turns - 1 - i, 0, 0)),
                pl.BlockSpec((1, rows, width), lambda i, *p: (low + turns - 1 - i, 0, 0)),
                whole,
                whole,
            ],
            scratch_shapes=[pltpu.VMEM((width, width), BF16) for _ in range(4)]
            + [pltpu.VMEM((width, width), F32)],
        ),
        out_shape=[
            jax.ShapeDtypeStruct((steps, width, width), BF16),
            jax.ShapeDtypeStruct((steps, rows, width), F32),
            jax.ShapeDtypeStruct((steps, rows, width), BF16),
            jax.ShapeDtypeStruct((width, width), BF16),
            jax.ShapeDtypeStruct((width, width), BF16),
        ],
        input_output_aliases={} if first else {base: 0, base + 1: 1, base + 2: 2},
        compiler_params=pltpu.CompilerParams(vmem_limit_bytes=32 * MIB),
        cost_estimate=pl.CostEstimate(
            flops=6 * turns * width**3, bytes_accessed=8 * turns * width * width, transcendentals=0
        ),
        name="compose",
    )(last, places, *args)


def upper_blocks(width):
    return [(a, b) for a in range(0, width, TILE) for b in range(a, width, TILE)]


def identity(size):
    row = lax.broadcasted_iota(jnp.int32, (size, size), 0)
    column = lax.broadcasted_iota(jnp.int32, (size, size), 1)
    return jnp.where(row == column, 1.0, 0.0).astype(BF16)


def fold(half_ref, packed_ref):
    one = identity(TILE)
    for n, (a, b) in enumerate(upper_blocks(half_ref.shape[0])):
        block = half_ref[a:a + TILE, b:b + TILE]
        if a != b:
            block = block.astype(F32) + nt(one, half_ref[b:b + TILE, a:a + TILE])
        packed_ref[n] = block.astype(BF16)


def arrived_sum(refs, n):
    value = refs[0][n]
    for extra in refs[1:]:
        value = value + extra[n]
    return value


def fold_kernel(half_ref, packed_ref):
    fold(half_ref, packed_ref)


def hop_kernel(arrived, factor_ref, half_ref, *refs):
    out_ref, covariance, middle, ahead = refs[arrived:]
    width = factor_ref.shape[0]
    for n, (a, b) in enumerate(upper_blocks(width)):
        covariance[a:a + TILE, b:b + TILE] = arrived_sum(refs[:arrived], n)
    for j in range(0, width, TILE):
        cols = slice(j, j + TILE)
        middle[:, cols] = jnp.dot(
            factor_ref[:, :j + TILE], covariance[:j + TILE, cols], preferred_element_type=F32
        ).astype(BF16)
    for j in range(0, width, TILE):
        cols = slice(j, j + TILE)
        ahead[:, cols] = (nt(middle[...], factor_ref[cols, :]) + half_ref[:, cols].astype(F32)).astype(BF16)
    fold(ahead, out_ref)


def hop(factor, half, packed):
    width = factor.shape[0]
    shape = (len(upper_blocks(width)), TILE, TILE)
    square = pltpu.VMEM((width, width), BF16)
    if not packed:
        return pl.pallas_call(
            fold_kernel,
            out_shape=jax.ShapeDtypeStruct(shape, BF16),
            compiler_params=pltpu.CompilerParams(vmem_limit_bytes=16 * MIB),
            name="fold",
        )(half)
    return pl.pallas_call(
        functools.partial(hop_kernel, len(packed)),
        out_shape=jax.ShapeDtypeStruct(shape, BF16),
        scratch_shapes=[square, square, square],
        compiler_params=pltpu.CompilerParams(vmem_limit_bytes=20 * MIB),
        cost_estimate=pl.CostEstimate(flops=4 * width**3, bytes_accessed=10 * width * width, transcendentals=0),
        name="hop",
    )(factor, half, *packed)


def finish_kernel(arrived, factor_ref, own_ref, mine_ref, *refs):
    out_ref, covariance, middle = refs[arrived:]
    turn = pl.program_id(0)
    rows = own_ref.shape[1]
    steps = mine_ref.shape[0]
    width = covariance.shape[0]

    @pl.when(turn == 0)
    def _():
        one = identity(TILE)
        for n, (a, b) in enumerate(upper_blocks(width)):
            block = arrived_sum(refs[:arrived], n)
            turned = nt(one, block)
            if a == b:
                covariance[a:a + TILE, b:b + TILE] = (block.astype(F32) + turned).astype(BF16)
            else:
                covariance[a:a + TILE, b:b + TILE] = block
                covariance[b:b + TILE, a:a + TILE] = turned.astype(BF16)
        mine = mine_ref[...].reshape(steps * rows, width)
        for j in range(0, width, TILE):
            cols = slice(j, j + TILE)
            middle[:, cols] = jnp.dot(mine, covariance[:, cols], preferred_element_type=F32).astype(BF16)

    left = middle[pl.ds(pl.multiple_of(turn * rows, 16), rows), :]
    out_ref[0] = nt(left, factor_ref[0]) + own_ref[0]


def finish(factors, own, mine, packed):
    steps, rows, width = own.shape
    whole = pl.BlockSpec(packed[0].shape, lambda i: (0, 0, 0))
    return pl.pallas_call(
        functools.partial(finish_kernel, len(packed)),
        grid=(steps,),
        in_specs=[
            pl.BlockSpec((1, width, width), lambda i: (i, 0, 0)),
            pl.BlockSpec((1, rows, width), lambda i: (i, 0, 0)),
            pl.BlockSpec(mine.shape, lambda i: (0, 0, 0)),
        ]
        + [whole] * len(packed),
        out_specs=pl.BlockSpec((1, rows, width), lambda i: (i, 0, 0)),
        scratch_shapes=[pltpu.VMEM((width, width), BF16), pltpu.VMEM((steps * rows, width), BF16)],
        out_shape=jax.ShapeDtypeStruct((steps, rows, width), F32),
        compiler_params=pltpu.CompilerParams(vmem_limit_bytes=24 * MIB),
        name="finish",
    )(factors, own, mine, *packed)


def ring_order(line, across):
    cycle = []
    for a in range(line):
        columns = list(range(1, across))
        cycle += [a * across + b for b in (columns if a % 2 == 0 else columns[::-1])]
    return cycle + [a * across for a in reversed(range(line))]


def pieces(steps):
    small = max(steps // 8, 1)
    cuts = [0, small, 2 * small, (steps + 2 * small) // 2, steps]
    return list(zip(cuts, cuts[1:]))[::-1]


def local(gains, increments, terminal):
    count = lax.axis_size("tile")
    blocks = lax.axis_size("tm")
    line = math.gcd(count, LINE)
    steps = gains.shape[0]
    place = lax.axis_index("tile").astype(jnp.int32)
    last = (lax.axis_index("tm") == blocks - 1).astype(jnp.int32).reshape(1)
    cycle = ring_order(line, count // line)

    def passed(array, way):
        return lax.ppermute(array, "tile", [(cycle[n], cycle[(n + way) % count]) for n in range(count)])

    def origins(way):
        table = [[cycle[(cycle.index(d) - way * hop) % count] for hop in range(count)] for d in range(count)]
        return jnp.asarray(table, jnp.int32)[place]

    ranges = pieces(steps)
    *own, end = pack(place.reshape(1), gains, increments, terminal, count, ranges)
    end = lax.all_gather(end, "tile")
    arrived = []
    for turn, array in enumerate(own):
        way = 1 if turn % 2 == 0 else -1
        if turn >= 2:
            before = arrived[turn - 2]
            array, before[GATE] = lax.optimization_barrier((array, before[GATE]))
            for hop_count in range(GATE + 1, count):
                before[hop_count] = passed(before[hop_count - 1], way)
        found = [array]
        for hop_count in range(1, count):
            found.append(passed(found[-1], way))
        arrived.append(found)
    state = None
    for turn, (low, high) in enumerate(ranges):
        places = origins(1 if turn % 2 == 0 else -1)
        state = compose(last, places, arrived[turn], end, state, low, high - low, steps)
    factors, own, mine, factor, half = state
    packed = []
    for turn in range(blocks - 1, 0, -1):
        packed.append(lax.ppermute(hop(factor, half, packed), "tm", [(turn, turn - 1)]))
    return finish(factors, own, mine, packed)


def solution(mesh):
    return jax.shard_map(
        local,
        mesh=mesh,
        in_specs=(P("tm", "tile", None), P("tm", "tile", None), P("tile", None)),
        out_specs=P("tm", "tile", None),
        check_vma=False,
    )
```

```python
import functools
import math

import jax
import jax.numpy as jnp
from jax import lax
from jax.experimental import pallas as pl
from jax.experimental.pallas import tpu as pltpu
from jax.sharding import PartitionSpec as P

BF16 = jnp.bfloat16
F32 = jnp.float32
LANES = 128
TILE = 256
LINE = 4
GATE = 3
MIB = 1024 * 1024


def half_width(rows, count):
    used = (count // 2 + 1) * rows
    return used, -(-used // LANES) * LANES


def nt(left, right):
    return lax.dot_general(left, right, (((1,), (1,)), ((), ())), preferred_element_type=F32)


def packed_half(increment, place, count):
    rows, width = increment.shape
    used, half = half_width(rows, count)
    turned = pltpu.roll(increment, lax.rem(width - place * rows, width), 1)[:, :half]
    column = lax.broadcasted_iota(jnp.int32, turned.shape, 1)
    halved = (column < rows) | (column >= used - rows)
    weight = jnp.where(column < used, jnp.where(halved, 0.5, 1.0), 0.0)
    return (turned * weight).astype(BF16)


def unpacked_half(piece, start, width):
    piece = piece.astype(F32)
    rest = width - piece.shape[1]
    wide = jnp.concatenate([piece, jnp.zeros((piece.shape[0], rest), F32)], axis=1) if rest else piece
    return pltpu.roll(wide, start, 1)


def pack_kernel(count, ranges, place_ref, gain_ref, increment_ref, *packed_refs):
    width = gain_ref.shape[2]
    stride = width + half_width(gain_ref.shape[1], count)[1]
    place = place_ref[0]
    for (low, high), packed_ref in zip(ranges, packed_refs):
        for step in range(low, high):
            base = (step - low) * stride
            packed_ref[:, base:base + width] = gain_ref[step]
            packed_ref[:, base + width:base + stride] = packed_half(increment_ref[step], place, count)


def pack(place, gains, increments, count, ranges):
    rows, width = gains.shape[1:]
    half = half_width(rows, count)[1]
    lanes = [(high - low) * (width + half) for low, high in ranges]
    vmem = pl.BlockSpec(memory_space=pltpu.VMEM)
    return pl.pallas_call(
        functools.partial(pack_kernel, count, ranges),
        in_specs=[pl.BlockSpec(memory_space=pltpu.SMEM), vmem, vmem],
        out_specs=[vmem] * len(lanes),
        out_shape=[jax.ShapeDtypeStruct((rows, size), BF16) for size in lanes],
        compiler_params=pltpu.CompilerParams(vmem_limit_bytes=12 * MIB),
        name="pack",
    )(place, gains, increments)


def compose_kernel(count, first, last_ref, places_ref, *refs):
    blocks, refs = refs[:count], refs[count:]
    if first:
        end, refs = refs[0], refs[1:]
    else:
        half_in, factor_in, refs = refs[0], refs[1], refs[4:]
    factor_out, own_out, mine_out, half_end, gain, factor, half, middle, total = refs
    width = factor.shape[0]
    rows = width // count
    turn = pl.program_id(0)
    starts = [pl.multiple_of(places_ref[n] * rows, 16) for n in range(count)]
    for start, block in zip(starts, blocks):
        gain[pl.ds(start, rows), :] = block[:, :width]

    @pl.when(turn == 0)
    def _():
        if first:
            factor[...] = gain[...]
            scale = jnp.where(last_ref[0] == 1, 0.5, 0.0)
            half[...] = (end[...].astype(F32) * scale).astype(BF16)
        else:
            factor[...] = factor_in[0]
            half[...] = half_in[...]

    def extend():
        for j in range(0, width, TILE):
            cols = slice(j, j + TILE)
            factor[:, cols] = jnp.dot(gain[...], factor[:, cols], preferred_element_type=F32).astype(BF16)

    if first:
        pl.when(turn > 0)(extend)
    else:
        extend()
    for j in range(0, width, TILE):
        cols = slice(j, j + TILE)
        middle[:, cols] = jnp.dot(gain[...], half[:, cols], preferred_element_type=F32).astype(BF16)
    for j in range(0, width, TILE):
        total[:, j:j + TILE] = nt(middle[...], gain[j:j + TILE, :])
    for start, block in zip(starts, blocks):
        span = pl.ds(start, rows)
        half[span, :] = (total[span, :] + unpacked_half(block[:, width:], start, width)).astype(BF16)

    mine = starts[0]
    picked = lax.broadcasted_iota(jnp.int32, (rows, width), 1) == mine + lax.broadcasted_iota(
        jnp.int32, (rows, width), 0
    )
    own = half[pl.ds(mine, rows), :].astype(F32)
    own_out[0] = own + nt(jnp.where(picked, 1.0, 0.0).astype(BF16), half[...])
    mine_out[0] = factor[pl.ds(mine, rows), :]
    factor_out[0] = factor[...]

    @pl.when(turn == pl.num_programs(0) - 1)
    def _():
        half_end[...] = half[...]


def compose(last, places, blocks, end, state, low, turns, steps):
    count = len(blocks)
    rows = blocks[0].shape[0]
    width = rows * count
    stride = width + half_width(rows, count)[1]
    first = state is None
    whole = pl.BlockSpec((width, width), lambda i, *p: (0, 0))
    anywhere = pl.BlockSpec(memory_space=pl.ANY)
    in_specs = [pl.BlockSpec((rows, stride), lambda i, *p: (0, turns - 1 - i))] * count
    if first:
        in_specs += [whole]
        args = [*blocks, end]
    else:
        after = pl.BlockSpec((1, width, width), lambda i, *p: (low + turns, 0, 0))
        in_specs += [whole, after, anywhere, anywhere]
        args = [*blocks, state[3], state[0], state[1], state[2]]
    base = 2 + count + 1
    return pl.pallas_call(
        functools.partial(compose_kernel, count, first),
        grid_spec=pltpu.PrefetchScalarGridSpec(
            num_scalar_prefetch=2,
            grid=(turns,),
            in_specs=in_specs,
            out_specs=[
                pl.BlockSpec((1, width, width), lambda i, *p: (low + turns - 1 - i, 0, 0)),
                pl.BlockSpec((1, rows, width), lambda i, *p: (low + turns - 1 - i, 0, 0)),
                pl.BlockSpec((1, rows, width), lambda i, *p: (low + turns - 1 - i, 0, 0)),
                whole,
            ],
            scratch_shapes=[pltpu.VMEM((width, width), BF16) for _ in range(4)]
            + [pltpu.VMEM((width, width), F32)],
        ),
        out_shape=[
            jax.ShapeDtypeStruct((steps, width, width), BF16),
            jax.ShapeDtypeStruct((steps, rows, width), F32),
            jax.ShapeDtypeStruct((steps, rows, width), BF16),
            jax.ShapeDtypeStruct((width, width), BF16),
        ],
        input_output_aliases={} if first else {base: 0, base + 1: 1, base + 2: 2},
        compiler_params=pltpu.CompilerParams(vmem_limit_bytes=25 * MIB),
        cost_estimate=pl.CostEstimate(
            flops=6 * turns * width**3, bytes_accessed=8 * turns * width * width, transcendentals=0
        ),
        name="compose",
    )(last, places, *args)


def upper_blocks(width):
    return [(a, b) for a in range(0, width, TILE) for b in range(a, width, TILE)]


def identity(size):
    row = lax.broadcasted_iota(jnp.int32, (size, size), 0)
    column = lax.broadcasted_iota(jnp.int32, (size, size), 1)
    return jnp.where(row == column, 1.0, 0.0).astype(BF16)


def fold(half_ref, packed_ref):
    one = identity(TILE)
    for n, (a, b) in enumerate(upper_blocks(half_ref.shape[0])):
        block = half_ref[a:a + TILE, b:b + TILE]
        if a != b:
            block = block.astype(F32) + nt(one, half_ref[b:b + TILE, a:a + TILE])
        packed_ref[n] = block.astype(BF16)


def arrived_sum(refs, n):
    value = refs[0][n]
    for extra in refs[1:]:
        value = value + extra[n]
    return value


def fold_kernel(half_ref, packed_ref):
    fold(half_ref, packed_ref)


def hop_kernel(arrived, factor_ref, half_ref, *refs):
    out_ref, covariance, middle, ahead = refs[arrived:]
    width = factor_ref.shape[1]
    for n, (a, b) in enumerate(upper_blocks(width)):
        covariance[a:a + TILE, b:b + TILE] = arrived_sum(refs[:arrived], n)
    for j in range(0, width, TILE):
        cols = slice(j, j + TILE)
        middle[:, cols] = jnp.dot(
            factor_ref[0, :, :j + TILE], covariance[:j + TILE, cols], preferred_element_type=F32
        ).astype(BF16)
    for j in range(0, width, TILE):
        cols = slice(j, j + TILE)
        ahead[:, cols] = (nt(middle[...], factor_ref[0, cols, :]) + half_ref[:, cols].astype(F32)).astype(BF16)
    fold(ahead, out_ref)


def hop(factors, half, packed):
    width = half.shape[0]
    shape = (len(upper_blocks(width)), TILE, TILE)
    square = pltpu.VMEM((width, width), BF16)
    if not packed:
        return pl.pallas_call(
            fold_kernel,
            out_shape=jax.ShapeDtypeStruct(shape, BF16),
            compiler_params=pltpu.CompilerParams(vmem_limit_bytes=12 * MIB),
            name="fold",
        )(half)
    blocks = pl.BlockSpec(shape, lambda i: (0, 0, 0))
    return pl.pallas_call(
        functools.partial(hop_kernel, len(packed)),
        grid=(1,),
        in_specs=[
            pl.BlockSpec((1, width, width), lambda i: (0, 0, 0)),
            pl.BlockSpec((width, width), lambda i: (0, 0)),
        ]
        + [blocks] * len(packed),
        out_specs=blocks,
        out_shape=jax.ShapeDtypeStruct(shape, BF16),
        scratch_shapes=[square, square, square],
        compiler_params=pltpu.CompilerParams(vmem_limit_bytes=20 * MIB),
        cost_estimate=pl.CostEstimate(flops=4 * width**3, bytes_accessed=10 * width * width, transcendentals=0),
        name="hop",
    )(factors, half, *packed)


def finish_kernel(arrived, factor_ref, own_ref, mine_ref, *refs):
    out_ref, covariance, middle = refs[arrived:]
    turn = pl.program_id(0)
    rows = own_ref.shape[1]
    steps = mine_ref.shape[0]
    width = covariance.shape[0]

    @pl.when(turn == 0)
    def _():
        one = identity(TILE)
        for n, (a, b) in enumerate(upper_blocks(width)):
            block = arrived_sum(refs[:arrived], n)
            turned = nt(one, block)
            if a == b:
                covariance[a:a + TILE, b:b + TILE] = (block.astype(F32) + turned).astype(BF16)
            else:
                covariance[a:a + TILE, b:b + TILE] = block
                covariance[b:b + TILE, a:a + TILE] = turned.astype(BF16)
        mine = mine_ref[...].reshape(steps * rows, width)
        for j in range(0, width, TILE):
            cols = slice(j, j + TILE)
            middle[:, cols] = jnp.dot(mine, covariance[:, cols], preferred_element_type=F32).astype(BF16)

    left = middle[pl.ds(pl.multiple_of(turn * rows, 16), rows), :]
    out_ref[0] = nt(left, factor_ref[0]) + own_ref[0]


def finish(factors, own, mine, packed):
    steps, rows, width = own.shape
    whole = pl.BlockSpec(packed[0].shape, lambda i: (0, 0, 0))
    return pl.pallas_call(
        functools.partial(finish_kernel, len(packed)),
        grid=(steps,),
        in_specs=[
            pl.BlockSpec((1, width, width), lambda i: (i, 0, 0)),
            pl.BlockSpec((1, rows, width), lambda i: (i, 0, 0)),
            pl.BlockSpec(mine.shape, lambda i: (0, 0, 0)),
        ]
        + [whole] * len(packed),
        out_specs=pl.BlockSpec((1, rows, width), lambda i: (i, 0, 0)),
        scratch_shapes=[pltpu.VMEM((width, width), BF16), pltpu.VMEM((steps * rows, width), BF16)],
        out_shape=jax.ShapeDtypeStruct((steps, rows, width), F32),
        compiler_params=pltpu.CompilerParams(vmem_limit_bytes=24 * MIB),
        name="finish",
    )(factors, own, mine, *packed)


def ring_order(line, across):
    cycle = []
    for a in range(line):
        columns = list(range(1, across))
        cycle += [a * across + b for b in (columns if a % 2 == 0 else columns[::-1])]
    return cycle + [a * across for a in reversed(range(line))]


def pieces(steps):
    small = max(steps // 8, 1)
    cuts = [0, 2 * small, 4 * small, 6 * small, steps]
    return list(zip(cuts, cuts[1:]))[::-1]


def local(gains, increments, terminal):
    count = lax.axis_size("tile")
    blocks = lax.axis_size("tm")
    line = math.gcd(count, LINE)
    steps = gains.shape[0]
    place = lax.axis_index("tile").astype(jnp.int32)
    last = (lax.axis_index("tm") == blocks - 1).astype(jnp.int32).reshape(1)
    cycle = ring_order(line, count // line)

    def passed(array, way):
        return lax.ppermute(array, "tile", [(cycle[n], cycle[(n + way) % count]) for n in range(count)])

    def origins(way):
        table = [[cycle[(cycle.index(d) - way * hop) % count] for hop in range(count)] for d in range(count)]
        return jnp.asarray(table, jnp.int32)[place]

    ranges = pieces(steps)
    own = pack(place.reshape(1), gains, increments, count, ranges)
    end = lax.all_gather(terminal.astype(BF16), "tile", axis=0, tiled=True)
    arrived = []
    for turn, array in enumerate(own):
        way = 1 if turn % 2 == 0 else -1
        if turn >= 2:
            before = arrived[turn - 2]
            array, before[GATE] = lax.optimization_barrier((array, before[GATE]))
            for hop_count in range(GATE + 1, count):
                before[hop_count] = passed(before[hop_count - 1], way)
        found = [array]
        for hop_count in range(1, count):
            found.append(passed(found[-1], way))
        arrived.append(found)
    state = None
    for turn, (low, high) in enumerate(ranges):
        places = origins(1 if turn % 2 == 0 else -1)
        state = compose(last, places, arrived[turn], end, state, low, high - low, steps)
    factors, own, mine, half = state
    packed = []
    for turn in range(blocks - 1, 0, -1):
        packed.append(lax.ppermute(hop(factors, half, packed), "tm", [(turn, turn - 1)]))
    return finish(factors, own, mine, packed)


def solution(mesh):
    return jax.shard_map(
        local,
        mesh=mesh,
        in_specs=(P("tm", "tile", None), P("tm", "tile", None), P("tile", None)),
        out_specs=P("tm", "tile", None),
        check_vma=False,
    )
```

```python
import functools
import math

import jax
import jax.numpy as jnp
from jax import lax
from jax.experimental import pallas as pl
from jax.experimental.pallas import tpu as pltpu
from jax.sharding import PartitionSpec as P

BF16 = jnp.bfloat16
F32 = jnp.float32
LANES = 128
TILE = 256
LINE = 4
GATE = 3
MIB = 1024 * 1024


def half_width(rows, count):
    used = (count // 2 + 1) * rows
    return used, -(-used // LANES) * LANES


def nt(left, right):
    return lax.dot_general(left, right, (((1,), (1,)), ((), ())), preferred_element_type=F32)


def packed_half(increment, place, count):
    rows, width = increment.shape
    used, half = half_width(rows, count)
    turned = pltpu.roll(increment, lax.rem(width - place * rows, width), 1)[:, :half]
    column = lax.broadcasted_iota(jnp.int32, turned.shape, 1)
    halved = (column < rows) | (column >= used - rows)
    weight = jnp.where(column < used, jnp.where(halved, 0.5, 1.0), 0.0)
    return (turned * weight).astype(BF16)


def unpacked_half(piece, start, width):
    piece = piece.astype(F32)
    rest = width - piece.shape[1]
    wide = jnp.concatenate([piece, jnp.zeros((piece.shape[0], rest), F32)], axis=1) if rest else piece
    return pltpu.roll(wide, start, 1)


def pack_kernel(count, ranges, place_ref, gain_ref, increment_ref, *packed_refs):
    width = gain_ref.shape[2]
    stride = width + half_width(gain_ref.shape[1], count)[1]
    place = place_ref[0]
    for (low, high), packed_ref in zip(ranges, packed_refs):
        for step in range(low, high):
            base = (step - low) * stride
            packed_ref[:, base:base + width] = gain_ref[step]
            packed_ref[:, base + width:base + stride] = packed_half(increment_ref[step], place, count)


def pack(place, gains, increments, count, ranges):
    rows, width = gains.shape[1:]
    half = half_width(rows, count)[1]
    lanes = [(high - low) * (width + half) for low, high in ranges]
    vmem = pl.BlockSpec(memory_space=pltpu.VMEM)
    return pl.pallas_call(
        functools.partial(pack_kernel, count, ranges),
        in_specs=[pl.BlockSpec(memory_space=pltpu.SMEM), vmem, vmem],
        out_specs=[vmem] * len(lanes),
        out_shape=[jax.ShapeDtypeStruct((rows, size), BF16) for size in lanes],
        compiler_params=pltpu.CompilerParams(vmem_limit_bytes=12 * MIB),
        name="pack",
    )(place, gains, increments)


def assemble(starts, blocks, gain, fresh):
    rows = blocks[0].shape[0]
    width = gain.shape[0]
    for start, block in zip(starts, blocks):
        gain[pl.ds(start, rows), :] = block[:, :width]
        fresh[pl.ds(start, rows), :] = unpacked_half(block[:, width:], start, width).astype(BF16)


def advance(gain, half, fresh, middle):
    width = half.shape[0]
    for j in range(0, width, TILE):
        cols = slice(j, j + TILE)
        middle[:, cols] = jnp.dot(gain[...], half[:, cols], preferred_element_type=F32).astype(BF16)
    for j in range(0, width, TILE):
        cols = slice(j, j + TILE)
        half[:, cols] = (nt(middle[...], gain[cols, :]) + fresh[:, cols].astype(F32)).astype(BF16)


def extend(gain, factor):
    for j in range(0, factor.shape[0], TILE):
        cols = slice(j, j + TILE)
        factor[:, cols] = jnp.dot(gain[...], factor[:, cols], preferred_element_type=F32).astype(BF16)


def whole_rows(half, mine, rows):
    picked = lax.broadcasted_iota(jnp.int32, (rows, half.shape[0]), 1) == mine + lax.broadcasted_iota(
        jnp.int32, (rows, half.shape[0]), 0
    )
    own = half[pl.ds(mine, rows), :].astype(F32)
    return own + nt(jnp.where(picked, 1.0, 0.0).astype(BF16), half[...])


def compose_kernel(count, first, last_ref, places_ref, *refs):
    blocks, refs = refs[:count], refs[count:]
    half_in, refs = refs[0], refs[1:]
    if not first:
        factor_in, refs = refs[0], refs[3:]
    factor_out, own_out, mine_out, half, gain, factor, fresh, middle = refs
    rows = blocks[0].shape[0]
    starts = [pl.multiple_of(places_ref[n] * rows, 16) for n in range(count)]
    assemble(starts, blocks, gain, fresh)

    @pl.when(pl.program_id(0) == 0)
    def _():
        if first:
            factor[...] = gain[...]
            half[...] = (half_in[...].astype(F32) * jnp.where(last_ref[0] == 1, 0.5, 0.0)).astype(BF16)
        else:
            factor[...] = factor_in[0]
            half[...] = half_in[...]

    if first:
        pl.when(pl.program_id(0) > 0)(lambda: extend(gain, factor))
    else:
        extend(gain, factor)
    advance(gain, half, fresh, middle)
    own_out[0] = whole_rows(half, starts[0], rows)
    mine_out[0] = factor[pl.ds(starts[0], rows), :]
    factor_out[0] = factor[...]


def square(width, place=None):
    if place is None:
        return pl.BlockSpec((width, width), lambda i, *p: (0, 0), pipeline_mode=pl.Buffered(1))
    return pl.BlockSpec((1, width, width), lambda i, *p: (place(i), 0, 0))


def compose(last, places, blocks, half, state, low, turns, steps):
    count = len(blocks)
    rows = blocks[0].shape[0]
    width = rows * count
    stride = width + half_width(rows, count)[1]
    first = state is None
    anywhere = pl.BlockSpec(memory_space=pl.ANY)
    in_specs = [pl.BlockSpec((rows, stride), lambda i, *p: (0, turns - 1 - i))] * count + [square(width)]
    if not first:
        after = pl.BlockSpec((1, width, width), lambda i, *p: (low + turns, 0, 0), pipeline_mode=pl.Buffered(1))
        in_specs += [after, anywhere, anywhere]
    band = pl.BlockSpec((1, rows, width), lambda i, *p: (low + turns - 1 - i, 0, 0))
    base = 2 + count + 1
    return pl.pallas_call(
        functools.partial(compose_kernel, count, first),
        grid_spec=pltpu.PrefetchScalarGridSpec(
            num_scalar_prefetch=2,
            grid=(turns,),
            in_specs=in_specs,
            out_specs=[square(width, lambda i: low + turns - 1 - i), band, band, square(width)],
            scratch_shapes=[pltpu.VMEM((width, width), BF16) for _ in range(4)],
        ),
        out_shape=[
            jax.ShapeDtypeStruct((steps, width, width), BF16),
            jax.ShapeDtypeStruct((steps, rows, width), F32),
            jax.ShapeDtypeStruct((steps, rows, width), BF16),
            jax.ShapeDtypeStruct((width, width), BF16),
        ],
        input_output_aliases={} if first else {base: 0, base + 1: 1, base + 2: 2},
        compiler_params=pltpu.CompilerParams(vmem_limit_bytes=18 * MIB),
        cost_estimate=pl.CostEstimate(
            flops=6 * turns * width**3, bytes_accessed=8 * turns * width * width, transcendentals=0
        ),
        name="compose",
    )(last, places, *blocks, half, *(() if first else state))


def chain_kernel(count, places_ref, *refs):
    blocks, refs = refs[:count], refs[count:]
    half_in, refs = refs[0], refs[-6:]
    gain_out, half_out, gain, half, fresh, middle = refs
    rows = blocks[0].shape[0]
    starts = [pl.multiple_of(places_ref[n] * rows, 16) for n in range(count)]
    assemble(starts, blocks, gain, fresh)

    @pl.when(pl.program_id(0) == 0)
    def _():
        half[...] = half_in[...].reshape(half.shape)

    gain_out[0] = gain[...]
    advance(gain, half, fresh, middle)
    half_out[0] = half[...]


def chain(places, blocks, half, state, low, turns, steps):
    count = len(blocks)
    rows = blocks[0].shape[0]
    width = rows * count
    stride = width + half_width(rows, count)[1]
    anywhere = pl.BlockSpec(memory_space=pl.ANY)
    in_specs = [pl.BlockSpec((rows, stride), lambda i, *p: (0, turns - 1 - i))] * count
    if state is None:
        in_specs += [square(width)]
        args = [half]
    else:
        in_specs += [
            pl.BlockSpec((1, width, width), lambda i, *p: (low + turns, 0, 0), pipeline_mode=pl.Buffered(1)),
            anywhere,
        ]
        args = [state[1], state[0]]
    whole = square(width, lambda i: low + turns - 1 - i)
    return pl.pallas_call(
        functools.partial(chain_kernel, count),
        grid_spec=pltpu.PrefetchScalarGridSpec(
            num_scalar_prefetch=1,
            grid=(turns,),
            in_specs=in_specs,
            out_specs=[whole, whole],
            scratch_shapes=[pltpu.VMEM((width, width), BF16) for _ in range(4)],
        ),
        out_shape=[jax.ShapeDtypeStruct((steps, width, width), BF16)] * 2,
        input_output_aliases={} if state is None else {1 + count + 1: 0, 1 + count: 1},
        compiler_params=pltpu.CompilerParams(vmem_limit_bytes=18 * MIB),
        cost_estimate=pl.CostEstimate(
            flops=4 * turns * width**3, bytes_accessed=8 * turns * width * width, transcendentals=0
        ),
        name="chain",
    )(places, *blocks, *args)


def factors_kernel(place_ref, gain_ref, factor_in, mine_ref, factor_out, mine_out, factor):
    del mine_ref
    rows = mine_out.shape[1]

    @pl.when(pl.program_id(0) == 0)
    def _():
        factor[...] = factor_in[0]

    extend(gain_ref.at[0], factor)
    mine_out[0] = factor[pl.ds(pl.multiple_of(place_ref[0] * rows, 16), rows), :]
    factor_out[0] = factor[...]


def extend_factors(place, gains, factors, mine):
    turns, width, _ = gains.shape
    steps, rows, _ = mine.shape
    anywhere = pl.BlockSpec(memory_space=pl.ANY)
    return pl.pallas_call(
        factors_kernel,
        grid_spec=pltpu.PrefetchScalarGridSpec(
            num_scalar_prefetch=1,
            grid=(turns,),
            in_specs=[square(width, lambda i: turns - 1 - i), square(width, lambda i: turns), anywhere],
            out_specs=[
                square(width, lambda i: turns - 1 - i),
                pl.BlockSpec((1, rows, width), lambda i, *p: (turns - 1 - i, 0, 0)),
            ],
            scratch_shapes=[pltpu.VMEM((width, width), BF16)],
        ),
        out_shape=[
            jax.ShapeDtypeStruct((steps, width, width), BF16),
            jax.ShapeDtypeStruct((steps, rows, width), BF16),
        ],
        input_output_aliases={2: 0, 3: 1},
        compiler_params=pltpu.CompilerParams(vmem_limit_bytes=12 * MIB),
        cost_estimate=pl.CostEstimate(
            flops=2 * turns * width**3, bytes_accessed=4 * turns * width * width, transcendentals=0
        ),
        name="extend_factors",
    )(place, gains, factors, mine)


def rows_kernel(place_ref, half_ref, own_ref, own_out):
    del own_ref
    rows = own_out.shape[1]
    own_out[0] = whole_rows(half_ref.at[0], pl.multiple_of(place_ref[0] * rows, 16), rows)


def own_rows(place, halves, own):
    turns, width, _ = halves.shape
    steps, rows, _ = own.shape
    return pl.pallas_call(
        rows_kernel,
        grid_spec=pltpu.PrefetchScalarGridSpec(
            num_scalar_prefetch=1,
            grid=(turns,),
            in_specs=[square(width, lambda i: i), pl.BlockSpec(memory_space=pl.ANY)],
            out_specs=pl.BlockSpec((1, rows, width), lambda i, *p: (i, 0, 0)),
        ),
        out_shape=jax.ShapeDtypeStruct((steps, rows, width), F32),
        input_output_aliases={2: 0},
        compiler_params=pltpu.CompilerParams(vmem_limit_bytes=8 * MIB),
        cost_estimate=pl.CostEstimate(
            flops=2 * turns * rows * width**2, bytes_accessed=2 * turns * width * width, transcendentals=0
        ),
        name="own_rows",
    )(place, halves, own)


def upper_blocks(width):
    return [(a, b) for a in range(0, width, TILE) for b in range(a, width, TILE)]


def identity(size):
    row = lax.broadcasted_iota(jnp.int32, (size, size), 0)
    column = lax.broadcasted_iota(jnp.int32, (size, size), 1)
    return jnp.where(row == column, 1.0, 0.0).astype(BF16)


def fold(half_ref, packed_ref):
    one = identity(TILE)
    for n, (a, b) in enumerate(upper_blocks(half_ref.shape[0])):
        block = half_ref[a:a + TILE, b:b + TILE]
        if a != b:
            block = block.astype(F32) + nt(one, half_ref[b:b + TILE, a:a + TILE])
        packed_ref[n] = block.astype(BF16)


def arrived_sum(refs, n):
    value = refs[0][n]
    for extra in refs[1:]:
        value = value + extra[n]
    return value


def fold_kernel(half_ref, packed_ref):
    fold(half_ref.at[0], packed_ref)


def hop_kernel(arrived, factor_ref, half_ref, *refs):
    out_ref, covariance, middle, ahead = refs[arrived:]
    width = factor_ref.shape[1]
    for n, (a, b) in enumerate(upper_blocks(width)):
        covariance[a:a + TILE, b:b + TILE] = arrived_sum(refs[:arrived], n)
    for j in range(0, width, TILE):
        cols = slice(j, j + TILE)
        middle[:, cols] = jnp.dot(
            factor_ref[0, :, :j + TILE], covariance[:j + TILE, cols], preferred_element_type=F32
        ).astype(BF16)
    for j in range(0, width, TILE):
        cols = slice(j, j + TILE)
        ahead[:, cols] = (nt(middle[...], factor_ref[0, cols, :]) + half_ref[0, :, cols].astype(F32)).astype(BF16)
    fold(ahead, out_ref)


def hop(factors, halves, packed):
    width = halves.shape[1]
    shape = (len(upper_blocks(width)), TILE, TILE)
    blocks = pl.BlockSpec(shape, lambda i: (0, 0, 0), pipeline_mode=pl.Buffered(1))
    whole = pl.BlockSpec((1, width, width), lambda i: (0, 0, 0), pipeline_mode=pl.Buffered(1))
    if not packed:
        return pl.pallas_call(
            fold_kernel,
            grid=(1,),
            in_specs=[whole],
            out_specs=blocks,
            out_shape=jax.ShapeDtypeStruct(shape, BF16),
            compiler_params=pltpu.CompilerParams(vmem_limit_bytes=8 * MIB),
            name="fold",
        )(halves)
    return pl.pallas_call(
        functools.partial(hop_kernel, len(packed)),
        grid=(1,),
        in_specs=[whole, whole] + [blocks] * len(packed),
        out_specs=blocks,
        out_shape=jax.ShapeDtypeStruct(shape, BF16),
        scratch_shapes=[pltpu.VMEM((width, width), BF16)] * 3,
        compiler_params=pltpu.CompilerParams(vmem_limit_bytes=16 * MIB),
        cost_estimate=pl.CostEstimate(flops=4 * width**3, bytes_accessed=10 * width * width, transcendentals=0),
        name="hop",
    )(factors, halves, *packed)


def finish_kernel(arrived, factor_ref, own_ref, mine_ref, *refs):
    out_ref, covariance, middle = refs[arrived:]
    turn = pl.program_id(0)
    rows = own_ref.shape[1]
    steps = mine_ref.shape[0]
    width = covariance.shape[0]

    @pl.when(turn == 0)
    def _():
        one = identity(TILE)
        for n, (a, b) in enumerate(upper_blocks(width)):
            block = arrived_sum(refs[:arrived], n)
            turned = nt(one, block)
            if a == b:
                covariance[a:a + TILE, b:b + TILE] = (block.astype(F32) + turned).astype(BF16)
            else:
                covariance[a:a + TILE, b:b + TILE] = block
                covariance[b:b + TILE, a:a + TILE] = turned.astype(BF16)
        mine = mine_ref[...].reshape(steps * rows, width)
        for j in range(0, width, TILE):
            cols = slice(j, j + TILE)
            middle[:, cols] = jnp.dot(mine, covariance[:, cols], preferred_element_type=F32).astype(BF16)

    left = middle[pl.ds(pl.multiple_of(turn * rows, 16), rows), :]
    out_ref[0] = nt(left, factor_ref[0]) + own_ref[0]


def finish(factors, own, mine, packed):
    steps, rows, width = own.shape
    whole = pl.BlockSpec(packed[0].shape, lambda i: (0, 0, 0), pipeline_mode=pl.Buffered(1))
    return pl.pallas_call(
        functools.partial(finish_kernel, len(packed)),
        grid=(steps,),
        in_specs=[
            pl.BlockSpec((1, width, width), lambda i: (i, 0, 0)),
            pl.BlockSpec((1, rows, width), lambda i: (i, 0, 0)),
            pl.BlockSpec(mine.shape, lambda i: (0, 0, 0), pipeline_mode=pl.Buffered(1)),
        ]
        + [whole] * len(packed),
        out_specs=pl.BlockSpec((1, rows, width), lambda i: (i, 0, 0)),
        scratch_shapes=[pltpu.VMEM((width, width), BF16), pltpu.VMEM((steps * rows, width), BF16)],
        out_shape=jax.ShapeDtypeStruct((steps, rows, width), F32),
        compiler_params=pltpu.CompilerParams(vmem_limit_bytes=20 * MIB),
        name="finish",
    )(factors, own, mine, *packed)


def ring_order(line, across):
    cycle = []
    for a in range(line):
        columns = list(range(1, across))
        cycle += [a * across + b for b in (columns if a % 2 == 0 else columns[::-1])]
    return cycle + [a * across for a in reversed(range(line))]


def pieces(steps):
    small = max(steps // 8, 1)
    cuts = [0, 2 * small, 4 * small, 6 * small, steps]
    return list(zip(cuts, cuts[1:]))[::-1]


def local(gains, increments, terminal):
    count = lax.axis_size("tile")
    blocks = lax.axis_size("tm")
    line = math.gcd(count, LINE)
    steps = gains.shape[0]
    place = lax.axis_index("tile").astype(jnp.int32)
    last = (lax.axis_index("tm") == blocks - 1).astype(jnp.int32).reshape(1)
    cycle = ring_order(line, count // line)

    def passed(array, way):
        return lax.ppermute(array, "tile", [(cycle[n], cycle[(n + way) % count]) for n in range(count)])

    def origins(way):
        table = [[cycle[(cycle.index(d) - way * hop) % count] for hop in range(count)] for d in range(count)]
        return jnp.asarray(table, jnp.int32)[place]

    ranges = pieces(steps)
    own = pack(place.reshape(1), gains, increments, count, ranges)
    own, end = lax.optimization_barrier((own, terminal.astype(BF16)))
    end = lax.all_gather(end, "tile", axis=0, tiled=True)
    arrived = []
    for turn, array in enumerate(own):
        way = 1 if turn % 2 == 0 else -1
        if turn >= 2:
            before = arrived[turn - 2]
            array, before[GATE] = lax.optimization_barrier((array, before[GATE]))
            for hop_count in range(GATE + 1, count):
                before[hop_count] = passed(before[hop_count - 1], way)
                if hop_count == GATE + 1:
                    before[hop_count], end = lax.optimization_barrier((before[hop_count], end))
        found = [array]
        for hop_count in range(1, count):
            found.append(passed(found[-1], way))
        arrived.append(found)
    state, half = None, end
    for turn in range(2):
        reached = count - 3 + turn
        blocks_here, _ = lax.optimization_barrier((arrived[turn], (arrived[2][reached], arrived[3][reached])))
        low, high = ranges[turn]
        *state, half = compose(last, origins(1 - 2 * turn), blocks_here, half, state, low, high - low, steps)
    factors, own, mine = state
    early = None
    for turn in range(2, 4):
        low, high = ranges[turn]
        early = chain(origins(5 - 2 * turn), arrived[turn], half, early, low, high - low, ranges[2][1])
    factors, mine = extend_factors(place.reshape(1), early[0], factors, mine)
    own = own_rows(place.reshape(1), early[1], own)
    packed = []
    for turn in range(blocks - 1, 0, -1):
        packed.append(lax.ppermute(hop(factors, early[1], packed), "tm", [(turn, turn - 1)]))
    return finish(factors, own, mine, packed)


def solution(mesh):
    return jax.shard_map(
        local,
        mesh=mesh,
        in_specs=(P("tm", "tile", None), P("tm", "tile", None), P("tile", None)),
        out_specs=P("tm", "tile", None),
        check_vma=False,
    )
```

```python
import functools
import math

import jax
import jax.numpy as jnp
from jax import lax
from jax.experimental import pallas as pl
from jax.experimental.pallas import tpu as pltpu
from jax.sharding import PartitionSpec as P

BF16 = jnp.bfloat16
F32 = jnp.float32
LANES = 128
TILE = 256
LINE = 4
GATE = 2
MIB = 1024 * 1024
CLAIM = 60 * MIB


def half_width(rows, count):
    used = (count // 2 + 1) * rows
    return used, -(-used // LANES) * LANES


def nt(left, right):
    return lax.dot_general(left, right, (((1,), (1,)), ((), ())), preferred_element_type=F32)


def packed_half(increment, place, count):
    rows, width = increment.shape
    used, half = half_width(rows, count)
    turned = pltpu.roll(increment, lax.rem(width - place * rows, width), 1)[:, :half]
    column = lax.broadcasted_iota(jnp.int32, turned.shape, 1)
    halved = (column < rows) | (column >= used - rows)
    weight = jnp.where(column < used, jnp.where(halved, 0.5, 1.0), 0.0)
    return (turned * weight).astype(BF16)


def unpacked_half(piece, start, width):
    piece = piece.astype(F32)
    rest = width - piece.shape[1]
    wide = jnp.concatenate([piece, jnp.zeros((piece.shape[0], rest), F32)], axis=1) if rest else piece
    return pltpu.roll(wide, start, 1) if start else wide


def pack_kernel(count, ranges, place_ref, gain_ref, increment_ref, terminal_ref, *packed_refs):
    width = gain_ref.shape[2]
    half = half_width(gain_ref.shape[1], count)[1]
    stride = width + half
    place = place_ref[0]
    for (low, high), packed_ref in zip(ranges, packed_refs):
        for step in range(low, high):
            base = (step - low) * stride
            packed_ref[:, base:base + width] = gain_ref[step]
            packed_ref[:, base + width:base + stride] = packed_half(increment_ref[step], place, count)
    end = packed_half(terminal_ref[...], place, count)
    for turn in range(2):
        base = (ranges[turn][1] - ranges[turn][0]) * stride
        packed_refs[turn][:, base:] = end[:, turn * half // 2:(turn + 1) * half // 2]


def pack(place, gains, increments, terminal, count, ranges):
    rows, width = gains.shape[1:]
    half = half_width(rows, count)[1]
    lanes = [(high - low) * (width + half) + half // 2 * (n < 2) for n, (low, high) in enumerate(ranges)]
    vmem = pl.BlockSpec(memory_space=pltpu.VMEM)
    return pl.pallas_call(
        functools.partial(pack_kernel, count, ranges),
        in_specs=[pl.BlockSpec(memory_space=pltpu.SMEM), vmem, vmem, vmem],
        out_specs=[vmem] * len(lanes),
        out_shape=[jax.ShapeDtypeStruct((rows, size), BF16) for size in lanes],
        compiler_params=pltpu.CompilerParams(vmem_limit_bytes=CLAIM),
        name="pack",
    )(place, gains, increments, terminal)


def unpack(raw, half):
    count, rows, _ = raw.shape
    for n in range(count):
        half[n * rows:(n + 1) * rows, :] = unpacked_half(raw[n], n * rows, half.shape[1]).astype(BF16)


def origins(place, cycle, way):
    count = len(cycle)

    def look(table, at):
        return sum(jnp.where(at == n, value, 0) for n, value in enumerate(table))

    spot = look([cycle.index(d) for d in range(count)], place)
    return [look(cycle, lax.rem(spot - way * n + count, count)) for n in range(count)]


def assemble(places, blocks, gain, fresh, raw):
    rows = blocks[0].shape[0]
    width = gain.shape[0]
    for place, block in zip(places, blocks):
        gain[pl.ds(pl.multiple_of(place * rows, 16), rows), :] = block[:, :width]
        raw[place] = block[:, width:]
    unpack(raw, fresh)


def advance(gain, half, fresh, middle):
    width = half.shape[0]
    for j in range(0, width, TILE):
        cols = slice(j, j + TILE)
        middle[:, cols] = jnp.dot(gain[...], half[:, cols], preferred_element_type=F32).astype(BF16)
    for j in range(0, width, TILE):
        cols = slice(j, j + TILE)
        half[:, cols] = (nt(middle[...], gain[cols, :]) + fresh[:, cols].astype(F32)).astype(BF16)


def extend(gain, factor):
    for j in range(0, factor.shape[0], TILE):
        cols = slice(j, j + TILE)
        factor[:, cols] = jnp.dot(gain[...], factor[:, cols], preferred_element_type=F32).astype(BF16)


def whole_rows(half, mine, rows):
    picked = lax.broadcasted_iota(jnp.int32, (rows, half.shape[0]), 1) == mine + lax.broadcasted_iota(
        jnp.int32, (rows, half.shape[0]), 0
    )
    own = half[pl.ds(mine, rows), :].astype(F32)
    return own + nt(jnp.where(picked, 1.0, 0.0).astype(BF16), half[...])


def compose_kernel(cycle, way, first, last_ref, place_ref, *refs):
    count = len(cycle)
    places = origins(place_ref[0], cycle, way)
    blocks, refs = refs[:count], refs[count:]
    if first:
        ends, refs = refs[:2 * count], refs[2 * count:]
    else:
        half_in, factor_in, refs = refs[0], refs[1], refs[4:]
    factor_out, own_out, mine_out, half, gain, factor, fresh, middle, raw = refs
    rows = blocks[0].shape[0]

    @pl.when(pl.program_id(0) == 0)
    def _():
        if first:
            scale = jnp.where(last_ref[0] == 1, 1.0, 0.0).astype(BF16)
            cut = ends[0].shape[1]
            for n, end in enumerate(ends):
                spots = places if n < count else origins(place_ref[0], cycle, -way)
                raw[spots[n % count], :, n // count * cut:(n // count + 1) * cut] = end[...] * scale
            unpack(raw, half)
        else:
            factor[...] = factor_in[0]
            half[...] = half_in[...]

    assemble(places, blocks, gain, fresh, raw)
    if first:

        @pl.when(pl.program_id(0) == 0)
        def _():
            factor[...] = gain[...]

        pl.when(pl.program_id(0) > 0)(lambda: extend(gain, factor))
    else:
        extend(gain, factor)
    advance(gain, half, fresh, middle)
    mine = pl.multiple_of(place_ref[0] * rows, 16)
    own_out[0] = whole_rows(half, mine, rows)
    mine_out[0] = factor[pl.ds(mine, rows), :]
    factor_out[0] = factor[...]


def square(width, place=None):
    if place is None:
        return pl.BlockSpec((width, width), lambda i, *p: (0, 0), pipeline_mode=pl.Buffered(1))
    return pl.BlockSpec((1, width, width), lambda i, *p: (place(i), 0, 0))


def compose(last, place, cycle, way, blocks, ends, state, half, low, turns, steps):
    count = len(blocks)
    rows = blocks[0].shape[0]
    width = rows * count
    lanes = half_width(rows, count)[1]
    stride = width + lanes
    first = state is None
    anywhere = pl.BlockSpec(memory_space=pl.ANY)
    in_specs = [pl.BlockSpec((rows, stride), lambda i, *p: (0, turns - 1 - i))] * count
    if first:
        at = turns * stride // (lanes // 2)
        in_specs += [
            pl.BlockSpec((rows, lanes // 2), lambda i, *p: (0, at), pipeline_mode=pl.Buffered(1))
        ] * len(ends)
        args = ends
    else:
        after = pl.BlockSpec((1, width, width), lambda i, *p: (low + turns, 0, 0), pipeline_mode=pl.Buffered(1))
        in_specs += [square(width), after, anywhere, anywhere]
        args = [half, *state]
    band = pl.BlockSpec((1, rows, width), lambda i, *p: (low + turns - 1 - i, 0, 0))
    base = 2 + count + 1
    return pl.pallas_call(
        functools.partial(compose_kernel, cycle, way, first),
        grid_spec=pltpu.PrefetchScalarGridSpec(
            num_scalar_prefetch=2,
            grid=(turns,),
            in_specs=in_specs,
            out_specs=[square(width, lambda i: low + turns - 1 - i), band, band, square(width)],
            scratch_shapes=[pltpu.VMEM((width, width), BF16)] * 4 + [pltpu.VMEM((count, rows, lanes), BF16)],
        ),
        out_shape=[
            jax.ShapeDtypeStruct((steps, width, width), BF16),
            jax.ShapeDtypeStruct((steps, rows, width), F32),
            jax.ShapeDtypeStruct((steps, rows, width), BF16),
            jax.ShapeDtypeStruct((width, width), BF16),
        ],
        input_output_aliases={} if first else {base: 0, base + 1: 1, base + 2: 2},
        compiler_params=pltpu.CompilerParams(vmem_limit_bytes=18 * MIB),
        cost_estimate=pl.CostEstimate(
            flops=6 * turns * width**3, bytes_accessed=8 * turns * width * width, transcendentals=0
        ),
        name="compose",
    )(last, place, *blocks, *args)


def chain_kernel(cycle, way, place_ref, *refs):
    count = len(cycle)
    places = origins(place_ref[0], cycle, way)
    blocks, refs = refs[:count], refs[count:]
    half_in, refs = refs[0], refs[-7:]
    gain_out, half_out, gain, half, fresh, middle, raw = refs

    @pl.when(pl.program_id(0) == 0)
    def _():
        half[...] = half_in[...].reshape(half.shape)

    assemble(places, blocks, gain, fresh, raw)
    gain_out[0] = gain[...]
    advance(gain, half, fresh, middle)
    half_out[0] = half[...]


def chain(place, cycle, way, blocks, half, state, low, turns, steps):
    count = len(blocks)
    rows = blocks[0].shape[0]
    width = rows * count
    lanes = half_width(rows, count)[1]
    anywhere = pl.BlockSpec(memory_space=pl.ANY)
    in_specs = [pl.BlockSpec((rows, width + lanes), lambda i, *p: (0, turns - 1 - i))] * count
    if state is None:
        in_specs += [square(width)]
        args = [half]
    else:
        in_specs += [
            pl.BlockSpec((1, width, width), lambda i, *p: (low + turns, 0, 0), pipeline_mode=pl.Buffered(1)),
            anywhere,
        ]
        args = [state[1], state[0]]
    whole = square(width, lambda i: low + turns - 1 - i)
    return pl.pallas_call(
        functools.partial(chain_kernel, cycle, way),
        grid_spec=pltpu.PrefetchScalarGridSpec(
            num_scalar_prefetch=1,
            grid=(turns,),
            in_specs=in_specs,
            out_specs=[whole, whole],
            scratch_shapes=[pltpu.VMEM((width, width), BF16)] * 4 + [pltpu.VMEM((count, rows, lanes), BF16)],
        ),
        out_shape=[jax.ShapeDtypeStruct((steps, width, width), BF16)] * 2,
        input_output_aliases={} if state is None else {1 + count + 1: 0, 1 + count: 1},
        compiler_params=pltpu.CompilerParams(vmem_limit_bytes=18 * MIB),
        cost_estimate=pl.CostEstimate(
            flops=4 * turns * width**3, bytes_accessed=8 * turns * width * width, transcendentals=0
        ),
        name="chain",
    )(place, *blocks, *args)


def factors_kernel(place_ref, gain_ref, factor_in, mine_ref, factor_out, mine_out, factor):
    del mine_ref
    rows = mine_out.shape[1]

    @pl.when(pl.program_id(0) == 0)
    def _():
        factor[...] = factor_in[0]

    extend(gain_ref.at[0], factor)
    mine_out[0] = factor[pl.ds(pl.multiple_of(place_ref[0] * rows, 16), rows), :]
    factor_out[0] = factor[...]


def extend_factors(place, gains, factors, mine):
    turns, width, _ = gains.shape
    steps, rows, _ = mine.shape
    anywhere = pl.BlockSpec(memory_space=pl.ANY)
    return pl.pallas_call(
        factors_kernel,
        grid_spec=pltpu.PrefetchScalarGridSpec(
            num_scalar_prefetch=1,
            grid=(turns,),
            in_specs=[square(width, lambda i: turns - 1 - i), square(width, lambda i: turns), anywhere],
            out_specs=[
                square(width, lambda i: turns - 1 - i),
                pl.BlockSpec((1, rows, width), lambda i, *p: (turns - 1 - i, 0, 0)),
            ],
            scratch_shapes=[pltpu.VMEM((width, width), BF16)],
        ),
        out_shape=[
            jax.ShapeDtypeStruct((steps, width, width), BF16),
            jax.ShapeDtypeStruct((steps, rows, width), BF16),
        ],
        input_output_aliases={2: 0, 3: 1},
        compiler_params=pltpu.CompilerParams(vmem_limit_bytes=12 * MIB),
        cost_estimate=pl.CostEstimate(
            flops=2 * turns * width**3, bytes_accessed=4 * turns * width * width, transcendentals=0
        ),
        name="extend_factors",
    )(place, gains, factors, mine)


def rows_kernel(place_ref, half_ref, own_ref, own_out):
    del own_ref
    rows = own_out.shape[1]
    own_out[0] = whole_rows(half_ref.at[0], pl.multiple_of(place_ref[0] * rows, 16), rows)


def own_rows(place, halves, own):
    turns, width, _ = halves.shape
    steps, rows, _ = own.shape
    return pl.pallas_call(
        rows_kernel,
        grid_spec=pltpu.PrefetchScalarGridSpec(
            num_scalar_prefetch=1,
            grid=(turns,),
            in_specs=[square(width, lambda i: i), pl.BlockSpec(memory_space=pl.ANY)],
            out_specs=pl.BlockSpec((1, rows, width), lambda i, *p: (i, 0, 0)),
        ),
        out_shape=jax.ShapeDtypeStruct((steps, rows, width), F32),
        input_output_aliases={2: 0},
        compiler_params=pltpu.CompilerParams(vmem_limit_bytes=8 * MIB),
        cost_estimate=pl.CostEstimate(
            flops=2 * turns * rows * width**2, bytes_accessed=2 * turns * width * width, transcendentals=0
        ),
        name="own_rows",
    )(place, halves, own)


def upper_blocks(width):
    return [(a, b) for a in range(0, width, TILE) for b in range(a, width, TILE)]


def identity(size):
    row = lax.broadcasted_iota(jnp.int32, (size, size), 0)
    column = lax.broadcasted_iota(jnp.int32, (size, size), 1)
    return jnp.where(row == column, 1.0, 0.0).astype(BF16)


def fold(half_ref, packed_ref):
    one = identity(TILE)
    for n, (a, b) in enumerate(upper_blocks(half_ref.shape[0])):
        block = half_ref[a:a + TILE, b:b + TILE]
        if a != b:
            block = block.astype(F32) + nt(one, half_ref[b:b + TILE, a:a + TILE])
        packed_ref[n] = block.astype(BF16)


def arrived_sum(refs, n):
    value = refs[0][n]
    for extra in refs[1:]:
        value = value + extra[n]
    return value


def fold_kernel(half_ref, packed_ref):
    fold(half_ref.at[0], packed_ref)


def hop_kernel(arrived, factor_ref, half_ref, *refs):
    out_ref, covariance, middle, ahead = refs[arrived:]
    width = factor_ref.shape[1]
    for n, (a, b) in enumerate(upper_blocks(width)):
        covariance[a:a + TILE, b:b + TILE] = arrived_sum(refs[:arrived], n)
    for j in range(0, width, TILE):
        cols = slice(j, j + TILE)
        middle[:, cols] = jnp.dot(
            factor_ref[0, :, :j + TILE], covariance[:j + TILE, cols], preferred_element_type=F32
        ).astype(BF16)
    for j in range(0, width, TILE):
        cols = slice(j, j + TILE)
        ahead[:, cols] = (nt(middle[...], factor_ref[0, cols, :]) + half_ref[0, :, cols].astype(F32)).astype(BF16)
    fold(ahead, out_ref)


def hop(factors, halves, packed):
    width = halves.shape[1]
    shape = (len(upper_blocks(width)), TILE, TILE)
    blocks = pl.BlockSpec(shape, lambda i: (0, 0, 0), pipeline_mode=pl.Buffered(1))
    whole = pl.BlockSpec((1, width, width), lambda i: (0, 0, 0), pipeline_mode=pl.Buffered(1))
    if not packed:
        return pl.pallas_call(
            fold_kernel,
            grid=(1,),
            in_specs=[whole],
            out_specs=blocks,
            out_shape=jax.ShapeDtypeStruct(shape, BF16),
            compiler_params=pltpu.CompilerParams(vmem_limit_bytes=8 * MIB),
            name="fold",
        )(halves)
    return pl.pallas_call(
        functools.partial(hop_kernel, len(packed)),
        grid=(1,),
        in_specs=[whole, whole] + [blocks] * len(packed),
        out_specs=blocks,
        out_shape=jax.ShapeDtypeStruct(shape, BF16),
        scratch_shapes=[pltpu.VMEM((width, width), BF16)] * 3,
        compiler_params=pltpu.CompilerParams(vmem_limit_bytes=16 * MIB),
        cost_estimate=pl.CostEstimate(flops=4 * width**3, bytes_accessed=10 * width * width, transcendentals=0),
        name="hop",
    )(factors, halves, *packed)


def finish_kernel(arrived, factor_ref, own_ref, mine_ref, *refs):
    out_ref, covariance, middle = refs[arrived:]
    turn = pl.program_id(0)
    rows = own_ref.shape[1]
    steps = mine_ref.shape[0]
    width = covariance.shape[0]

    @pl.when(turn == 0)
    def _():
        one = identity(TILE)
        for n, (a, b) in enumerate(upper_blocks(width)):
            block = arrived_sum(refs[:arrived], n)
            turned = nt(one, block)
            if a == b:
                covariance[a:a + TILE, b:b + TILE] = (block.astype(F32) + turned).astype(BF16)
            else:
                covariance[a:a + TILE, b:b + TILE] = block
                covariance[b:b + TILE, a:a + TILE] = turned.astype(BF16)
        mine = mine_ref[...].reshape(steps * rows, width)
        for j in range(0, width, TILE):
            cols = slice(j, j + TILE)
            middle[:, cols] = jnp.dot(mine, covariance[:, cols], preferred_element_type=F32).astype(BF16)

    left = middle[pl.ds(pl.multiple_of(turn * rows, 16), rows), :]
    out_ref[0] = nt(left, factor_ref[0]) + own_ref[0]


def finish(factors, own, mine, packed):
    steps, rows, width = own.shape
    whole = pl.BlockSpec(packed[0].shape, lambda i: (0, 0, 0), pipeline_mode=pl.Buffered(1))
    return pl.pallas_call(
        functools.partial(finish_kernel, len(packed)),
        grid=(steps,),
        in_specs=[
            pl.BlockSpec((1, width, width), lambda i: (i, 0, 0)),
            pl.BlockSpec((1, rows, width), lambda i: (i, 0, 0)),
            pl.BlockSpec(mine.shape, lambda i: (0, 0, 0), pipeline_mode=pl.Buffered(1)),
        ]
        + [whole] * len(packed),
        out_specs=pl.BlockSpec((1, rows, width), lambda i: (i, 0, 0)),
        scratch_shapes=[pltpu.VMEM((width, width), BF16), pltpu.VMEM((steps * rows, width), BF16)],
        out_shape=jax.ShapeDtypeStruct((steps, rows, width), F32),
        compiler_params=pltpu.CompilerParams(vmem_limit_bytes=20 * MIB),
        name="finish",
    )(factors, own, mine, *packed)


def ring_order(line, across):
    cycle = []
    for a in range(line):
        columns = list(range(1, across))
        cycle += [a * across + b for b in (columns if a % 2 == 0 else columns[::-1])]
    return cycle + [a * across for a in reversed(range(line))]


def pieces(steps):
    small = max(steps // 8, 1)
    cuts = [0, 2 * small, 4 * small, 6 * small, steps]
    return list(zip(cuts, cuts[1:]))[::-1]


def local(gains, increments, terminal):
    count = lax.axis_size("tile")
    blocks = lax.axis_size("tm")
    line = math.gcd(count, LINE)
    steps = gains.shape[0]
    place = lax.axis_index("tile").astype(jnp.int32).reshape(1)
    last = (lax.axis_index("tm") == blocks - 1).astype(jnp.int32).reshape(1)
    cycle = ring_order(line, count // line)

    def passed(array, way):
        return lax.ppermute(array, "tile", [(cycle[n], cycle[(n + way) % count]) for n in range(count)])

    ranges = pieces(steps)
    own = pack(place, gains, increments, terminal, count, ranges)
    own, last = lax.optimization_barrier((own, last))
    arrived = []
    for turn, array in enumerate(own):
        way = 1 if turn % 2 == 0 else -1
        if turn >= 2:
            before = arrived[turn - 2]
            array, before[GATE] = lax.optimization_barrier((array, before[GATE]))
            for hop_count in range(GATE + 1, count):
                before[hop_count] = passed(before[hop_count - 1], way)
        found = [array]
        for hop_count in range(1, count):
            found.append(passed(found[-1], way))
        arrived.append(found)
    state, half = None, None
    for turn in range(2):
        reached = count - 3 + turn
        arrived[:2], _ = lax.optimization_barrier((arrived[:2], (arrived[2][reached], arrived[3][reached])))
        ends = [] if turn else arrived[0] + arrived[1]
        low, high = ranges[turn]
        *state, half = compose(last, place, cycle, 1 - 2 * turn, arrived[turn], ends, state, half, low, high - low, steps)
    factors, own, mine = state
    early = None
    for turn in range(2, 4):
        low, high = ranges[turn]
        early = chain(place, cycle, 5 - 2 * turn, arrived[turn], half, early, low, high - low, ranges[2][1])
    factors, mine = extend_factors(place, early[0], factors, mine)
    own = own_rows(place, early[1], own)
    packed = []
    for turn in range(blocks - 1, 0, -1):
        packed.append(lax.ppermute(hop(factors, early[1], packed), "tm", [(turn, turn - 1)]))
    return finish(factors, own, mine, packed)


def solution(mesh):
    return jax.shard_map(
        local,
        mesh=mesh,
        in_specs=(P("tm", "tile", None), P("tm", "tile", None), P("tile", None)),
        out_specs=P("tm", "tile", None),
        check_vma=False,
    )
```

```python
import functools
import math

import jax
import jax.numpy as jnp
from jax import lax
from jax.experimental import pallas as pl
from jax.experimental.pallas import tpu as pltpu
from jax.sharding import PartitionSpec as P

BF16 = jnp.bfloat16
F32 = jnp.float32
LANES = 128
TILE = 256
LINE = 4
GATE = 2
MIB = 1024 * 1024
CLAIM = 60 * MIB


def nt(left, right):
    return lax.dot_general(left, right, (((1,), (1,)), ((), ())), preferred_element_type=F32)


def packed_half(increment, place, count):
    rows, width = increment.shape
    turned = pltpu.roll(increment, lax.rem(width - place * rows, width), 1)
    column = lax.broadcasted_iota(jnp.int32, (rows, width // 2), 1)
    main = turned[:, :width // 2] * jnp.where(column < rows, 0.5, 1.0)
    opposite = turned[:, width // 2:width // 2 + LANES]
    lower = opposite[rows // 2:]
    side = jnp.concatenate([lower, pltpu.roll(lower, LANES - rows // 2, 1)], axis=0)
    return main.astype(BF16), jnp.where(place < count // 2, opposite, side)


def unpacked_half(main, extra, block, count):
    rows = main.shape[0]
    width = rows * count
    column = lax.broadcasted_iota(jnp.int32, extra.shape, 1)
    extra = jnp.where(column < rows // 2, extra, 0.0)
    if block >= count // 2:
        lower = extra[:rows // 2] + pltpu.roll(extra[rows // 2:], rows // 2, 1)
        extra = jnp.concatenate([jnp.zeros_like(lower), lower], axis=0)
    rest = jnp.zeros((rows, width // 2 - LANES), F32)
    wide = jnp.concatenate([main.astype(F32), extra, rest], axis=1)
    return pltpu.roll(wide, block * rows, 1) if block else wide


def pack_kernel(count, ranges, place_ref, gain_ref, increment_ref, *refs):
    outs = refs[-len(ranges):]
    rows, width = gain_ref.shape[1:]
    stride = width + width // 2
    place = place_ref[0]
    base = min(low for low, _ in ranges)
    column = lax.broadcasted_iota(jnp.int32, (rows, LANES), 1)
    for (low, high), packed_ref in zip(ranges, outs):
        extras = jnp.zeros((rows, LANES), F32)
        for step in range(high - low):
            at = step * stride
            main, extra = packed_half(increment_ref[low - base + step], place, count)
            packed_ref[:, at:at + width] = gain_ref[low - base + step]
            packed_ref[:, at + width:at + stride] = main
            shift = step * rows // 2
            here = (column >= shift) & (column < shift + rows // 2)
            extras = jnp.where(here, pltpu.roll(extra, shift, 1) if shift else extra, extras)
        packed_ref[:, (high - low) * stride:(high - low) * stride + LANES] = extras.astype(BF16)
    if len(refs) > len(ranges):
        main, extra = packed_half(refs[0][...], place, count)
        at = (ranges[0][1] - ranges[0][0]) * stride + LANES
        outs[0][:, at:] = main[:, :2 * LANES]
        outs[1][:, at:at + LANES] = main[:, 2 * LANES:]
        outs[1][:, at + LANES:] = extra.astype(BF16)


def pack(place, gains, increments, terminal, count, ranges):
    rows, width = gains.shape[1:]
    first, size = ranges[1][0], ranges[0][1] - ranges[1][0]
    ends = [] if terminal is None else [terminal]
    lanes = [(high - low) * (width + width // 2) + LANES * (1 + 2 * len(ends)) for low, high in ranges]
    some = pl.BlockSpec((size, rows, width), lambda i, p: (first // size, 0, 0))
    return pl.pallas_call(
        functools.partial(pack_kernel, count, ranges),
        grid_spec=pltpu.PrefetchScalarGridSpec(
            num_scalar_prefetch=1,
            grid=(1,),
            in_specs=[some, some] + [pl.BlockSpec((rows, width), lambda i, p: (0, 0))] * len(ends),
            out_specs=[pl.BlockSpec((rows, n), lambda i, p: (0, 0)) for n in lanes],
        ),
        out_shape=[jax.ShapeDtypeStruct((rows, n), BF16) for n in lanes],
        compiler_params=pltpu.CompilerParams(vmem_limit_bytes=CLAIM if ends else 14 * MIB),
        name="pack",
    )(place, gains, increments, *ends)


def unpack(raw, extras, step, half):
    count, rows, _ = raw.shape
    shift = lax.rem(LANES - step * (rows // 2), LANES)
    for n in range(count):
        extra = pltpu.roll(extras[n].astype(F32), shift, 1)
        half[n * rows:(n + 1) * rows, :] = unpacked_half(raw[n], extra, n, count).astype(BF16)


def origins(place, cycle, way):
    count = len(cycle)

    def look(table, at):
        return sum(jnp.where(at == n, value, 0) for n, value in enumerate(table))

    spot = look([cycle.index(d) for d in range(count)], place)
    return [look(cycle, lax.rem(spot - way * n + count, count)) for n in range(count)]


def assemble(places, blocks, sides, step, gain, fresh, raw, extras):
    rows = blocks[0].shape[0]
    width = gain.shape[0]
    for place, block, side in zip(places, blocks, sides):
        gain[pl.ds(pl.multiple_of(place * rows, 16), rows), :] = block[:, :width]
        raw[place] = block[:, width:]
        extras[place] = side[...]
    unpack(raw, extras, step, fresh)


def advance(gain, half, fresh, middle):
    width = half.shape[0]
    for j in range(0, width, TILE):
        cols = slice(j, j + TILE)
        middle[:, cols] = jnp.dot(gain[...], half[:, cols], preferred_element_type=F32).astype(BF16)
    for j in range(0, width, TILE):
        cols = slice(j, j + TILE)
        half[:, cols] = (nt(middle[...], gain[cols, :]) + fresh[:, cols].astype(F32)).astype(BF16)


def extend(gain, factor):
    for j in range(0, factor.shape[0], TILE):
        cols = slice(j, j + TILE)
        factor[:, cols] = jnp.dot(gain[...], factor[:, cols], preferred_element_type=F32).astype(BF16)


def whole_rows(half, mine, rows):
    picked = lax.broadcasted_iota(jnp.int32, (rows, half.shape[0]), 1) == mine + lax.broadcasted_iota(
        jnp.int32, (rows, half.shape[0]), 0
    )
    own = half[pl.ds(mine, rows), :].astype(F32)
    return own + nt(jnp.where(picked, 1.0, 0.0).astype(BF16), half[...])


def compose_kernel(cycle, way, first, last_ref, place_ref, *refs):
    count = len(cycle)
    places = origins(place_ref[0], cycle, way)
    blocks, sides, refs = refs[:count], refs[count:2 * count], refs[2 * count:]
    if first:
        ends, refs = refs[:4 * count], refs[4 * count:]
    else:
        half_in, factor_in, refs = refs[0], refs[1], refs[4:]
    factor_out, own_out, mine_out, half, gain, factor, fresh, middle, raw, extras = refs
    rows = blocks[0].shape[0]

    @pl.when(pl.program_id(0) == 0)
    def _():
        if first:
            scale = jnp.where(last_ref[0] == 1, 1.0, 0.0).astype(BF16)
            back = origins(place_ref[0], cycle, -way)
            for n in range(count):
                raw[places[n], :, :LANES] = ends[n][...] * scale
                raw[places[n], :, LANES:2 * LANES] = ends[count + n][...] * scale
                raw[back[n], :, 2 * LANES:] = ends[2 * count + n][...] * scale
                extras[back[n]] = ends[3 * count + n][...] * scale
            unpack(raw, extras, 0, half)
        else:
            factor[...] = factor_in[0]
            half[...] = half_in[...]

    step = pl.num_programs(0) - 1 - pl.program_id(0)
    assemble(places, blocks, sides, step, gain, fresh, raw, extras)
    if first:

        @pl.when(pl.program_id(0) == 0)
        def _():
            factor[...] = gain[...]

        pl.when(pl.program_id(0) > 0)(lambda: extend(gain, factor))
    else:
        extend(gain, factor)
    advance(gain, half, fresh, middle)
    mine = pl.multiple_of(place_ref[0] * rows, 16)
    own_out[0] = whole_rows(half, mine, rows)
    mine_out[0] = factor[pl.ds(mine, rows), :]
    factor_out[0] = factor[...]


def square(width, place=None):
    if place is None:
        return pl.BlockSpec((width, width), lambda i, *p: (0, 0), pipeline_mode=pl.Buffered(1))
    return pl.BlockSpec((1, width, width), lambda i, *p: (place(i), 0, 0))


def row_specs(blocks, turns):
    rows = blocks[0].shape[0]
    stride = rows * len(blocks) * 3 // 2
    step = pl.BlockSpec((rows, stride), lambda i, *p: (0, turns - 1 - i))
    side = pl.BlockSpec((rows, LANES), lambda i, *p: (0, turns * stride // LANES), pipeline_mode=pl.Buffered(1))
    return [step] * len(blocks) + [side] * len(blocks)


def row_scratch(count, rows):
    width = count * rows
    return [pltpu.VMEM((width, width), BF16)] * 4 + [
        pltpu.VMEM((count, rows, width // 2), BF16),
        pltpu.VMEM((count, rows, LANES), BF16),
    ]


def compose(last, place, cycle, way, blocks, ends, state, half, low, turns, steps):
    count = len(blocks)
    rows = blocks[0].shape[0]
    width = rows * count
    first = state is None
    anywhere = pl.BlockSpec(memory_space=pl.ANY)
    in_specs = row_specs(blocks, turns)
    if first:
        at = turns * width * 3 // 2 // LANES + 1
        for n in (at, at + 1):
            tile = pl.BlockSpec((rows, LANES), lambda i, *p, n=n: (0, n), pipeline_mode=pl.Buffered(1))
            in_specs += [tile] * count
        in_specs += in_specs[-2 * count:]
        args = ends[:count] * 2 + ends[count:] * 2
    else:
        after = pl.BlockSpec((1, width, width), lambda i, *p: (low + turns, 0, 0), pipeline_mode=pl.Buffered(1))
        in_specs += [square(width), after, anywhere, anywhere]
        args = [half, *state]
    band = pl.BlockSpec((1, rows, width), lambda i, *p: (low + turns - 1 - i, 0, 0))
    base = 2 + 2 * count + 1
    return pl.pallas_call(
        functools.partial(compose_kernel, cycle, way, first),
        grid_spec=pltpu.PrefetchScalarGridSpec(
            num_scalar_prefetch=2,
            grid=(turns,),
            in_specs=in_specs,
            out_specs=[square(width, lambda i: low + turns - 1 - i), band, band, square(width)],
            scratch_shapes=row_scratch(count, rows),
        ),
        out_shape=[
            jax.ShapeDtypeStruct((steps, width, width), BF16),
            jax.ShapeDtypeStruct((steps, rows, width), F32),
            jax.ShapeDtypeStruct((steps, rows, width), BF16),
            jax.ShapeDtypeStruct((width, width), BF16),
        ],
        input_output_aliases={} if first else {base: 0, base + 1: 1, base + 2: 2},
        compiler_params=pltpu.CompilerParams(vmem_limit_bytes=18 * MIB),
        cost_estimate=pl.CostEstimate(
            flops=6 * turns * width**3, bytes_accessed=8 * turns * width * width, transcendentals=0
        ),
        name="compose",
    )(last, place, *blocks, *blocks, *args)


def chain_kernel(cycle, way, place_ref, *refs):
    count = len(cycle)
    places = origins(place_ref[0], cycle, way)
    blocks, sides, refs = refs[:count], refs[count:2 * count], refs[2 * count:]
    half_in, refs = refs[0], refs[-8:]
    gain_out, half_out, gain, half, fresh, middle, raw, extras = refs

    @pl.when(pl.program_id(0) == 0)
    def _():
        half[...] = half_in[...].reshape(half.shape)

    step = pl.num_programs(0) - 1 - pl.program_id(0)
    assemble(places, blocks, sides, step, gain, fresh, raw, extras)
    gain_out[0] = gain[...]
    advance(gain, half, fresh, middle)
    half_out[0] = half[...]


def chain(place, cycle, way, blocks, half, state, low, turns, steps):
    count = len(blocks)
    rows = blocks[0].shape[0]
    width = rows * count
    anywhere = pl.BlockSpec(memory_space=pl.ANY)
    in_specs = row_specs(blocks, turns)
    if state is None:
        in_specs += [square(width)]
        args = [half]
    else:
        in_specs += [
            pl.BlockSpec((1, width, width), lambda i, *p: (low + turns, 0, 0), pipeline_mode=pl.Buffered(1)),
            anywhere,
        ]
        args = [state[1], state[0]]
    whole = square(width, lambda i: low + turns - 1 - i)
    return pl.pallas_call(
        functools.partial(chain_kernel, cycle, way),
        grid_spec=pltpu.PrefetchScalarGridSpec(
            num_scalar_prefetch=1,
            grid=(turns,),
            in_specs=in_specs,
            out_specs=[whole, whole],
            scratch_shapes=row_scratch(count, rows),
        ),
        out_shape=[jax.ShapeDtypeStruct((steps, width, width), BF16)] * 2,
        input_output_aliases={} if state is None else {1 + 2 * count + 1: 0, 1 + 2 * count: 1},
        compiler_params=pltpu.CompilerParams(vmem_limit_bytes=18 * MIB),
        cost_estimate=pl.CostEstimate(
            flops=4 * turns * width**3, bytes_accessed=8 * turns * width * width, transcendentals=0
        ),
        name="chain",
    )(place, *blocks, *blocks, *args)


def factors_kernel(place_ref, gain_ref, factor_in, mine_ref, factor_out, mine_out, factor):
    del mine_ref
    rows = mine_out.shape[1]

    @pl.when(pl.program_id(0) == 0)
    def _():
        factor[...] = factor_in[0]

    extend(gain_ref.at[0], factor)
    mine_out[0] = factor[pl.ds(pl.multiple_of(place_ref[0] * rows, 16), rows), :]
    factor_out[0] = factor[...]


def extend_factors(place, gains, factors, mine):
    turns, width, _ = gains.shape
    steps, rows, _ = mine.shape
    anywhere = pl.BlockSpec(memory_space=pl.ANY)
    return pl.pallas_call(
        factors_kernel,
        grid_spec=pltpu.PrefetchScalarGridSpec(
            num_scalar_prefetch=1,
            grid=(turns,),
            in_specs=[square(width, lambda i: turns - 1 - i), square(width, lambda i: turns), anywhere],
            out_specs=[
                square(width, lambda i: turns - 1 - i),
                pl.BlockSpec((1, rows, width), lambda i, *p: (turns - 1 - i, 0, 0)),
            ],
            scratch_shapes=[pltpu.VMEM((width, width), BF16)],
        ),
        out_shape=[
            jax.ShapeDtypeStruct((steps, width, width), BF16),
            jax.ShapeDtypeStruct((steps, rows, width), BF16),
        ],
        input_output_aliases={2: 0, 3: 1},
        compiler_params=pltpu.CompilerParams(vmem_limit_bytes=12 * MIB),
        cost_estimate=pl.CostEstimate(
            flops=2 * turns * width**3, bytes_accessed=4 * turns * width * width, transcendentals=0
        ),
        name="extend_factors",
    )(place, gains, factors, mine)


def rows_kernel(place_ref, half_ref, own_ref, own_out):
    del own_ref
    rows = own_out.shape[1]
    own_out[0] = whole_rows(half_ref.at[0], pl.multiple_of(place_ref[0] * rows, 16), rows)


def own_rows(place, halves, own):
    turns, width, _ = halves.shape
    steps, rows, _ = own.shape
    return pl.pallas_call(
        rows_kernel,
        grid_spec=pltpu.PrefetchScalarGridSpec(
            num_scalar_prefetch=1,
            grid=(turns,),
            in_specs=[square(width, lambda i: i), pl.BlockSpec(memory_space=pl.ANY)],
            out_specs=pl.BlockSpec((1, rows, width), lambda i, *p: (i, 0, 0)),
        ),
        out_shape=jax.ShapeDtypeStruct((steps, rows, width), F32),
        input_output_aliases={2: 0},
        compiler_params=pltpu.CompilerParams(vmem_limit_bytes=8 * MIB),
        cost_estimate=pl.CostEstimate(
            flops=2 * turns * rows * width**2, bytes_accessed=2 * turns * width * width, transcendentals=0
        ),
        name="own_rows",
    )(place, halves, own)


def upper_blocks(width):
    return [(a, b) for a in range(0, width, TILE) for b in range(a, width, TILE)]


def identity(size):
    row = lax.broadcasted_iota(jnp.int32, (size, size), 0)
    column = lax.broadcasted_iota(jnp.int32, (size, size), 1)
    return jnp.where(row == column, 1.0, 0.0).astype(BF16)


def fold(half_ref, packed_ref):
    one = identity(TILE)
    for n, (a, b) in enumerate(upper_blocks(half_ref.shape[0])):
        block = half_ref[a:a + TILE, b:b + TILE]
        if a != b:
            block = block.astype(F32) + nt(one, half_ref[b:b + TILE, a:a + TILE])
        packed_ref[n] = block.astype(BF16)


def arrived_sum(refs, n):
    value = refs[0][n]
    for extra in refs[1:]:
        value = value + extra[n]
    return value


def fold_kernel(half_ref, packed_ref):
    fold(half_ref.at[0], packed_ref)


def hop_kernel(arrived, factor_ref, half_ref, *refs):
    out_ref, covariance, middle, ahead = refs[arrived:]
    width = factor_ref.shape[1]
    for n, (a, b) in enumerate(upper_blocks(width)):
        covariance[a:a + TILE, b:b + TILE] = arrived_sum(refs[:arrived], n)
    for j in range(0, width, TILE):
        cols = slice(j, j + TILE)
        middle[:, cols] = jnp.dot(
            factor_ref[0, :, :j + TILE], covariance[:j + TILE, cols], preferred_element_type=F32
        ).astype(BF16)
    for j in range(0, width, TILE):
        cols = slice(j, j + TILE)
        ahead[:, cols] = (nt(middle[...], factor_ref[0, cols, :]) + half_ref[0, :, cols].astype(F32)).astype(BF16)
    fold(ahead, out_ref)


def hop(factors, halves, packed):
    width = halves.shape[1]
    shape = (len(upper_blocks(width)), TILE, TILE)
    blocks = pl.BlockSpec(shape, lambda i: (0, 0, 0), pipeline_mode=pl.Buffered(1))
    whole = pl.BlockSpec((1, width, width), lambda i: (0, 0, 0), pipeline_mode=pl.Buffered(1))
    if not packed:
        return pl.pallas_call(
            fold_kernel,
            grid=(1,),
            in_specs=[whole],
            out_specs=blocks,
            out_shape=jax.ShapeDtypeStruct(shape, BF16),
            compiler_params=pltpu.CompilerParams(vmem_limit_bytes=8 * MIB),
            name="fold",
        )(halves)
    return pl.pallas_call(
        functools.partial(hop_kernel, len(packed)),
        grid=(1,),
        in_specs=[whole, whole] + [blocks] * len(packed),
        out_specs=blocks,
        out_shape=jax.ShapeDtypeStruct(shape, BF16),
        scratch_shapes=[pltpu.VMEM((width, width), BF16)] * 3,
        compiler_params=pltpu.CompilerParams(vmem_limit_bytes=16 * MIB),
        cost_estimate=pl.CostEstimate(flops=4 * width**3, bytes_accessed=10 * width * width, transcendentals=0),
        name="hop",
    )(factors, halves, *packed)


def finish_kernel(arrived, factor_ref, own_ref, mine_ref, *refs):
    out_ref, covariance, middle = refs[arrived:]
    turn = pl.program_id(0)
    rows = own_ref.shape[1]
    steps = mine_ref.shape[0]
    width = covariance.shape[0]

    @pl.when(turn == 0)
    def _():
        one = identity(TILE)
        for n, (a, b) in enumerate(upper_blocks(width)):
            block = arrived_sum(refs[:arrived], n)
            turned = nt(one, block)
            if a == b:
                covariance[a:a + TILE, b:b + TILE] = (block.astype(F32) + turned).astype(BF16)
            else:
                covariance[a:a + TILE, b:b + TILE] = block
                covariance[b:b + TILE, a:a + TILE] = turned.astype(BF16)
        mine = mine_ref[...].reshape(steps * rows, width)
        for j in range(0, width, TILE):
            cols = slice(j, j + TILE)
            middle[:, cols] = jnp.dot(mine, covariance[:, cols], preferred_element_type=F32).astype(BF16)

    left = middle[pl.ds(pl.multiple_of(turn * rows, 16), rows), :]
    out_ref[0] = nt(left, factor_ref[0]) + own_ref[0]


def finish(factors, own, mine, packed):
    steps, rows, width = own.shape
    whole = pl.BlockSpec(packed[0].shape, lambda i: (0, 0, 0), pipeline_mode=pl.Buffered(1))
    return pl.pallas_call(
        functools.partial(finish_kernel, len(packed)),
        grid=(steps,),
        in_specs=[
            pl.BlockSpec((1, width, width), lambda i: (i, 0, 0)),
            pl.BlockSpec((1, rows, width), lambda i: (i, 0, 0)),
            pl.BlockSpec(mine.shape, lambda i: (0, 0, 0), pipeline_mode=pl.Buffered(1)),
        ]
        + [whole] * len(packed),
        out_specs=pl.BlockSpec((1, rows, width), lambda i: (i, 0, 0)),
        scratch_shapes=[pltpu.VMEM((width, width), BF16), pltpu.VMEM((steps * rows, width), BF16)],
        out_shape=jax.ShapeDtypeStruct((steps, rows, width), F32),
        compiler_params=pltpu.CompilerParams(vmem_limit_bytes=20 * MIB),
        name="finish",
    )(factors, own, mine, *packed)


def ring_order(line, across):
    cycle = []
    for a in range(line):
        columns = list(range(1, across))
        cycle += [a * across + b for b in (columns if a % 2 == 0 else columns[::-1])]
    return cycle + [a * across for a in reversed(range(line))]


def pieces(steps):
    small = max(steps // 8, 1)
    cuts = [0, 2 * small, 4 * small, 6 * small, steps]
    return list(zip(cuts, cuts[1:]))[::-1]


def local(gains, increments, terminal):
    count = lax.axis_size("tile")
    blocks = lax.axis_size("tm")
    line = math.gcd(count, LINE)
    steps = gains.shape[0]
    place = lax.axis_index("tile").astype(jnp.int32).reshape(1)
    last = (lax.axis_index("tm") == blocks - 1).astype(jnp.int32).reshape(1)
    cycle = ring_order(line, count // line)

    def passed(array, way):
        return lax.ppermute(array, "tile", [(cycle[n], cycle[(n + way) % count]) for n in range(count)])

    ranges = pieces(steps)
    own = list(pack(place, gains, increments, terminal, count, ranges[:2]))
    own += pack(place, gains, increments, None, count, ranges[2:])
    own[:2], last = lax.optimization_barrier((own[:2], last))
    arrived = []
    for turn, array in enumerate(own):
        way = 1 if turn % 2 == 0 else -1
        if turn >= 2:
            before = arrived[turn - 2]
            array, before[GATE] = lax.optimization_barrier((array, before[GATE]))
            for hop_count in range(GATE + 1, count):
                before[hop_count] = passed(before[hop_count - 1], way)
        found = [array]
        for hop_count in range(1, count):
            found.append(passed(found[-1], way))
        arrived.append(found)
    state, half = None, None
    for turn in range(2):
        reached = count - 3 + turn
        arrived[:2], _ = lax.optimization_barrier((arrived[:2], (arrived[2][reached], arrived[3][reached])))
        ends = [] if turn else arrived[0] + arrived[1]
        low, high = ranges[turn]
        *state, half = compose(last, place, cycle, 1 - 2 * turn, arrived[turn], ends, state, half, low, high - low, steps)
    factors, own, mine = state
    early = None
    for turn in range(2, 4):
        low, high = ranges[turn]
        early = chain(place, cycle, 5 - 2 * turn, arrived[turn], half, early, low, high - low, ranges[2][1])
    factors, mine = extend_factors(place, early[0], factors, mine)
    own = own_rows(place, early[1], own)
    packed = []
    for turn in range(blocks - 1, 0, -1):
        packed.append(lax.ppermute(hop(factors, early[1], packed), "tm", [(turn, turn - 1)]))
    return finish(factors, own, mine, packed)


def solution(mesh):
    return jax.shard_map(
        local,
        mesh=mesh,
        in_specs=(P("tm", "tile", None), P("tm", "tile", None), P("tile", None)),
        out_specs=P("tm", "tile", None),
        check_vma=False,
    )
```

```python
import functools
import math

import jax
import jax.numpy as jnp
from jax import lax
from jax.experimental import pallas as pl
from jax.experimental.pallas import tpu as pltpu
from jax.sharding import PartitionSpec as P

BF16 = jnp.bfloat16
F32 = jnp.float32
LANES = 128
TILE = 256
LINE = 4
GATE = 2
MIB = 1024 * 1024
CLAIM = 60 * MIB


def nt(left, right):
    return lax.dot_general(left, right, (((1,), (1,)), ((), ())), preferred_element_type=F32)


def packed_half(increment, place, count):
    rows, width = increment.shape
    turned = pltpu.roll(increment, lax.rem(width - place * rows, width), 1)
    column = lax.broadcasted_iota(jnp.int32, (rows, width // 2), 1)
    main = turned[:, :width // 2] * jnp.where(column < rows, 0.5, 1.0)
    opposite = turned[:, width // 2:width // 2 + LANES]
    lower = opposite[rows // 2:]
    side = jnp.concatenate([lower, pltpu.roll(lower, LANES - rows // 2, 1)], axis=0)
    return main.astype(BF16), jnp.where(place < count // 2, opposite, side)


def unpacked_half(main, extra, block, count):
    rows = main.shape[0]
    width = rows * count
    column = lax.broadcasted_iota(jnp.int32, extra.shape, 1)
    extra = jnp.where(column < rows // 2, extra, 0.0)
    if block >= count // 2:
        lower = extra[:rows // 2] + pltpu.roll(extra[rows // 2:], rows // 2, 1)
        extra = jnp.concatenate([jnp.zeros_like(lower), lower], axis=0)
    rest = jnp.zeros((rows, width // 2 - LANES), F32)
    wide = jnp.concatenate([main.astype(F32), extra, rest], axis=1)
    return pltpu.roll(wide, block * rows, 1) if block else wide


def pack_kernel(count, ranges, place_ref, gain_ref, increment_ref, *refs):
    outs = refs[-len(ranges):]
    rows, width = gain_ref.shape[1:]
    stride = width + width // 2
    place = place_ref[0]
    base = min(low for low, _ in ranges)
    column = lax.broadcasted_iota(jnp.int32, (rows, LANES), 1)
    for (low, high), packed_ref in zip(ranges, outs):
        extras = jnp.zeros((rows, LANES), F32)
        for step in range(high - low):
            at = step * stride
            main, extra = packed_half(increment_ref[low - base + step], place, count)
            packed_ref[:, at:at + width] = gain_ref[low - base + step]
            packed_ref[:, at + width:at + stride] = main
            shift = step * rows // 2
            here = (column >= shift) & (column < shift + rows // 2)
            extras = jnp.where(here, pltpu.roll(extra, shift, 1) if shift else extra, extras)
        packed_ref[:, (high - low) * stride:(high - low) * stride + LANES] = extras.astype(BF16)
    if len(refs) > len(ranges):
        main, extra = packed_half(refs[0][...], place, count)
        at = (ranges[0][1] - ranges[0][0]) * stride + LANES
        outs[0][:, at:] = main[:, :2 * LANES]
        outs[1][:, at:at + LANES] = main[:, 2 * LANES:]
        outs[1][:, at + LANES:] = extra.astype(BF16)


def pack(place, gains, increments, terminal, count, ranges):
    rows, width = gains.shape[1:]
    first, size = ranges[1][0], ranges[0][1] - ranges[1][0]
    ends = [] if terminal is None else [terminal]
    lanes = [(high - low) * (width + width // 2) + LANES * (1 + 2 * len(ends)) for low, high in ranges]
    some = pl.BlockSpec((size, rows, width), lambda i, p: (first // size, 0, 0))
    return pl.pallas_call(
        functools.partial(pack_kernel, count, ranges),
        grid_spec=pltpu.PrefetchScalarGridSpec(
            num_scalar_prefetch=1,
            grid=(1,),
            in_specs=[some, some] + [pl.BlockSpec((rows, width), lambda i, p: (0, 0))] * len(ends),
            out_specs=[pl.BlockSpec((rows, n), lambda i, p: (0, 0)) for n in lanes],
        ),
        out_shape=[jax.ShapeDtypeStruct((rows, n), BF16) for n in lanes],
        compiler_params=pltpu.CompilerParams(vmem_limit_bytes=CLAIM if ends else 14 * MIB),
        name="pack",
    )(place, gains, increments, *ends)


def unpack(raw, extras, step, half):
    count, rows, _ = raw.shape
    shift = lax.rem(LANES - step * (rows // 2), LANES)
    for n in range(count):
        extra = pltpu.roll(extras[n].astype(F32), shift, 1)
        half[n * rows:(n + 1) * rows, :] = unpacked_half(raw[n], extra, n, count).astype(BF16)


def origins(place, cycle, way):
    count = len(cycle)

    def look(table, at):
        return sum(jnp.where(at == n, value, 0) for n, value in enumerate(table))

    spot = look([cycle.index(d) for d in range(count)], place)
    return [look(cycle, lax.rem(spot - way * n + count, count)) for n in range(count)]


def assemble(places, blocks, sides, step, gain, fresh, raw, extras):
    rows = blocks[0].shape[0]
    width = gain.shape[0]
    for place, block, side in zip(places, blocks, sides):
        gain[pl.ds(pl.multiple_of(place * rows, 16), rows), :] = block[:, :width]
        raw[place] = block[:, width:]
        extras[place] = side[...]
    unpack(raw, extras, step, fresh)


def advance(gain, half, fresh, middle):
    width = half.shape[0]
    for j in range(0, width, TILE):
        cols = slice(j, j + TILE)
        middle[:, cols] = jnp.dot(gain[...], half[:, cols], preferred_element_type=F32).astype(BF16)
    for j in range(0, width, TILE):
        cols = slice(j, j + TILE)
        half[:, cols] = (nt(middle[...], gain[cols, :]) + fresh[:, cols].astype(F32)).astype(BF16)


def extend(gain, factor):
    for j in range(0, factor.shape[0], TILE):
        cols = slice(j, j + TILE)
        factor[:, cols] = jnp.dot(gain[...], factor[:, cols], preferred_element_type=F32).astype(BF16)


def whole_rows(half, mine, rows):
    picked = lax.broadcasted_iota(jnp.int32, (rows, half.shape[0]), 1) == mine + lax.broadcasted_iota(
        jnp.int32, (rows, half.shape[0]), 0
    )
    own = half[pl.ds(mine, rows), :].astype(F32)
    return own + nt(jnp.where(picked, 1.0, 0.0).astype(BF16), half[...])


def compose_kernel(cycle, way, first, last_ref, place_ref, *refs):
    count = len(cycle)
    places = origins(place_ref[0], cycle, way)
    blocks, sides, refs = refs[:count], refs[count:2 * count], refs[2 * count:]
    if first:
        ends, refs = refs[:4 * count], refs[4 * count:]
    else:
        half_in, factor_in, refs = refs[0], refs[1], refs[4:]
    factor_out, own_out, mine_out, half, gain, factor, fresh, middle, raw, extras = refs
    rows = blocks[0].shape[0]

    @pl.when(pl.program_id(0) == 0)
    def _():
        if first:
            scale = jnp.where(last_ref[0] == 1, 1.0, 0.0).astype(BF16)
            back = origins(place_ref[0], cycle, -way)
            for n in range(count):
                raw[places[n], :, :LANES] = ends[n][...] * scale
                raw[places[n], :, LANES:2 * LANES] = ends[count + n][...] * scale
                raw[back[n], :, 2 * LANES:] = ends[2 * count + n][...] * scale
                extras[back[n]] = ends[3 * count + n][...] * scale
            unpack(raw, extras, 0, half)
        else:
            factor[...] = factor_in[0]
            half[...] = half_in[...]

    step = pl.num_programs(0) - 1 - pl.program_id(0)
    assemble(places, blocks, sides, step, gain, fresh, raw, extras)
    if first:

        @pl.when(pl.program_id(0) == 0)
        def _():
            factor[...] = gain[...]

        pl.when(pl.program_id(0) > 0)(lambda: extend(gain, factor))
    else:
        extend(gain, factor)
    advance(gain, half, fresh, middle)
    mine = pl.multiple_of(place_ref[0] * rows, 16)
    own_out[0] = whole_rows(half, mine, rows)
    mine_out[0] = factor[pl.ds(mine, rows), :]
    factor_out[0] = factor[...]


def square(width, place=None):
    if place is None:
        return pl.BlockSpec((width, width), lambda i, *p: (0, 0), pipeline_mode=pl.Buffered(1))
    return pl.BlockSpec((1, width, width), lambda i, *p: (place(i), 0, 0))


def row_specs(blocks, turns):
    rows = blocks[0].shape[0]
    stride = rows * len(blocks) * 3 // 2
    step = pl.BlockSpec((rows, stride), lambda i, *p: (0, turns - 1 - i))
    side = pl.BlockSpec((rows, LANES), lambda i, *p: (0, turns * stride // LANES), pipeline_mode=pl.Buffered(1))
    return [step] * len(blocks) + [side] * len(blocks)


def row_scratch(count, rows):
    width = count * rows
    return [pltpu.VMEM((width, width), BF16)] * 4 + [
        pltpu.VMEM((count, rows, width // 2), BF16),
        pltpu.VMEM((count, rows, LANES), BF16),
    ]


def compose(last, place, cycle, way, blocks, ends, state, half, low, turns, steps):
    count = len(blocks)
    rows = blocks[0].shape[0]
    width = rows * count
    first = state is None
    anywhere = pl.BlockSpec(memory_space=pl.ANY)
    in_specs = row_specs(blocks, turns)
    if first:
        at = turns * width * 3 // 2 // LANES + 1
        for n in (at, at + 1):
            tile = pl.BlockSpec((rows, LANES), lambda i, *p, n=n: (0, n), pipeline_mode=pl.Buffered(1))
            in_specs += [tile] * count
        in_specs += in_specs[-2 * count:]
        args = ends[:count] * 2 + ends[count:] * 2
    else:
        after = pl.BlockSpec((1, width, width), lambda i, *p: (low + turns, 0, 0), pipeline_mode=pl.Buffered(1))
        in_specs += [square(width), after, anywhere, anywhere]
        args = [half, *state]
    band = pl.BlockSpec((1, rows, width), lambda i, *p: (low + turns - 1 - i, 0, 0))
    base = 2 + 2 * count + 1
    return pl.pallas_call(
        functools.partial(compose_kernel, cycle, way, first),
        grid_spec=pltpu.PrefetchScalarGridSpec(
            num_scalar_prefetch=2,
            grid=(turns,),
            in_specs=in_specs,
            out_specs=[square(width, lambda i: low + turns - 1 - i), band, band, square(width)],
            scratch_shapes=row_scratch(count, rows),
        ),
        out_shape=[
            jax.ShapeDtypeStruct((steps, width, width), BF16),
            jax.ShapeDtypeStruct((steps, rows, width), F32),
            jax.ShapeDtypeStruct((steps, rows, width), BF16),
            jax.ShapeDtypeStruct((width, width), BF16),
        ],
        input_output_aliases={} if first else {base: 0, base + 1: 1, base + 2: 2},
        compiler_params=pltpu.CompilerParams(vmem_limit_bytes=18 * MIB),
        cost_estimate=pl.CostEstimate(
            flops=6 * turns * width**3, bytes_accessed=8 * turns * width * width, transcendentals=0
        ),
        name="compose",
    )(last, place, *blocks, *blocks, *args)


def chain_kernel(cycle, way, turns, place_ref, *refs):
    count = len(cycle)
    places = origins(place_ref[0], cycle, way)
    blocks, refs = refs[:count], refs[count:]
    half_in, refs = refs[0], refs[-9:]
    gain_out, half_out, half, middle, raw, extras, gain, fresh, spare = refs
    gains, freshes = (gain, spare.at[0]), (fresh, spare.at[1])
    rows, width = blocks[0].shape[0], half.shape[0]
    stride = width * 3 // 2
    side = slice(turns * stride, turns * stride + LANES)

    def prepare(turn):
        step = turns - 1 - turn
        lanes = slice(step * stride, (step + 1) * stride)
        parts = [block.at[:, lanes] for block in blocks]
        sides = [block.at[:, side] for block in blocks]
        assemble(places, parts, sides, step, gains[turn % 2], freshes[turn % 2], raw, extras)

    for turn in range(turns):

        @pl.when(pl.program_id(0) == turn)
        def _():
            if turn == 0:
                half[...] = half_in[...].reshape(half.shape)
                prepare(0)
            gain_out[0] = gains[turn % 2][...]
            if turn + 1 < turns:
                prepare(turn + 1)
            advance(gains[turn % 2], half, freshes[turn % 2], middle)
            half_out[0] = half[...]


def chain(place, cycle, way, blocks, half, state, low, turns, steps):
    count = len(blocks)
    rows = blocks[0].shape[0]
    width = rows * count
    anywhere = pl.BlockSpec(memory_space=pl.ANY)
    in_specs = [pl.BlockSpec(blocks[0].shape, lambda i, *p: (0, 0), pipeline_mode=pl.Buffered(1))] * count
    if state is None:
        in_specs += [square(width)]
        args = [half]
    else:
        in_specs += [
            pl.BlockSpec((1, width, width), lambda i, *p: (low + turns, 0, 0), pipeline_mode=pl.Buffered(1)),
            anywhere,
        ]
        args = [state[1], state[0]]
    whole = square(width, lambda i: low + turns - 1 - i)
    return pl.pallas_call(
        functools.partial(chain_kernel, cycle, way, turns),
        grid_spec=pltpu.PrefetchScalarGridSpec(
            num_scalar_prefetch=1,
            grid=(turns,),
            in_specs=in_specs,
            out_specs=[whole, whole],
            scratch_shapes=[
                pltpu.VMEM((width, width), BF16),
                pltpu.VMEM((width, width), BF16),
                pltpu.VMEM((count, rows, width // 2), BF16),
                pltpu.VMEM((count, rows, LANES), BF16),
                pltpu.VMEM((width, width), BF16),
                pltpu.VMEM((width, width), BF16),
                pltpu.VMEM((2, width, width), BF16),
            ],
        ),
        out_shape=[jax.ShapeDtypeStruct((steps, width, width), BF16)] * 2,
        input_output_aliases={} if state is None else {1 + count + 1: 0, 1 + count: 1},
        compiler_params=pltpu.CompilerParams(vmem_limit_bytes=18 * MIB),
        cost_estimate=pl.CostEstimate(
            flops=4 * turns * width**3, bytes_accessed=8 * turns * width * width, transcendentals=0
        ),
        name="chain",
    )(place, *blocks, *args)


def factors_kernel(place_ref, gain_ref, factor_in, mine_ref, factor_out, mine_out, factor):
    del mine_ref
    rows = mine_out.shape[1]

    @pl.when(pl.program_id(0) == 0)
    def _():
        factor[...] = factor_in[0]

    extend(gain_ref.at[0], factor)
    mine_out[0] = factor[pl.ds(pl.multiple_of(place_ref[0] * rows, 16), rows), :]
    factor_out[0] = factor[...]


def extend_factors(place, gains, factors, mine):
    turns, width, _ = gains.shape
    steps, rows, _ = mine.shape
    anywhere = pl.BlockSpec(memory_space=pl.ANY)
    return pl.pallas_call(
        factors_kernel,
        grid_spec=pltpu.PrefetchScalarGridSpec(
            num_scalar_prefetch=1,
            grid=(turns,),
            in_specs=[square(width, lambda i: turns - 1 - i), square(width, lambda i: turns), anywhere],
            out_specs=[
                square(width, lambda i: turns - 1 - i),
                pl.BlockSpec((1, rows, width), lambda i, *p: (turns - 1 - i, 0, 0)),
            ],
            scratch_shapes=[pltpu.VMEM((width, width), BF16)],
        ),
        out_shape=[
            jax.ShapeDtypeStruct((steps, width, width), BF16),
            jax.ShapeDtypeStruct((steps, rows, width), BF16),
        ],
        input_output_aliases={2: 0, 3: 1},
        compiler_params=pltpu.CompilerParams(vmem_limit_bytes=12 * MIB),
        cost_estimate=pl.CostEstimate(
            flops=2 * turns * width**3, bytes_accessed=4 * turns * width * width, transcendentals=0
        ),
        name="extend_factors",
    )(place, gains, factors, mine)


def rows_kernel(place_ref, half_ref, own_ref, own_out):
    del own_ref
    rows = own_out.shape[1]
    own_out[0] = whole_rows(half_ref.at[0], pl.multiple_of(place_ref[0] * rows, 16), rows)


def own_rows(place, halves, own):
    turns, width, _ = halves.shape
    steps, rows, _ = own.shape
    return pl.pallas_call(
        rows_kernel,
        grid_spec=pltpu.PrefetchScalarGridSpec(
            num_scalar_prefetch=1,
            grid=(turns,),
            in_specs=[square(width, lambda i: i), pl.BlockSpec(memory_space=pl.ANY)],
            out_specs=pl.BlockSpec((1, rows, width), lambda i, *p: (i, 0, 0)),
        ),
        out_shape=jax.ShapeDtypeStruct((steps, rows, width), F32),
        input_output_aliases={2: 0},
        compiler_params=pltpu.CompilerParams(vmem_limit_bytes=8 * MIB),
        cost_estimate=pl.CostEstimate(
            flops=2 * turns * rows * width**2, bytes_accessed=2 * turns * width * width, transcendentals=0
        ),
        name="own_rows",
    )(place, halves, own)


def upper_blocks(width):
    return [(a, b) for a in range(0, width, TILE) for b in range(a, width, TILE)]


def identity(size):
    row = lax.broadcasted_iota(jnp.int32, (size, size), 0)
    column = lax.broadcasted_iota(jnp.int32, (size, size), 1)
    return jnp.where(row == column, 1.0, 0.0).astype(BF16)


def fold(half_ref, packed_ref):
    one = identity(TILE)
    for n, (a, b) in enumerate(upper_blocks(half_ref.shape[0])):
        block = half_ref[a:a + TILE, b:b + TILE]
        if a != b:
            block = block.astype(F32) + nt(one, half_ref[b:b + TILE, a:a + TILE])
        packed_ref[n] = block.astype(BF16)


def arrived_sum(refs, n):
    value = refs[0][n]
    for extra in refs[1:]:
        value = value + extra[n]
    return value


def fold_kernel(half_ref, packed_ref):
    fold(half_ref.at[0], packed_ref)


def hop_kernel(arrived, factor_ref, half_ref, *refs):
    out_ref, covariance, middle, ahead = refs[arrived:]
    width = factor_ref.shape[1]
    for n, (a, b) in enumerate(upper_blocks(width)):
        covariance[a:a + TILE, b:b + TILE] = arrived_sum(refs[:arrived], n)
    for j in range(0, width, TILE):
        cols = slice(j, j + TILE)
        middle[:, cols] = jnp.dot(
            factor_ref[0, :, :j + TILE], covariance[:j + TILE, cols], preferred_element_type=F32
        ).astype(BF16)
    for j in range(0, width, TILE):
        cols = slice(j, j + TILE)
        ahead[:, cols] = (nt(middle[...], factor_ref[0, cols, :]) + half_ref[0, :, cols].astype(F32)).astype(BF16)
    fold(ahead, out_ref)


def hop(factors, halves, packed):
    width = halves.shape[1]
    shape = (len(upper_blocks(width)), TILE, TILE)
    blocks = pl.BlockSpec(shape, lambda i: (0, 0, 0), pipeline_mode=pl.Buffered(1))
    whole = pl.BlockSpec((1, width, width), lambda i: (0, 0, 0), pipeline_mode=pl.Buffered(1))
    if not packed:
        return pl.pallas_call(
            fold_kernel,
            grid=(1,),
            in_specs=[whole],
            out_specs=blocks,
            out_shape=jax.ShapeDtypeStruct(shape, BF16),
            compiler_params=pltpu.CompilerParams(vmem_limit_bytes=8 * MIB),
            name="fold",
        )(halves)
    return pl.pallas_call(
        functools.partial(hop_kernel, len(packed)),
        grid=(1,),
        in_specs=[whole, whole] + [blocks] * len(packed),
        out_specs=blocks,
        out_shape=jax.ShapeDtypeStruct(shape, BF16),
        scratch_shapes=[pltpu.VMEM((width, width), BF16)] * 3,
        compiler_params=pltpu.CompilerParams(vmem_limit_bytes=16 * MIB),
        cost_estimate=pl.CostEstimate(flops=4 * width**3, bytes_accessed=10 * width * width, transcendentals=0),
        name="hop",
    )(factors, halves, *packed)


def finish_kernel(arrived, factor_ref, own_ref, mine_ref, *refs):
    out_ref, covariance, middle = refs[arrived:]
    turn = pl.program_id(0)
    rows = own_ref.shape[1]
    steps = mine_ref.shape[0]
    width = covariance.shape[0]

    @pl.when(turn == 0)
    def _():
        one = identity(TILE)
        for n, (a, b) in enumerate(upper_blocks(width)):
            block = arrived_sum(refs[:arrived], n)
            turned = nt(one, block)
            if a == b:
                covariance[a:a + TILE, b:b + TILE] = (block.astype(F32) + turned).astype(BF16)
            else:
                covariance[a:a + TILE, b:b + TILE] = block
                covariance[b:b + TILE, a:a + TILE] = turned.astype(BF16)
        mine = mine_ref[...].reshape(steps * rows, width)
        for j in range(0, width, TILE):
            cols = slice(j, j + TILE)
            middle[:, cols] = jnp.dot(mine, covariance[:, cols], preferred_element_type=F32).astype(BF16)

    for n in range(out_ref.shape[0]):
        at = (turn * out_ref.shape[0] + n) * rows
        left = middle[pl.ds(pl.multiple_of(at, 16), rows), :]
        out_ref[n] = nt(left, factor_ref[n]) + own_ref[n]


def finish(factors, own, mine, packed):
    steps, rows, width = own.shape
    some = 2 if steps % 2 == 0 else 1
    whole = pl.BlockSpec(packed[0].shape, lambda i: (0, 0, 0), pipeline_mode=pl.Buffered(1))
    band = pl.BlockSpec((some, rows, width), lambda i: (i, 0, 0))
    return pl.pallas_call(
        functools.partial(finish_kernel, len(packed)),
        grid=(steps // some,),
        in_specs=[
            pl.BlockSpec((some, width, width), lambda i: (i, 0, 0)),
            band,
            pl.BlockSpec(mine.shape, lambda i: (0, 0, 0), pipeline_mode=pl.Buffered(1)),
        ]
        + [whole] * len(packed),
        out_specs=band,
        scratch_shapes=[pltpu.VMEM((width, width), BF16), pltpu.VMEM((steps * rows, width), BF16)],
        out_shape=jax.ShapeDtypeStruct((steps, rows, width), F32),
        compiler_params=pltpu.CompilerParams(vmem_limit_bytes=24 * MIB),
        name="finish",
    )(factors, own, mine, *packed)


def ring_order(line, across):
    cycle = []
    for a in range(line):
        columns = list(range(1, across))
        cycle += [a * across + b for b in (columns if a % 2 == 0 else columns[::-1])]
    return cycle + [a * across for a in reversed(range(line))]


def pieces(steps):
    small = max(steps // 8, 1)
    cuts = [0, 2 * small, 4 * small, 6 * small, steps]
    return list(zip(cuts, cuts[1:]))[::-1]


def local(gains, increments, terminal):
    count = lax.axis_size("tile")
    blocks = lax.axis_size("tm")
    line = math.gcd(count, LINE)
    steps = gains.shape[0]
    place = lax.axis_index("tile").astype(jnp.int32).reshape(1)
    last = (lax.axis_index("tm") == blocks - 1).astype(jnp.int32).reshape(1)
    cycle = ring_order(line, count // line)

    def passed(array, way):
        return lax.ppermute(array, "tile", [(cycle[n], cycle[(n + way) % count]) for n in range(count)])

    ranges = pieces(steps)
    own = list(pack(place, gains, increments, terminal, count, ranges[:2]))
    own += pack(place, gains, increments, None, count, ranges[2:])
    own[:2], last = lax.optimization_barrier((own[:2], last))
    arrived = []
    for turn, array in enumerate(own):
        way = 1 if turn % 2 == 0 else -1
        if turn >= 2:
            before = arrived[turn - 2]
            array, before[GATE] = lax.optimization_barrier((array, before[GATE]))
            for hop_count in range(GATE + 1, count):
                before[hop_count] = passed(before[hop_count - 1], way)
        found = [array]
        for hop_count in range(1, count):
            found.append(passed(found[-1], way))
        arrived.append(found)
    state, half = None, None
    for turn in range(2):
        reached = count - 3 + turn
        arrived[:2], _ = lax.optimization_barrier((arrived[:2], (arrived[2][reached], arrived[3][reached])))
        ends = [] if turn else arrived[0] + arrived[1]
        low, high = ranges[turn]
        *state, half = compose(last, place, cycle, 1 - 2 * turn, arrived[turn], ends, state, half, low, high - low, steps)
    factors, own, mine = state
    early = None
    for turn in range(2, 4):
        low, high = ranges[turn]
        early = chain(place, cycle, 5 - 2 * turn, arrived[turn], half, early, low, high - low, ranges[2][1])
    factors, mine = extend_factors(place, early[0], factors, mine)
    own = own_rows(place, early[1], own)
    packed = []
    for turn in range(blocks - 1, 0, -1):
        packed.append(lax.ppermute(hop(factors, early[1], packed), "tm", [(turn, turn - 1)]))
    return finish(factors, own, mine, packed)


def solution(mesh):
    return jax.shard_map(
        local,
        mesh=mesh,
        in_specs=(P("tm", "tile", None), P("tm", "tile", None), P("tile", None)),
        out_specs=P("tm", "tile", None),
        check_vma=False,
    )
```

```python
import functools
import math

import jax
import jax.numpy as jnp
from jax import lax
from jax.experimental import pallas as pl
from jax.experimental.pallas import tpu as pltpu
from jax.sharding import PartitionSpec as P

BF16 = jnp.bfloat16
F32 = jnp.float32
LANES = 128
TILE = 256
LINE = 4
MIB = 1024 * 1024
CLAIM = 60 * MIB


def nt(left, right):
    return lax.dot_general(left, right, (((1,), (1,)), ((), ())), preferred_element_type=F32)


def packed_half(increment, place, count):
    rows, width = increment.shape
    turned = pltpu.roll(increment, lax.rem(width - place * rows, width), 1)
    column = lax.broadcasted_iota(jnp.int32, (rows, width // 2), 1)
    main = turned[:, :width // 2] * jnp.where(column < rows, 0.5, 1.0)
    opposite = turned[:, width // 2:width // 2 + LANES]
    lower = opposite[rows // 2:]
    side = jnp.concatenate([lower, pltpu.roll(lower, LANES - rows // 2, 1)], axis=0)
    return main.astype(BF16), jnp.where(place < count // 2, opposite, side)


def unpacked_half(main, extra, block, count):
    rows = main.shape[0]
    width = rows * count
    column = lax.broadcasted_iota(jnp.int32, extra.shape, 1)
    extra = jnp.where(column < rows // 2, extra, 0.0)
    if block >= count // 2:
        lower = extra[:rows // 2] + pltpu.roll(extra[rows // 2:], rows // 2, 1)
        extra = jnp.concatenate([jnp.zeros_like(lower), lower], axis=0)
    rest = jnp.zeros((rows, width // 2 - LANES), F32)
    wide = jnp.concatenate([main.astype(F32), extra, rest], axis=1)
    return pltpu.roll(wide, block * rows, 1) if block else wide


def pack_kernel(count, ranges, place_ref, gain_ref, increment_ref, *refs):
    outs = refs[-len(ranges):]
    rows, width = gain_ref.shape[1:]
    stride = width + width // 2
    place = place_ref[0]
    base = min(low for low, _ in ranges)
    column = lax.broadcasted_iota(jnp.int32, (rows, LANES), 1)
    for (low, high), packed_ref in zip(ranges, outs):
        extras = jnp.zeros((rows, LANES), F32)
        for step in range(high - low):
            at = step * stride
            main, extra = packed_half(increment_ref[low - base + step], place, count)
            packed_ref[:, at:at + width] = gain_ref[low - base + step]
            packed_ref[:, at + width:at + stride] = main
            shift = step * rows // 2
            here = (column >= shift) & (column < shift + rows // 2)
            extras = jnp.where(here, pltpu.roll(extra, shift, 1) if shift else extra, extras)
        packed_ref[:, (high - low) * stride:(high - low) * stride + LANES] = extras.astype(BF16)
    if len(refs) > len(ranges):
        main, extra = packed_half(refs[0][...], place, count)
        at = (ranges[0][1] - ranges[0][0]) * stride + LANES
        outs[0][:, at:at + width // 2] = main
        outs[0][:, at + width // 2:] = extra.astype(BF16)


def pack(place, gains, increments, terminal, count, ranges):
    rows, width = gains.shape[1:]
    first, size = ranges[1][0], ranges[0][1] - ranges[1][0]
    ends = [] if terminal is None else [terminal]
    lanes = [(high - low) * (width + width // 2) + LANES for low, high in ranges]
    lanes[0] += (width // 2 + LANES) * len(ends)
    some = pl.BlockSpec((size, rows, width), lambda i, p: (first // size, 0, 0))
    return pl.pallas_call(
        functools.partial(pack_kernel, count, ranges),
        grid_spec=pltpu.PrefetchScalarGridSpec(
            num_scalar_prefetch=1,
            grid=(1,),
            in_specs=[some, some] + [pl.BlockSpec((rows, width), lambda i, p: (0, 0))] * len(ends),
            out_specs=[pl.BlockSpec((rows, n), lambda i, p: (0, 0)) for n in lanes],
        ),
        out_shape=[jax.ShapeDtypeStruct((rows, n), BF16) for n in lanes],
        compiler_params=pltpu.CompilerParams(vmem_limit_bytes=CLAIM if ends else 14 * MIB),
        name="pack",
    )(place, gains, increments, *ends)


def unpack(raw, extras, step, half):
    count, rows, _ = raw.shape
    shift = lax.rem(LANES - step * (rows // 2), LANES)
    for n in range(count):
        extra = pltpu.roll(extras[n].astype(F32), shift, 1)
        half[n * rows:(n + 1) * rows, :] = unpacked_half(raw[n], extra, n, count).astype(BF16)


def origins(place, cycle, right):
    count = len(cycle)

    def look(table, at):
        return sum(jnp.where(at == n, value, 0) for n, value in enumerate(table))

    spot = look([cycle.index(d) for d in range(count)], place)
    hops = [0] + [-n for n in range(1, right + 1)] + list(range(1, count - right))
    return [look(cycle, lax.rem(spot + n + count, count)) for n in hops]


def assemble(places, blocks, sides, step, gain, fresh, raw, extras):
    rows = blocks[0].shape[0]
    width = gain.shape[0]
    for place, block, side in zip(places, blocks, sides):
        gain[pl.ds(pl.multiple_of(place * rows, 16), rows), :] = block[:, :width]
        raw[place] = block[:, width:]
        extras[place] = side[...]
    unpack(raw, extras, step, fresh)


def advance(gain, half, fresh, middle):
    width = half.shape[0]
    for j in range(0, width, TILE):
        cols = slice(j, j + TILE)
        middle[:, cols] = jnp.dot(gain[...], half[:, cols], preferred_element_type=F32).astype(BF16)
    for j in range(0, width, TILE):
        cols = slice(j, j + TILE)
        half[:, cols] = (nt(middle[...], gain[cols, :]) + fresh[:, cols].astype(F32)).astype(BF16)


def extend(gain, factor):
    for j in range(0, factor.shape[0], TILE):
        cols = slice(j, j + TILE)
        factor[:, cols] = jnp.dot(gain[...], factor[:, cols], preferred_element_type=F32).astype(BF16)


def whole_rows(half, mine, rows):
    picked = lax.broadcasted_iota(jnp.int32, (rows, half.shape[0]), 1) == mine + lax.broadcasted_iota(
        jnp.int32, (rows, half.shape[0]), 0
    )
    own = half[pl.ds(mine, rows), :].astype(F32)
    return own + nt(jnp.where(picked, 1.0, 0.0).astype(BF16), half[...])


def compose_kernel(cycle, right, first, last_ref, place_ref, *refs):
    count = len(cycle)
    places = origins(place_ref[0], cycle, right)
    blocks, sides, refs = refs[:count], refs[count:2 * count], refs[2 * count:]
    tiles = blocks[0].shape[1] // 3 // LANES
    if first:
        ends, refs = refs[:(tiles + 1) * count], refs[(tiles + 1) * count:]
    else:
        half_in, factor_in, refs = refs[0], refs[1], refs[4:]
    factor_out, own_out, mine_out, half, gain, factor, fresh, middle, raw, extras = refs
    rows = blocks[0].shape[0]

    @pl.when(pl.program_id(0) == 0)
    def _():
        if first:
            scale = jnp.where(last_ref[0] == 1, 1.0, 0.0).astype(BF16)
            for n in range(count):
                for tile in range(tiles):
                    lanes = slice(tile * LANES, (tile + 1) * LANES)
                    raw[places[n], :, lanes] = ends[tile * count + n][...] * scale
                extras[places[n]] = ends[tiles * count + n][...] * scale
            unpack(raw, extras, 0, half)
        else:
            factor[...] = factor_in[0]
            half[...] = half_in[...]

    step = pl.num_programs(0) - 1 - pl.program_id(0)
    assemble(places, blocks, sides, step, gain, fresh, raw, extras)
    if first:

        @pl.when(pl.program_id(0) == 0)
        def _():
            factor[...] = gain[...]

        pl.when(pl.program_id(0) > 0)(lambda: extend(gain, factor))
    else:
        extend(gain, factor)
    advance(gain, half, fresh, middle)
    mine = pl.multiple_of(place_ref[0] * rows, 16)
    own_out[0] = whole_rows(half, mine, rows)
    mine_out[0] = factor[pl.ds(mine, rows), :]
    factor_out[0] = factor[...]


def square(width, place=None):
    if place is None:
        return pl.BlockSpec((width, width), lambda i, *p: (0, 0), pipeline_mode=pl.Buffered(1))
    return pl.BlockSpec((1, width, width), lambda i, *p: (place(i), 0, 0))


def row_specs(blocks, turns):
    rows = blocks[0].shape[0]
    stride = rows * len(blocks) * 3 // 2
    step = pl.BlockSpec((rows, stride), lambda i, *p: (0, turns - 1 - i))
    side = pl.BlockSpec((rows, LANES), lambda i, *p: (0, turns * stride // LANES), pipeline_mode=pl.Buffered(1))
    return [step] * len(blocks) + [side] * len(blocks)


def row_scratch(count, rows):
    width = count * rows
    return [pltpu.VMEM((width, width), BF16)] * 4 + [
        pltpu.VMEM((count, rows, width // 2), BF16),
        pltpu.VMEM((count, rows, LANES), BF16),
    ]


def compose(last, place, cycle, right, blocks, state, half, low, turns, steps):
    count = len(blocks)
    rows = blocks[0].shape[0]
    width = rows * count
    first = state is None
    anywhere = pl.BlockSpec(memory_space=pl.ANY)
    in_specs = row_specs(blocks, turns)
    if first:
        at = turns * width * 3 // 2 // LANES + 1
        tiles = width // 2 // LANES + 1
        for n in range(at, at + tiles):
            tile = pl.BlockSpec((rows, LANES), lambda i, *p, n=n: (0, n), pipeline_mode=pl.Buffered(1))
            in_specs += [tile] * count
        args = list(blocks) * tiles
    else:
        after = pl.BlockSpec((1, width, width), lambda i, *p: (low + turns, 0, 0), pipeline_mode=pl.Buffered(1))
        in_specs += [square(width), after, anywhere, anywhere]
        args = [half, *state]
    band = pl.BlockSpec((1, rows, width), lambda i, *p: (low + turns - 1 - i, 0, 0))
    base = 2 + 2 * count + 1
    return pl.pallas_call(
        functools.partial(compose_kernel, cycle, right, first),
        grid_spec=pltpu.PrefetchScalarGridSpec(
            num_scalar_prefetch=2,
            grid=(turns,),
            in_specs=in_specs,
            out_specs=[square(width, lambda i: low + turns - 1 - i), band, band, square(width)],
            scratch_shapes=row_scratch(count, rows),
        ),
        out_shape=[
            jax.ShapeDtypeStruct((steps, width, width), BF16),
            jax.ShapeDtypeStruct((steps, rows, width), F32),
            jax.ShapeDtypeStruct((steps, rows, width), BF16),
            jax.ShapeDtypeStruct((width, width), BF16),
        ],
        input_output_aliases={} if first else {base: 0, base + 1: 1, base + 2: 2},
        compiler_params=pltpu.CompilerParams(vmem_limit_bytes=18 * MIB),
        cost_estimate=pl.CostEstimate(
            flops=6 * turns * width**3, bytes_accessed=8 * turns * width * width, transcendentals=0
        ),
        name="compose",
    )(last, place, *blocks, *blocks, *args)


def chain_kernel(cycle, right, turns, place_ref, *refs):
    count = len(cycle)
    places = origins(place_ref[0], cycle, right)
    blocks, refs = refs[:count], refs[count:]
    half_in, refs = refs[0], refs[-9:]
    gain_out, half_out, half, middle, raw, extras, gain, fresh, spare = refs
    gains, freshes = (gain, spare.at[0]), (fresh, spare.at[1])
    rows, width = blocks[0].shape[0], half.shape[0]
    stride = width * 3 // 2
    side = slice(turns * stride, turns * stride + LANES)

    def prepare(turn):
        step = turns - 1 - turn
        lanes = slice(step * stride, (step + 1) * stride)
        parts = [block.at[:, lanes] for block in blocks]
        sides = [block.at[:, side] for block in blocks]
        assemble(places, parts, sides, step, gains[turn % 2], freshes[turn % 2], raw, extras)

    for turn in range(turns):

        @pl.when(pl.program_id(0) == turn)
        def _():
            if turn == 0:
                half[...] = half_in[...]
                prepare(0)
            gain_out[0] = gains[turn % 2][...]
            if turn + 1 < turns:
                prepare(turn + 1)
            advance(gains[turn % 2], half, freshes[turn % 2], middle)
            half_out[0] = half[...]


def chain(place, cycle, right, blocks, half, turns):
    count = len(blocks)
    rows = blocks[0].shape[0]
    width = rows * count
    in_specs = [pl.BlockSpec(blocks[0].shape, lambda i, *p: (0, 0), pipeline_mode=pl.Buffered(1))] * count
    whole = square(width, lambda i: turns - 1 - i)
    return pl.pallas_call(
        functools.partial(chain_kernel, cycle, right, turns),
        grid_spec=pltpu.PrefetchScalarGridSpec(
            num_scalar_prefetch=1,
            grid=(turns,),
            in_specs=in_specs + [square(width)],
            out_specs=[whole, whole],
            scratch_shapes=[
                pltpu.VMEM((width, width), BF16),
                pltpu.VMEM((width, width), BF16),
                pltpu.VMEM((count, rows, width // 2), BF16),
                pltpu.VMEM((count, rows, LANES), BF16),
                pltpu.VMEM((width, width), BF16),
                pltpu.VMEM((width, width), BF16),
                pltpu.VMEM((2, width, width), BF16),
            ],
        ),
        out_shape=[jax.ShapeDtypeStruct((turns, width, width), BF16)] * 2,
        compiler_params=pltpu.CompilerParams(vmem_limit_bytes=18 * MIB),
        cost_estimate=pl.CostEstimate(
            flops=4 * turns * width**3, bytes_accessed=8 * turns * width * width, transcendentals=0
        ),
        name="chain",
    )(place, *blocks, half)


def factors_kernel(place_ref, gain_ref, factor_in, mine_ref, factor_out, mine_out, factor):
    del mine_ref
    rows = mine_out.shape[1]

    @pl.when(pl.program_id(0) == 0)
    def _():
        factor[...] = factor_in[0]

    extend(gain_ref.at[0], factor)
    mine_out[0] = factor[pl.ds(pl.multiple_of(place_ref[0] * rows, 16), rows), :]
    factor_out[0] = factor[...]


def extend_factors(place, gains, factors, mine):
    turns, width, _ = gains.shape
    steps, rows, _ = mine.shape
    anywhere = pl.BlockSpec(memory_space=pl.ANY)
    return pl.pallas_call(
        factors_kernel,
        grid_spec=pltpu.PrefetchScalarGridSpec(
            num_scalar_prefetch=1,
            grid=(turns,),
            in_specs=[square(width, lambda i: turns - 1 - i), square(width, lambda i: turns), anywhere],
            out_specs=[
                square(width, lambda i: turns - 1 - i),
                pl.BlockSpec((1, rows, width), lambda i, *p: (turns - 1 - i, 0, 0)),
            ],
            scratch_shapes=[pltpu.VMEM((width, width), BF16)],
        ),
        out_shape=[
            jax.ShapeDtypeStruct((steps, width, width), BF16),
            jax.ShapeDtypeStruct((steps, rows, width), BF16),
        ],
        input_output_aliases={2: 0, 3: 1},
        compiler_params=pltpu.CompilerParams(vmem_limit_bytes=12 * MIB),
        cost_estimate=pl.CostEstimate(
            flops=2 * turns * width**3, bytes_accessed=4 * turns * width * width, transcendentals=0
        ),
        name="extend_factors",
    )(place, gains, factors, mine)


def rows_kernel(place_ref, half_ref, own_ref, own_out):
    del own_ref
    rows = own_out.shape[1]
    own_out[0] = whole_rows(half_ref.at[0], pl.multiple_of(place_ref[0] * rows, 16), rows)


def own_rows(place, halves, own):
    turns, width, _ = halves.shape
    steps, rows, _ = own.shape
    return pl.pallas_call(
        rows_kernel,
        grid_spec=pltpu.PrefetchScalarGridSpec(
            num_scalar_prefetch=1,
            grid=(turns,),
            in_specs=[square(width, lambda i: i), pl.BlockSpec(memory_space=pl.ANY)],
            out_specs=pl.BlockSpec((1, rows, width), lambda i, *p: (i, 0, 0)),
        ),
        out_shape=jax.ShapeDtypeStruct((steps, rows, width), F32),
        input_output_aliases={2: 0},
        compiler_params=pltpu.CompilerParams(vmem_limit_bytes=8 * MIB),
        cost_estimate=pl.CostEstimate(
            flops=2 * turns * rows * width**2, bytes_accessed=2 * turns * width * width, transcendentals=0
        ),
        name="own_rows",
    )(place, halves, own)


def upper_blocks(width):
    return [(a, b) for a in range(0, width, TILE) for b in range(a, width, TILE)]


def identity(size):
    row = lax.broadcasted_iota(jnp.int32, (size, size), 0)
    column = lax.broadcasted_iota(jnp.int32, (size, size), 1)
    return jnp.where(row == column, 1.0, 0.0).astype(BF16)


def fold(half_ref, packed_ref):
    one = identity(TILE)
    for n, (a, b) in enumerate(upper_blocks(half_ref.shape[0])):
        block = half_ref[a:a + TILE, b:b + TILE]
        if a != b:
            block = block.astype(F32) + nt(one, half_ref[b:b + TILE, a:a + TILE])
        packed_ref[n] = block.astype(BF16)


def arrived_sum(refs, n):
    value = refs[0][n]
    for extra in refs[1:]:
        value = value + extra[n]
    return value


def fold_kernel(half_ref, packed_ref):
    fold(half_ref.at[0], packed_ref)


def hop_kernel(arrived, factor_ref, half_ref, *refs):
    out_ref, covariance, middle, ahead = refs[arrived:]
    width = factor_ref.shape[1]
    for n, (a, b) in enumerate(upper_blocks(width)):
        covariance[a:a + TILE, b:b + TILE] = arrived_sum(refs[:arrived], n)
    for j in range(0, width, TILE):
        cols = slice(j, j + TILE)
        middle[:, cols] = jnp.dot(
            factor_ref[0, :, :j + TILE], covariance[:j + TILE, cols], preferred_element_type=F32
        ).astype(BF16)
    for j in range(0, width, TILE):
        cols = slice(j, j + TILE)
        ahead[:, cols] = (nt(middle[...], factor_ref[0, cols, :]) + half_ref[0, :, cols].astype(F32)).astype(BF16)
    fold(ahead, out_ref)


def hop(factors, halves, packed):
    width = halves.shape[1]
    shape = (len(upper_blocks(width)), TILE, TILE)
    blocks = pl.BlockSpec(shape, lambda i: (0, 0, 0), pipeline_mode=pl.Buffered(1))
    whole = pl.BlockSpec((1, width, width), lambda i: (0, 0, 0), pipeline_mode=pl.Buffered(1))
    if not packed:
        return pl.pallas_call(
            fold_kernel,
            grid=(1,),
            in_specs=[whole],
            out_specs=blocks,
            out_shape=jax.ShapeDtypeStruct(shape, BF16),
            compiler_params=pltpu.CompilerParams(vmem_limit_bytes=8 * MIB),
            name="fold",
        )(halves)
    return pl.pallas_call(
        functools.partial(hop_kernel, len(packed)),
        grid=(1,),
        in_specs=[whole, whole] + [blocks] * len(packed),
        out_specs=blocks,
        out_shape=jax.ShapeDtypeStruct(shape, BF16),
        scratch_shapes=[pltpu.VMEM((width, width), BF16)] * 3,
        compiler_params=pltpu.CompilerParams(vmem_limit_bytes=16 * MIB),
        cost_estimate=pl.CostEstimate(flops=4 * width**3, bytes_accessed=10 * width * width, transcendentals=0),
        name="hop",
    )(factors, halves, *packed)


def finish_kernel(arrived, factor_ref, own_ref, mine_ref, *refs):
    out_ref, covariance, middle = refs[arrived:]
    turn = pl.program_id(0)
    rows = own_ref.shape[1]
    steps = mine_ref.shape[0]
    width = covariance.shape[0]

    @pl.when(turn == 0)
    def _():
        one = identity(TILE)
        for n, (a, b) in enumerate(upper_blocks(width)):
            block = arrived_sum(refs[:arrived], n)
            turned = nt(one, block)
            if a == b:
                covariance[a:a + TILE, b:b + TILE] = (block.astype(F32) + turned).astype(BF16)
            else:
                covariance[a:a + TILE, b:b + TILE] = block
                covariance[b:b + TILE, a:a + TILE] = turned.astype(BF16)
        mine = mine_ref[...].reshape(steps * rows, width)
        for j in range(0, width, TILE):
            cols = slice(j, j + TILE)
            middle[:, cols] = jnp.dot(mine, covariance[:, cols], preferred_element_type=F32).astype(BF16)

    for n in range(out_ref.shape[0]):
        at = (turn * out_ref.shape[0] + n) * rows
        left = middle[pl.ds(pl.multiple_of(at, 16), rows), :]
        out_ref[n] = nt(left, factor_ref[n]) + own_ref[n]


def finish(factors, own, mine, packed):
    steps, rows, width = own.shape
    some = 2 if steps % 2 == 0 else 1
    whole = pl.BlockSpec(packed[0].shape, lambda i: (0, 0, 0), pipeline_mode=pl.Buffered(1))
    band = pl.BlockSpec((some, rows, width), lambda i: (i, 0, 0))
    return pl.pallas_call(
        functools.partial(finish_kernel, len(packed)),
        grid=(steps // some,),
        in_specs=[
            pl.BlockSpec((some, width, width), lambda i: (i, 0, 0)),
            band,
            pl.BlockSpec(mine.shape, lambda i: (0, 0, 0), pipeline_mode=pl.Buffered(1)),
        ]
        + [whole] * len(packed),
        out_specs=band,
        scratch_shapes=[pltpu.VMEM((width, width), BF16), pltpu.VMEM((steps * rows, width), BF16)],
        out_shape=jax.ShapeDtypeStruct((steps, rows, width), F32),
        compiler_params=pltpu.CompilerParams(vmem_limit_bytes=24 * MIB),
        name="finish",
    )(factors, own, mine, *packed)


def ring_order(line, across):
    cycle = []
    for a in range(line):
        columns = list(range(1, across))
        cycle += [a * across + b for b in (columns if a % 2 == 0 else columns[::-1])]
    return cycle + [a * across for a in reversed(range(line))]


def pieces(steps):
    size = steps // 4
    return [(low, low + size) for low in reversed(range(0, steps, size))]


def local(gains, increments, terminal):
    count = lax.axis_size("tile")
    blocks = lax.axis_size("tm")
    line = math.gcd(count, LINE)
    steps = gains.shape[0]
    place = lax.axis_index("tile").astype(jnp.int32).reshape(1)
    last = (lax.axis_index("tm") == blocks - 1).astype(jnp.int32).reshape(1)
    cycle = ring_order(line, count // line)

    def passed(array, way):
        return lax.ppermute(array, "tile", [(cycle[n], cycle[(n + way) % count]) for n in range(count)])

    ranges = pieces(steps)
    own = list(pack(place, gains, increments, terminal, count, ranges[:2]))
    own += pack(place, gains, increments, None, count, ranges[2:])
    own[:2], last = lax.optimization_barrier((own[:2], last))
    rights = [count // 2 - turn % 2 for turn in range(len(own))]
    found = []
    for turn, array in enumerate(own):
        found.append({})
        for way, hops in ((1, rights[turn]), (-1, count - 1 - rights[turn])):
            source = array
            if turn:
                before = found[turn - 1][way]
                gate = len(before) - 3
                source, before[gate] = lax.optimization_barrier((source, before[gate]))
                for n in range(gate + 1, len(before)):
                    before[n] = passed(before[n - 1], way)
            found[turn][way] = [source]
            for _ in range(hops):
                found[turn][way].append(passed(found[turn][way][-1], way))
    ties = [
        [found[1][1][2], found[2][1][1], found[1][-1][3], found[2][-1][1]],
        [found[2][1][2], found[2][-1][2], found[3][-1][1]],
        [found[3][1][-2], found[3][-1][-2]],
    ]
    state, half = None, None
    for turn, (low, high) in enumerate(ranges):
        parts = [own[turn]] + found[turn][1][1:] + found[turn][-1][1:]
        if turn < len(ties):
            parts, _ = lax.optimization_barrier((parts, ties[turn]))
            *state, half = compose(last, place, cycle, rights[turn], parts, state, half, low, high - low, steps)
        else:
            early = chain(place, cycle, rights[turn], parts, half, high)
    factors, own, mine = state
    factors, mine = extend_factors(place, early[0], factors, mine)
    own = own_rows(place, early[1], own)
    packed = []
    for turn in range(blocks - 1, 0, -1):
        packed.append(lax.ppermute(hop(factors, early[1], packed), "tm", [(turn, turn - 1)]))
    return finish(factors, own, mine, packed)


def solution(mesh):
    return jax.shard_map(
        local,
        mesh=mesh,
        in_specs=(P("tm", "tile", None), P("tm", "tile", None), P("tile", None)),
        out_specs=P("tm", "tile", None),
        check_vma=False,
    )
```

```python
import functools
import math

import jax
import jax.numpy as jnp
from jax import lax
from jax.experimental import pallas as pl
from jax.experimental.pallas import tpu as pltpu
from jax.sharding import PartitionSpec as P

BF16 = jnp.bfloat16
F32 = jnp.float32
LANES = 128
TILE = 256
LINE = 4
MIB = 1024 * 1024
CLAIM = 60 * MIB


def nt(left, right):
    return lax.dot_general(left, right, (((1,), (1,)), ((), ())), preferred_element_type=F32)


def packed_half(increment, place, count):
    rows, width = increment.shape
    turned = pltpu.roll(increment, lax.rem(width - place * rows, width), 1)
    column = lax.broadcasted_iota(jnp.int32, (rows, width // 2), 1)
    main = turned[:, :width // 2] * jnp.where(column < rows, 0.5, 1.0)
    opposite = turned[:, width // 2:width // 2 + LANES]
    lower = opposite[rows // 2:]
    side = jnp.concatenate([lower, pltpu.roll(lower, LANES - rows // 2, 1)], axis=0)
    return main.astype(BF16), jnp.where(place < count // 2, opposite, side)


def unpacked_half(main, extra, block, count):
    rows = main.shape[0]
    width = rows * count
    column = lax.broadcasted_iota(jnp.int32, extra.shape, 1)
    extra = jnp.where(column < rows // 2, extra, 0.0)
    if block >= count // 2:
        lower = extra[:rows // 2] + pltpu.roll(extra[rows // 2:], rows // 2, 1)
        extra = jnp.concatenate([jnp.zeros_like(lower), lower], axis=0)
    rest = jnp.zeros((rows, width // 2 - LANES), F32)
    wide = jnp.concatenate([main.astype(F32), extra, rest], axis=1)
    return pltpu.roll(wide, block * rows, 1) if block else wide


def pack_kernel(count, ranges, place_ref, block_ref, gain_ref, increment_ref, *refs):
    outs = refs[-len(ranges):]
    rows, width = gain_ref.shape[1:]
    stride = width + width // 2
    place = place_ref[0]
    base = min(low for low, _ in ranges)
    column = lax.broadcasted_iota(jnp.int32, (rows, LANES), 1)
    for (low, high), packed_ref in zip(ranges, outs):
        extras = jnp.zeros((rows, LANES), F32)
        for step in range(high - low):
            at = step * stride
            main, extra = packed_half(increment_ref[low - base + step], place, count)
            packed_ref[:, at:at + width] = gain_ref[low - base + step]
            packed_ref[:, at + width:at + stride] = main
            shift = step * rows // 2
            here = (column >= shift) & (column < shift + rows // 2)
            extras = jnp.where(here, pltpu.roll(extra, shift, 1) if shift else extra, extras)
        packed_ref[:, (high - low) * stride:(high - low) * stride + LANES] = extras.astype(BF16)
    if len(refs) > len(ranges):
        main, extra = packed_half(refs[0][...], place, count)
        at = (ranges[0][1] - ranges[0][0]) * stride + LANES
        tiles = [main[:, n:n + LANES].astype(F32) for n in range(0, width // 2, LANES)] + [extra]
        outs[0][:, at:] = sum(jnp.where(block_ref[0] == n, tile, 0.0) for n, tile in enumerate(tiles)).astype(BF16)


def pack(place, block, gains, increments, terminal, count, ranges):
    rows, width = gains.shape[1:]
    first, size = ranges[1][0], ranges[0][1] - ranges[1][0]
    ends = [] if terminal is None else [terminal]
    lanes = [(high - low) * (width + width // 2) + LANES for low, high in ranges]
    lanes[0] += LANES * len(ends)
    some = pl.BlockSpec((size, rows, width), lambda i, *p: (first // size, 0, 0))
    return pl.pallas_call(
        functools.partial(pack_kernel, count, ranges),
        grid_spec=pltpu.PrefetchScalarGridSpec(
            num_scalar_prefetch=2,
            grid=(1,),
            in_specs=[some, some] + [pl.BlockSpec((rows, width), lambda i, *p: (0, 0))] * len(ends),
            out_specs=[pl.BlockSpec((rows, n), lambda i, *p: (0, 0)) for n in lanes],
        ),
        out_shape=[jax.ShapeDtypeStruct((rows, n), BF16) for n in lanes],
        compiler_params=pltpu.CompilerParams(vmem_limit_bytes=CLAIM if ends else 14 * MIB),
        name="pack",
    )(place, block, gains, increments, *ends)


def collect_kernel(cycle, right, place_ref, *refs):
    out_ref = refs[-1]
    for place, tile in zip(origins(place_ref[0], cycle, right), refs):
        out_ref[place] = tile[...]


def collect(place, cycle, right, blocks):
    rows, lanes = blocks[0].shape
    tile = pl.BlockSpec((rows, LANES), lambda i, *p: (0, lanes // LANES - 1), pipeline_mode=pl.Buffered(1))
    return pl.pallas_call(
        functools.partial(collect_kernel, cycle, right),
        grid_spec=pltpu.PrefetchScalarGridSpec(
            num_scalar_prefetch=1,
            grid=(1,),
            in_specs=[tile] * len(blocks),
            out_specs=pl.BlockSpec((len(blocks), rows, LANES), lambda i, *p: (0, 0, 0)),
        ),
        out_shape=jax.ShapeDtypeStruct((len(blocks), rows, LANES), BF16),
        compiler_params=pltpu.CompilerParams(vmem_limit_bytes=6 * MIB),
        name="collect",
    )(place, *blocks)


def unpack(raw, extras, step, half):
    count, rows, _ = raw.shape
    shift = lax.rem(LANES - step * (rows // 2), LANES)
    for n in range(count):
        extra = pltpu.roll(extras[n].astype(F32), shift, 1)
        half[n * rows:(n + 1) * rows, :] = unpacked_half(raw[n], extra, n, count).astype(BF16)


def origins(place, cycle, right):
    count = len(cycle)

    def look(table, at):
        return sum(jnp.where(at == n, value, 0) for n, value in enumerate(table))

    spot = look([cycle.index(d) for d in range(count)], place)
    hops = [0] + [-n for n in range(1, right + 1)] + list(range(1, count - right))
    return [look(cycle, lax.rem(spot + n + count, count)) for n in hops]


def assemble(places, blocks, sides, step, gain, fresh, raw, extras):
    rows = blocks[0].shape[0]
    width = gain.shape[0]
    for place, block, side in zip(places, blocks, sides):
        gain[pl.ds(pl.multiple_of(place * rows, 16), rows), :] = block[:, :width]
        raw[place] = block[:, width:]
        extras[place] = side[...]
    unpack(raw, extras, step, fresh)


def advance(gain, half, fresh, middle):
    width = half.shape[0]
    for j in range(0, width, TILE):
        cols = slice(j, j + TILE)
        middle[:, cols] = jnp.dot(gain[...], half[:, cols], preferred_element_type=F32).astype(BF16)
    for j in range(0, width, TILE):
        cols = slice(j, j + TILE)
        half[:, cols] = (nt(middle[...], gain[cols, :]) + fresh[:, cols].astype(F32)).astype(BF16)


def extend(gain, factor):
    for j in range(0, factor.shape[0], TILE):
        cols = slice(j, j + TILE)
        factor[:, cols] = jnp.dot(gain[...], factor[:, cols], preferred_element_type=F32).astype(BF16)


def whole_rows(half, mine, rows):
    picked = lax.broadcasted_iota(jnp.int32, (rows, half.shape[0]), 1) == mine + lax.broadcasted_iota(
        jnp.int32, (rows, half.shape[0]), 0
    )
    own = half[pl.ds(mine, rows), :].astype(F32)
    return own + nt(jnp.where(picked, 1.0, 0.0).astype(BF16), half[...])


def compose_kernel(cycle, right, first, last_ref, place_ref, *refs):
    count = len(cycle)
    places = origins(place_ref[0], cycle, right)
    blocks, sides, refs = refs[:count], refs[count:2 * count], refs[2 * count:]
    if first:
        tiles = blocks[0].shape[1] // 3 // LANES + 1
        ends, refs = refs[:tiles], refs[tiles:]
    else:
        half_in, factor_in, refs = refs[0], refs[1], refs[4:]
    factor_out, own_out, mine_out, half, gain, factor, fresh, middle, raw, extras = refs
    rows = blocks[0].shape[0]

    @pl.when(pl.program_id(0) == 0)
    def _():
        if first:
            scale = jnp.where(last_ref[0] == 1, 1.0, 0.0).astype(BF16)
            for n, end in enumerate(ends[:-1]):
                raw[:, :, n * LANES:(n + 1) * LANES] = end[...] * scale
            extras[...] = ends[-1][...] * scale
            unpack(raw, extras, 0, half)
        else:
            factor[...] = factor_in[0]
            half[...] = half_in[...]

    step = pl.num_programs(0) - 1 - pl.program_id(0)
    assemble(places, blocks, sides, step, gain, fresh, raw, extras)
    if first:

        @pl.when(pl.program_id(0) == 0)
        def _():
            factor[...] = gain[...]

        pl.when(pl.program_id(0) > 0)(lambda: extend(gain, factor))
    else:
        extend(gain, factor)
    advance(gain, half, fresh, middle)
    mine = pl.multiple_of(place_ref[0] * rows, 16)
    own_out[0] = whole_rows(half, mine, rows)
    mine_out[0] = factor[pl.ds(mine, rows), :]
    factor_out[0] = factor[...]


def square(width, place=None):
    if place is None:
        return pl.BlockSpec((width, width), lambda i, *p: (0, 0), pipeline_mode=pl.Buffered(1))
    return pl.BlockSpec((1, width, width), lambda i, *p: (place(i), 0, 0))


def row_specs(blocks, turns):
    rows = blocks[0].shape[0]
    stride = rows * len(blocks) * 3 // 2
    step = pl.BlockSpec((rows, stride), lambda i, *p: (0, turns - 1 - i))
    side = pl.BlockSpec((rows, LANES), lambda i, *p: (0, turns * stride // LANES), pipeline_mode=pl.Buffered(1))
    return [step] * len(blocks) + [side] * len(blocks)


def row_scratch(count, rows):
    width = count * rows
    return [pltpu.VMEM((width, width), BF16)] * 4 + [
        pltpu.VMEM((count, rows, width // 2), BF16),
        pltpu.VMEM((count, rows, LANES), BF16),
    ]


def compose(last, place, cycle, right, blocks, ends, state, half, low, turns, steps):
    count = len(blocks)
    rows = blocks[0].shape[0]
    width = rows * count
    first = state is None
    anywhere = pl.BlockSpec(memory_space=pl.ANY)
    in_specs = row_specs(blocks, turns)
    if first:
        in_specs += [pl.BlockSpec(end.shape, lambda i, *p: (0, 0, 0), pipeline_mode=pl.Buffered(1)) for end in ends]
        args = ends
    else:
        after = pl.BlockSpec((1, width, width), lambda i, *p: (low + turns, 0, 0), pipeline_mode=pl.Buffered(1))
        in_specs += [square(width), after, anywhere, anywhere]
        args = [half, *state]
    band = pl.BlockSpec((1, rows, width), lambda i, *p: (low + turns - 1 - i, 0, 0))
    base = 2 + 2 * count + 1
    return pl.pallas_call(
        functools.partial(compose_kernel, cycle, right, first),
        grid_spec=pltpu.PrefetchScalarGridSpec(
            num_scalar_prefetch=2,
            grid=(turns,),
            in_specs=in_specs,
            out_specs=[square(width, lambda i: low + turns - 1 - i), band, band, square(width)],
            scratch_shapes=row_scratch(count, rows),
        ),
        out_shape=[
            jax.ShapeDtypeStruct((steps, width, width), BF16),
            jax.ShapeDtypeStruct((steps, rows, width), F32),
            jax.ShapeDtypeStruct((steps, rows, width), BF16),
            jax.ShapeDtypeStruct((width, width), BF16),
        ],
        input_output_aliases={} if first else {base: 0, base + 1: 1, base + 2: 2},
        compiler_params=pltpu.CompilerParams(vmem_limit_bytes=18 * MIB),
        cost_estimate=pl.CostEstimate(
            flops=6 * turns * width**3, bytes_accessed=8 * turns * width * width, transcendentals=0
        ),
        name="compose",
    )(last, place, *blocks, *blocks, *args)


def chain_kernel(cycle, right, turns, place_ref, *refs):
    count = len(cycle)
    places = origins(place_ref[0], cycle, right)
    blocks, refs = refs[:count], refs[count:]
    half_in, refs = refs[0], refs[-9:]
    gain_out, half_out, half, middle, raw, extras, gain, fresh, spare = refs
    gains, freshes = (gain, spare.at[0]), (fresh, spare.at[1])
    rows, width = blocks[0].shape[0], half.shape[0]
    stride = width * 3 // 2
    side = slice(turns * stride, turns * stride + LANES)

    def prepare(turn):
        step = turns - 1 - turn
        lanes = slice(step * stride, (step + 1) * stride)
        parts = [block.at[:, lanes] for block in blocks]
        sides = [block.at[:, side] for block in blocks]
        assemble(places, parts, sides, step, gains[turn % 2], freshes[turn % 2], raw, extras)

    for turn in range(turns):

        @pl.when(pl.program_id(0) == turn)
        def _():
            if turn == 0:
                half[...] = half_in[...]
                prepare(0)
            gain_out[0] = gains[turn % 2][...]
            if turn + 1 < turns:
                prepare(turn + 1)
            advance(gains[turn % 2], half, freshes[turn % 2], middle)
            half_out[0] = half[...]


def chain(place, cycle, right, blocks, half, turns):
    count = len(blocks)
    rows = blocks[0].shape[0]
    width = rows * count
    in_specs = [pl.BlockSpec(blocks[0].shape, lambda i, *p: (0, 0), pipeline_mode=pl.Buffered(1))] * count
    whole = square(width, lambda i: turns - 1 - i)
    return pl.pallas_call(
        functools.partial(chain_kernel, cycle, right, turns),
        grid_spec=pltpu.PrefetchScalarGridSpec(
            num_scalar_prefetch=1,
            grid=(turns,),
            in_specs=in_specs + [square(width)],
            out_specs=[whole, whole],
            scratch_shapes=[
                pltpu.VMEM((width, width), BF16),
                pltpu.VMEM((width, width), BF16),
                pltpu.VMEM((count, rows, width // 2), BF16),
                pltpu.VMEM((count, rows, LANES), BF16),
                pltpu.VMEM((width, width), BF16),
                pltpu.VMEM((width, width), BF16),
                pltpu.VMEM((2, width, width), BF16),
            ],
        ),
        out_shape=[jax.ShapeDtypeStruct((turns, width, width), BF16)] * 2,
        compiler_params=pltpu.CompilerParams(vmem_limit_bytes=18 * MIB),
        cost_estimate=pl.CostEstimate(
            flops=4 * turns * width**3, bytes_accessed=8 * turns * width * width, transcendentals=0
        ),
        name="chain",
    )(place, *blocks, half)


def factors_kernel(place_ref, gain_ref, factor_in, mine_ref, factor_out, mine_out, factor):
    del mine_ref
    rows = mine_out.shape[1]

    @pl.when(pl.program_id(0) == 0)
    def _():
        factor[...] = factor_in[0]

    extend(gain_ref.at[0], factor)
    mine_out[0] = factor[pl.ds(pl.multiple_of(place_ref[0] * rows, 16), rows), :]
    factor_out[0] = factor[...]


def extend_factors(place, gains, factors, mine):
    turns, width, _ = gains.shape
    steps, rows, _ = mine.shape
    anywhere = pl.BlockSpec(memory_space=pl.ANY)
    return pl.pallas_call(
        factors_kernel,
        grid_spec=pltpu.PrefetchScalarGridSpec(
            num_scalar_prefetch=1,
            grid=(turns,),
            in_specs=[square(width, lambda i: turns - 1 - i), square(width, lambda i: turns), anywhere],
            out_specs=[
                square(width, lambda i: turns - 1 - i),
                pl.BlockSpec((1, rows, width), lambda i, *p: (turns - 1 - i, 0, 0)),
            ],
            scratch_shapes=[pltpu.VMEM((width, width), BF16)],
        ),
        out_shape=[
            jax.ShapeDtypeStruct((steps, width, width), BF16),
            jax.ShapeDtypeStruct((steps, rows, width), BF16),
        ],
        input_output_aliases={2: 0, 3: 1},
        compiler_params=pltpu.CompilerParams(vmem_limit_bytes=12 * MIB),
        cost_estimate=pl.CostEstimate(
            flops=2 * turns * width**3, bytes_accessed=4 * turns * width * width, transcendentals=0
        ),
        name="extend_factors",
    )(place, gains, factors, mine)


def rows_kernel(place_ref, half_ref, own_ref, own_out):
    del own_ref
    rows = own_out.shape[1]
    own_out[0] = whole_rows(half_ref.at[0], pl.multiple_of(place_ref[0] * rows, 16), rows)


def own_rows(place, halves, own):
    turns, width, _ = halves.shape
    steps, rows, _ = own.shape
    return pl.pallas_call(
        rows_kernel,
        grid_spec=pltpu.PrefetchScalarGridSpec(
            num_scalar_prefetch=1,
            grid=(turns,),
            in_specs=[square(width, lambda i: i), pl.BlockSpec(memory_space=pl.ANY)],
            out_specs=pl.BlockSpec((1, rows, width), lambda i, *p: (i, 0, 0)),
        ),
        out_shape=jax.ShapeDtypeStruct((steps, rows, width), F32),
        input_output_aliases={2: 0},
        compiler_params=pltpu.CompilerParams(vmem_limit_bytes=8 * MIB),
        cost_estimate=pl.CostEstimate(
            flops=2 * turns * rows * width**2, bytes_accessed=2 * turns * width * width, transcendentals=0
        ),
        name="own_rows",
    )(place, halves, own)


def upper_blocks(width):
    return [(a, b) for a in range(0, width, TILE) for b in range(a, width, TILE)]


def identity(size):
    row = lax.broadcasted_iota(jnp.int32, (size, size), 0)
    column = lax.broadcasted_iota(jnp.int32, (size, size), 1)
    return jnp.where(row == column, 1.0, 0.0).astype(BF16)


def fold(half_ref, packed_ref):
    one = identity(TILE)
    for n, (a, b) in enumerate(upper_blocks(half_ref.shape[0])):
        block = half_ref[a:a + TILE, b:b + TILE]
        if a != b:
            block = block.astype(F32) + nt(one, half_ref[b:b + TILE, a:a + TILE])
        packed_ref[n] = block.astype(BF16)


def arrived_sum(refs, n):
    value = refs[0][n]
    for extra in refs[1:]:
        value = value + extra[n]
    return value


def fold_kernel(half_ref, packed_ref):
    fold(half_ref.at[0], packed_ref)


def hop_kernel(arrived, factor_ref, half_ref, *refs):
    out_ref, covariance, middle, ahead = refs[arrived:]
    width = factor_ref.shape[1]
    for n, (a, b) in enumerate(upper_blocks(width)):
        covariance[a:a + TILE, b:b + TILE] = arrived_sum(refs[:arrived], n)
    for j in range(0, width, TILE):
        cols = slice(j, j + TILE)
        middle[:, cols] = jnp.dot(
            factor_ref[0, :, :j + TILE], covariance[:j + TILE, cols], preferred_element_type=F32
        ).astype(BF16)
    for j in range(0, width, TILE):
        cols = slice(j, j + TILE)
        ahead[:, cols] = (nt(middle[...], factor_ref[0, cols, :]) + half_ref[0, :, cols].astype(F32)).astype(BF16)
    fold(ahead, out_ref)


def hop(factors, halves, packed):
    width = halves.shape[1]
    shape = (len(upper_blocks(width)), TILE, TILE)
    blocks = pl.BlockSpec(shape, lambda i: (0, 0, 0), pipeline_mode=pl.Buffered(1))
    whole = pl.BlockSpec((1, width, width), lambda i: (0, 0, 0), pipeline_mode=pl.Buffered(1))
    if not packed:
        return pl.pallas_call(
            fold_kernel,
            grid=(1,),
            in_specs=[whole],
            out_specs=blocks,
            out_shape=jax.ShapeDtypeStruct(shape, BF16),
            compiler_params=pltpu.CompilerParams(vmem_limit_bytes=8 * MIB),
            name="fold",
        )(halves)
    return pl.pallas_call(
        functools.partial(hop_kernel, len(packed)),
        grid=(1,),
        in_specs=[whole, whole] + [blocks] * len(packed),
        out_specs=blocks,
        out_shape=jax.ShapeDtypeStruct(shape, BF16),
        scratch_shapes=[pltpu.VMEM((width, width), BF16)] * 3,
        compiler_params=pltpu.CompilerParams(vmem_limit_bytes=16 * MIB),
        cost_estimate=pl.CostEstimate(flops=4 * width**3, bytes_accessed=10 * width * width, transcendentals=0),
        name="hop",
    )(factors, halves, *packed)


def finish_kernel(arrived, factor_ref, own_ref, mine_ref, *refs):
    out_ref, covariance, middle = refs[arrived:]
    turn = pl.program_id(0)
    rows = own_ref.shape[1]
    steps = mine_ref.shape[0]
    width = covariance.shape[0]

    @pl.when(turn == 0)
    def _():
        one = identity(TILE)
        for n, (a, b) in enumerate(upper_blocks(width)):
            block = arrived_sum(refs[:arrived], n)
            turned = nt(one, block)
            if a == b:
                covariance[a:a + TILE, b:b + TILE] = (block.astype(F32) + turned).astype(BF16)
            else:
                covariance[a:a + TILE, b:b + TILE] = block
                covariance[b:b + TILE, a:a + TILE] = turned.astype(BF16)
        mine = mine_ref[...].reshape(steps * rows, width)
        for j in range(0, width, TILE):
            cols = slice(j, j + TILE)
            middle[:, cols] = jnp.dot(mine, covariance[:, cols], preferred_element_type=F32).astype(BF16)

    for n in range(out_ref.shape[0]):
        at = (turn * out_ref.shape[0] + n) * rows
        left = middle[pl.ds(pl.multiple_of(at, 16), rows), :]
        out_ref[n] = nt(left, factor_ref[n]) + own_ref[n]


def finish(factors, own, mine, packed):
    steps, rows, width = own.shape
    some = 2 if steps % 2 == 0 else 1
    whole = pl.BlockSpec(packed[0].shape, lambda i: (0, 0, 0), pipeline_mode=pl.Buffered(1))
    band = pl.BlockSpec((some, rows, width), lambda i: (i, 0, 0))
    return pl.pallas_call(
        functools.partial(finish_kernel, len(packed)),
        grid=(steps // some,),
        in_specs=[
            pl.BlockSpec((some, width, width), lambda i: (i, 0, 0)),
            band,
            pl.BlockSpec(mine.shape, lambda i: (0, 0, 0), pipeline_mode=pl.Buffered(1)),
        ]
        + [whole] * len(packed),
        out_specs=band,
        scratch_shapes=[pltpu.VMEM((width, width), BF16), pltpu.VMEM((steps * rows, width), BF16)],
        out_shape=jax.ShapeDtypeStruct((steps, rows, width), F32),
        compiler_params=pltpu.CompilerParams(vmem_limit_bytes=24 * MIB),
        name="finish",
    )(factors, own, mine, *packed)


def ring_order(line, across):
    cycle = []
    for a in range(line):
        columns = list(range(1, across))
        cycle += [a * across + b for b in (columns if a % 2 == 0 else columns[::-1])]
    return cycle + [a * across for a in reversed(range(line))]


def pieces(steps):
    size = steps // 4
    return [(low, low + size) for low in reversed(range(0, steps, size))]


def local(gains, increments, terminal):
    count = lax.axis_size("tile")
    blocks = lax.axis_size("tm")
    line = math.gcd(count, LINE)
    steps = gains.shape[0]
    place = lax.axis_index("tile").astype(jnp.int32).reshape(1)
    block = lax.axis_index("tm").astype(jnp.int32).reshape(1)
    last = (block == blocks - 1).astype(jnp.int32)
    cycle = ring_order(line, count // line)

    def passed(array, way):
        return lax.ppermute(array, "tile", [(cycle[n], cycle[(n + way) % count]) for n in range(count)])

    ranges = pieces(steps)
    own = list(pack(place, block, gains, increments, terminal, count, ranges[:2]))
    own += pack(place, block, gains, increments, None, count, ranges[2:])
    own[:2], last = lax.optimization_barrier((own[:2], last))
    rights = [count // 2 - turn % 2 for turn in range(len(own))]
    found = []
    for turn, array in enumerate(own):
        found.append({})
        for way, hops in ((1, rights[turn]), (-1, count - 1 - rights[turn])):
            source = array
            if turn > 1:
                before = found[turn - 1][way]
                gate = count // 2 - 1 if turn == 2 else len(before) - 3
                source, before[gate] = lax.optimization_barrier((source, before[gate]))
                for n in range(gate + 1, len(before)):
                    before[n] = passed(before[n - 1], way)
            found[turn][way] = [source]
            for _ in range(hops):
                found[turn][way].append(passed(found[turn][way][-1], way))
    ties = [
        [found[2][1][1], found[2][-1][1], found[1][-1][-1]],
        [found[2][1][2], found[2][-1][2], found[3][-1][1]],
        [found[3][1][-2], found[3][-1][-2]],
    ]
    tile = collect(place, cycle, rights[0], [own[0]] + found[0][1][1:] + found[0][-1][1:])
    ends = [
        lax.ppermute(tile, "tm", [(n, blocks - 1)]) if n < blocks - 1 else tile
        for n in range(gains.shape[2] // 2 // LANES + 1)
    ]
    state, half = None, None
    for turn, (low, high) in enumerate(ranges):
        parts = [own[turn]] + found[turn][1][1:] + found[turn][-1][1:]
        if turn < len(ties):
            parts, _ = lax.optimization_barrier((parts, ties[turn]))
            *state, half = compose(last, place, cycle, rights[turn], parts, ends, state, half, low, high - low, steps)
        else:
            early = chain(place, cycle, rights[turn], parts, half, high)
    factors, own, mine = state
    factors, mine = extend_factors(place, early[0], factors, mine)
    own = own_rows(place, early[1], own)
    packed = []
    for turn in range(blocks - 1, 0, -1):
        packed.append(lax.ppermute(hop(factors, early[1], packed), "tm", [(turn, turn - 1)]))
    return finish(factors, own, mine, packed)


def solution(mesh):
    return jax.shard_map(
        local,
        mesh=mesh,
        in_specs=(P("tm", "tile", None), P("tm", "tile", None), P("tile", None)),
        out_specs=P("tm", "tile", None),
        check_vma=False,
    )
```

```python
import functools
import math

import jax
import jax.numpy as jnp
from jax import lax
from jax.experimental import pallas as pl
from jax.experimental.pallas import tpu as pltpu
from jax.sharding import PartitionSpec as P

BF16 = jnp.bfloat16
F32 = jnp.float32
LANES = 128
TILE = 256
LINE = 4
MIB = 1024 * 1024
CLAIM = 60 * MIB


def nt(left, right):
    return lax.dot_general(left, right, (((1,), (1,)), ((), ())), preferred_element_type=F32)


def packed_half(increment, place, count):
    rows, width = increment.shape
    turned = pltpu.roll(increment, lax.rem(width - place * rows, width), 1)
    column = lax.broadcasted_iota(jnp.int32, (rows, width // 2), 1)
    main = turned[:, :width // 2] * jnp.where(column < rows, 0.5, 1.0)
    opposite = turned[:, width // 2:width // 2 + LANES]
    lower = opposite[rows // 2:]
    side = jnp.concatenate([lower, pltpu.roll(lower, LANES - rows // 2, 1)], axis=0)
    return main.astype(BF16), jnp.where(place < count // 2, opposite, side)


def unpacked_half(main, extra, block, count):
    rows = main.shape[0]
    width = rows * count
    column = lax.broadcasted_iota(jnp.int32, extra.shape, 1)
    extra = jnp.where(column < rows // 2, extra, 0.0)
    if block >= count // 2:
        lower = extra[:rows // 2] + pltpu.roll(extra[rows // 2:], rows // 2, 1)
        extra = jnp.concatenate([jnp.zeros_like(lower), lower], axis=0)
    rest = jnp.zeros((rows, width // 2 - LANES), F32)
    wide = jnp.concatenate([main.astype(F32), extra, rest], axis=1)
    return pltpu.roll(wide, block * rows, 1) if block else wide


def pack_kernel(count, ranges, place_ref, block_ref, gain_ref, increment_ref, *refs):
    outs = refs[-len(ranges):]
    rows, width = gain_ref.shape[1:]
    stride = width + width // 2
    place = place_ref[0]
    base = min(low for low, _ in ranges)
    column = lax.broadcasted_iota(jnp.int32, (rows, LANES), 1)
    for (low, high), packed_ref in zip(ranges, outs):
        extras = jnp.zeros((rows, LANES), F32)
        for step in range(high - low):
            at = step * stride
            main, extra = packed_half(increment_ref[low - base + step], place, count)
            packed_ref[:, at:at + width] = gain_ref[low - base + step]
            packed_ref[:, at + width:at + stride] = main
            shift = step * rows // 2
            here = (column >= shift) & (column < shift + rows // 2)
            extras = jnp.where(here, pltpu.roll(extra, shift, 1) if shift else extra, extras)
        packed_ref[:, (high - low) * stride:(high - low) * stride + LANES] = extras.astype(BF16)
    if len(refs) > len(ranges):
        main, extra = packed_half(refs[0][...], place, count)
        at = (ranges[0][1] - ranges[0][0]) * stride + LANES
        tiles = [main[:, n:n + LANES].astype(F32) for n in range(0, width // 2, LANES)] + [extra]
        outs[0][:, at:] = sum(jnp.where(block_ref[0] == n, tile, 0.0) for n, tile in enumerate(tiles)).astype(BF16)


def pack(place, block, gains, increments, terminal, count, ranges):
    rows, width = gains.shape[1:]
    first, size = ranges[1][0], ranges[0][1] - ranges[1][0]
    ends = [] if terminal is None else [terminal]
    lanes = [(high - low) * (width + width // 2) + LANES for low, high in ranges]
    lanes[0] += LANES * len(ends)
    some = pl.BlockSpec((size, rows, width), lambda i, *p: (first // size, 0, 0))
    return pl.pallas_call(
        functools.partial(pack_kernel, count, ranges),
        grid_spec=pltpu.PrefetchScalarGridSpec(
            num_scalar_prefetch=2,
            grid=(1,),
            in_specs=[some, some] + [pl.BlockSpec((rows, width), lambda i, *p: (0, 0))] * len(ends),
            out_specs=[pl.BlockSpec((rows, n), lambda i, *p: (0, 0)) for n in lanes],
        ),
        out_shape=[jax.ShapeDtypeStruct((rows, n), BF16) for n in lanes],
        compiler_params=pltpu.CompilerParams(vmem_limit_bytes=CLAIM if ends else 14 * MIB),
        name="pack",
    )(place, block, gains, increments, *ends)


def collect_kernel(cycle, right, place_ref, *refs):
    out_ref = refs[-1]
    for place, tile in zip(origins(place_ref[0], cycle, right), refs):
        out_ref[place] = tile[...]


def collect(place, cycle, right, blocks):
    rows, lanes = blocks[0].shape
    tile = pl.BlockSpec((rows, LANES), lambda i, *p: (0, lanes // LANES - 1), pipeline_mode=pl.Buffered(1))
    return pl.pallas_call(
        functools.partial(collect_kernel, cycle, right),
        grid_spec=pltpu.PrefetchScalarGridSpec(
            num_scalar_prefetch=1,
            grid=(1,),
            in_specs=[tile] * len(blocks),
            out_specs=pl.BlockSpec((len(blocks), rows, LANES), lambda i, *p: (0, 0, 0)),
        ),
        out_shape=jax.ShapeDtypeStruct((len(blocks), rows, LANES), BF16),
        compiler_params=pltpu.CompilerParams(vmem_limit_bytes=6 * MIB),
        name="collect",
    )(place, *blocks)


def unpack(raw, extras, step, half):
    count, rows, _ = raw.shape
    shift = lax.rem(LANES - step * (rows // 2), LANES)
    for n in range(count):
        extra = pltpu.roll(extras[n].astype(F32), shift, 1)
        half[n * rows:(n + 1) * rows, :] = unpacked_half(raw[n], extra, n, count).astype(BF16)


def origins(place, cycle, right):
    count = len(cycle)

    def look(table, at):
        return sum(jnp.where(at == n, value, 0) for n, value in enumerate(table))

    spot = look([cycle.index(d) for d in range(count)], place)
    hops = [0] + [-n for n in range(1, right + 1)] + list(range(1, count - right))
    return [look(cycle, lax.rem(spot + n + count, count)) for n in hops]


def assemble(places, blocks, sides, step, gain, fresh, raw, extras):
    rows = blocks[0].shape[0]
    width = gain.shape[0]
    for place, block, side in zip(places, blocks, sides):
        gain[pl.ds(pl.multiple_of(place * rows, 16), rows), :] = block[:, :width]
        raw[place] = block[:, width:]
        extras[place] = side[...]
    unpack(raw, extras, step, fresh)


def advance(gain, half, fresh, middle):
    width = half.shape[0]
    for j in range(0, width, TILE):
        cols = slice(j, j + TILE)
        middle[:, cols] = jnp.dot(gain[...], half[:, cols], preferred_element_type=F32).astype(BF16)
    for j in range(0, width, TILE):
        cols = slice(j, j + TILE)
        half[:, cols] = (nt(middle[...], gain[cols, :]) + fresh[:, cols].astype(F32)).astype(BF16)


def extend(gain, factor):
    for j in range(0, factor.shape[0], TILE):
        cols = slice(j, j + TILE)
        factor[:, cols] = jnp.dot(gain[...], factor[:, cols], preferred_element_type=F32).astype(BF16)


def whole_rows(half, mine, rows):
    picked = lax.broadcasted_iota(jnp.int32, (rows, half.shape[0]), 1) == mine + lax.broadcasted_iota(
        jnp.int32, (rows, half.shape[0]), 0
    )
    own = half[pl.ds(mine, rows), :].astype(F32)
    return own + nt(jnp.where(picked, 1.0, 0.0).astype(BF16), half[...])


def compose_kernel(cycle, right, first, last_ref, place_ref, *refs):
    count = len(cycle)
    places = origins(place_ref[0], cycle, right)
    blocks, sides, refs = refs[:count], refs[count:2 * count], refs[2 * count:]
    if first:
        tiles = blocks[0].shape[1] // 3 // LANES + 1
        ends, refs = refs[:tiles], refs[tiles:]
    else:
        half_in, factor_in, refs = refs[0], refs[1], refs[4:]
    factor_out, own_out, mine_out, half, gain, factor, fresh, middle, raw, extras = refs
    rows = blocks[0].shape[0]

    @pl.when(pl.program_id(0) == 0)
    def _():
        if first:
            scale = jnp.where(last_ref[0] == 1, 1.0, 0.0).astype(BF16)
            for n, end in enumerate(ends[:-1]):
                raw[:, :, n * LANES:(n + 1) * LANES] = end[...] * scale
            extras[...] = ends[-1][...] * scale
            unpack(raw, extras, 0, half)
        else:
            factor[...] = factor_in[0]
            half[...] = half_in[...]

    step = pl.num_programs(0) - 1 - pl.program_id(0)
    assemble(places, blocks, sides, step, gain, fresh, raw, extras)
    if first:

        @pl.when(pl.program_id(0) == 0)
        def _():
            factor[...] = gain[...]

        pl.when(pl.program_id(0) > 0)(lambda: extend(gain, factor))
    else:
        extend(gain, factor)
    advance(gain, half, fresh, middle)
    mine = pl.multiple_of(place_ref[0] * rows, 16)
    own_out[0] = whole_rows(half, mine, rows)
    mine_out[0] = factor[pl.ds(mine, rows), :]
    factor_out[0] = factor[...]


def square(width, place=None):
    if place is None:
        return pl.BlockSpec((width, width), lambda i, *p: (0, 0), pipeline_mode=pl.Buffered(1))
    return pl.BlockSpec((1, width, width), lambda i, *p: (place(i), 0, 0))


def row_specs(blocks, turns):
    rows = blocks[0].shape[0]
    stride = rows * len(blocks) * 3 // 2
    step = pl.BlockSpec((rows, stride), lambda i, *p: (0, turns - 1 - i))
    side = pl.BlockSpec((rows, LANES), lambda i, *p: (0, turns * stride // LANES), pipeline_mode=pl.Buffered(1))
    return [step] * len(blocks) + [side] * len(blocks)


def row_scratch(count, rows):
    width = count * rows
    return [pltpu.VMEM((width, width), BF16)] * 4 + [
        pltpu.VMEM((count, rows, width // 2), BF16),
        pltpu.VMEM((count, rows, LANES), BF16),
    ]


def compose(last, place, cycle, right, blocks, ends, state, half, low, turns, steps):
    count = len(blocks)
    rows = blocks[0].shape[0]
    width = rows * count
    first = state is None
    anywhere = pl.BlockSpec(memory_space=pl.ANY)
    in_specs = row_specs(blocks, turns)
    if first:
        in_specs += [pl.BlockSpec(end.shape, lambda i, *p: (0, 0, 0), pipeline_mode=pl.Buffered(1)) for end in ends]
        args = ends
    else:
        after = pl.BlockSpec((1, width, width), lambda i, *p: (low + turns, 0, 0), pipeline_mode=pl.Buffered(1))
        in_specs += [square(width), after, anywhere, anywhere]
        args = [half, *state]
    band = pl.BlockSpec((1, rows, width), lambda i, *p: (low + turns - 1 - i, 0, 0))
    base = 2 + 2 * count + 1
    return pl.pallas_call(
        functools.partial(compose_kernel, cycle, right, first),
        grid_spec=pltpu.PrefetchScalarGridSpec(
            num_scalar_prefetch=2,
            grid=(turns,),
            in_specs=in_specs,
            out_specs=[square(width, lambda i: low + turns - 1 - i), band, band, square(width)],
            scratch_shapes=row_scratch(count, rows),
        ),
        out_shape=[
            jax.ShapeDtypeStruct((steps, width, width), BF16),
            jax.ShapeDtypeStruct((steps, rows, width), F32),
            jax.ShapeDtypeStruct((steps, rows, width), BF16),
            jax.ShapeDtypeStruct((width, width), BF16),
        ],
        input_output_aliases={} if first else {base: 0, base + 1: 1, base + 2: 2},
        compiler_params=pltpu.CompilerParams(vmem_limit_bytes=18 * MIB),
        cost_estimate=pl.CostEstimate(
            flops=6 * turns * width**3, bytes_accessed=8 * turns * width * width, transcendentals=0
        ),
        name="compose",
    )(last, place, *blocks, *blocks, *args)


def chain_kernel(cycle, right, turns, place_ref, *refs):
    count = len(cycle)
    places = origins(place_ref[0], cycle, right)
    blocks, refs = refs[:count], refs[count:]
    half_in, refs = refs[0], refs[-9:]
    gain_out, half_out, half, middle, raw, extras, gain, fresh, spare = refs
    gains, freshes = (gain, spare.at[0]), (fresh, spare.at[1])
    rows, width = blocks[0].shape[0], half.shape[0]
    stride = width * 3 // 2
    side = slice(turns * stride, turns * stride + LANES)

    def prepare(turn):
        step = turns - 1 - turn
        lanes = slice(step * stride, (step + 1) * stride)
        parts = [block.at[:, lanes] for block in blocks]
        sides = [block.at[:, side] for block in blocks]
        assemble(places, parts, sides, step, gains[turn % 2], freshes[turn % 2], raw, extras)

    for turn in range(turns):

        @pl.when(pl.program_id(0) == turn)
        def _():
            if turn == 0:
                half[...] = half_in[...]
                prepare(0)
            gain_out[0] = gains[turn % 2][...]
            if turn + 1 < turns:
                prepare(turn + 1)
            advance(gains[turn % 2], half, freshes[turn % 2], middle)
            half_out[0] = half[...]


def chain(place, cycle, right, blocks, half, turns):
    count = len(blocks)
    rows = blocks[0].shape[0]
    width = rows * count
    in_specs = [pl.BlockSpec(blocks[0].shape, lambda i, *p: (0, 0), pipeline_mode=pl.Buffered(1))] * count
    whole = square(width, lambda i: turns - 1 - i)
    return pl.pallas_call(
        functools.partial(chain_kernel, cycle, right, turns),
        grid_spec=pltpu.PrefetchScalarGridSpec(
            num_scalar_prefetch=1,
            grid=(turns,),
            in_specs=in_specs + [square(width)],
            out_specs=[whole, whole],
            scratch_shapes=[
                pltpu.VMEM((width, width), BF16),
                pltpu.VMEM((width, width), BF16),
                pltpu.VMEM((count, rows, width // 2), BF16),
                pltpu.VMEM((count, rows, LANES), BF16),
                pltpu.VMEM((width, width), BF16),
                pltpu.VMEM((width, width), BF16),
                pltpu.VMEM((2, width, width), BF16),
            ],
        ),
        out_shape=[jax.ShapeDtypeStruct((turns, width, width), BF16)] * 2,
        compiler_params=pltpu.CompilerParams(vmem_limit_bytes=18 * MIB),
        cost_estimate=pl.CostEstimate(
            flops=4 * turns * width**3, bytes_accessed=8 * turns * width * width, transcendentals=0
        ),
        name="chain",
    )(place, *blocks, half)


def factors_kernel(place_ref, gain_ref, factor_in, mine_ref, factor_out, mine_out, factor):
    del mine_ref
    rows = mine_out.shape[1]

    @pl.when(pl.program_id(0) == 0)
    def _():
        factor[...] = factor_in[0]

    extend(gain_ref.at[0], factor)
    mine_out[0] = factor[pl.ds(pl.multiple_of(place_ref[0] * rows, 16), rows), :]
    factor_out[0] = factor[...]


def extend_factors(place, gains, factors, mine):
    turns, width, _ = gains.shape
    steps, rows, _ = mine.shape
    anywhere = pl.BlockSpec(memory_space=pl.ANY)
    return pl.pallas_call(
        factors_kernel,
        grid_spec=pltpu.PrefetchScalarGridSpec(
            num_scalar_prefetch=1,
            grid=(turns,),
            in_specs=[square(width, lambda i: turns - 1 - i), square(width, lambda i: turns), anywhere],
            out_specs=[
                square(width, lambda i: turns - 1 - i),
                pl.BlockSpec((1, rows, width), lambda i, *p: (turns - 1 - i, 0, 0)),
            ],
            scratch_shapes=[pltpu.VMEM((width, width), BF16)],
        ),
        out_shape=[
            jax.ShapeDtypeStruct((steps, width, width), BF16),
            jax.ShapeDtypeStruct((steps, rows, width), BF16),
        ],
        input_output_aliases={2: 0, 3: 1},
        compiler_params=pltpu.CompilerParams(vmem_limit_bytes=12 * MIB),
        cost_estimate=pl.CostEstimate(
            flops=2 * turns * width**3, bytes_accessed=4 * turns * width * width, transcendentals=0
        ),
        name="extend_factors",
    )(place, gains, factors, mine)


def rows_kernel(place_ref, half_ref, own_ref, own_out):
    del own_ref
    rows = own_out.shape[1]
    own_out[0] = whole_rows(half_ref.at[0], pl.multiple_of(place_ref[0] * rows, 16), rows)


def own_rows(place, halves, own):
    turns, width, _ = halves.shape
    steps, rows, _ = own.shape
    return pl.pallas_call(
        rows_kernel,
        grid_spec=pltpu.PrefetchScalarGridSpec(
            num_scalar_prefetch=1,
            grid=(turns,),
            in_specs=[square(width, lambda i: i), pl.BlockSpec(memory_space=pl.ANY)],
            out_specs=pl.BlockSpec((1, rows, width), lambda i, *p: (i, 0, 0)),
        ),
        out_shape=jax.ShapeDtypeStruct((steps, rows, width), F32),
        input_output_aliases={2: 0},
        compiler_params=pltpu.CompilerParams(vmem_limit_bytes=8 * MIB),
        cost_estimate=pl.CostEstimate(
            flops=2 * turns * rows * width**2, bytes_accessed=2 * turns * width * width, transcendentals=0
        ),
        name="own_rows",
    )(place, halves, own)


def upper_blocks(width):
    return [(a, b) for a in range(0, width, TILE) for b in range(a, width, TILE)]


def identity(size):
    row = lax.broadcasted_iota(jnp.int32, (size, size), 0)
    column = lax.broadcasted_iota(jnp.int32, (size, size), 1)
    return jnp.where(row == column, 1.0, 0.0).astype(BF16)


def fold(half_ref, packed_ref):
    one = identity(TILE)
    for n, (a, b) in enumerate(upper_blocks(half_ref.shape[0])):
        block = half_ref[a:a + TILE, b:b + TILE]
        if a != b:
            block = block.astype(F32) + nt(one, half_ref[b:b + TILE, a:a + TILE])
        packed_ref[n] = block.astype(BF16)


def arrived_sum(refs, n):
    value = refs[0][n]
    for extra in refs[1:]:
        value = value + extra[n]
    return value


def fold_kernel(half_ref, packed_ref):
    fold(half_ref.at[0], packed_ref)


def hop_kernel(arrived, factor_ref, half_ref, *refs):
    out_ref, covariance, middle, ahead = refs[arrived:]
    width = factor_ref.shape[1]
    for n, (a, b) in enumerate(upper_blocks(width)):
        covariance[a:a + TILE, b:b + TILE] = arrived_sum(refs[:arrived], n)
    for j in range(0, width, TILE):
        cols = slice(j, j + TILE)
        middle[:, cols] = jnp.dot(
            factor_ref[0, :, :j + TILE], covariance[:j + TILE, cols], preferred_element_type=F32
        ).astype(BF16)
    for j in range(0, width, TILE):
        cols = slice(j, j + TILE)
        ahead[:, cols] = (nt(middle[...], factor_ref[0, cols, :]) + half_ref[0, :, cols].astype(F32)).astype(BF16)
    fold(ahead, out_ref)


def hop(factors, halves, packed):
    width = halves.shape[1]
    shape = (len(upper_blocks(width)), TILE, TILE)
    blocks = pl.BlockSpec(shape, lambda i: (0, 0, 0), pipeline_mode=pl.Buffered(1))
    whole = pl.BlockSpec((1, width, width), lambda i: (0, 0, 0), pipeline_mode=pl.Buffered(1))
    if not packed:
        return pl.pallas_call(
            fold_kernel,
            grid=(1,),
            in_specs=[whole],
            out_specs=blocks,
            out_shape=jax.ShapeDtypeStruct(shape, BF16),
            compiler_params=pltpu.CompilerParams(vmem_limit_bytes=8 * MIB),
            name="fold",
        )(halves)
    return pl.pallas_call(
        functools.partial(hop_kernel, len(packed)),
        grid=(1,),
        in_specs=[whole, whole] + [blocks] * len(packed),
        out_specs=blocks,
        out_shape=jax.ShapeDtypeStruct(shape, BF16),
        scratch_shapes=[pltpu.VMEM((width, width), BF16)] * 3,
        compiler_params=pltpu.CompilerParams(vmem_limit_bytes=16 * MIB),
        cost_estimate=pl.CostEstimate(flops=4 * width**3, bytes_accessed=10 * width * width, transcendentals=0),
        name="hop",
    )(factors, halves, *packed)


def finish_kernel(arrived, factor_ref, own_ref, mine_ref, *refs):
    out_ref, covariance, middle = refs[arrived:]
    turn = pl.program_id(0)
    rows = own_ref.shape[1]
    steps = mine_ref.shape[0]
    width = covariance.shape[0]

    @pl.when(turn == 0)
    def _():
        one = identity(TILE)
        for n, (a, b) in enumerate(upper_blocks(width)):
            block = arrived_sum(refs[:arrived], n)
            turned = nt(one, block)
            if a == b:
                covariance[a:a + TILE, b:b + TILE] = (block.astype(F32) + turned).astype(BF16)
            else:
                covariance[a:a + TILE, b:b + TILE] = block
                covariance[b:b + TILE, a:a + TILE] = turned.astype(BF16)
        mine = mine_ref[...].reshape(steps * rows, width)
        for j in range(0, width, TILE):
            cols = slice(j, j + TILE)
            middle[:, cols] = jnp.dot(mine, covariance[:, cols], preferred_element_type=F32).astype(BF16)

    for n in range(out_ref.shape[0]):
        at = (turn * out_ref.shape[0] + n) * rows
        left = middle[pl.ds(pl.multiple_of(at, 16), rows), :]
        out_ref[n] = nt(left, factor_ref[n]) + own_ref[n]


def finish(factors, own, mine, packed):
    steps, rows, width = own.shape
    some = 2 if steps % 2 == 0 else 1
    whole = pl.BlockSpec(packed[0].shape, lambda i: (0, 0, 0), pipeline_mode=pl.Buffered(1))
    band = pl.BlockSpec((some, rows, width), lambda i: (i, 0, 0))
    return pl.pallas_call(
        functools.partial(finish_kernel, len(packed)),
        grid=(steps // some,),
        in_specs=[
            pl.BlockSpec((some, width, width), lambda i: (i, 0, 0)),
            band,
            pl.BlockSpec(mine.shape, lambda i: (0, 0, 0), pipeline_mode=pl.Buffered(1)),
        ]
        + [whole] * len(packed),
        out_specs=band,
        scratch_shapes=[pltpu.VMEM((width, width), BF16), pltpu.VMEM((steps * rows, width), BF16)],
        out_shape=jax.ShapeDtypeStruct((steps, rows, width), F32),
        compiler_params=pltpu.CompilerParams(vmem_limit_bytes=24 * MIB),
        name="finish",
    )(factors, own, mine, *packed)


def ring_order(line, across):
    cycle = []
    for a in range(line):
        columns = list(range(1, across))
        cycle += [a * across + b for b in (columns if a % 2 == 0 else columns[::-1])]
    return cycle + [a * across for a in reversed(range(line))]


def pieces(steps):
    size = steps // 4
    return [(low, low + size) for low in reversed(range(0, steps, size))]


def local(gains, increments, terminal):
    count = lax.axis_size("tile")
    blocks = lax.axis_size("tm")
    line = math.gcd(count, LINE)
    steps = gains.shape[0]
    place = lax.axis_index("tile").astype(jnp.int32).reshape(1)
    block = lax.axis_index("tm").astype(jnp.int32).reshape(1)
    last = (block == blocks - 1).astype(jnp.int32)
    cycle = ring_order(line, count // line)

    def passed(array, way):
        return lax.ppermute(array, "tile", [(cycle[n], cycle[(n + way) % count]) for n in range(count)])

    ranges = pieces(steps)
    own = list(pack(place, block, gains, increments, terminal, count, ranges[:2]))
    own += pack(place, block, gains, increments, None, count, ranges[2:])
    own[:2], last = lax.optimization_barrier((own[:2], last))
    rights = [count // 2 - turn % 2 for turn in range(len(own))]
    found = []
    for turn, array in enumerate(own):
        found.append({})
        for way, hops in ((1, rights[turn]), (-1, count - 1 - rights[turn])):
            source = array
            if turn > 1:
                before = found[0 if turn == 2 else turn - 1][way]
                gate = count // 2 - 1 if turn == 2 else len(before) - 3
                source, before[gate] = lax.optimization_barrier((source, before[gate]))
                for n in range(gate + 1, len(before)):
                    before[n] = passed(before[n - 1], way)
            found[turn][way] = [source]
            for _ in range(hops):
                found[turn][way].append(passed(found[turn][way][-1], way))
    ties = [
        [found[2][1][2], found[2][-1][2]],
        [found[2][1][3], found[2][-1][3]],
        [found[3][1][-2], found[3][-1][-2]],
    ]
    parts, _ = lax.optimization_barrier(
        (
            [own[0]] + found[0][1][1:] + found[0][-1][1:],
            [found[2][1][1], found[2][-1][1], found[1][1][-1], found[1][-1][-1]],
        )
    )
    tile = collect(place, cycle, rights[0], parts)
    ends = [
        lax.ppermute(tile, "tm", [(n, blocks - 1)]) if n < blocks - 1 else tile
        for n in range(gains.shape[2] // 2 // LANES + 1)
    ]
    state, half = None, None
    for turn, (low, high) in enumerate(ranges):
        parts = [own[turn]] + found[turn][1][1:] + found[turn][-1][1:]
        if turn < len(ties):
            parts, _ = lax.optimization_barrier((parts, ties[turn]))
            *state, half = compose(last, place, cycle, rights[turn], parts, ends, state, half, low, high - low, steps)
        else:
            early = chain(place, cycle, rights[turn], parts, half, high)
    factors, own, mine = state
    factors, mine = extend_factors(place, early[0], factors, mine)
    own = own_rows(place, early[1], own)
    packed = []
    for turn in range(blocks - 1, 0, -1):
        packed.append(lax.ppermute(hop(factors, early[1], packed), "tm", [(turn, turn - 1)]))
    return finish(factors, own, mine, packed)


def solution(mesh):
    return jax.shard_map(
        local,
        mesh=mesh,
        in_specs=(P("tm", "tile", None), P("tm", "tile", None), P("tile", None)),
        out_specs=P("tm", "tile", None),
        check_vma=False,
    )
```

```python
import functools
import math

import jax
import jax.numpy as jnp
from jax import lax
from jax.experimental import pallas as pl
from jax.experimental.pallas import tpu as pltpu
from jax.sharding import PartitionSpec as P

BF16 = jnp.bfloat16
F32 = jnp.float32
LANES = 128
TILE = 256
LINE = 4
MIB = 1024 * 1024
CLAIM = 60 * MIB


def nt(left, right):
    return lax.dot_general(left, right, (((1,), (1,)), ((), ())), preferred_element_type=F32)


def packed_half(increment, place, count):
    rows, width = increment.shape
    turned = pltpu.roll(increment, lax.rem(width - place * rows, width), 1)
    column = lax.broadcasted_iota(jnp.int32, (rows, width // 2), 1)
    main = turned[:, :width // 2] * jnp.where(column < rows, 0.5, 1.0)
    opposite = turned[:, width // 2:width // 2 + LANES]
    lower = opposite[rows // 2:]
    side = jnp.concatenate([lower, pltpu.roll(lower, LANES - rows // 2, 1)], axis=0)
    return main.astype(BF16), jnp.where(place < count // 2, opposite, side)


def unpacked_half(main, extra, block, count):
    rows = main.shape[0]
    width = rows * count
    column = lax.broadcasted_iota(jnp.int32, extra.shape, 1)
    extra = jnp.where(column < rows // 2, extra, 0.0)
    if block >= count // 2:
        lower = extra[:rows // 2] + pltpu.roll(extra[rows // 2:], rows // 2, 1)
        extra = jnp.concatenate([jnp.zeros_like(lower), lower], axis=0)
    rest = jnp.zeros((rows, width // 2 - LANES), F32)
    wide = jnp.concatenate([main.astype(F32), extra, rest], axis=1)
    return pltpu.roll(wide, block * rows, 1) if block else wide


def pack_kernel(count, ranges, place_ref, block_ref, gain_ref, increment_ref, *refs):
    outs = refs[-len(ranges):]
    rows, width = gain_ref.shape[1:]
    stride = width + width // 2
    place = place_ref[0]
    base = min(low for low, _ in ranges)
    column = lax.broadcasted_iota(jnp.int32, (rows, LANES), 1)
    for (low, high), packed_ref in zip(ranges, outs):
        extras = jnp.zeros((rows, LANES), F32)
        for step in range(high - low):
            at = step * stride
            main, extra = packed_half(increment_ref[low - base + step], place, count)
            packed_ref[:, at:at + width] = gain_ref[low - base + step]
            packed_ref[:, at + width:at + stride] = main
            shift = step * rows // 2
            here = (column >= shift) & (column < shift + rows // 2)
            extras = jnp.where(here, pltpu.roll(extra, shift, 1) if shift else extra, extras)
        packed_ref[:, (high - low) * stride:(high - low) * stride + LANES] = extras.astype(BF16)
    if len(refs) > len(ranges):
        main, extra = packed_half(refs[0][...], place, count)
        at = (ranges[0][1] - ranges[0][0]) * stride + LANES
        tiles = [main[:, n:n + LANES].astype(F32) for n in range(0, width // 2, LANES)] + [extra]
        outs[0][:, at:] = sum(jnp.where(block_ref[0] == n, tile, 0.0) for n, tile in enumerate(tiles)).astype(BF16)


def pack(place, block, gains, increments, terminal, count, ranges):
    rows, width = gains.shape[1:]
    first, size = ranges[-1][0], ranges[0][1] - ranges[-1][0]
    ends = [] if terminal is None else [terminal]
    lanes = [(high - low) * (width + width // 2) + LANES for low, high in ranges]
    lanes[0] += LANES * len(ends)
    some = pl.BlockSpec((size, rows, width), lambda i, *p: (first // size, 0, 0))
    return pl.pallas_call(
        functools.partial(pack_kernel, count, ranges),
        grid_spec=pltpu.PrefetchScalarGridSpec(
            num_scalar_prefetch=2,
            grid=(1,),
            in_specs=[some, some] + [pl.BlockSpec((rows, width), lambda i, *p: (0, 0))] * len(ends),
            out_specs=[pl.BlockSpec((rows, n), lambda i, *p: (0, 0)) for n in lanes],
        ),
        out_shape=[jax.ShapeDtypeStruct((rows, n), BF16) for n in lanes],
        compiler_params=pltpu.CompilerParams(vmem_limit_bytes=CLAIM if len(ranges) == 1 else 14 * MIB),
        name="pack",
    )(place, block, gains, increments, *ends)


def collect_kernel(cycle, right, place_ref, *refs):
    out_ref = refs[-1]
    for place, tile in zip(origins(place_ref[0], cycle, right), refs):
        out_ref[place] = tile[...]


def collect(place, cycle, right, blocks):
    rows, lanes = blocks[0].shape
    tile = pl.BlockSpec((rows, LANES), lambda i, *p: (0, lanes // LANES - 1), pipeline_mode=pl.Buffered(1))
    return pl.pallas_call(
        functools.partial(collect_kernel, cycle, right),
        grid_spec=pltpu.PrefetchScalarGridSpec(
            num_scalar_prefetch=1,
            grid=(1,),
            in_specs=[tile] * len(blocks),
            out_specs=pl.BlockSpec((len(blocks), rows, LANES), lambda i, *p: (0, 0, 0)),
        ),
        out_shape=jax.ShapeDtypeStruct((len(blocks), rows, LANES), BF16),
        compiler_params=pltpu.CompilerParams(vmem_limit_bytes=6 * MIB),
        name="collect",
    )(place, *blocks)


def unpack(raw, extras, step, half):
    count, rows, _ = raw.shape
    shift = lax.rem(LANES - step * (rows // 2), LANES)
    for n in range(count):
        extra = pltpu.roll(extras[n].astype(F32), shift, 1)
        half[n * rows:(n + 1) * rows, :] = unpacked_half(raw[n], extra, n, count).astype(BF16)


def origins(place, cycle, right):
    count = len(cycle)

    def look(table, at):
        return sum(jnp.where(at == n, value, 0) for n, value in enumerate(table))

    spot = look([cycle.index(d) for d in range(count)], place)
    hops = [0] + [-n for n in range(1, right + 1)] + list(range(1, count - right))
    return [look(cycle, lax.rem(spot + n + count, count)) for n in hops]


def assemble(places, blocks, sides, step, gain, fresh, raw, extras):
    rows = blocks[0].shape[0]
    width = gain.shape[0]
    for place, block, side in zip(places, blocks, sides):
        gain[pl.ds(pl.multiple_of(place * rows, 16), rows), :] = block[:, :width]
        raw[place] = block[:, width:]
        extras[place] = side[...]
    unpack(raw, extras, step, fresh)


def advance(gain, half, fresh, middle):
    width = half.shape[0]
    for j in range(0, width, TILE):
        cols = slice(j, j + TILE)
        middle[:, cols] = jnp.dot(gain[...], half[:, cols], preferred_element_type=F32).astype(BF16)
    for j in range(0, width, TILE):
        cols = slice(j, j + TILE)
        half[:, cols] = (nt(middle[...], gain[cols, :]) + fresh[:, cols].astype(F32)).astype(BF16)


def extend(gain, factor):
    for j in range(0, factor.shape[0], TILE):
        cols = slice(j, j + TILE)
        factor[:, cols] = jnp.dot(gain[...], factor[:, cols], preferred_element_type=F32).astype(BF16)


def whole_rows(half, mine, rows):
    picked = lax.broadcasted_iota(jnp.int32, (rows, half.shape[0]), 1) == mine + lax.broadcasted_iota(
        jnp.int32, (rows, half.shape[0]), 0
    )
    own = half[pl.ds(mine, rows), :].astype(F32)
    return own + nt(jnp.where(picked, 1.0, 0.0).astype(BF16), half[...])


def compose_kernel(cycle, right, first, last_ref, place_ref, *refs):
    count = len(cycle)
    places = origins(place_ref[0], cycle, right)
    blocks, sides, refs = refs[:count], refs[count:2 * count], refs[2 * count:]
    if first:
        tiles = blocks[0].shape[1] // 3 // LANES + 1
        ends, refs = refs[:tiles], refs[tiles:]
    else:
        half_in, factor_in, refs = refs[0], refs[1], refs[4:]
    factor_out, own_out, mine_out, half, gain, factor, fresh, middle, raw, extras = refs
    rows = blocks[0].shape[0]

    @pl.when(pl.program_id(0) == 0)
    def _():
        if first:
            scale = jnp.where(last_ref[0] == 1, 1.0, 0.0).astype(BF16)
            for n, end in enumerate(ends[:-1]):
                raw[:, :, n * LANES:(n + 1) * LANES] = end[...] * scale
            extras[...] = ends[-1][...] * scale
            unpack(raw, extras, 0, half)
        else:
            factor[...] = factor_in[0]
            half[...] = half_in[...]

    step = pl.num_programs(0) - 1 - pl.program_id(0)
    assemble(places, blocks, sides, step, gain, fresh, raw, extras)
    if first:

        @pl.when(pl.program_id(0) == 0)
        def _():
            factor[...] = gain[...]

        pl.when(pl.program_id(0) > 0)(lambda: extend(gain, factor))
    else:
        extend(gain, factor)
    advance(gain, half, fresh, middle)
    mine = pl.multiple_of(place_ref[0] * rows, 16)
    own_out[0] = whole_rows(half, mine, rows)
    mine_out[0] = factor[pl.ds(mine, rows), :]
    factor_out[0] = factor[...]


def square(width, place=None):
    if place is None:
        return pl.BlockSpec((width, width), lambda i, *p: (0, 0), pipeline_mode=pl.Buffered(1))
    return pl.BlockSpec((1, width, width), lambda i, *p: (place(i), 0, 0))


def row_specs(blocks, turns):
    rows = blocks[0].shape[0]
    stride = rows * len(blocks) * 3 // 2
    step = pl.BlockSpec((rows, stride), lambda i, *p: (0, turns - 1 - i))
    side = pl.BlockSpec((rows, LANES), lambda i, *p: (0, turns * stride // LANES), pipeline_mode=pl.Buffered(1))
    return [step] * len(blocks) + [side] * len(blocks)


def row_scratch(count, rows):
    width = count * rows
    return [pltpu.VMEM((width, width), BF16)] * 4 + [
        pltpu.VMEM((count, rows, width // 2), BF16),
        pltpu.VMEM((count, rows, LANES), BF16),
    ]


def compose(last, place, cycle, right, blocks, ends, state, half, low, turns, steps):
    count = len(blocks)
    rows = blocks[0].shape[0]
    width = rows * count
    first = state is None
    anywhere = pl.BlockSpec(memory_space=pl.ANY)
    in_specs = row_specs(blocks, turns)
    if first:
        in_specs += [pl.BlockSpec(end.shape, lambda i, *p: (0, 0, 0), pipeline_mode=pl.Buffered(1)) for end in ends]
        args = ends
    else:
        after = pl.BlockSpec((1, width, width), lambda i, *p: (low + turns, 0, 0), pipeline_mode=pl.Buffered(1))
        in_specs += [square(width), after, anywhere, anywhere]
        args = [half, *state]
    band = pl.BlockSpec((1, rows, width), lambda i, *p: (low + turns - 1 - i, 0, 0))
    base = 2 + 2 * count + 1
    return pl.pallas_call(
        functools.partial(compose_kernel, cycle, right, first),
        grid_spec=pltpu.PrefetchScalarGridSpec(
            num_scalar_prefetch=2,
            grid=(turns,),
            in_specs=in_specs,
            out_specs=[square(width, lambda i: low + turns - 1 - i), band, band, square(width)],
            scratch_shapes=row_scratch(count, rows),
        ),
        out_shape=[
            jax.ShapeDtypeStruct((steps, width, width), BF16),
            jax.ShapeDtypeStruct((steps, rows, width), F32),
            jax.ShapeDtypeStruct((steps, rows, width), BF16),
            jax.ShapeDtypeStruct((width, width), BF16),
        ],
        input_output_aliases={} if first else {base: 0, base + 1: 1, base + 2: 2},
        compiler_params=pltpu.CompilerParams(vmem_limit_bytes=18 * MIB),
        cost_estimate=pl.CostEstimate(
            flops=6 * turns * width**3, bytes_accessed=8 * turns * width * width, transcendentals=0
        ),
        name="compose",
    )(last, place, *blocks, *blocks, *args)


def chain_kernel(cycle, right, turns, place_ref, *refs):
    count = len(cycle)
    places = origins(place_ref[0], cycle, right)
    blocks, refs = refs[:count], refs[count:]
    half_in, refs = refs[0], refs[-10:]
    gain_out, half_out, packed_out, half, middle, raw, extras, gain, fresh, spare = refs
    gains, freshes = (gain, spare.at[0]), (fresh, spare.at[1])
    rows, width = blocks[0].shape[0], half.shape[0]
    stride = width * 3 // 2
    side = slice(turns * stride, turns * stride + LANES)

    def prepare(turn):
        step = turns - 1 - turn
        lanes = slice(step * stride, (step + 1) * stride)
        parts = [block.at[:, lanes] for block in blocks]
        sides = [block.at[:, side] for block in blocks]
        assemble(places, parts, sides, step, gains[turn % 2], freshes[turn % 2], raw, extras)

    for turn in range(turns):

        @pl.when(pl.program_id(0) == turn)
        def _():
            if turn == 0:
                half[...] = half_in[...]
                prepare(0)
            gain_out[0] = gains[turn % 2][...]
            if turn + 1 < turns:
                prepare(turn + 1)
            advance(gains[turn % 2], half, freshes[turn % 2], middle)
            half_out[0] = half[...]
            if turn == turns - 1:
                fold(half, packed_out)


def chain(place, cycle, right, blocks, half, turns):
    count = len(blocks)
    rows = blocks[0].shape[0]
    width = rows * count
    in_specs = [pl.BlockSpec(blocks[0].shape, lambda i, *p: (0, 0), pipeline_mode=pl.Buffered(1))] * count
    whole = square(width, lambda i: turns - 1 - i)
    return pl.pallas_call(
        functools.partial(chain_kernel, cycle, right, turns),
        grid_spec=pltpu.PrefetchScalarGridSpec(
            num_scalar_prefetch=1,
            grid=(turns,),
            in_specs=in_specs + [square(width)],
            out_specs=[whole, whole, pl.BlockSpec(blocks_shape(width), lambda i, *p: (0, 0, 0))],
            scratch_shapes=[
                pltpu.VMEM((width, width), BF16),
                pltpu.VMEM((width, width), BF16),
                pltpu.VMEM((count, rows, width // 2), BF16),
                pltpu.VMEM((count, rows, LANES), BF16),
                pltpu.VMEM((width, width), BF16),
                pltpu.VMEM((width, width), BF16),
                pltpu.VMEM((2, width, width), BF16),
            ],
        ),
        out_shape=[jax.ShapeDtypeStruct((turns, width, width), BF16)] * 2
        + [jax.ShapeDtypeStruct(blocks_shape(width), BF16)],
        compiler_params=pltpu.CompilerParams(vmem_limit_bytes=18 * MIB),
        cost_estimate=pl.CostEstimate(
            flops=4 * turns * width**3, bytes_accessed=8 * turns * width * width, transcendentals=0
        ),
        name="chain",
    )(place, *blocks, half)


def factors_kernel(place_ref, gain_ref, factor_in, mine_ref, factor_out, mine_out, factor):
    del mine_ref
    rows = mine_out.shape[1]

    @pl.when(pl.program_id(0) == 0)
    def _():
        factor[...] = factor_in[0]

    extend(gain_ref.at[0], factor)
    mine_out[0] = factor[pl.ds(pl.multiple_of(place_ref[0] * rows, 16), rows), :]
    factor_out[0] = factor[...]


def extend_factors(place, gains, factors, mine):
    turns, width, _ = gains.shape
    steps, rows, _ = mine.shape
    anywhere = pl.BlockSpec(memory_space=pl.ANY)
    return pl.pallas_call(
        factors_kernel,
        grid_spec=pltpu.PrefetchScalarGridSpec(
            num_scalar_prefetch=1,
            grid=(turns,),
            in_specs=[square(width, lambda i: turns - 1 - i), square(width, lambda i: turns), anywhere],
            out_specs=[
                square(width, lambda i: turns - 1 - i),
                pl.BlockSpec((1, rows, width), lambda i, *p: (turns - 1 - i, 0, 0)),
            ],
            scratch_shapes=[pltpu.VMEM((width, width), BF16)],
        ),
        out_shape=[
            jax.ShapeDtypeStruct((steps, width, width), BF16),
            jax.ShapeDtypeStruct((steps, rows, width), BF16),
        ],
        input_output_aliases={2: 0, 3: 1},
        compiler_params=pltpu.CompilerParams(vmem_limit_bytes=12 * MIB),
        cost_estimate=pl.CostEstimate(
            flops=2 * turns * width**3, bytes_accessed=4 * turns * width * width, transcendentals=0
        ),
        name="extend_factors",
    )(place, gains, factors, mine)


def rows_kernel(place_ref, half_ref, own_ref, own_out):
    del own_ref
    rows = own_out.shape[1]
    own_out[0] = whole_rows(half_ref.at[0], pl.multiple_of(place_ref[0] * rows, 16), rows)


def own_rows(place, halves, own):
    turns, width, _ = halves.shape
    steps, rows, _ = own.shape
    return pl.pallas_call(
        rows_kernel,
        grid_spec=pltpu.PrefetchScalarGridSpec(
            num_scalar_prefetch=1,
            grid=(turns,),
            in_specs=[square(width, lambda i: i), pl.BlockSpec(memory_space=pl.ANY)],
            out_specs=pl.BlockSpec((1, rows, width), lambda i, *p: (i, 0, 0)),
        ),
        out_shape=jax.ShapeDtypeStruct((steps, rows, width), F32),
        input_output_aliases={2: 0},
        compiler_params=pltpu.CompilerParams(vmem_limit_bytes=8 * MIB),
        cost_estimate=pl.CostEstimate(
            flops=2 * turns * rows * width**2, bytes_accessed=2 * turns * width * width, transcendentals=0
        ),
        name="own_rows",
    )(place, halves, own)


def upper_blocks(width):
    return [(a, b) for a in range(0, width, TILE) for b in range(a, width, TILE)]


def blocks_shape(width):
    return (len(upper_blocks(width)), TILE, TILE)


def identity(size):
    row = lax.broadcasted_iota(jnp.int32, (size, size), 0)
    column = lax.broadcasted_iota(jnp.int32, (size, size), 1)
    return jnp.where(row == column, 1.0, 0.0).astype(BF16)


def fold(half_ref, packed_ref):
    one = identity(TILE)
    for n, (a, b) in enumerate(upper_blocks(half_ref.shape[0])):
        block = half_ref[a:a + TILE, b:b + TILE]
        if a != b:
            block = block.astype(F32) + nt(one, half_ref[b:b + TILE, a:a + TILE])
        packed_ref[n] = block.astype(BF16)


def arrived_sum(refs, n):
    value = refs[0][n]
    for extra in refs[1:]:
        value = value + extra[n]
    return value


def hop_kernel(arrived, factor_ref, half_ref, *refs):
    out_ref, covariance, middle, ahead = refs[arrived:]
    width = factor_ref.shape[1]
    for n, (a, b) in enumerate(upper_blocks(width)):
        covariance[a:a + TILE, b:b + TILE] = arrived_sum(refs[:arrived], n)
    for j in range(0, width, TILE):
        cols = slice(j, j + TILE)
        middle[:, cols] = jnp.dot(
            factor_ref[0, :, :j + TILE], covariance[:j + TILE, cols], preferred_element_type=F32
        ).astype(BF16)
    for j in range(0, width, TILE):
        cols = slice(j, j + TILE)
        ahead[:, cols] = (nt(middle[...], factor_ref[0, cols, :]) + half_ref[0, :, cols].astype(F32)).astype(BF16)
    fold(ahead, out_ref)


def hop(factors, halves, packed):
    width = halves.shape[1]
    shape = blocks_shape(width)
    blocks = pl.BlockSpec(shape, lambda i: (0, 0, 0), pipeline_mode=pl.Buffered(1))
    whole = pl.BlockSpec((1, width, width), lambda i: (0, 0, 0), pipeline_mode=pl.Buffered(1))
    return pl.pallas_call(
        functools.partial(hop_kernel, len(packed)),
        grid=(1,),
        in_specs=[whole, whole] + [blocks] * len(packed),
        out_specs=blocks,
        out_shape=jax.ShapeDtypeStruct(shape, BF16),
        scratch_shapes=[pltpu.VMEM((width, width), BF16)] * 3,
        compiler_params=pltpu.CompilerParams(vmem_limit_bytes=16 * MIB),
        cost_estimate=pl.CostEstimate(flops=4 * width**3, bytes_accessed=10 * width * width, transcendentals=0),
        name="hop",
    )(factors, halves, *packed)


def finish_kernel(arrived, factor_ref, own_ref, mine_ref, *refs):
    out_ref, covariance, middle = refs[arrived:]
    turn = pl.program_id(0)
    rows = own_ref.shape[1]
    steps = mine_ref.shape[0]
    width = covariance.shape[0]

    @pl.when(turn == 0)
    def _():
        one = identity(TILE)
        for n, (a, b) in enumerate(upper_blocks(width)):
            block = arrived_sum(refs[:arrived], n)
            turned = nt(one, block)
            if a == b:
                covariance[a:a + TILE, b:b + TILE] = (block.astype(F32) + turned).astype(BF16)
            else:
                covariance[a:a + TILE, b:b + TILE] = block
                covariance[b:b + TILE, a:a + TILE] = turned.astype(BF16)
        mine = mine_ref[...].reshape(steps * rows, width)
        for j in range(0, width, TILE):
            cols = slice(j, j + TILE)
            middle[:, cols] = jnp.dot(mine, covariance[:, cols], preferred_element_type=F32).astype(BF16)

    for n in range(out_ref.shape[0]):
        at = (turn * out_ref.shape[0] + n) * rows
        left = middle[pl.ds(pl.multiple_of(at, 16), rows), :]
        out_ref[n] = nt(left, factor_ref[n]) + own_ref[n]


def finish(factors, own, mine, packed):
    steps, rows, width = own.shape
    some = 2 if steps % 2 == 0 else 1
    whole = pl.BlockSpec(packed[0].shape, lambda i: (0, 0, 0), pipeline_mode=pl.Buffered(1))
    band = pl.BlockSpec((some, rows, width), lambda i: (i, 0, 0))
    return pl.pallas_call(
        functools.partial(finish_kernel, len(packed)),
        grid=(steps // some,),
        in_specs=[
            pl.BlockSpec((some, width, width), lambda i: (i, 0, 0)),
            band,
            pl.BlockSpec(mine.shape, lambda i: (0, 0, 0), pipeline_mode=pl.Buffered(1)),
        ]
        + [whole] * len(packed),
        out_specs=band,
        scratch_shapes=[pltpu.VMEM((width, width), BF16), pltpu.VMEM((steps * rows, width), BF16)],
        out_shape=jax.ShapeDtypeStruct((steps, rows, width), F32),
        compiler_params=pltpu.CompilerParams(vmem_limit_bytes=24 * MIB),
        name="finish",
    )(factors, own, mine, *packed)


def ring_order(line, across):
    cycle = []
    for a in range(line):
        columns = list(range(1, across))
        cycle += [a * across + b for b in (columns if a % 2 == 0 else columns[::-1])]
    return cycle + [a * across for a in reversed(range(line))]


def pieces(steps):
    size = steps // 4
    return [(low, low + size) for low in reversed(range(0, steps, size))]


def local(gains, increments, terminal):
    count = lax.axis_size("tile")
    blocks = lax.axis_size("tm")
    line = math.gcd(count, LINE)
    steps = gains.shape[0]
    place = lax.axis_index("tile").astype(jnp.int32).reshape(1)
    block = lax.axis_index("tm").astype(jnp.int32).reshape(1)
    last = (block == blocks - 1).astype(jnp.int32)
    cycle = ring_order(line, count // line)

    def passed(array, way):
        return lax.ppermute(array, "tile", [(cycle[n], cycle[(n + way) % count]) for n in range(count)])

    ranges = pieces(steps)
    own = [
        *pack(place, block, gains, increments, terminal, count, ranges[:1]),
        *pack(place, block, gains, increments, None, count, ranges[1:2]),
        *pack(place, block, gains, increments, None, count, ranges[2:]),
    ]
    own[1], last = lax.optimization_barrier((own[1], last))
    rights = [count // 2 - turn % 2 for turn in range(len(own))]
    found = []
    for turn, array in enumerate(own):
        found.append({})
        for way, hops in ((1, rights[turn]), (-1, count - 1 - rights[turn])):
            source = array
            if turn > 1:
                before = found[turn - 1][way]
                gate = count // 2 - 1 if turn == 2 else len(before) - 3
                source, before[gate] = lax.optimization_barrier((source, before[gate]))
                for n in range(gate + 1, len(before)):
                    before[n] = passed(before[n - 1], way)
            found[turn][way] = [source]
            for _ in range(hops):
                found[turn][way].append(passed(found[turn][way][-1], way))
    ties = [
        [found[2][1][2], found[2][-1][2]],
        [found[2][1][3], found[2][-1][3]],
        [found[3][1][-2], found[3][-1][-2]],
    ]
    parts, _ = lax.optimization_barrier(
        (
            [own[0]] + found[0][1][1:] + found[0][-1][1:],
            [found[2][1][1], found[2][-1][1], found[1][1][-1], found[1][-1][-1]],
        )
    )
    tile = collect(place, cycle, rights[0], parts)
    ends = [
        lax.ppermute(tile, "tm", [(n, blocks - 1)]) if n < blocks - 1 else tile
        for n in range(gains.shape[2] // 2 // LANES + 1)
    ]
    state, half = None, None
    for turn, (low, high) in enumerate(ranges):
        parts = [own[turn]] + found[turn][1][1:] + found[turn][-1][1:]
        if turn < len(ties):
            parts, _ = lax.optimization_barrier((parts, ties[turn]))
            *state, half = compose(last, place, cycle, rights[turn], parts, ends, state, half, low, high - low, steps)
        else:
            early = chain(place, cycle, rights[turn], parts, half, high)
    factors, own, mine = state
    factors, mine = extend_factors(place, early[0], factors, mine)
    own = own_rows(place, early[1], own)
    packed = []
    for turn in range(blocks - 1, 0, -1):
        before = hop(factors, early[1], packed) if packed else early[2]
        packed.append(lax.ppermute(before, "tm", [(turn, turn - 1)]))
    return finish(factors, own, mine, packed)


def solution(mesh):
    return jax.shard_map(
        local,
        mesh=mesh,
        in_specs=(P("tm", "tile", None), P("tm", "tile", None), P("tile", None)),
        out_specs=P("tm", "tile", None),
        check_vma=False,
    )
```

```python
import functools
import math

import jax
import jax.numpy as jnp
from jax import lax
from jax.experimental import pallas as pl
from jax.experimental.pallas import tpu as pltpu
from jax.sharding import PartitionSpec as P

BF16 = jnp.bfloat16
F32 = jnp.float32
LANES = 128
TILE = 256
LINE = 4
MIB = 1024 * 1024
CLAIM = 60 * MIB


def nt(left, right):
    return lax.dot_general(left, right, (((1,), (1,)), ((), ())), preferred_element_type=F32)


def packed_half(increment, place, count):
    rows, width = increment.shape
    turned = pltpu.roll(increment, lax.rem(width - place * rows, width), 1)
    column = lax.broadcasted_iota(jnp.int32, (rows, width // 2), 1)
    main = turned[:, :width // 2] * jnp.where(column < rows, 0.5, 1.0)
    opposite = turned[:, width // 2:width // 2 + LANES]
    lower = opposite[rows // 2:]
    side = jnp.concatenate([lower, pltpu.roll(lower, LANES - rows // 2, 1)], axis=0)
    return main.astype(BF16), jnp.where(place < count // 2, opposite, side)


def unpacked_half(main, extra, block, count):
    rows = main.shape[0]
    width = rows * count
    column = lax.broadcasted_iota(jnp.int32, extra.shape, 1)
    extra = jnp.where(column < rows // 2, extra, 0.0)
    if block >= count // 2:
        lower = extra[:rows // 2] + pltpu.roll(extra[rows // 2:], rows // 2, 1)
        extra = jnp.concatenate([jnp.zeros_like(lower), lower], axis=0)
    rest = jnp.zeros((rows, width // 2 - LANES), F32)
    wide = jnp.concatenate([main.astype(F32), extra, rest], axis=1)
    return pltpu.roll(wide, block * rows, 1) if block else wide


def pack_kernel(count, ranges, place_ref, block_ref, gain_ref, increment_ref, *refs):
    outs = refs[-len(ranges):]
    rows, width = gain_ref.shape[1:]
    stride = width + width // 2
    place = place_ref[0]
    base = min(low for low, _ in ranges)
    column = lax.broadcasted_iota(jnp.int32, (rows, LANES), 1)
    for (low, high), packed_ref in zip(ranges, outs):
        extras = jnp.zeros((rows, LANES), F32)
        for step in range(high - low):
            at = step * stride
            main, extra = packed_half(increment_ref[low - base + step], place, count)
            packed_ref[:, at:at + width] = gain_ref[low - base + step]
            packed_ref[:, at + width:at + stride] = main
            shift = step * rows // 2
            here = (column >= shift) & (column < shift + rows // 2)
            extras = jnp.where(here, pltpu.roll(extra, shift, 1) if shift else extra, extras)
        packed_ref[:, (high - low) * stride:(high - low) * stride + LANES] = extras.astype(BF16)
    if len(refs) > len(ranges):
        main, extra = packed_half(refs[0][...], place, count)
        at = (ranges[0][1] - ranges[0][0]) * stride + LANES
        tiles = [main[:, n:n + LANES].astype(F32) for n in range(0, width // 2, LANES)] + [extra]
        outs[0][:, at:] = sum(jnp.where(block_ref[0] == n, tile, 0.0) for n, tile in enumerate(tiles)).astype(BF16)


def pack(place, block, gains, increments, terminal, count, ranges):
    rows, width = gains.shape[1:]
    first, size = ranges[-1][0], ranges[0][1] - ranges[-1][0]
    ends = [] if terminal is None else [terminal]
    lanes = [(high - low) * (width + width // 2) + LANES for low, high in ranges]
    lanes[0] += LANES * len(ends)
    some = pl.BlockSpec((size, rows, width), lambda i, *p: (first // size, 0, 0))
    return pl.pallas_call(
        functools.partial(pack_kernel, count, ranges),
        grid_spec=pltpu.PrefetchScalarGridSpec(
            num_scalar_prefetch=2,
            grid=(1,),
            in_specs=[some, some] + [pl.BlockSpec((rows, width), lambda i, *p: (0, 0))] * len(ends),
            out_specs=[pl.BlockSpec((rows, n), lambda i, *p: (0, 0)) for n in lanes],
        ),
        out_shape=[jax.ShapeDtypeStruct((rows, n), BF16) for n in lanes],
        compiler_params=pltpu.CompilerParams(vmem_limit_bytes=CLAIM if len(ranges) == 1 else 14 * MIB),
        name="pack",
    )(place, block, gains, increments, *ends)


def collect_kernel(cycle, right, place_ref, *refs):
    out_ref = refs[-1]
    for place, tile in zip(origins(place_ref[0], cycle, right), refs):
        out_ref[place] = tile[...]


def collect(place, cycle, right, blocks):
    rows, lanes = blocks[0].shape
    tile = pl.BlockSpec((rows, LANES), lambda i, *p: (0, lanes // LANES - 1), pipeline_mode=pl.Buffered(1))
    return pl.pallas_call(
        functools.partial(collect_kernel, cycle, right),
        grid_spec=pltpu.PrefetchScalarGridSpec(
            num_scalar_prefetch=1,
            grid=(1,),
            in_specs=[tile] * len(blocks),
            out_specs=pl.BlockSpec((len(blocks), rows, LANES), lambda i, *p: (0, 0, 0)),
        ),
        out_shape=jax.ShapeDtypeStruct((len(blocks), rows, LANES), BF16),
        compiler_params=pltpu.CompilerParams(vmem_limit_bytes=6 * MIB),
        name="collect",
    )(place, *blocks)


def unpack(raw, extras, step, half):
    count, rows, _ = raw.shape
    shift = lax.rem(LANES - step * (rows // 2), LANES)
    for n in range(count):
        extra = pltpu.roll(extras[n].astype(F32), shift, 1)
        half[n * rows:(n + 1) * rows, :] = unpacked_half(raw[n], extra, n, count).astype(BF16)


def origins(place, cycle, right):
    count = len(cycle)

    def look(table, at):
        return sum(jnp.where(at == n, value, 0) for n, value in enumerate(table))

    spot = look([cycle.index(d) for d in range(count)], place)
    hops = [0] + [-n for n in range(1, right + 1)] + list(range(1, count - right))
    return [look(cycle, lax.rem(spot + n + count, count)) for n in hops]


def assemble(places, blocks, sides, step, gain, fresh, raw, extras):
    rows = blocks[0].shape[0]
    width = gain.shape[0]
    for place, block, side in zip(places, blocks, sides):
        gain[pl.ds(pl.multiple_of(place * rows, 16), rows), :] = block[:, :width]
        raw[place] = block[:, width:]
        extras[place] = side[...]
    unpack(raw, extras, step, fresh)


def advance(gain, half, fresh, middle):
    width = half.shape[0]
    for j in range(0, width, TILE):
        cols = slice(j, j + TILE)
        middle[:, cols] = jnp.dot(gain[...], half[:, cols], preferred_element_type=F32).astype(BF16)
    for j in range(0, width, TILE):
        cols = slice(j, j + TILE)
        half[:, cols] = (nt(middle[...], gain[cols, :]) + fresh[:, cols].astype(F32)).astype(BF16)


def extend(gain, factor):
    for j in range(0, factor.shape[0], TILE):
        cols = slice(j, j + TILE)
        factor[:, cols] = jnp.dot(gain[...], factor[:, cols], preferred_element_type=F32).astype(BF16)


def whole_rows(half, mine, rows):
    picked = lax.broadcasted_iota(jnp.int32, (rows, half.shape[0]), 1) == mine + lax.broadcasted_iota(
        jnp.int32, (rows, half.shape[0]), 0
    )
    own = half[pl.ds(mine, rows), :].astype(F32)
    return own + nt(jnp.where(picked, 1.0, 0.0).astype(BF16), half[...])


def prepare(places, blocks, step, turns, gain, fresh, raw, extras):
    stride = gain.shape[0] * 3 // 2
    lanes, side = slice(step * stride, (step + 1) * stride), slice(turns * stride, turns * stride + LANES)
    parts, sides = [block.at[:, lanes] for block in blocks], [block.at[:, side] for block in blocks]
    assemble(places, parts, sides, step, gain, fresh, raw, extras)


def compose_kernel(cycle, right, turns, first, last_ref, place_ref, *refs):
    count = len(cycle)
    places = origins(place_ref[0], cycle, right)
    blocks, refs = refs[:count], refs[count:]
    if first:
        tiles = blocks[0].shape[0] * count // 2 // LANES + 1
        ends, refs = refs[:tiles], refs[tiles:]
    else:
        half_in, factor_in, refs = refs[0], refs[1], refs[3:]
    factor_out, mine_out, half_out, half, factor, middle, raw, extras, gain, fresh, spare = refs
    gains, freshes = (gain, spare.at[0]), (fresh, spare.at[1])
    rows = blocks[0].shape[0]
    mine = pl.multiple_of(place_ref[0] * rows, 16)
    for turn in range(turns):

        @pl.when(pl.program_id(0) == turn)
        def _():
            now = turn % 2
            if turn == 0 and first:
                scale = jnp.where(last_ref[0] == 1, 1.0, 0.0).astype(BF16)
                for n, end in enumerate(ends[:-1]):
                    raw[:, :, n * LANES:(n + 1) * LANES] = end[...] * scale
                extras[...] = ends[-1][...] * scale
                unpack(raw, extras, 0, half)
            elif turn == 0:
                factor[...] = factor_in[0]
                half[...] = half_in[...]
            if turn == 0:
                prepare(places, blocks, turns - 1, turns, gains[0], freshes[0], raw, extras)
            if turn == 0 and first:
                factor[...] = gains[0][...]
            else:
                extend(gains[now], factor)
            if turn + 1 < turns:
                prepare(places, blocks, turns - 2 - turn, turns, gains[1 - now], freshes[1 - now], raw, extras)
            advance(gains[now], half, freshes[now], middle)
            half_out[0] = half[...]
            mine_out[0] = factor[pl.ds(mine, rows), :]
            factor_out[0] = factor[...]


def square(width, place=None):
    if place is None:
        return pl.BlockSpec((width, width), lambda i, *p: (0, 0), pipeline_mode=pl.Buffered(1))
    return pl.BlockSpec((1, width, width), lambda i, *p: (place(i), 0, 0))


def row_specs(blocks):
    return [pl.BlockSpec(block.shape, lambda i, *p: (0, 0), pipeline_mode=pl.Buffered(1)) for block in blocks]


def row_scratch(count, rows):
    width = count * rows
    whole = pltpu.VMEM((width, width), BF16)
    return [
        whole,
        pltpu.VMEM((count, rows, width // 2), BF16),
        pltpu.VMEM((count, rows, LANES), BF16),
        whole,
        whole,
        pltpu.VMEM((2, width, width), BF16),
    ]


def compose(last, place, cycle, right, blocks, ends, state, half, low, turns, steps):
    count = len(blocks)
    rows = blocks[0].shape[0]
    width = rows * count
    first = state is None
    anywhere = pl.BlockSpec(memory_space=pl.ANY)
    in_specs = row_specs(blocks)
    if first:
        in_specs += [pl.BlockSpec(end.shape, lambda i, *p: (0, 0, 0), pipeline_mode=pl.Buffered(1)) for end in ends]
        args = ends
    else:
        after = pl.BlockSpec((1, width, width), lambda i, *p: (low + turns, 0, 0), pipeline_mode=pl.Buffered(1))
        in_specs += [square(width), after, anywhere]
        args = [half, *state]
    whole = square(width, lambda i: low + turns - 1 - i)
    band = pl.BlockSpec((1, rows, width), lambda i, *p: (low + turns - 1 - i, 0, 0))
    base = 2 + count + 1
    return pl.pallas_call(
        functools.partial(compose_kernel, cycle, right, turns, first),
        grid_spec=pltpu.PrefetchScalarGridSpec(
            num_scalar_prefetch=2,
            grid=(turns,),
            in_specs=in_specs,
            out_specs=[whole, band, square(width, lambda i: turns - 1 - i), square(width)],
            scratch_shapes=[pltpu.VMEM((width, width), BF16)] + row_scratch(count, rows),
        ),
        out_shape=[
            jax.ShapeDtypeStruct((steps, width, width), BF16),
            jax.ShapeDtypeStruct((steps, rows, width), BF16),
            jax.ShapeDtypeStruct((turns, width, width), BF16),
            jax.ShapeDtypeStruct((width, width), BF16),
        ],
        input_output_aliases={} if first else {base: 0, base + 1: 1},
        compiler_params=pltpu.CompilerParams(vmem_limit_bytes=22 * MIB),
        cost_estimate=pl.CostEstimate(
            flops=6 * turns * width**3, bytes_accessed=8 * turns * width * width, transcendentals=0
        ),
        name="compose",
    )(last, place, *blocks, *args)


def chain_kernel(cycle, right, turns, place_ref, *refs):
    count = len(cycle)
    places = origins(place_ref[0], cycle, right)
    blocks, refs = refs[:count], refs[count:]
    half_in, refs = refs[0], refs[1:]
    gain_out, half_out, packed_out, half, middle, raw, extras, gain, fresh, spare = refs
    gains, freshes = (gain, spare.at[0]), (fresh, spare.at[1])
    for turn in range(turns):

        @pl.when(pl.program_id(0) == turn)
        def _():
            now = turn % 2
            if turn == 0:
                half[...] = half_in[...]
                prepare(places, blocks, turns - 1, turns, gains[0], freshes[0], raw, extras)
            gain_out[0] = gains[now][...]
            if turn + 1 < turns:
                prepare(places, blocks, turns - 2 - turn, turns, gains[1 - now], freshes[1 - now], raw, extras)
            advance(gains[now], half, freshes[now], middle)
            half_out[0] = half[...]
            if turn == turns - 1:
                fold(half, packed_out)


def chain(place, cycle, right, blocks, half, turns):
    count = len(blocks)
    rows = blocks[0].shape[0]
    width = rows * count
    in_specs = row_specs(blocks) + [square(width)]
    whole = square(width, lambda i: turns - 1 - i)
    return pl.pallas_call(
        functools.partial(chain_kernel, cycle, right, turns),
        grid_spec=pltpu.PrefetchScalarGridSpec(
            num_scalar_prefetch=1,
            grid=(turns,),
            in_specs=in_specs,
            out_specs=[whole, whole, pl.BlockSpec(blocks_shape(width), lambda i, *p: (0, 0, 0))],
            scratch_shapes=[pltpu.VMEM((width, width), BF16)] + row_scratch(count, rows),
        ),
        out_shape=[
            jax.ShapeDtypeStruct((turns, width, width), BF16),
            jax.ShapeDtypeStruct((turns, width, width), BF16),
            jax.ShapeDtypeStruct(blocks_shape(width), BF16),
        ],
        compiler_params=pltpu.CompilerParams(vmem_limit_bytes=18 * MIB),
        cost_estimate=pl.CostEstimate(
            flops=4 * turns * width**3, bytes_accessed=8 * turns * width * width, transcendentals=0
        ),
        name="chain",
    )(place, *blocks, half)


def factors_kernel(place_ref, gain_ref, factor_in, mine_ref, factor_out, mine_out, factor):
    del mine_ref
    rows = mine_out.shape[1]

    @pl.when(pl.program_id(0) == 0)
    def _():
        factor[...] = factor_in[0]

    extend(gain_ref.at[0], factor)
    mine_out[0] = factor[pl.ds(pl.multiple_of(place_ref[0] * rows, 16), rows), :]
    factor_out[0] = factor[...]


def extend_factors(place, gains, factors, mine):
    turns, width, _ = gains.shape
    steps, rows, _ = mine.shape
    anywhere = pl.BlockSpec(memory_space=pl.ANY)
    return pl.pallas_call(
        factors_kernel,
        grid_spec=pltpu.PrefetchScalarGridSpec(
            num_scalar_prefetch=1,
            grid=(turns,),
            in_specs=[square(width, lambda i: turns - 1 - i), square(width, lambda i: turns), anywhere],
            out_specs=[
                square(width, lambda i: turns - 1 - i),
                pl.BlockSpec((1, rows, width), lambda i, *p: (turns - 1 - i, 0, 0)),
            ],
            scratch_shapes=[pltpu.VMEM((width, width), BF16)],
        ),
        out_shape=[
            jax.ShapeDtypeStruct((steps, width, width), BF16),
            jax.ShapeDtypeStruct((steps, rows, width), BF16),
        ],
        input_output_aliases={2: 0, 3: 1},
        compiler_params=pltpu.CompilerParams(vmem_limit_bytes=12 * MIB),
        cost_estimate=pl.CostEstimate(
            flops=2 * turns * width**3, bytes_accessed=4 * turns * width * width, transcendentals=0
        ),
        name="extend_factors",
    )(place, gains, factors, mine)


def rows_kernel(size, place_ref, *refs):
    own_out = refs[-1]
    rows = own_out.shape[1]
    mine = pl.multiple_of(place_ref[0] * rows, 16)
    for n, half_ref in enumerate(refs[:-1]):

        @pl.when(pl.program_id(0) // size == n)
        def _():
            own_out[0] = whole_rows(half_ref.at[0], mine, rows)


def own_rows(place, halves, rows):
    size, width, _ = halves[0].shape
    steps = size * len(halves)
    return pl.pallas_call(
        functools.partial(rows_kernel, size),
        grid_spec=pltpu.PrefetchScalarGridSpec(
            num_scalar_prefetch=1,
            grid=(steps,),
            in_specs=[
                square(width, lambda i, n=n: jnp.clip(i - n * size, 0, size - 1)) for n in range(len(halves))
            ],
            out_specs=pl.BlockSpec((1, rows, width), lambda i, *p: (i, 0, 0)),
        ),
        out_shape=jax.ShapeDtypeStruct((steps, rows, width), F32),
        compiler_params=pltpu.CompilerParams(vmem_limit_bytes=14 * MIB),
        cost_estimate=pl.CostEstimate(
            flops=2 * steps * rows * width**2, bytes_accessed=2 * steps * width * width, transcendentals=0
        ),
        name="own_rows",
    )(place, *halves)


def upper_blocks(width):
    return [(a, b) for a in range(0, width, TILE) for b in range(a, width, TILE)]


def blocks_shape(width):
    return (len(upper_blocks(width)), TILE, TILE)


def identity(size):
    row = lax.broadcasted_iota(jnp.int32, (size, size), 0)
    column = lax.broadcasted_iota(jnp.int32, (size, size), 1)
    return jnp.where(row == column, 1.0, 0.0).astype(BF16)


def fold(half_ref, packed_ref):
    one = identity(TILE)
    for n, (a, b) in enumerate(upper_blocks(half_ref.shape[0])):
        block = half_ref[a:a + TILE, b:b + TILE]
        if a != b:
            block = block.astype(F32) + nt(one, half_ref[b:b + TILE, a:a + TILE])
        packed_ref[n] = block.astype(BF16)


def arrived_sum(refs, n):
    value = refs[0][n]
    for extra in refs[1:]:
        value = value + extra[n]
    return value


def hop_kernel(arrived, factor_ref, half_ref, *refs):
    out_ref, covariance, middle, ahead = refs[arrived:]
    width = factor_ref.shape[1]
    for n, (a, b) in enumerate(upper_blocks(width)):
        covariance[a:a + TILE, b:b + TILE] = arrived_sum(refs[:arrived], n)
    for j in range(0, width, TILE):
        cols = slice(j, j + TILE)
        middle[:, cols] = jnp.dot(
            factor_ref[0, :, :j + TILE], covariance[:j + TILE, cols], preferred_element_type=F32
        ).astype(BF16)
    for j in range(0, width, TILE):
        cols = slice(j, j + TILE)
        ahead[:, cols] = (nt(middle[...], factor_ref[0, cols, :]) + half_ref[0, :, cols].astype(F32)).astype(BF16)
    fold(ahead, out_ref)


def hop(factors, halves, packed):
    width = halves.shape[1]
    shape = blocks_shape(width)
    blocks = pl.BlockSpec(shape, lambda i: (0, 0, 0), pipeline_mode=pl.Buffered(1))
    whole = pl.BlockSpec((1, width, width), lambda i: (0, 0, 0), pipeline_mode=pl.Buffered(1))
    return pl.pallas_call(
        functools.partial(hop_kernel, len(packed)),
        grid=(1,),
        in_specs=[whole, whole] + [blocks] * len(packed),
        out_specs=blocks,
        out_shape=jax.ShapeDtypeStruct(shape, BF16),
        scratch_shapes=[pltpu.VMEM((width, width), BF16)] * 3,
        compiler_params=pltpu.CompilerParams(vmem_limit_bytes=16 * MIB),
        cost_estimate=pl.CostEstimate(flops=4 * width**3, bytes_accessed=10 * width * width, transcendentals=0),
        name="hop",
    )(factors, halves, *packed)


def finish_kernel(arrived, factor_ref, own_ref, mine_ref, *refs):
    out_ref, covariance, middle = refs[arrived:]
    turn = pl.program_id(0)
    rows = own_ref.shape[1]
    steps = mine_ref.shape[0]
    width = covariance.shape[0]

    @pl.when(turn == 0)
    def _():
        one = identity(TILE)
        for n, (a, b) in enumerate(upper_blocks(width)):
            block = arrived_sum(refs[:arrived], n)
            turned = nt(one, block)
            if a == b:
                covariance[a:a + TILE, b:b + TILE] = (block.astype(F32) + turned).astype(BF16)
            else:
                covariance[a:a + TILE, b:b + TILE] = block
                covariance[b:b + TILE, a:a + TILE] = turned.astype(BF16)
        mine = mine_ref[...].reshape(steps * rows, width)
        for j in range(0, width, TILE):
            cols = slice(j, j + TILE)
            middle[:, cols] = jnp.dot(mine, covariance[:, cols], preferred_element_type=F32).astype(BF16)

    for n in range(out_ref.shape[0]):
        at = (turn * out_ref.shape[0] + n) * rows
        left = middle[pl.ds(pl.multiple_of(at, 16), rows), :]
        out_ref[n] = nt(left, factor_ref[n]) + own_ref[n]


def finish(factors, own, mine, packed):
    steps, rows, width = own.shape
    some = 2 if steps % 2 == 0 else 1
    whole = pl.BlockSpec(packed[0].shape, lambda i: (0, 0, 0), pipeline_mode=pl.Buffered(1))
    band = pl.BlockSpec((some, rows, width), lambda i: (i, 0, 0))
    return pl.pallas_call(
        functools.partial(finish_kernel, len(packed)),
        grid=(steps // some,),
        in_specs=[
            pl.BlockSpec((some, width, width), lambda i: (i, 0, 0)),
            band,
            pl.BlockSpec(mine.shape, lambda i: (0, 0, 0), pipeline_mode=pl.Buffered(1)),
        ]
        + [whole] * len(packed),
        out_specs=band,
        scratch_shapes=[pltpu.VMEM((width, width), BF16), pltpu.VMEM((steps * rows, width), BF16)],
        out_shape=jax.ShapeDtypeStruct((steps, rows, width), F32),
        compiler_params=pltpu.CompilerParams(vmem_limit_bytes=24 * MIB),
        name="finish",
    )(factors, own, mine, *packed)


def ring_order(line, across):
    cycle = []
    for a in range(line):
        columns = list(range(1, across))
        cycle += [a * across + b for b in (columns if a % 2 == 0 else columns[::-1])]
    return cycle + [a * across for a in reversed(range(line))]


def pieces(steps):
    size = steps // 4
    return [(low, low + size) for low in reversed(range(0, steps, size))]


def local(gains, increments, terminal):
    count = lax.axis_size("tile")
    blocks = lax.axis_size("tm")
    line = math.gcd(count, LINE)
    steps = gains.shape[0]
    place = lax.axis_index("tile").astype(jnp.int32).reshape(1)
    block = lax.axis_index("tm").astype(jnp.int32).reshape(1)
    last = (block == blocks - 1).astype(jnp.int32)
    cycle = ring_order(line, count // line)

    def passed(array, way):
        return lax.ppermute(array, "tile", [(cycle[n], cycle[(n + way) % count]) for n in range(count)])

    ranges = pieces(steps)
    own = [
        *pack(place, block, gains, increments, terminal, count, ranges[:1]),
        *pack(place, block, gains, increments, None, count, ranges[1:2]),
        *pack(place, block, gains, increments, None, count, ranges[2:]),
    ]
    own[1], last = lax.optimization_barrier((own[1], last))
    rights = [count // 2 - turn % 2 for turn in range(len(own))]
    found = []
    for turn, array in enumerate(own):
        found.append({})
        for way, hops in ((1, rights[turn]), (-1, count - 1 - rights[turn])):
            source = array
            if turn > 1:
                before = found[turn - 1][way]
                gate = count // 2 - 1 if turn == 2 else len(before) - 3
                source, before[gate] = lax.optimization_barrier((source, before[gate]))
                for n in range(gate + 1, len(before)):
                    before[n] = passed(before[n - 1], way)
            found[turn][way] = [source]
            for _ in range(hops):
                found[turn][way].append(passed(found[turn][way][-1], way))
    ties = [
        [found[2][1][2], found[2][-1][2]],
        [found[2][1][3], found[2][-1][3]],
        [found[3][1][-2], found[3][-1][-2]],
    ]
    parts, _ = lax.optimization_barrier(
        (
            [own[0]] + found[0][1][1:] + found[0][-1][1:],
            [found[2][1][1], found[2][-1][1], found[1][1][-1], found[1][-1][-1]],
        )
    )
    tile = collect(place, cycle, rights[0], parts)
    ends = [
        lax.ppermute(tile, "tm", [(n, blocks - 1)]) if n < blocks - 1 else tile
        for n in range(gains.shape[2] // 2 // LANES + 1)
    ]
    state, half = None, None
    halves = []
    for turn, (low, high) in enumerate(ranges):
        parts = [own[turn]] + found[turn][1][1:] + found[turn][-1][1:]
        if turn < len(ties):
            parts, _ = lax.optimization_barrier((parts, ties[turn]))
            *state, kept, half = compose(
                last, place, cycle, rights[turn], parts, ends, state, half, low, high - low, steps
            )
        else:
            late_gains, kept, folded = chain(place, cycle, rights[turn], parts, half, high)
        halves.insert(0, kept)
    factors, mine = extend_factors(place, late_gains, *state)
    packed = []
    for turn in range(blocks - 1, 0, -1):
        if turn == 1:
            own = own_rows(place, lax.optimization_barrier((halves, before))[0], gains.shape[1])
            packed, own = lax.optimization_barrier((packed, own))
        before = hop(factors, halves[0], packed) if packed else folded
        packed.append(lax.ppermute(before, "tm", [(turn, turn - 1)]))
    return finish(factors, own, mine, packed)


def solution(mesh):
    return jax.shard_map(
        local,
        mesh=mesh,
        in_specs=(P("tm", "tile", None), P("tm", "tile", None), P("tile", None)),
        out_specs=P("tm", "tile", None),
        check_vma=False,
    )
```

```python
import functools
import math

import jax
import jax.numpy as jnp
from jax import lax
from jax.experimental import pallas as pl
from jax.experimental.pallas import tpu as pltpu
from jax.sharding import PartitionSpec as P

BF16 = jnp.bfloat16
F32 = jnp.float32
LANES = 128
TILE = 256
LINE = 4
MIB = 1024 * 1024
CLAIM = 60 * MIB


def nt(left, right):
    return lax.dot_general(left, right, (((1,), (1,)), ((), ())), preferred_element_type=F32)


def packed_half(increment, place, count):
    rows, width = increment.shape
    turned = pltpu.roll(increment, lax.rem(width - place * rows, width), 1)
    column = lax.broadcasted_iota(jnp.int32, (rows, width // 2), 1)
    main = turned[:, :width // 2] * jnp.where(column < rows, 0.5, 1.0)
    opposite = turned[:, width // 2:width // 2 + LANES]
    lower = opposite[rows // 2:]
    side = jnp.concatenate([lower, pltpu.roll(lower, LANES - rows // 2, 1)], axis=0)
    return main.astype(BF16), jnp.where(place < count // 2, opposite, side)


def unpacked_half(main, extra, block, count):
    rows = main.shape[0]
    width = rows * count
    column = lax.broadcasted_iota(jnp.int32, extra.shape, 1)
    extra = jnp.where(column < rows // 2, extra, 0.0)
    if block >= count // 2:
        lower = extra[:rows // 2] + pltpu.roll(extra[rows // 2:], rows // 2, 1)
        extra = jnp.concatenate([jnp.zeros_like(lower), lower], axis=0)
    rest = jnp.zeros((rows, width // 2 - LANES), F32)
    wide = jnp.concatenate([main.astype(F32), extra, rest], axis=1)
    return pltpu.roll(wide, block * rows, 1) if block else wide


def pack_kernel(count, ranges, place_ref, block_ref, gain_ref, increment_ref, *refs):
    outs = refs[-len(ranges):]
    rows, width = gain_ref.shape[1:]
    stride = width + width // 2
    place = place_ref[0]
    base = min(low for low, _ in ranges)
    column = lax.broadcasted_iota(jnp.int32, (rows, LANES), 1)
    for (low, high), packed_ref in zip(ranges, outs):
        extras = jnp.zeros((rows, LANES), F32)
        for step in range(high - low):
            at = step * stride
            main, extra = packed_half(increment_ref[low - base + step], place, count)
            packed_ref[:, at:at + width] = gain_ref[low - base + step]
            packed_ref[:, at + width:at + stride] = main
            shift = step * rows // 2
            here = (column >= shift) & (column < shift + rows // 2)
            extras = jnp.where(here, pltpu.roll(extra, shift, 1) if shift else extra, extras)
        packed_ref[:, (high - low) * stride:(high - low) * stride + LANES] = extras.astype(BF16)
    if len(refs) > len(ranges):
        main, extra = packed_half(refs[0][...], place, count)
        at = (ranges[0][1] - ranges[0][0]) * stride + LANES
        tiles = [main[:, n:n + LANES].astype(F32) for n in range(0, width // 2, LANES)] + [extra]
        outs[0][:, at:] = sum(jnp.where(block_ref[0] == n, tile, 0.0) for n, tile in enumerate(tiles)).astype(BF16)


def pack(place, block, gains, increments, terminal, count, ranges):
    rows, width = gains.shape[1:]
    first, size = ranges[-1][0], ranges[0][1] - ranges[-1][0]
    ends = [] if terminal is None else [terminal]
    lanes = [(high - low) * (width + width // 2) + LANES for low, high in ranges]
    lanes[0] += LANES * len(ends)
    some = pl.BlockSpec((size, rows, width), lambda i, *p: (first // size, 0, 0))
    return pl.pallas_call(
        functools.partial(pack_kernel, count, ranges),
        grid_spec=pltpu.PrefetchScalarGridSpec(
            num_scalar_prefetch=2,
            grid=(1,),
            in_specs=[some, some] + [pl.BlockSpec((rows, width), lambda i, *p: (0, 0))] * len(ends),
            out_specs=[pl.BlockSpec((rows, n), lambda i, *p: (0, 0)) for n in lanes],
        ),
        out_shape=[jax.ShapeDtypeStruct((rows, n), BF16) for n in lanes],
        compiler_params=pltpu.CompilerParams(vmem_limit_bytes=CLAIM if len(ranges) == 1 else 14 * MIB),
        name="pack",
    )(place, block, gains, increments, *ends)


def collect_kernel(cycle, right, place_ref, *refs):
    out_ref = refs[-1]
    for place, tile in zip(origins(place_ref[0], cycle, right), refs):
        out_ref[place] = tile[...]


def collect(place, cycle, right, blocks):
    rows, lanes = blocks[0].shape
    tile = pl.BlockSpec((rows, LANES), lambda i, *p: (0, lanes // LANES - 1), pipeline_mode=pl.Buffered(1))
    return pl.pallas_call(
        functools.partial(collect_kernel, cycle, right),
        grid_spec=pltpu.PrefetchScalarGridSpec(
            num_scalar_prefetch=1,
            grid=(1,),
            in_specs=[tile] * len(blocks),
            out_specs=pl.BlockSpec((len(blocks), rows, LANES), lambda i, *p: (0, 0, 0)),
        ),
        out_shape=jax.ShapeDtypeStruct((len(blocks), rows, LANES), BF16),
        compiler_params=pltpu.CompilerParams(vmem_limit_bytes=6 * MIB),
        name="collect",
    )(place, *blocks)


def unpack(raw, extras, step, half):
    count, rows, _ = raw.shape
    shift = lax.rem(LANES - step * (rows // 2), LANES)
    for n in range(count):
        extra = pltpu.roll(extras[n].astype(F32), shift, 1)
        half[n * rows:(n + 1) * rows, :] = unpacked_half(raw[n], extra, n, count).astype(BF16)


def origins(place, cycle, right):
    count = len(cycle)

    def look(table, at):
        return sum(jnp.where(at == n, value, 0) for n, value in enumerate(table))

    spot = look([cycle.index(d) for d in range(count)], place)
    hops = [0] + [-n for n in range(1, right + 1)] + list(range(1, count - right))
    return [look(cycle, lax.rem(spot + n + count, count)) for n in hops]


def assemble(places, blocks, sides, step, gain, fresh, raw, extras):
    rows = blocks[0].shape[0]
    width = gain.shape[0]
    for place, block, side in zip(places, blocks, sides):
        gain[pl.ds(pl.multiple_of(place * rows, 16), rows), :] = block[:, :width]
        raw[place] = block[:, width:]
        extras[place] = side[...]
    unpack(raw, extras, step, fresh)


def advance(gain, half, fresh, middle, out=None):
    out = half if out is None else out
    width = half.shape[0]
    for j in range(0, width, TILE):
        cols = slice(j, j + TILE)
        middle[:, cols] = jnp.dot(gain[...], half[:, cols], preferred_element_type=F32).astype(BF16)
    for j in range(0, width, TILE):
        cols = slice(j, j + TILE)
        out[:, cols] = (nt(middle[...], gain[cols, :]) + fresh[:, cols].astype(F32)).astype(BF16)


def extend(gain, factor):
    for j in range(0, factor.shape[0], TILE):
        cols = slice(j, j + TILE)
        factor[:, cols] = jnp.dot(gain[...], factor[:, cols], preferred_element_type=F32).astype(BF16)


def whole_rows(half, mine, rows):
    picked = lax.broadcasted_iota(jnp.int32, (rows, half.shape[0]), 1) == mine + lax.broadcasted_iota(
        jnp.int32, (rows, half.shape[0]), 0
    )
    own = half[pl.ds(mine, rows), :].astype(F32)
    return own + nt(jnp.where(picked, 1.0, 0.0).astype(BF16), half[...])


def prepare(places, blocks, step, turns, gain, fresh, raw, extras):
    stride = gain.shape[0] * 3 // 2
    lanes, side = slice(step * stride, (step + 1) * stride), slice(turns * stride, turns * stride + LANES)
    parts, sides = [block.at[:, lanes] for block in blocks], [block.at[:, side] for block in blocks]
    assemble(places, parts, sides, step, gain, fresh, raw, extras)


def compose_kernel(cycle, right, turns, first, last_ref, place_ref, *refs):
    count = len(cycle)
    places = origins(place_ref[0], cycle, right)
    blocks, refs = refs[:count], refs[count:]
    if first:
        tiles = blocks[0].shape[0] * count // 2 // LANES + 1
        ends, refs = refs[:tiles], refs[tiles:]
    else:
        half_in, factor_in, refs = refs[0], refs[1], refs[3:]
    factor_out, mine_out, half_out, half, factor, middle, raw, extras, gain, fresh, spare = refs
    gains, freshes = (gain, spare.at[0]), (fresh, spare.at[1])
    rows = blocks[0].shape[0]
    mine = pl.multiple_of(place_ref[0] * rows, 16)
    for turn in range(turns):

        @pl.when(pl.program_id(0) == turn)
        def _():
            now = turn % 2
            if turn == 0 and first:
                scale = jnp.where(last_ref[0] == 1, 1.0, 0.0).astype(BF16)
                for n, end in enumerate(ends[:-1]):
                    raw[:, :, n * LANES:(n + 1) * LANES] = end[...] * scale
                extras[...] = ends[-1][...] * scale
                unpack(raw, extras, 0, half)
            elif turn == 0:
                factor[...] = factor_in[0]
                half[...] = half_in[...]
            if turn == 0:
                prepare(places, blocks, turns - 1, turns, gains[0], freshes[0], raw, extras)
            if turn == 0 and first:
                factor[...] = gains[0][...]
            else:
                extend(gains[now], factor)
            if turn + 1 < turns:
                prepare(places, blocks, turns - 2 - turn, turns, gains[1 - now], freshes[1 - now], raw, extras)
            advance(gains[now], half, freshes[now], middle)
            half_out[0] = half[...]
            mine_out[0] = factor[pl.ds(mine, rows), :]
            factor_out[0] = factor[...]


def square(width, place=None):
    if place is None:
        return pl.BlockSpec((width, width), lambda i, *p: (0, 0), pipeline_mode=pl.Buffered(1))
    return pl.BlockSpec((1, width, width), lambda i, *p: (place(i), 0, 0))


def row_specs(blocks):
    return [pl.BlockSpec(block.shape, lambda i, *p: (0, 0), pipeline_mode=pl.Buffered(1)) for block in blocks]


def row_scratch(count, rows):
    width = count * rows
    whole = pltpu.VMEM((width, width), BF16)
    return [
        whole,
        pltpu.VMEM((count, rows, width // 2), BF16),
        pltpu.VMEM((count, rows, LANES), BF16),
        whole,
        whole,
        pltpu.VMEM((2, width, width), BF16),
    ]


def compose(last, place, cycle, right, blocks, ends, state, half, low, turns, steps):
    count = len(blocks)
    rows = blocks[0].shape[0]
    width = rows * count
    first = state is None
    anywhere = pl.BlockSpec(memory_space=pl.ANY)
    in_specs = row_specs(blocks)
    if first:
        in_specs += [pl.BlockSpec(end.shape, lambda i, *p: (0, 0, 0), pipeline_mode=pl.Buffered(1)) for end in ends]
        args = ends
    else:
        after = pl.BlockSpec((1, width, width), lambda i, *p: (low + turns, 0, 0), pipeline_mode=pl.Buffered(1))
        in_specs += [square(width), after, anywhere]
        args = [half, *state]
    whole = square(width, lambda i: low + turns - 1 - i)
    band = pl.BlockSpec((1, rows, width), lambda i, *p: (low + turns - 1 - i, 0, 0))
    base = 2 + count + 1
    return pl.pallas_call(
        functools.partial(compose_kernel, cycle, right, turns, first),
        grid_spec=pltpu.PrefetchScalarGridSpec(
            num_scalar_prefetch=2,
            grid=(turns,),
            in_specs=in_specs,
            out_specs=[whole, band, square(width, lambda i: turns - 1 - i), square(width)],
            scratch_shapes=[pltpu.VMEM((width, width), BF16)] + row_scratch(count, rows),
        ),
        out_shape=[
            jax.ShapeDtypeStruct((steps, width, width), BF16),
            jax.ShapeDtypeStruct((steps, rows, width), BF16),
            jax.ShapeDtypeStruct((turns, width, width), BF16),
            jax.ShapeDtypeStruct((width, width), BF16),
        ],
        input_output_aliases={} if first else {base: 0, base + 1: 1},
        compiler_params=pltpu.CompilerParams(vmem_limit_bytes=22 * MIB),
        cost_estimate=pl.CostEstimate(
            flops=6 * turns * width**3, bytes_accessed=8 * turns * width * width, transcendentals=0
        ),
        name="compose",
    )(last, place, *blocks, *args)


def chain_kernel(cycle, right, turns, place_ref, *refs):
    count = len(cycle)
    places = origins(place_ref[0], cycle, right)
    blocks, refs = refs[:count], refs[count:]
    half, gain_out, half_out, packed_out, middle, raw, extras, fresh = refs
    prepare(places, blocks, turns - 1, turns, gain_out.at[turns - 1], fresh.at[0], raw, extras)
    for turn in range(turns):
        step = turns - 1 - turn
        if step:
            prepare(places, blocks, step - 1, turns, gain_out.at[step - 1], fresh.at[(turn + 1) % 2], raw, extras)
        advance(gain_out.at[step], half, fresh.at[turn % 2], middle, half_out.at[step])
        half = half_out.at[step]
    fold(half, packed_out)


def chain(place, cycle, right, blocks, half, turns):
    count = len(blocks)
    rows = blocks[0].shape[0]
    width = rows * count
    vmem = pl.BlockSpec(memory_space=pltpu.VMEM)
    return pl.pallas_call(
        functools.partial(chain_kernel, cycle, right, turns),
        in_specs=[pl.BlockSpec(memory_space=pltpu.SMEM)] + [vmem] * (count + 1),
        out_specs=[vmem] * 3,
        out_shape=[
            jax.ShapeDtypeStruct((turns, width, width), BF16),
            jax.ShapeDtypeStruct((turns, width, width), BF16),
            jax.ShapeDtypeStruct(blocks_shape(width), BF16),
        ],
        scratch_shapes=[
            pltpu.VMEM((width, width), BF16),
            pltpu.VMEM((count, rows, width // 2), BF16),
            pltpu.VMEM((count, rows, LANES), BF16),
            pltpu.VMEM((2, width, width), BF16),
        ],
        compiler_params=pltpu.CompilerParams(vmem_limit_bytes=26 * MIB),
        cost_estimate=pl.CostEstimate(
            flops=4 * turns * width**3, bytes_accessed=8 * turns * width * width, transcendentals=0
        ),
        name="chain",
    )(place, *blocks, half)


def factors_kernel(place_ref, gain_ref, factor_in, mine_ref, factor_out, mine_out, factor):
    del mine_ref
    rows = mine_out.shape[1]

    @pl.when(pl.program_id(0) == 0)
    def _():
        factor[...] = factor_in[0]

    extend(gain_ref.at[0], factor)
    mine_out[0] = factor[pl.ds(pl.multiple_of(place_ref[0] * rows, 16), rows), :]
    factor_out[0] = factor[...]


def extend_factors(place, gains, factors, mine):
    turns, width, _ = gains.shape
    steps, rows, _ = mine.shape
    anywhere = pl.BlockSpec(memory_space=pl.ANY)
    return pl.pallas_call(
        factors_kernel,
        grid_spec=pltpu.PrefetchScalarGridSpec(
            num_scalar_prefetch=1,
            grid=(turns,),
            in_specs=[square(width, lambda i: turns - 1 - i), square(width, lambda i: turns), anywhere],
            out_specs=[
                square(width, lambda i: turns - 1 - i),
                pl.BlockSpec((1, rows, width), lambda i, *p: (turns - 1 - i, 0, 0)),
            ],
            scratch_shapes=[pltpu.VMEM((width, width), BF16)],
        ),
        out_shape=[
            jax.ShapeDtypeStruct((steps, width, width), BF16),
            jax.ShapeDtypeStruct((steps, rows, width), BF16),
        ],
        input_output_aliases={2: 0, 3: 1},
        compiler_params=pltpu.CompilerParams(vmem_limit_bytes=12 * MIB),
        cost_estimate=pl.CostEstimate(
            flops=2 * turns * width**3, bytes_accessed=4 * turns * width * width, transcendentals=0
        ),
        name="extend_factors",
    )(place, gains, factors, mine)


def rows_kernel(size, place_ref, *refs):
    own_out = refs[-1]
    rows = own_out.shape[1]
    mine = pl.multiple_of(place_ref[0] * rows, 16)
    for n, half_ref in enumerate(refs[:-1]):

        @pl.when(pl.program_id(0) // size == n)
        def _():
            own_out[0] = whole_rows(half_ref.at[0], mine, rows)


def own_rows(place, halves, rows):
    size, width, _ = halves[0].shape
    steps = size * len(halves)
    return pl.pallas_call(
        functools.partial(rows_kernel, size),
        grid_spec=pltpu.PrefetchScalarGridSpec(
            num_scalar_prefetch=1,
            grid=(steps,),
            in_specs=[
                square(width, lambda i, n=n: jnp.clip(i - n * size, 0, size - 1)) for n in range(len(halves))
            ],
            out_specs=pl.BlockSpec((1, rows, width), lambda i, *p: (i, 0, 0)),
        ),
        out_shape=jax.ShapeDtypeStruct((steps, rows, width), F32),
        compiler_params=pltpu.CompilerParams(vmem_limit_bytes=14 * MIB),
        cost_estimate=pl.CostEstimate(
            flops=2 * steps * rows * width**2, bytes_accessed=2 * steps * width * width, transcendentals=0
        ),
        name="own_rows",
    )(place, *halves)


def upper_blocks(width):
    return [(a, b) for a in range(0, width, TILE) for b in range(a, width, TILE)]


def blocks_shape(width):
    return (len(upper_blocks(width)), TILE, TILE)


def identity(size):
    row = lax.broadcasted_iota(jnp.int32, (size, size), 0)
    column = lax.broadcasted_iota(jnp.int32, (size, size), 1)
    return jnp.where(row == column, 1.0, 0.0).astype(BF16)


def fold(half_ref, packed_ref):
    one = identity(TILE)
    for n, (a, b) in enumerate(upper_blocks(half_ref.shape[0])):
        block = half_ref[a:a + TILE, b:b + TILE]
        if a != b:
            block = block.astype(F32) + nt(one, half_ref[b:b + TILE, a:a + TILE])
        packed_ref[n] = block.astype(BF16)


def arrived_sum(refs, n):
    value = refs[0][n]
    for extra in refs[1:]:
        value = value + extra[n]
    return value


def hop_kernel(arrived, factor_ref, half_ref, *refs):
    out_ref, covariance, middle, ahead = refs[arrived:]
    width = factor_ref.shape[1]
    for n, (a, b) in enumerate(upper_blocks(width)):
        covariance[a:a + TILE, b:b + TILE] = arrived_sum(refs[:arrived], n)
    for j in range(0, width, TILE):
        cols = slice(j, j + TILE)
        middle[:, cols] = jnp.dot(
            factor_ref[0, :, :j + TILE], covariance[:j + TILE, cols], preferred_element_type=F32
        ).astype(BF16)
    for j in range(0, width, TILE):
        cols = slice(j, j + TILE)
        ahead[:, cols] = (nt(middle[...], factor_ref[0, cols, :]) + half_ref[0, :, cols].astype(F32)).astype(BF16)
    fold(ahead, out_ref)


def hop(factors, halves, packed):
    width = halves.shape[1]
    vmem = pl.BlockSpec(memory_space=pltpu.VMEM)
    return pl.pallas_call(
        functools.partial(hop_kernel, len(packed)),
        in_specs=[vmem] * (2 + len(packed)),
        out_specs=vmem,
        out_shape=jax.ShapeDtypeStruct(blocks_shape(width), BF16),
        scratch_shapes=[pltpu.VMEM((width, width), BF16)] * 3,
        compiler_params=pltpu.CompilerParams(vmem_limit_bytes=24 * MIB),
        cost_estimate=pl.CostEstimate(flops=4 * width**3, bytes_accessed=10 * width * width, transcendentals=0),
        name="hop",
    )(factors, halves, *packed)


def finish_kernel(arrived, factor_ref, own_ref, mine_ref, *refs):
    out_ref, covariance, middle = refs[arrived:]
    turn = pl.program_id(0)
    rows = own_ref.shape[1]
    steps = mine_ref.shape[0]
    width = covariance.shape[0]

    @pl.when(turn == 0)
    def _():
        one = identity(TILE)
        for n, (a, b) in enumerate(upper_blocks(width)):
            block = arrived_sum(refs[:arrived], n)
            turned = nt(one, block)
            if a == b:
                covariance[a:a + TILE, b:b + TILE] = (block.astype(F32) + turned).astype(BF16)
            else:
                covariance[a:a + TILE, b:b + TILE] = block
                covariance[b:b + TILE, a:a + TILE] = turned.astype(BF16)
        mine = mine_ref[...].reshape(steps * rows, width)
        for j in range(0, width, TILE):
            cols = slice(j, j + TILE)
            middle[:, cols] = jnp.dot(mine, covariance[:, cols], preferred_element_type=F32).astype(BF16)

    for n in range(out_ref.shape[0]):
        at = (turn * out_ref.shape[0] + n) * rows
        left = middle[pl.ds(pl.multiple_of(at, 16), rows), :]
        out_ref[n] = nt(left, factor_ref[n]) + own_ref[n]


def finish(factors, own, mine, packed):
    steps, rows, width = own.shape
    some = 2 if steps % 2 == 0 else 1
    whole = pl.BlockSpec(packed[0].shape, lambda i: (0, 0, 0), pipeline_mode=pl.Buffered(1))
    band = pl.BlockSpec((some, rows, width), lambda i: (i, 0, 0))
    return pl.pallas_call(
        functools.partial(finish_kernel, len(packed)),
        grid=(steps // some,),
        in_specs=[
            pl.BlockSpec((some, width, width), lambda i: (i, 0, 0)),
            band,
            pl.BlockSpec(mine.shape, lambda i: (0, 0, 0), pipeline_mode=pl.Buffered(1)),
        ]
        + [whole] * len(packed),
        out_specs=band,
        scratch_shapes=[pltpu.VMEM((width, width), BF16), pltpu.VMEM((steps * rows, width), BF16)],
        out_shape=jax.ShapeDtypeStruct((steps, rows, width), F32),
        compiler_params=pltpu.CompilerParams(vmem_limit_bytes=24 * MIB),
        name="finish",
    )(factors, own, mine, *packed)


def ring_order(line, across):
    cycle = []
    for a in range(line):
        columns = list(range(1, across))
        cycle += [a * across + b for b in (columns if a % 2 == 0 else columns[::-1])]
    return cycle + [a * across for a in reversed(range(line))]


def pieces(steps):
    size = steps // 4
    return [(low, low + size) for low in reversed(range(0, steps, size))]


def local(gains, increments, terminal):
    count = lax.axis_size("tile")
    blocks = lax.axis_size("tm")
    line = math.gcd(count, LINE)
    steps = gains.shape[0]
    place = lax.axis_index("tile").astype(jnp.int32).reshape(1)
    block = lax.axis_index("tm").astype(jnp.int32).reshape(1)
    last = (block == blocks - 1).astype(jnp.int32)
    cycle = ring_order(line, count // line)

    def passed(array, way):
        return lax.ppermute(array, "tile", [(cycle[n], cycle[(n + way) % count]) for n in range(count)])

    ranges = pieces(steps)
    own = [
        *pack(place, block, gains, increments, terminal, count, ranges[:1]),
        *pack(place, block, gains, increments, None, count, ranges[1:2]),
        *pack(place, block, gains, increments, None, count, ranges[2:]),
    ]
    own[1], last = lax.optimization_barrier((own[1], last))
    rights = [count // 2 - turn % 2 for turn in range(len(own))]
    found = []
    for turn, array in enumerate(own):
        found.append({})
        for way, hops in ((1, rights[turn]), (-1, count - 1 - rights[turn])):
            source = array
            if turn > 1:
                before = found[turn - 1][way]
                gate = count // 2 - 1 if turn == 2 else len(before) - 3
                source, before[gate] = lax.optimization_barrier((source, before[gate]))
                for n in range(gate + 1, len(before)):
                    before[n] = passed(before[n - 1], way)
            found[turn][way] = [source]
            for _ in range(hops):
                found[turn][way].append(passed(found[turn][way][-1], way))
    ties = [
        [found[2][1][2], found[2][-1][2]],
        [found[2][1][3], found[2][-1][3]],
        [found[3][1][-2], found[3][-1][-2]],
    ]
    parts, _ = lax.optimization_barrier(
        (
            [own[0]] + found[0][1][1:] + found[0][-1][1:],
            [found[2][1][1], found[2][-1][1], found[1][1][-1], found[1][-1][-1]],
        )
    )
    tile = collect(place, cycle, rights[0], parts)
    ends = [
        lax.ppermute(tile, "tm", [(n, blocks - 1)]) if n < blocks - 1 else tile
        for n in range(gains.shape[2] // 2 // LANES + 1)
    ]
    state, half = None, None
    halves = []
    for turn, (low, high) in enumerate(ranges):
        parts = [own[turn]] + found[turn][1][1:] + found[turn][-1][1:]
        if turn < len(ties):
            parts, _ = lax.optimization_barrier((parts, ties[turn]))
            *state, kept, half = compose(
                last, place, cycle, rights[turn], parts, ends, state, half, low, high - low, steps
            )
        else:
            late_gains, kept, folded = chain(place, cycle, rights[turn], parts, half, high)
        halves.insert(0, kept)
    factors, mine = extend_factors(place, late_gains, *state)
    packed = []
    for turn in range(blocks - 1, 0, -1):
        if turn == 1:
            own = own_rows(place, lax.optimization_barrier((halves, before))[0], gains.shape[1])
            packed, own = lax.optimization_barrier((packed, own))
        before = hop(factors, halves[0], packed) if packed else folded
        packed.append(lax.ppermute(before, "tm", [(turn, turn - 1)]))
    return finish(factors, own, mine, packed)


def solution(mesh):
    return jax.shard_map(
        local,
        mesh=mesh,
        in_specs=(P("tm", "tile", None), P("tm", "tile", None), P("tile", None)),
        out_specs=P("tm", "tile", None),
        check_vma=False,
    )
```

```python
import functools
import math

import jax
import jax.numpy as jnp
from jax import lax
from jax.experimental import pallas as pl
from jax.experimental.pallas import tpu as pltpu
from jax.sharding import PartitionSpec as P

BF16 = jnp.bfloat16
F32 = jnp.float32
LANES = 128
TILE = 256
LINE = 4
MIB = 1024 * 1024
CLAIM = 60 * MIB


def nt(left, right):
    return lax.dot_general(left, right, (((1,), (1,)), ((), ())), preferred_element_type=F32)


def packed_half(increment, place, count):
    rows, width = increment.shape
    turned = pltpu.roll(increment, lax.rem(width - place * rows, width), 1)
    column = lax.broadcasted_iota(jnp.int32, (rows, width // 2), 1)
    main = turned[:, :width // 2] * jnp.where(column < rows, 0.5, 1.0)
    opposite = turned[:, width // 2:width // 2 + LANES]
    lower = opposite[rows // 2:]
    side = jnp.concatenate([lower, pltpu.roll(lower, LANES - rows // 2, 1)], axis=0)
    return main.astype(BF16), jnp.where(place < count // 2, opposite, side)


def unpacked_half(main, extra, block, count):
    rows = main.shape[0]
    width = rows * count
    column = lax.broadcasted_iota(jnp.int32, extra.shape, 1)
    extra = jnp.where(column < rows // 2, extra, 0.0)
    if block >= count // 2:
        lower = extra[:rows // 2] + pltpu.roll(extra[rows // 2:], rows // 2, 1)
        extra = jnp.concatenate([jnp.zeros_like(lower), lower], axis=0)
    rest = jnp.zeros((rows, width // 2 - LANES), F32)
    wide = jnp.concatenate([main.astype(F32), extra, rest], axis=1)
    return pltpu.roll(wide, block * rows, 1) if block else wide


def pack_kernel(count, ranges, place_ref, block_ref, gain_ref, increment_ref, *refs):
    outs = refs[-len(ranges):]
    rows, width = gain_ref.shape[1:]
    stride = width + width // 2
    place = place_ref[0]
    base = min(low for low, _ in ranges)
    column = lax.broadcasted_iota(jnp.int32, (rows, LANES), 1)
    for (low, high), packed_ref in zip(ranges, outs):
        extras = jnp.zeros((rows, LANES), F32)
        for step in range(high - low):
            at = step * stride
            main, extra = packed_half(increment_ref[low - base + step], place, count)
            packed_ref[:, at:at + width] = gain_ref[low - base + step]
            packed_ref[:, at + width:at + stride] = main
            shift = step * rows // 2
            here = (column >= shift) & (column < shift + rows // 2)
            extras = jnp.where(here, pltpu.roll(extra, shift, 1) if shift else extra, extras)
        packed_ref[:, (high - low) * stride:(high - low) * stride + LANES] = extras.astype(BF16)
    if len(refs) > len(ranges):
        main, extra = packed_half(refs[0][...], place, count)
        at = (ranges[0][1] - ranges[0][0]) * stride + LANES
        tiles = [main[:, n:n + LANES].astype(F32) for n in range(0, width // 2, LANES)] + [extra]
        outs[0][:, at:] = sum(jnp.where(block_ref[0] == n, tile, 0.0) for n, tile in enumerate(tiles)).astype(BF16)


def pack(place, block, gains, increments, terminal, count, ranges):
    rows, width = gains.shape[1:]
    first, size = ranges[-1][0], ranges[0][1] - ranges[-1][0]
    ends = [] if terminal is None else [terminal]
    lanes = [(high - low) * (width + width // 2) + LANES for low, high in ranges]
    lanes[0] += LANES * len(ends)
    some = pl.BlockSpec((size, rows, width), lambda i, *p: (first // size, 0, 0))
    return pl.pallas_call(
        functools.partial(pack_kernel, count, ranges),
        grid_spec=pltpu.PrefetchScalarGridSpec(
            num_scalar_prefetch=2,
            grid=(1,),
            in_specs=[some, some] + [pl.BlockSpec((rows, width), lambda i, *p: (0, 0))] * len(ends),
            out_specs=[pl.BlockSpec((rows, n), lambda i, *p: (0, 0)) for n in lanes],
        ),
        out_shape=[jax.ShapeDtypeStruct((rows, n), BF16) for n in lanes],
        compiler_params=pltpu.CompilerParams(vmem_limit_bytes=CLAIM if len(ranges) == 1 else 14 * MIB),
        name="pack",
    )(place, block, gains, increments, *ends)


def collect_kernel(cycle, right, place_ref, *refs):
    out_ref = refs[-1]
    for place, tile in zip(origins(place_ref[0], cycle, right), refs):
        out_ref[place] = tile[...]


def collect(place, cycle, right, blocks):
    rows, lanes = blocks[0].shape
    tile = pl.BlockSpec((rows, LANES), lambda i, *p: (0, lanes // LANES - 1), pipeline_mode=pl.Buffered(1))
    return pl.pallas_call(
        functools.partial(collect_kernel, cycle, right),
        grid_spec=pltpu.PrefetchScalarGridSpec(
            num_scalar_prefetch=1,
            grid=(1,),
            in_specs=[tile] * len(blocks),
            out_specs=pl.BlockSpec((len(blocks), rows, LANES), lambda i, *p: (0, 0, 0)),
        ),
        out_shape=jax.ShapeDtypeStruct((len(blocks), rows, LANES), BF16),
        compiler_params=pltpu.CompilerParams(vmem_limit_bytes=6 * MIB),
        name="collect",
    )(place, *blocks)


def unpack(raw, extras, step, half):
    count, rows, _ = raw.shape
    shift = lax.rem(LANES - step * (rows // 2), LANES)
    for n in range(count):
        extra = pltpu.roll(extras[n].astype(F32), shift, 1)
        half[n * rows:(n + 1) * rows, :] = unpacked_half(raw[n], extra, n, count).astype(BF16)


def origins(place, cycle, right):
    count = len(cycle)

    def look(table, at):
        return sum(jnp.where(at == n, value, 0) for n, value in enumerate(table))

    spot = look([cycle.index(d) for d in range(count)], place)
    hops = [0] + [-n for n in range(1, right + 1)] + list(range(1, count - right))
    return [look(cycle, lax.rem(spot + n + count, count)) for n in hops]


def assemble(places, blocks, sides, step, gain, fresh, raw, extras):
    rows = blocks[0].shape[0]
    width = gain.shape[0]
    for place, block, side in zip(places, blocks, sides):
        gain[pl.ds(pl.multiple_of(place * rows, 16), rows), :] = block[:, :width]
        raw[place] = block[:, width:]
        extras[place] = side[...]
    unpack(raw, extras, step, fresh)


def advance(gain, half, fresh, middle, out=None):
    out = half if out is None else out
    width = half.shape[0]
    for j in range(0, width, TILE):
        cols = slice(j, j + TILE)
        middle[:, cols] = jnp.dot(gain[...], half[:, cols], preferred_element_type=F32).astype(BF16)
    for j in range(0, width, TILE):
        cols = slice(j, j + TILE)
        out[:, cols] = (nt(middle[...], gain[cols, :]) + fresh[:, cols].astype(F32)).astype(BF16)


def extend(gain, factor):
    for j in range(0, factor.shape[0], TILE):
        cols = slice(j, j + TILE)
        factor[:, cols] = jnp.dot(gain[...], factor[:, cols], preferred_element_type=F32).astype(BF16)


def whole_rows(half, mine, rows):
    picked = lax.broadcasted_iota(jnp.int32, (rows, half.shape[0]), 1) == mine + lax.broadcasted_iota(
        jnp.int32, (rows, half.shape[0]), 0
    )
    own = half[pl.ds(mine, rows), :].astype(F32)
    return own + nt(jnp.where(picked, 1.0, 0.0).astype(BF16), half[...])


def prepare(places, blocks, step, turns, gain, fresh, raw, extras):
    stride = gain.shape[0] * 3 // 2
    lanes, side = slice(step * stride, (step + 1) * stride), slice(turns * stride, turns * stride + LANES)
    parts, sides = [block.at[:, lanes] for block in blocks], [block.at[:, side] for block in blocks]
    assemble(places, parts, sides, step, gain, fresh, raw, extras)


def compose_kernel(cycle, right, turns, first, last_ref, place_ref, *refs):
    count = len(cycle)
    places = origins(place_ref[0], cycle, right)
    blocks, refs = refs[:count], refs[count:]
    if first:
        tiles = blocks[0].shape[0] * count // 2 // LANES + 1
        ends, refs = refs[:tiles], refs[tiles:]
    else:
        half_in, factor_in, refs = refs[0], refs[1], refs[3:]
    factor_out, mine_out, half_out, half, factor, middle, raw, extras, gain, fresh, spare = refs
    gains, freshes = (gain, spare.at[0]), (fresh, spare.at[1])
    rows = blocks[0].shape[0]
    mine = pl.multiple_of(place_ref[0] * rows, 16)
    for turn in range(turns):

        @pl.when(pl.program_id(0) == turn)
        def _():
            now = turn % 2
            if turn == 0 and first:
                scale = jnp.where(last_ref[0] == 1, 1.0, 0.0).astype(BF16)
                for n, end in enumerate(ends[:-1]):
                    raw[:, :, n * LANES:(n + 1) * LANES] = end[...] * scale
                extras[...] = ends[-1][...] * scale
                unpack(raw, extras, 0, half)
            elif turn == 0:
                factor[...] = factor_in[0]
                half[...] = half_in[...]
            if turn == 0:
                prepare(places, blocks, turns - 1, turns, gains[0], freshes[0], raw, extras)
            if turn == 0 and first:
                factor[...] = gains[0][...]
            else:
                extend(gains[now], factor)
            if turn + 1 < turns:
                prepare(places, blocks, turns - 2 - turn, turns, gains[1 - now], freshes[1 - now], raw, extras)
            advance(gains[now], half, freshes[now], middle)
            half_out[0] = half[...]
            mine_out[0] = factor[pl.ds(mine, rows), :]
            factor_out[0] = factor[...]


def square(width, place=None):
    if place is None:
        return pl.BlockSpec((width, width), lambda i, *p: (0, 0), pipeline_mode=pl.Buffered(1))
    return pl.BlockSpec((1, width, width), lambda i, *p: (place(i), 0, 0))


def row_specs(blocks):
    return [pl.BlockSpec(block.shape, lambda i, *p: (0, 0), pipeline_mode=pl.Buffered(1)) for block in blocks]


def row_scratch(count, rows):
    width = count * rows
    whole = pltpu.VMEM((width, width), BF16)
    return [
        whole,
        pltpu.VMEM((count, rows, width // 2), BF16),
        pltpu.VMEM((count, rows, LANES), BF16),
        whole,
        whole,
        pltpu.VMEM((2, width, width), BF16),
    ]


def compose(last, place, cycle, right, blocks, ends, state, half, low, turns, steps):
    count = len(blocks)
    rows = blocks[0].shape[0]
    width = rows * count
    first = state is None
    anywhere = pl.BlockSpec(memory_space=pl.ANY)
    in_specs = row_specs(blocks)
    if first:
        in_specs += [pl.BlockSpec(end.shape, lambda i, *p: (0, 0, 0), pipeline_mode=pl.Buffered(1)) for end in ends]
        args = ends
    else:
        after = pl.BlockSpec((1, width, width), lambda i, *p: (low + turns, 0, 0), pipeline_mode=pl.Buffered(1))
        in_specs += [square(width), after, anywhere]
        args = [half, *state]
    whole = square(width, lambda i: low + turns - 1 - i)
    band = pl.BlockSpec((1, rows, width), lambda i, *p: (low + turns - 1 - i, 0, 0))
    base = 2 + count + 1
    return pl.pallas_call(
        functools.partial(compose_kernel, cycle, right, turns, first),
        grid_spec=pltpu.PrefetchScalarGridSpec(
            num_scalar_prefetch=2,
            grid=(turns,),
            in_specs=in_specs,
            out_specs=[whole, band, square(width, lambda i: turns - 1 - i), square(width)],
            scratch_shapes=[pltpu.VMEM((width, width), BF16)] + row_scratch(count, rows),
        ),
        out_shape=[
            jax.ShapeDtypeStruct((steps, width, width), BF16),
            jax.ShapeDtypeStruct((steps, rows, width), BF16),
            jax.ShapeDtypeStruct((turns, width, width), BF16),
            jax.ShapeDtypeStruct((width, width), BF16),
        ],
        input_output_aliases={} if first else {base: 0, base + 1: 1},
        compiler_params=pltpu.CompilerParams(vmem_limit_bytes=22 * MIB),
        cost_estimate=pl.CostEstimate(
            flops=6 * turns * width**3, bytes_accessed=8 * turns * width * width, transcendentals=0
        ),
        name="compose",
    )(last, place, *blocks, *args)


def chain_kernel(cycle, right, turns, place_ref, *refs):
    count = len(cycle)
    places = origins(place_ref[0], cycle, right)
    blocks, refs = refs[:count], refs[count:]
    half, gain_out, half_out, packed_out, middle, raw, extras, fresh = refs
    prepare(places, blocks, turns - 1, turns, gain_out.at[turns - 1], fresh.at[0], raw, extras)
    for turn in range(turns):
        step = turns - 1 - turn
        if step:
            prepare(places, blocks, step - 1, turns, gain_out.at[step - 1], fresh.at[(turn + 1) % 2], raw, extras)
        advance(gain_out.at[step], half, fresh.at[turn % 2], middle, half_out.at[step])
        half = half_out.at[step]
    fold(half, packed_out)


def chain(place, cycle, right, blocks, half, turns):
    count = len(blocks)
    rows = blocks[0].shape[0]
    width = rows * count
    vmem = pl.BlockSpec(memory_space=pltpu.VMEM)
    return pl.pallas_call(
        functools.partial(chain_kernel, cycle, right, turns),
        in_specs=[pl.BlockSpec(memory_space=pltpu.SMEM)] + [vmem] * (count + 1),
        out_specs=[vmem] * 3,
        out_shape=[
            jax.ShapeDtypeStruct((turns, width, width), BF16),
            jax.ShapeDtypeStruct((turns, width, width), BF16),
            jax.ShapeDtypeStruct(blocks_shape(width), BF16),
        ],
        scratch_shapes=[
            pltpu.VMEM((width, width), BF16),
            pltpu.VMEM((count, rows, width // 2), BF16),
            pltpu.VMEM((count, rows, LANES), BF16),
            pltpu.VMEM((2, width, width), BF16),
        ],
        compiler_params=pltpu.CompilerParams(vmem_limit_bytes=26 * MIB),
        cost_estimate=pl.CostEstimate(
            flops=4 * turns * width**3, bytes_accessed=8 * turns * width * width, transcendentals=0
        ),
        name="chain",
    )(place, *blocks, half)


def factors_kernel(place_ref, gain_ref, factor_in, mine_ref, factor_out, mine_out, factor):
    del mine_ref
    rows = mine_out.shape[1]

    @pl.when(pl.program_id(0) == 0)
    def _():
        factor[...] = factor_in[0]

    extend(gain_ref.at[0], factor)
    mine_out[0] = factor[pl.ds(pl.multiple_of(place_ref[0] * rows, 16), rows), :]
    factor_out[0] = factor[...]


def extend_factors(place, gains, factors, mine):
    turns, width, _ = gains.shape
    steps, rows, _ = mine.shape
    anywhere = pl.BlockSpec(memory_space=pl.ANY)
    return pl.pallas_call(
        factors_kernel,
        grid_spec=pltpu.PrefetchScalarGridSpec(
            num_scalar_prefetch=1,
            grid=(turns,),
            in_specs=[square(width, lambda i: turns - 1 - i), square(width, lambda i: turns), anywhere],
            out_specs=[
                square(width, lambda i: turns - 1 - i),
                pl.BlockSpec((1, rows, width), lambda i, *p: (turns - 1 - i, 0, 0)),
            ],
            scratch_shapes=[pltpu.VMEM((width, width), BF16)],
        ),
        out_shape=[
            jax.ShapeDtypeStruct((steps, width, width), BF16),
            jax.ShapeDtypeStruct((steps, rows, width), BF16),
        ],
        input_output_aliases={2: 0, 3: 1},
        compiler_params=pltpu.CompilerParams(vmem_limit_bytes=12 * MIB),
        cost_estimate=pl.CostEstimate(
            flops=2 * turns * width**3, bytes_accessed=4 * turns * width * width, transcendentals=0
        ),
        name="extend_factors",
    )(place, gains, factors, mine)


def rows_kernel(size, place_ref, *refs):
    own_out = refs[-1]
    rows = own_out.shape[1]
    mine = pl.multiple_of(place_ref[0] * rows, 16)
    for n, half_ref in enumerate(refs[:-1]):

        @pl.when(pl.program_id(0) // size == n)
        def _():
            own_out[0] = whole_rows(half_ref.at[0], mine, rows)


def own_rows(place, halves, rows):
    size, width, _ = halves[0].shape
    steps = size * len(halves)
    return pl.pallas_call(
        functools.partial(rows_kernel, size),
        grid_spec=pltpu.PrefetchScalarGridSpec(
            num_scalar_prefetch=1,
            grid=(steps,),
            in_specs=[
                square(width, lambda i, n=n: jnp.clip(i - n * size, 0, size - 1)) for n in range(len(halves))
            ],
            out_specs=pl.BlockSpec((1, rows, width), lambda i, *p: (i, 0, 0)),
        ),
        out_shape=jax.ShapeDtypeStruct((steps, rows, width), F32),
        compiler_params=pltpu.CompilerParams(vmem_limit_bytes=14 * MIB),
        cost_estimate=pl.CostEstimate(
            flops=2 * steps * rows * width**2, bytes_accessed=2 * steps * width * width, transcendentals=0
        ),
        name="own_rows",
    )(place, *halves)


def upper_blocks(width):
    return [(a, b) for a in range(0, width, TILE) for b in range(a, width, TILE)]


def blocks_shape(width):
    return (len(upper_blocks(width)), TILE, TILE)


def identity(size):
    row = lax.broadcasted_iota(jnp.int32, (size, size), 0)
    column = lax.broadcasted_iota(jnp.int32, (size, size), 1)
    return jnp.where(row == column, 1.0, 0.0).astype(BF16)


def fold(half_ref, packed_ref):
    one = identity(TILE)
    for n, (a, b) in enumerate(upper_blocks(half_ref.shape[0])):
        block = half_ref[a:a + TILE, b:b + TILE]
        if a != b:
            block = block.astype(F32) + nt(one, half_ref[b:b + TILE, a:a + TILE])
        packed_ref[n] = block.astype(BF16)


def arrived_sum(refs, n):
    value = refs[0][n]
    for extra in refs[1:]:
        value = value + extra[n]
    return value


def hop_kernel(arrived, factor_ref, half_ref, *refs):
    out_ref, covariance, middle, ahead = refs[arrived:]
    width = factor_ref.shape[1]
    for n, (a, b) in enumerate(upper_blocks(width)):
        covariance[a:a + TILE, b:b + TILE] = arrived_sum(refs[:arrived], n)
    for j in range(0, width, TILE):
        cols = slice(j, j + TILE)
        middle[:, cols] = jnp.dot(
            factor_ref[0, :, :j + TILE], covariance[:j + TILE, cols], preferred_element_type=F32
        ).astype(BF16)
    for j in range(0, width, TILE):
        cols = slice(j, j + TILE)
        ahead[:, cols] = (nt(middle[...], factor_ref[0, cols, :]) + half_ref[0, :, cols].astype(F32)).astype(BF16)
    fold(ahead, out_ref)


def hop(factors, halves, packed):
    width = halves.shape[1]
    vmem = pl.BlockSpec(memory_space=pltpu.VMEM)
    return pl.pallas_call(
        functools.partial(hop_kernel, len(packed)),
        in_specs=[vmem] * (2 + len(packed)),
        out_specs=vmem,
        out_shape=jax.ShapeDtypeStruct(blocks_shape(width), BF16),
        scratch_shapes=[pltpu.VMEM((width, width), BF16)] * 3,
        compiler_params=pltpu.CompilerParams(vmem_limit_bytes=24 * MIB),
        cost_estimate=pl.CostEstimate(flops=4 * width**3, bytes_accessed=10 * width * width, transcendentals=0),
        name="hop",
    )(factors, halves, *packed)


def finish_kernel(arrived, factor_ref, own_ref, mine_ref, *refs):
    out_ref, covariance, middle, rows_out, copied = refs[arrived:]
    steps, rows, width = own_ref.shape
    one = identity(TILE)
    for n, (a, b) in enumerate(upper_blocks(width)):
        block = arrived_sum(refs[:arrived], n)
        turned = nt(one, block)
        if a == b:
            covariance[a:a + TILE, b:b + TILE] = (block.astype(F32) + turned).astype(BF16)
        else:
            covariance[a:a + TILE, b:b + TILE] = block
            covariance[b:b + TILE, a:a + TILE] = turned.astype(BF16)
    mine = mine_ref[...].reshape(steps * rows, width)
    for j in range(0, width, TILE):
        cols = slice(j, j + TILE)
        middle[:, cols] = jnp.dot(mine, covariance[:, cols], preferred_element_type=F32).astype(BF16)
    copies = []
    for n in range(steps):
        rows_out[n] = nt(middle[n * rows:(n + 1) * rows, :], factor_ref[n]) + own_ref[n]
        copies.append(pltpu.make_async_copy(rows_out.at[n], out_ref.at[n], copied.at[n]))
        copies[-1].start()
    for copy in copies:
        copy.wait()


def finish(factors, own, mine, packed):
    steps, rows, width = own.shape
    vmem = pl.BlockSpec(memory_space=pltpu.VMEM)
    return pl.pallas_call(
        functools.partial(finish_kernel, len(packed)),
        in_specs=[vmem] * (3 + len(packed)),
        out_specs=pl.BlockSpec(memory_space=pl.ANY),
        scratch_shapes=[
            pltpu.VMEM((width, width), BF16),
            pltpu.VMEM((steps * rows, width), BF16),
            pltpu.VMEM((steps, rows, width), F32),
            pltpu.SemaphoreType.DMA((steps,)),
        ],
        out_shape=jax.ShapeDtypeStruct((steps, rows, width), F32),
        compiler_params=pltpu.CompilerParams(vmem_limit_bytes=26 * MIB),
        name="finish",
    )(factors, own, mine, *packed)


def ring_order(line, across):
    cycle = []
    for a in range(line):
        columns = list(range(1, across))
        cycle += [a * across + b for b in (columns if a % 2 == 0 else columns[::-1])]
    return cycle + [a * across for a in reversed(range(line))]


def pieces(steps):
    size = steps // 4
    return [(low, low + size) for low in reversed(range(0, steps, size))]


def local(gains, increments, terminal):
    count = lax.axis_size("tile")
    blocks = lax.axis_size("tm")
    line = math.gcd(count, LINE)
    steps = gains.shape[0]
    place = lax.axis_index("tile").astype(jnp.int32).reshape(1)
    block = lax.axis_index("tm").astype(jnp.int32).reshape(1)
    last = (block == blocks - 1).astype(jnp.int32)
    cycle = ring_order(line, count // line)

    def passed(array, way):
        return lax.ppermute(array, "tile", [(cycle[n], cycle[(n + way) % count]) for n in range(count)])

    ranges = pieces(steps)
    own = [
        *pack(place, block, gains, increments, terminal, count, ranges[:1]),
        *pack(place, block, gains, increments, None, count, ranges[1:2]),
        *pack(place, block, gains, increments, None, count, ranges[2:]),
    ]
    own[1], last = lax.optimization_barrier((own[1], last))
    rights = [count // 2 - turn % 2 for turn in range(len(own))]
    found = []
    for turn, array in enumerate(own):
        found.append({})
        for way, hops in ((1, rights[turn]), (-1, count - 1 - rights[turn])):
            source = array
            if turn > 1:
                before = found[turn - 1][way]
                gate = count // 2 - 1 if turn == 2 else len(before) - 3
                source, before[gate] = lax.optimization_barrier((source, before[gate]))
                for n in range(gate + 1, len(before)):
                    before[n] = passed(before[n - 1], way)
            found[turn][way] = [source]
            for _ in range(hops):
                found[turn][way].append(passed(found[turn][way][-1], way))
    ties = [
        [found[2][1][2], found[2][-1][2]],
        [found[2][1][3], found[2][-1][3]],
        [found[3][1][-2], found[3][-1][-2]],
    ]
    parts, _ = lax.optimization_barrier(
        (
            [own[0]] + found[0][1][1:] + found[0][-1][1:],
            [found[2][1][1], found[2][-1][1], found[1][1][-1], found[1][-1][-1]],
        )
    )
    tile = collect(place, cycle, rights[0], parts)
    ends = [
        lax.ppermute(tile, "tm", [(n, blocks - 1)]) if n < blocks - 1 else tile
        for n in range(gains.shape[2] // 2 // LANES + 1)
    ]
    state, half = None, None
    halves = []
    for turn, (low, high) in enumerate(ranges):
        parts = [own[turn]] + found[turn][1][1:] + found[turn][-1][1:]
        if turn < len(ties):
            parts, _ = lax.optimization_barrier((parts, ties[turn]))
            *state, kept, half = compose(
                last, place, cycle, rights[turn], parts, ends, state, half, low, high - low, steps
            )
        else:
            late_gains, kept, folded = chain(place, cycle, rights[turn], parts, half, high)
        halves.insert(0, kept)
    factors, mine = extend_factors(place, late_gains, *state)
    packed = []
    for turn in range(blocks - 1, 0, -1):
        if turn == 1:
            own = own_rows(place, lax.optimization_barrier((halves, before))[0], gains.shape[1])
            packed, own = lax.optimization_barrier((packed, own))
        before = hop(factors, halves[0], packed) if packed else folded
        packed.append(lax.ppermute(before, "tm", [(turn, turn - 1)]))
    return finish(factors, own, mine, packed)


def solution(mesh):
    return jax.shard_map(
        local,
        mesh=mesh,
        in_specs=(P("tm", "tile", None), P("tm", "tile", None), P("tile", None)),
        out_specs=P("tm", "tile", None),
        check_vma=False,
    )
```

```python
import functools
import math

import jax
import jax.numpy as jnp
from jax import lax
from jax.experimental import pallas as pl
from jax.experimental.pallas import tpu as pltpu
from jax.sharding import PartitionSpec as P

BF16 = jnp.bfloat16
F32 = jnp.float32
LANES = 128
TILE = 256
LINE = 4
MIB = 1024 * 1024
CLAIM = 60 * MIB


def nt(left, right):
    return lax.dot_general(left, right, (((1,), (1,)), ((), ())), preferred_element_type=F32)


def packed_half(increment, place, count):
    rows, width = increment.shape
    turned = pltpu.roll(increment, lax.rem(width - place * rows, width), 1)
    column = lax.broadcasted_iota(jnp.int32, (rows, width // 2), 1)
    main = turned[:, :width // 2] * jnp.where(column < rows, 0.5, 1.0)
    opposite = turned[:, width // 2:width // 2 + LANES]
    lower = opposite[rows // 2:]
    side = jnp.concatenate([lower, pltpu.roll(lower, LANES - rows // 2, 1)], axis=0)
    return main.astype(BF16), jnp.where(place < count // 2, opposite, side)


def unpacked_half(main, extra, block, count):
    rows = main.shape[0]
    width = rows * count
    column = lax.broadcasted_iota(jnp.int32, extra.shape, 1)
    extra = jnp.where(column < rows // 2, extra, 0.0)
    if block >= count // 2:
        lower = extra[:rows // 2] + pltpu.roll(extra[rows // 2:], rows // 2, 1)
        extra = jnp.concatenate([jnp.zeros_like(lower), lower], axis=0)
    rest = jnp.zeros((rows, width // 2 - LANES), F32)
    wide = jnp.concatenate([main.astype(F32), extra, rest], axis=1)
    return pltpu.roll(wide, block * rows, 1) if block else wide


def pack_kernel(count, ranges, place_ref, block_ref, gain_ref, increment_ref, *refs):
    outs = refs[-len(ranges):]
    rows, width = gain_ref.shape[1:]
    stride = width + width // 2
    place = place_ref[0]
    base = min(low for low, _ in ranges)
    column = lax.broadcasted_iota(jnp.int32, (rows, LANES), 1)
    for (low, high), packed_ref in zip(ranges, outs):
        extras = jnp.zeros((rows, LANES), F32)
        for step in range(high - low):
            at = step * stride
            main, extra = packed_half(increment_ref[low - base + step], place, count)
            packed_ref[:, at:at + width] = gain_ref[low - base + step]
            packed_ref[:, at + width:at + stride] = main
            shift = step * rows // 2
            here = (column >= shift) & (column < shift + rows // 2)
            extras = jnp.where(here, pltpu.roll(extra, shift, 1) if shift else extra, extras)
        packed_ref[:, (high - low) * stride:(high - low) * stride + LANES] = extras.astype(BF16)
    if len(refs) > len(ranges):
        main, extra = packed_half(refs[0][...], place, count)
        at = (ranges[0][1] - ranges[0][0]) * stride + LANES
        tiles = [main[:, n:n + LANES].astype(F32) for n in range(0, width // 2, LANES)] + [extra]
        outs[0][:, at:] = sum(jnp.where(block_ref[0] == n, tile, 0.0) for n, tile in enumerate(tiles)).astype(BF16)


def pack(place, block, gains, increments, terminal, count, ranges):
    rows, width = gains.shape[1:]
    first, size = ranges[-1][0], ranges[0][1] - ranges[-1][0]
    ends = [] if terminal is None else [terminal]
    lanes = [(high - low) * (width + width // 2) + LANES for low, high in ranges]
    lanes[0] += LANES * len(ends)
    some = pl.BlockSpec((size, rows, width), lambda i, *p: (first // size, 0, 0))
    return pl.pallas_call(
        functools.partial(pack_kernel, count, ranges),
        grid_spec=pltpu.PrefetchScalarGridSpec(
            num_scalar_prefetch=2,
            grid=(1,),
            in_specs=[some, some] + [pl.BlockSpec((rows, width), lambda i, *p: (0, 0))] * len(ends),
            out_specs=[pl.BlockSpec((rows, n), lambda i, *p: (0, 0)) for n in lanes],
        ),
        out_shape=[jax.ShapeDtypeStruct((rows, n), BF16) for n in lanes],
        compiler_params=pltpu.CompilerParams(vmem_limit_bytes=CLAIM if len(ranges) == 1 else 14 * MIB),
        name="pack",
    )(place, block, gains, increments, *ends)


def collect_kernel(cycle, right, place_ref, *refs):
    out_ref = refs[-1]
    for place, tile in zip(origins(place_ref[0], cycle, right), refs):
        out_ref[place] = tile[...]


def collect(place, cycle, right, blocks):
    rows, lanes = blocks[0].shape
    tile = pl.BlockSpec((rows, LANES), lambda i, *p: (0, lanes // LANES - 1), pipeline_mode=pl.Buffered(1))
    return pl.pallas_call(
        functools.partial(collect_kernel, cycle, right),
        grid_spec=pltpu.PrefetchScalarGridSpec(
            num_scalar_prefetch=1,
            grid=(1,),
            in_specs=[tile] * len(blocks),
            out_specs=pl.BlockSpec((len(blocks), rows, LANES), lambda i, *p: (0, 0, 0)),
        ),
        out_shape=jax.ShapeDtypeStruct((len(blocks), rows, LANES), BF16),
        compiler_params=pltpu.CompilerParams(vmem_limit_bytes=6 * MIB),
        name="collect",
    )(place, *blocks)


def unpack(raw, extras, step, half):
    count, rows, _ = raw.shape
    shift = lax.rem(LANES - step * (rows // 2), LANES)
    for n in range(count):
        extra = pltpu.roll(extras[n].astype(F32), shift, 1)
        half[n * rows:(n + 1) * rows, :] = unpacked_half(raw[n], extra, n, count).astype(BF16)


def origins(place, cycle, right):
    count = len(cycle)

    def look(table, at):
        return sum(jnp.where(at == n, value, 0) for n, value in enumerate(table))

    spot = look([cycle.index(d) for d in range(count)], place)
    hops = [0] + [-n for n in range(1, right + 1)] + list(range(1, count - right))
    return [look(cycle, lax.rem(spot + n + count, count)) for n in hops]


def assemble(places, blocks, sides, step, gain, fresh, raw, extras):
    rows = blocks[0].shape[0]
    width = gain.shape[0]
    for place, block, side in zip(places, blocks, sides):
        gain[pl.ds(pl.multiple_of(place * rows, 16), rows), :] = block[:, :width]
        raw[place] = block[:, width:]
        extras[place] = side[...]
    unpack(raw, extras, step, fresh)


def advance(gain, half, fresh, middle, out=None):
    out = half if out is None else out
    width = half.shape[0]
    for j in range(0, width, TILE):
        cols = slice(j, j + TILE)
        middle[:, cols] = jnp.dot(gain[...], half[:, cols], preferred_element_type=F32).astype(BF16)
    for j in range(0, width, TILE):
        cols = slice(j, j + TILE)
        out[:, cols] = (nt(middle[...], gain[cols, :]) + fresh[:, cols].astype(F32)).astype(BF16)


def extend(gain, factor):
    for j in range(0, factor.shape[0], TILE):
        cols = slice(j, j + TILE)
        factor[:, cols] = jnp.dot(gain[...], factor[:, cols], preferred_element_type=F32).astype(BF16)


def whole_rows(half, mine, rows):
    picked = lax.broadcasted_iota(jnp.int32, (rows, half.shape[0]), 1) == mine + lax.broadcasted_iota(
        jnp.int32, (rows, half.shape[0]), 0
    )
    own = half[pl.ds(mine, rows), :].astype(F32)
    return own + nt(jnp.where(picked, 1.0, 0.0).astype(BF16), half[...])


def prepare(places, blocks, step, turns, gain, fresh, raw, extras):
    stride = gain.shape[0] * 3 // 2
    lanes, side = slice(step * stride, (step + 1) * stride), slice(turns * stride, turns * stride + LANES)
    parts, sides = [block.at[:, lanes] for block in blocks], [block.at[:, side] for block in blocks]
    assemble(places, parts, sides, step, gain, fresh, raw, extras)


def compose_kernel(cycle, right, turns, first, last_ref, place_ref, *refs):
    count = len(cycle)
    places = origins(place_ref[0], cycle, right)
    blocks, refs = refs[:count], refs[count:]
    if first:
        tiles = blocks[0].shape[0] * count // 2 // LANES + 1
        ends, refs = refs[:tiles], refs[tiles:]
    else:
        half_in, factor_in, refs = refs[0], refs[1], refs[3:]
    factor_out, mine_out, half_out, half, factor, middle, raw, extras, gain, fresh, spare = refs
    gains, freshes = (gain, spare.at[0]), (fresh, spare.at[1])
    rows = blocks[0].shape[0]
    mine = pl.multiple_of(place_ref[0] * rows, 16)
    for turn in range(turns):

        @pl.when(pl.program_id(0) == turn)
        def _():
            now = turn % 2
            if turn == 0 and first:
                scale = jnp.where(last_ref[0] == 1, 1.0, 0.0).astype(BF16)
                for n, end in enumerate(ends[:-1]):
                    raw[:, :, n * LANES:(n + 1) * LANES] = end[...] * scale
                extras[...] = ends[-1][...] * scale
                unpack(raw, extras, 0, half)
            elif turn == 0:
                factor[...] = factor_in[0]
                half[...] = half_in[...]
            if turn == 0:
                prepare(places, blocks, turns - 1, turns, gains[0], freshes[0], raw, extras)
            if turn == 0 and first:
                factor[...] = gains[0][...]
            else:
                extend(gains[now], factor)
            if turn + 1 < turns:
                prepare(places, blocks, turns - 2 - turn, turns, gains[1 - now], freshes[1 - now], raw, extras)
            advance(gains[now], half, freshes[now], middle)
            half_out[0] = half[...]
            mine_out[0] = factor[pl.ds(mine, rows), :]
            factor_out[0] = factor[...]


def square(width, place=None):
    if place is None:
        return pl.BlockSpec((width, width), lambda i, *p: (0, 0), pipeline_mode=pl.Buffered(1))
    return pl.BlockSpec((1, width, width), lambda i, *p: (place(i), 0, 0))


def row_specs(blocks):
    return [pl.BlockSpec(block.shape, lambda i, *p: (0, 0), pipeline_mode=pl.Buffered(1)) for block in blocks]


def row_scratch(count, rows):
    width = count * rows
    whole = pltpu.VMEM((width, width), BF16)
    return [
        whole,
        pltpu.VMEM((count, rows, width // 2), BF16),
        pltpu.VMEM((count, rows, LANES), BF16),
        whole,
        whole,
        pltpu.VMEM((2, width, width), BF16),
    ]


def compose(last, place, cycle, right, blocks, ends, state, half, low, turns, steps):
    count = len(blocks)
    rows = blocks[0].shape[0]
    width = rows * count
    first = state is None
    anywhere = pl.BlockSpec(memory_space=pl.ANY)
    in_specs = row_specs(blocks)
    if first:
        in_specs += [pl.BlockSpec(end.shape, lambda i, *p: (0, 0, 0), pipeline_mode=pl.Buffered(1)) for end in ends]
        args = ends
    else:
        after = pl.BlockSpec((1, width, width), lambda i, *p: (low + turns, 0, 0), pipeline_mode=pl.Buffered(1))
        in_specs += [square(width), after, anywhere]
        args = [half, *state]
    whole = square(width, lambda i: low + turns - 1 - i)
    band = pl.BlockSpec((1, rows, width), lambda i, *p: (low + turns - 1 - i, 0, 0))
    base = 2 + count + 1
    return pl.pallas_call(
        functools.partial(compose_kernel, cycle, right, turns, first),
        grid_spec=pltpu.PrefetchScalarGridSpec(
            num_scalar_prefetch=2,
            grid=(turns,),
            in_specs=in_specs,
            out_specs=[whole, band, square(width, lambda i: turns - 1 - i), square(width)],
            scratch_shapes=[pltpu.VMEM((width, width), BF16)] + row_scratch(count, rows),
        ),
        out_shape=[
            jax.ShapeDtypeStruct((steps, width, width), BF16),
            jax.ShapeDtypeStruct((steps, rows, width), BF16),
            jax.ShapeDtypeStruct((turns, width, width), BF16),
            jax.ShapeDtypeStruct((width, width), BF16),
        ],
        input_output_aliases={} if first else {base: 0, base + 1: 1},
        compiler_params=pltpu.CompilerParams(vmem_limit_bytes=22 * MIB),
        cost_estimate=pl.CostEstimate(
            flops=6 * turns * width**3, bytes_accessed=8 * turns * width * width, transcendentals=0
        ),
        name="compose",
    )(last, place, *blocks, *args)


def chain_kernel(cycle, right, turns, place_ref, *refs):
    count = len(cycle)
    places = origins(place_ref[0], cycle, right)
    blocks, refs = refs[:count], refs[count:]
    half, gain_out, half_out, packed_out, middle, raw, extras, fresh = refs
    prepare(places, blocks, turns - 1, turns, gain_out.at[turns - 1], fresh.at[0], raw, extras)
    for turn in range(turns):
        step = turns - 1 - turn
        if step:
            prepare(places, blocks, step - 1, turns, gain_out.at[step - 1], fresh.at[(turn + 1) % 2], raw, extras)
        advance(gain_out.at[step], half, fresh.at[turn % 2], middle, half_out.at[step])
        half = half_out.at[step]
    fold(half, packed_out)


def chain(place, cycle, right, blocks, half, turns):
    count = len(blocks)
    rows = blocks[0].shape[0]
    width = rows * count
    vmem = pl.BlockSpec(memory_space=pltpu.VMEM)
    return pl.pallas_call(
        functools.partial(chain_kernel, cycle, right, turns),
        in_specs=[pl.BlockSpec(memory_space=pltpu.SMEM)] + [vmem] * (count + 1),
        out_specs=[vmem] * 3,
        out_shape=[
            jax.ShapeDtypeStruct((turns, width, width), BF16),
            jax.ShapeDtypeStruct((turns, width, width), BF16),
            jax.ShapeDtypeStruct(blocks_shape(width), BF16),
        ],
        scratch_shapes=[
            pltpu.VMEM((width, width), BF16),
            pltpu.VMEM((count, rows, width // 2), BF16),
            pltpu.VMEM((count, rows, LANES), BF16),
            pltpu.VMEM((2, width, width), BF16),
        ],
        compiler_params=pltpu.CompilerParams(vmem_limit_bytes=26 * MIB),
        cost_estimate=pl.CostEstimate(
            flops=4 * turns * width**3, bytes_accessed=8 * turns * width * width, transcendentals=0
        ),
        name="chain",
    )(place, *blocks, half)


def factors_kernel(place_ref, gain_ref, factor_in, mine_ref, factor_out, mine_out, factor):
    del mine_ref
    rows = mine_out.shape[1]

    @pl.when(pl.program_id(0) == 0)
    def _():
        factor[...] = factor_in[0]

    extend(gain_ref.at[0], factor)
    mine_out[0] = factor[pl.ds(pl.multiple_of(place_ref[0] * rows, 16), rows), :]
    factor_out[0] = factor[...]


def extend_factors(place, gains, factors, mine):
    turns, width, _ = gains.shape
    steps, rows, _ = mine.shape
    anywhere = pl.BlockSpec(memory_space=pl.ANY)
    return pl.pallas_call(
        factors_kernel,
        grid_spec=pltpu.PrefetchScalarGridSpec(
            num_scalar_prefetch=1,
            grid=(turns,),
            in_specs=[square(width, lambda i: turns - 1 - i), square(width, lambda i: turns), anywhere],
            out_specs=[
                square(width, lambda i: turns - 1 - i),
                pl.BlockSpec((1, rows, width), lambda i, *p: (turns - 1 - i, 0, 0)),
            ],
            scratch_shapes=[pltpu.VMEM((width, width), BF16)],
        ),
        out_shape=[
            jax.ShapeDtypeStruct((steps, width, width), BF16),
            jax.ShapeDtypeStruct((steps, rows, width), BF16),
        ],
        input_output_aliases={2: 0, 3: 1},
        compiler_params=pltpu.CompilerParams(vmem_limit_bytes=12 * MIB),
        cost_estimate=pl.CostEstimate(
            flops=2 * turns * width**3, bytes_accessed=4 * turns * width * width, transcendentals=0
        ),
        name="extend_factors",
    )(place, gains, factors, mine)


def rows_kernel(size, place_ref, *refs):
    own_out = refs[-1]
    rows = own_out.shape[1]
    mine = pl.multiple_of(place_ref[0] * rows, 16)
    for n, half_ref in enumerate(refs[:-1]):

        @pl.when(pl.program_id(0) // size == n)
        def _():
            own_out[0] = whole_rows(half_ref.at[0], mine, rows)


def own_rows(place, halves, rows):
    size, width, _ = halves[0].shape
    steps = size * len(halves)
    return pl.pallas_call(
        functools.partial(rows_kernel, size),
        grid_spec=pltpu.PrefetchScalarGridSpec(
            num_scalar_prefetch=1,
            grid=(steps,),
            in_specs=[
                square(width, lambda i, n=n: jnp.clip(i - n * size, 0, size - 1)) for n in range(len(halves))
            ],
            out_specs=pl.BlockSpec((1, rows, width), lambda i, *p: (i, 0, 0)),
        ),
        out_shape=jax.ShapeDtypeStruct((steps, rows, width), F32),
        compiler_params=pltpu.CompilerParams(vmem_limit_bytes=14 * MIB),
        cost_estimate=pl.CostEstimate(
            flops=2 * steps * rows * width**2, bytes_accessed=2 * steps * width * width, transcendentals=0
        ),
        name="own_rows",
    )(place, *halves)


def upper_blocks(width):
    return [(a, b) for a in range(0, width, LANES) for b in range(a, width, LANES)]


def blocks_shape(width):
    return (len(upper_blocks(width)), LANES, LANES)


def identity(size):
    row = lax.broadcasted_iota(jnp.int32, (size, size), 0)
    column = lax.broadcasted_iota(jnp.int32, (size, size), 1)
    return jnp.where(row == column, 1.0, 0.0).astype(BF16)


def fold(half_ref, packed_ref):
    one = identity(LANES)
    for n, (a, b) in enumerate(upper_blocks(half_ref.shape[0])):
        block = half_ref[a:a + LANES, b:b + LANES]
        if a != b:
            block = block.astype(F32) + nt(one, half_ref[b:b + LANES, a:a + LANES])
        packed_ref[n] = block.astype(BF16)


def arrived_sum(refs, n):
    value = refs[0][n]
    for extra in refs[1:]:
        value = value + extra[n]
    return value


def hop_kernel(arrived, factor_ref, half_ref, *refs):
    out_ref, covariance, middle, ahead = refs[arrived:]
    width = factor_ref.shape[1]
    for n, (a, b) in enumerate(upper_blocks(width)):
        covariance[a:a + LANES, b:b + LANES] = arrived_sum(refs[:arrived], n)
    for a in range(0, width, TILE):
        covariance[a + LANES:a + TILE, a:a + LANES] = jnp.zeros((LANES, LANES), BF16)
    for j in range(0, width, TILE):
        cols = slice(j, j + TILE)
        middle[:, cols] = jnp.dot(
            factor_ref[0, :, :j + TILE], covariance[:j + TILE, cols], preferred_element_type=F32
        ).astype(BF16)
    for j in range(0, width, TILE):
        cols = slice(j, j + TILE)
        ahead[:, cols] = (nt(middle[...], factor_ref[0, cols, :]) + half_ref[0, :, cols].astype(F32)).astype(BF16)
    fold(ahead, out_ref)


def hop(factors, halves, packed):
    width = halves.shape[1]
    vmem = pl.BlockSpec(memory_space=pltpu.VMEM)
    return pl.pallas_call(
        functools.partial(hop_kernel, len(packed)),
        in_specs=[vmem] * (2 + len(packed)),
        out_specs=vmem,
        out_shape=jax.ShapeDtypeStruct(blocks_shape(width), BF16),
        scratch_shapes=[pltpu.VMEM((width, width), BF16)] * 3,
        compiler_params=pltpu.CompilerParams(vmem_limit_bytes=24 * MIB),
        cost_estimate=pl.CostEstimate(flops=4 * width**3, bytes_accessed=10 * width * width, transcendentals=0),
        name="hop",
    )(factors, halves, *packed)


def finish_kernel(arrived, factor_ref, own_ref, mine_ref, *refs):
    out_ref, covariance, middle, rows_out, copied = refs[arrived:]
    steps, rows, width = own_ref.shape
    one = identity(LANES)
    for n, (a, b) in enumerate(upper_blocks(width)):
        block = arrived_sum(refs[:arrived], n)
        turned = nt(one, block)
        if a == b:
            covariance[a:a + LANES, b:b + LANES] = (block.astype(F32) + turned).astype(BF16)
        else:
            covariance[a:a + LANES, b:b + LANES] = block
            covariance[b:b + LANES, a:a + LANES] = turned.astype(BF16)
    mine = mine_ref[...].reshape(steps * rows, width)
    for j in range(0, width, TILE):
        cols = slice(j, j + TILE)
        middle[:, cols] = jnp.dot(mine, covariance[:, cols], preferred_element_type=F32).astype(BF16)
    copies = []
    for n in range(steps):
        rows_out[n] = nt(middle[n * rows:(n + 1) * rows, :], factor_ref[n]) + own_ref[n]
        copies.append(pltpu.make_async_copy(rows_out.at[n], out_ref.at[n], copied.at[n]))
        copies[-1].start()
    for copy in copies:
        copy.wait()


def finish(factors, own, mine, packed):
    steps, rows, width = own.shape
    vmem = pl.BlockSpec(memory_space=pltpu.VMEM)
    return pl.pallas_call(
        functools.partial(finish_kernel, len(packed)),
        in_specs=[vmem] * (3 + len(packed)),
        out_specs=pl.BlockSpec(memory_space=pl.ANY),
        scratch_shapes=[
            pltpu.VMEM((width, width), BF16),
            pltpu.VMEM((steps * rows, width), BF16),
            pltpu.VMEM((steps, rows, width), F32),
            pltpu.SemaphoreType.DMA((steps,)),
        ],
        out_shape=jax.ShapeDtypeStruct((steps, rows, width), F32),
        compiler_params=pltpu.CompilerParams(vmem_limit_bytes=26 * MIB),
        name="finish",
    )(factors, own, mine, *packed)


def ring_order(line, across):
    cycle = []
    for a in range(line):
        columns = list(range(1, across))
        cycle += [a * across + b for b in (columns if a % 2 == 0 else columns[::-1])]
    return cycle + [a * across for a in reversed(range(line))]


def pieces(steps):
    size = steps // 4
    return [(low, low + size) for low in reversed(range(0, steps, size))]


def local(gains, increments, terminal):
    count = lax.axis_size("tile")
    blocks = lax.axis_size("tm")
    line = math.gcd(count, LINE)
    steps = gains.shape[0]
    place = lax.axis_index("tile").astype(jnp.int32).reshape(1)
    block = lax.axis_index("tm").astype(jnp.int32).reshape(1)
    last = (block == blocks - 1).astype(jnp.int32)
    cycle = ring_order(line, count // line)

    def passed(array, way):
        return lax.ppermute(array, "tile", [(cycle[n], cycle[(n + way) % count]) for n in range(count)])

    ranges = pieces(steps)
    own = [
        *pack(place, block, gains, increments, terminal, count, ranges[:1]),
        *pack(place, block, gains, increments, None, count, ranges[1:2]),
        *pack(place, block, gains, increments, None, count, ranges[2:]),
    ]
    own[1], last = lax.optimization_barrier((own[1], last))
    rights = [count // 2 - turn % 2 for turn in range(len(own))]
    found = []
    for turn, array in enumerate(own):
        found.append({})
        for way, hops in ((1, rights[turn]), (-1, count - 1 - rights[turn])):
            source = array
            if turn > 1:
                before = found[turn - 1][way]
                gate = count // 2 - 1 if turn == 2 else len(before) - 3
                source, before[gate] = lax.optimization_barrier((source, before[gate]))
                for n in range(gate + 1, len(before)):
                    before[n] = passed(before[n - 1], way)
            found[turn][way] = [source]
            for _ in range(hops):
                found[turn][way].append(passed(found[turn][way][-1], way))
    ties = [
        [found[2][1][2], found[2][-1][2]],
        [found[2][1][3], found[2][-1][3]],
        [found[3][1][-2], found[3][-1][-2]],
    ]
    parts, _ = lax.optimization_barrier(
        (
            [own[0]] + found[0][1][1:] + found[0][-1][1:],
            [found[2][1][1], found[2][-1][1], found[1][1][-1], found[1][-1][-1]],
        )
    )
    tile = collect(place, cycle, rights[0], parts)
    ends = [
        lax.ppermute(tile, "tm", [(n, blocks - 1)]) if n < blocks - 1 else tile
        for n in range(gains.shape[2] // 2 // LANES + 1)
    ]
    state, half = None, None
    halves = []
    for turn, (low, high) in enumerate(ranges):
        parts = [own[turn]] + found[turn][1][1:] + found[turn][-1][1:]
        if turn < len(ties):
            parts, _ = lax.optimization_barrier((parts, ties[turn]))
            *state, kept, half = compose(
                last, place, cycle, rights[turn], parts, ends, state, half, low, high - low, steps
            )
        else:
            late_gains, kept, folded = chain(place, cycle, rights[turn], parts, half, high)
        halves.insert(0, kept)
    factors, mine = extend_factors(place, late_gains, *state)
    packed = []
    for turn in range(blocks - 1, 0, -1):
        if turn == 1:
            own = own_rows(place, lax.optimization_barrier((halves, before))[0], gains.shape[1])
            packed, own = lax.optimization_barrier((packed, own))
        before = hop(factors, halves[0], packed) if packed else folded
        packed.append(lax.ppermute(before, "tm", [(turn, turn - 1)]))
    return finish(factors, own, mine, packed)


def solution(mesh):
    return jax.shard_map(
        local,
        mesh=mesh,
        in_specs=(P("tm", "tile", None), P("tm", "tile", None), P("tile", None)),
        out_specs=P("tm", "tile", None),
        check_vma=False,
    )
```

```python
import functools
import math

import jax
import jax.numpy as jnp
from jax import lax
from jax.experimental import pallas as pl
from jax.experimental.pallas import tpu as pltpu
from jax.sharding import PartitionSpec as P

BF16 = jnp.bfloat16
F32 = jnp.float32
LANES = 128
TILE = 256
LINE = 4
MIB = 1024 * 1024
CLAIM = 60 * MIB


def nt(left, right):
    return lax.dot_general(left, right, (((1,), (1,)), ((), ())), preferred_element_type=F32)


def packed_half(increment, place, count):
    rows, width = increment.shape
    turned = pltpu.roll(increment, lax.rem(width - place * rows, width), 1)
    column = lax.broadcasted_iota(jnp.int32, (rows, width // 2), 1)
    main = turned[:, :width // 2] * jnp.where(column < rows, 0.5, 1.0)
    opposite = turned[:, width // 2:width // 2 + LANES]
    lower = opposite[rows // 2:]
    side = jnp.concatenate([lower, pltpu.roll(lower, LANES - rows // 2, 1)], axis=0)
    return main.astype(BF16), jnp.where(place < count // 2, opposite, side)


def unpacked_half(main, extra, block, count):
    rows = main.shape[0]
    width = rows * count
    column = lax.broadcasted_iota(jnp.int32, extra.shape, 1)
    extra = jnp.where(column < rows // 2, extra, 0.0)
    if block >= count // 2:
        lower = extra[:rows // 2] + pltpu.roll(extra[rows // 2:], rows // 2, 1)
        extra = jnp.concatenate([jnp.zeros_like(lower), lower], axis=0)
    rest = jnp.zeros((rows, width // 2 - LANES), F32)
    wide = jnp.concatenate([main.astype(F32), extra, rest], axis=1)
    return pltpu.roll(wide, block * rows, 1) if block else wide


def pack_kernel(count, ranges, place_ref, block_ref, gain_ref, increment_ref, *refs):
    outs = refs[-len(ranges):]
    rows, width = gain_ref.shape[1:]
    stride = width + width // 2
    place = place_ref[0]
    base = min(low for low, _ in ranges)
    column = lax.broadcasted_iota(jnp.int32, (rows, LANES), 1)
    for (low, high), packed_ref in zip(ranges, outs):
        extras = jnp.zeros((rows, LANES), F32)
        for step in range(high - low):
            at = step * stride
            main, extra = packed_half(increment_ref[low - base + step], place, count)
            packed_ref[:, at:at + width] = gain_ref[low - base + step]
            packed_ref[:, at + width:at + stride] = main
            shift = step * rows // 2
            here = (column >= shift) & (column < shift + rows // 2)
            extras = jnp.where(here, pltpu.roll(extra, shift, 1) if shift else extra, extras)
        packed_ref[:, (high - low) * stride:(high - low) * stride + LANES] = extras.astype(BF16)
    if len(refs) > len(ranges):
        main, extra = packed_half(refs[0][...], place, count)
        at = (ranges[0][1] - ranges[0][0]) * stride + LANES
        tiles = [main[:, n:n + LANES].astype(F32) for n in range(0, width // 2, LANES)] + [extra]
        outs[0][:, at:] = sum(jnp.where(block_ref[0] == n, tile, 0.0) for n, tile in enumerate(tiles)).astype(BF16)


def pack(place, block, gains, increments, terminal, count, ranges):
    rows, width = gains.shape[1:]
    first, size = ranges[-1][0], ranges[0][1] - ranges[-1][0]
    ends = [] if terminal is None else [terminal]
    lanes = [(high - low) * (width + width // 2) + LANES for low, high in ranges]
    lanes[0] += LANES * len(ends)
    some = pl.BlockSpec((size, rows, width), lambda i, *p: (first // size, 0, 0))
    return pl.pallas_call(
        functools.partial(pack_kernel, count, ranges),
        grid_spec=pltpu.PrefetchScalarGridSpec(
            num_scalar_prefetch=2,
            grid=(1,),
            in_specs=[some, some] + [pl.BlockSpec((rows, width), lambda i, *p: (0, 0))] * len(ends),
            out_specs=[pl.BlockSpec((rows, n), lambda i, *p: (0, 0)) for n in lanes],
        ),
        out_shape=[jax.ShapeDtypeStruct((rows, n), BF16) for n in lanes],
        compiler_params=pltpu.CompilerParams(vmem_limit_bytes=CLAIM if len(ranges) == 1 else 14 * MIB),
        name="pack",
    )(place, block, gains, increments, *ends)


def collect_kernel(cycle, right, place_ref, *refs):
    out_ref = refs[-1]
    for place, tile in zip(origins(place_ref[0], cycle, right), refs):
        out_ref[place] = tile[...]


def collect(place, cycle, right, blocks):
    rows, lanes = blocks[0].shape
    tile = pl.BlockSpec((rows, LANES), lambda i, *p: (0, lanes // LANES - 1), pipeline_mode=pl.Buffered(1))
    return pl.pallas_call(
        functools.partial(collect_kernel, cycle, right),
        grid_spec=pltpu.PrefetchScalarGridSpec(
            num_scalar_prefetch=1,
            grid=(1,),
            in_specs=[tile] * len(blocks),
            out_specs=pl.BlockSpec((len(blocks), rows, LANES), lambda i, *p: (0, 0, 0)),
        ),
        out_shape=jax.ShapeDtypeStruct((len(blocks), rows, LANES), BF16),
        compiler_params=pltpu.CompilerParams(vmem_limit_bytes=6 * MIB),
        name="collect",
    )(place, *blocks)


def unpack(raw, extras, step, half):
    count, rows, _ = raw.shape
    shift = lax.rem(LANES - step * (rows // 2), LANES)
    for n in range(count):
        extra = pltpu.roll(extras[n].astype(F32), shift, 1)
        half[n * rows:(n + 1) * rows, :] = unpacked_half(raw[n], extra, n, count).astype(BF16)


def origins(place, cycle, right):
    count = len(cycle)

    def look(table, at):
        return sum(jnp.where(at == n, value, 0) for n, value in enumerate(table))

    spot = look([cycle.index(d) for d in range(count)], place)
    hops = [0] + [-n for n in range(1, right + 1)] + list(range(1, count - right))
    return [look(cycle, lax.rem(spot + n + count, count)) for n in hops]


def assemble(places, blocks, sides, step, gain, fresh, raw, extras):
    rows = blocks[0].shape[0]
    width = gain.shape[0]
    for place, block, side in zip(places, blocks, sides):
        gain[pl.ds(pl.multiple_of(place * rows, 16), rows), :] = block[:, :width]
        raw[place] = block[:, width:]
        extras[place] = side[...]
    unpack(raw, extras, step, fresh)


def advance(gain, half, fresh, middle, out=None):
    out = half if out is None else out
    width = half.shape[0]
    for j in range(0, width, TILE):
        cols = slice(j, j + TILE)
        middle[:, cols] = jnp.dot(gain[...], half[:, cols], preferred_element_type=F32).astype(BF16)
    for j in range(0, width, TILE):
        cols = slice(j, j + TILE)
        out[:, cols] = (nt(middle[...], gain[cols, :]) + fresh[:, cols].astype(F32)).astype(BF16)


def extend(gain, factor):
    for j in range(0, factor.shape[0], TILE):
        cols = slice(j, j + TILE)
        factor[:, cols] = jnp.dot(gain[...], factor[:, cols], preferred_element_type=F32).astype(BF16)


def whole_rows(half, mine, rows):
    picked = lax.broadcasted_iota(jnp.int32, (rows, half.shape[0]), 1) == mine + lax.broadcasted_iota(
        jnp.int32, (rows, half.shape[0]), 0
    )
    own = half[pl.ds(mine, rows), :].astype(F32)
    return own + nt(jnp.where(picked, 1.0, 0.0).astype(BF16), half[...])


def prepare(places, blocks, step, turns, gain, fresh, raw, extras):
    stride = gain.shape[0] * 3 // 2
    lanes, side = slice(step * stride, (step + 1) * stride), slice(turns * stride, turns * stride + LANES)
    parts, sides = [block.at[:, lanes] for block in blocks], [block.at[:, side] for block in blocks]
    assemble(places, parts, sides, step, gain, fresh, raw, extras)


def compose_kernel(cycle, right, turns, first, last_ref, place_ref, *refs):
    count = len(cycle)
    places = origins(place_ref[0], cycle, right)
    blocks, refs = refs[:count], refs[count:]
    if first:
        tiles = blocks[0].shape[0] * count // 2 // LANES + 1
        ends, refs = refs[:tiles], refs[tiles:]
    else:
        half_in, factor_in, refs = refs[0], refs[1], refs[3:]
    factor_out, mine_out, half_out, half, factor, middle, raw, extras, gain, fresh, spare = refs
    gains, freshes = (gain, spare.at[0]), (fresh, spare.at[1])
    rows = blocks[0].shape[0]
    mine = pl.multiple_of(place_ref[0] * rows, 16)
    for turn in range(turns):

        @pl.when(pl.program_id(0) == turn)
        def _():
            now = turn % 2
            if turn == 0 and first:
                scale = jnp.where(last_ref[0] == 1, 1.0, 0.0).astype(BF16)
                for n, end in enumerate(ends[:-1]):
                    raw[:, :, n * LANES:(n + 1) * LANES] = end[...] * scale
                extras[...] = ends[-1][...] * scale
                unpack(raw, extras, 0, half)
            elif turn == 0:
                factor[...] = factor_in[0]
                half[...] = half_in[...]
            if turn == 0:
                prepare(places, blocks, turns - 1, turns, gains[0], freshes[0], raw, extras)
            if turn == 0 and first:
                factor[...] = gains[0][...]
            else:
                extend(gains[now], factor)
            if turn + 1 < turns:
                prepare(places, blocks, turns - 2 - turn, turns, gains[1 - now], freshes[1 - now], raw, extras)
            advance(gains[now], half, freshes[now], middle)
            half_out[0] = half[...]
            mine_out[0] = factor[pl.ds(mine, rows), :]
            factor_out[0] = factor[...]


def square(width, place=None):
    if place is None:
        return pl.BlockSpec((width, width), lambda i, *p: (0, 0), pipeline_mode=pl.Buffered(1))
    return pl.BlockSpec((1, width, width), lambda i, *p: (place(i), 0, 0))


def row_specs(blocks):
    return [pl.BlockSpec(block.shape, lambda i, *p: (0, 0), pipeline_mode=pl.Buffered(1)) for block in blocks]


def row_scratch(count, rows):
    width = count * rows
    whole = pltpu.VMEM((width, width), BF16)
    return [
        whole,
        pltpu.VMEM((count, rows, width // 2), BF16),
        pltpu.VMEM((count, rows, LANES), BF16),
        whole,
        whole,
        pltpu.VMEM((2, width, width), BF16),
    ]


def compose(last, place, cycle, right, blocks, ends, state, half, low, turns, steps):
    count = len(blocks)
    rows = blocks[0].shape[0]
    width = rows * count
    first = state is None
    anywhere = pl.BlockSpec(memory_space=pl.ANY)
    in_specs = row_specs(blocks)
    if first:
        in_specs += [pl.BlockSpec(end.shape, lambda i, *p: (0, 0, 0), pipeline_mode=pl.Buffered(1)) for end in ends]
        args = ends
    else:
        after = pl.BlockSpec((1, width, width), lambda i, *p: (low + turns, 0, 0), pipeline_mode=pl.Buffered(1))
        in_specs += [square(width), after, anywhere]
        args = [half, *state]
    whole = square(width, lambda i: low + turns - 1 - i)
    band = pl.BlockSpec((1, rows, width), lambda i, *p: (low + turns - 1 - i, 0, 0))
    base = 2 + count + 1
    return pl.pallas_call(
        functools.partial(compose_kernel, cycle, right, turns, first),
        grid_spec=pltpu.PrefetchScalarGridSpec(
            num_scalar_prefetch=2,
            grid=(turns,),
            in_specs=in_specs,
            out_specs=[whole, band, square(width, lambda i: turns - 1 - i), square(width)],
            scratch_shapes=[pltpu.VMEM((width, width), BF16)] + row_scratch(count, rows),
        ),
        out_shape=[
            jax.ShapeDtypeStruct((steps, width, width), BF16),
            jax.ShapeDtypeStruct((steps, rows, width), BF16),
            jax.ShapeDtypeStruct((turns, width, width), BF16),
            jax.ShapeDtypeStruct((width, width), BF16),
        ],
        input_output_aliases={} if first else {base: 0, base + 1: 1},
        compiler_params=pltpu.CompilerParams(vmem_limit_bytes=22 * MIB),
        cost_estimate=pl.CostEstimate(
            flops=6 * turns * width**3, bytes_accessed=8 * turns * width * width, transcendentals=0
        ),
        name="compose",
    )(last, place, *blocks, *args)


def chain_kernel(cycle, right, turns, place_ref, *refs):
    count = len(cycle)
    places = origins(place_ref[0], cycle, right)
    blocks, refs = refs[:count], refs[count:]
    half, gain_out, half_out, packed_out, middle, raw, extras, fresh = refs
    prepare(places, blocks, turns - 1, turns, gain_out.at[turns - 1], fresh.at[0], raw, extras)
    for turn in range(turns):
        step = turns - 1 - turn
        if step:
            prepare(places, blocks, step - 1, turns, gain_out.at[step - 1], fresh.at[(turn + 1) % 2], raw, extras)
        advance(gain_out.at[step], half, fresh.at[turn % 2], middle, half_out.at[step])
        half = half_out.at[step]
    fold(half, packed_out)


def chain(place, cycle, right, blocks, half, turns):
    count = len(blocks)
    rows = blocks[0].shape[0]
    width = rows * count
    vmem = pl.BlockSpec(memory_space=pltpu.VMEM)
    return pl.pallas_call(
        functools.partial(chain_kernel, cycle, right, turns),
        in_specs=[pl.BlockSpec(memory_space=pltpu.SMEM)] + [vmem] * (count + 1),
        out_specs=[vmem] * 3,
        out_shape=[
            jax.ShapeDtypeStruct((turns, width, width), BF16),
            jax.ShapeDtypeStruct((turns, width, width), BF16),
            jax.ShapeDtypeStruct(blocks_shape(width), BF16),
        ],
        scratch_shapes=[
            pltpu.VMEM((width, width), BF16),
            pltpu.VMEM((count, rows, width // 2), BF16),
            pltpu.VMEM((count, rows, LANES), BF16),
            pltpu.VMEM((2, width, width), BF16),
        ],
        compiler_params=pltpu.CompilerParams(vmem_limit_bytes=26 * MIB),
        cost_estimate=pl.CostEstimate(
            flops=4 * turns * width**3, bytes_accessed=8 * turns * width * width, transcendentals=0
        ),
        name="chain",
    )(place, *blocks, half)


def factors_kernel(place_ref, gain_ref, factor_in, mine_ref, factor_out, mine_out, factor):
    del mine_ref
    rows = mine_out.shape[1]

    @pl.when(pl.program_id(0) == 0)
    def _():
        factor[...] = factor_in[0]

    extend(gain_ref.at[0], factor)
    mine_out[0] = factor[pl.ds(pl.multiple_of(place_ref[0] * rows, 16), rows), :]
    factor_out[0] = factor[...]


def extend_factors(place, gains, factors, mine):
    turns, width, _ = gains.shape
    steps, rows, _ = mine.shape
    anywhere = pl.BlockSpec(memory_space=pl.ANY)
    return pl.pallas_call(
        factors_kernel,
        grid_spec=pltpu.PrefetchScalarGridSpec(
            num_scalar_prefetch=1,
            grid=(turns,),
            in_specs=[square(width, lambda i: turns - 1 - i), square(width, lambda i: turns), anywhere],
            out_specs=[
                square(width, lambda i: turns - 1 - i),
                pl.BlockSpec((1, rows, width), lambda i, *p: (turns - 1 - i, 0, 0)),
            ],
            scratch_shapes=[pltpu.VMEM((width, width), BF16)],
        ),
        out_shape=[
            jax.ShapeDtypeStruct((steps, width, width), BF16),
            jax.ShapeDtypeStruct((steps, rows, width), BF16),
        ],
        input_output_aliases={2: 0, 3: 1},
        compiler_params=pltpu.CompilerParams(vmem_limit_bytes=12 * MIB),
        cost_estimate=pl.CostEstimate(
            flops=2 * turns * width**3, bytes_accessed=4 * turns * width * width, transcendentals=0
        ),
        name="extend_factors",
    )(place, gains, factors, mine)


def rows_kernel(size, place_ref, *refs):
    own_out = refs[-1]
    rows = own_out.shape[1]
    mine = pl.multiple_of(place_ref[0] * rows, 16)
    for n, half_ref in enumerate(refs[:-1]):

        @pl.when(pl.program_id(0) // size == n)
        def _():
            own_out[0] = whole_rows(half_ref.at[0], mine, rows)


def own_rows(place, halves, rows):
    size, width, _ = halves[0].shape
    steps = size * len(halves)
    return pl.pallas_call(
        functools.partial(rows_kernel, size),
        grid_spec=pltpu.PrefetchScalarGridSpec(
            num_scalar_prefetch=1,
            grid=(steps,),
            in_specs=[
                square(width, lambda i, n=n: jnp.clip(i - n * size, 0, size - 1)) for n in range(len(halves))
            ],
            out_specs=pl.BlockSpec((1, rows, width), lambda i, *p: (i, 0, 0)),
        ),
        out_shape=jax.ShapeDtypeStruct((steps, rows, width), F32),
        compiler_params=pltpu.CompilerParams(vmem_limit_bytes=14 * MIB),
        cost_estimate=pl.CostEstimate(
            flops=2 * steps * rows * width**2, bytes_accessed=2 * steps * width * width, transcendentals=0
        ),
        name="own_rows",
    )(place, *halves)


def upper_blocks(width):
    return [(a, b) for a in range(0, width, LANES) for b in range(a, width, LANES)]


def blocks_shape(width):
    return (len(upper_blocks(width)), LANES, LANES)


def identity(size):
    row = lax.broadcasted_iota(jnp.int32, (size, size), 0)
    column = lax.broadcasted_iota(jnp.int32, (size, size), 1)
    return jnp.where(row == column, 1.0, 0.0).astype(BF16)


def fold(half_ref, packed_ref):
    one = identity(LANES)
    for n, (a, b) in enumerate(upper_blocks(half_ref.shape[0])):
        block = half_ref[a:a + LANES, b:b + LANES]
        if a != b:
            block = block.astype(F32) + nt(one, half_ref[b:b + LANES, a:a + LANES])
        packed_ref[n] = block.astype(BF16)


def arrived_sum(refs, n):
    value = refs[0][n]
    for extra in refs[1:]:
        value = value + extra[n]
    return value


def hop_kernel(arrived, factor_ref, half_ref, *refs):
    out_ref, covariance, middle, ahead = refs[arrived:]
    width = factor_ref.shape[1]
    for n, (a, b) in enumerate(upper_blocks(width)):
        covariance[a:a + LANES, b:b + LANES] = arrived_sum(refs[:arrived], n)
    for a in range(0, width, TILE):
        covariance[a + LANES:a + TILE, a:a + LANES] = jnp.zeros((LANES, LANES), BF16)
    for j in range(0, width, TILE):
        cols = slice(j, j + TILE)
        middle[:, cols] = jnp.dot(
            factor_ref[0, :, :j + TILE], covariance[:j + TILE, cols], preferred_element_type=F32
        ).astype(BF16)
    for j in range(0, width, TILE):
        cols = slice(j, j + TILE)
        ahead[:, cols] = (nt(middle[...], factor_ref[0, cols, :]) + half_ref[0, :, cols].astype(F32)).astype(BF16)
    fold(ahead, out_ref)


def hop(factors, halves, packed):
    width = halves.shape[1]
    vmem = pl.BlockSpec(memory_space=pltpu.VMEM)
    return pl.pallas_call(
        functools.partial(hop_kernel, len(packed)),
        in_specs=[vmem] * (2 + len(packed)),
        out_specs=vmem,
        out_shape=jax.ShapeDtypeStruct(blocks_shape(width), BF16),
        scratch_shapes=[pltpu.VMEM((width, width), BF16)] * 3,
        compiler_params=pltpu.CompilerParams(vmem_limit_bytes=24 * MIB),
        cost_estimate=pl.CostEstimate(flops=4 * width**3, bytes_accessed=10 * width * width, transcendentals=0),
        name="hop",
    )(factors, halves, *packed)


def finish_kernel(arrived, factor_ref, own_ref, mine_ref, *refs):
    out_ref, covariance, middle, rows_out, copied = refs[arrived:]
    steps, rows, width = own_ref.shape
    one = identity(LANES)
    for n, (a, b) in enumerate(upper_blocks(width)):
        block = arrived_sum(refs[:arrived], n)
        turned = nt(one, block)
        if a == b:
            covariance[a:a + LANES, b:b + LANES] = (block.astype(F32) + turned).astype(BF16)
        else:
            covariance[a:a + LANES, b:b + LANES] = block
            covariance[b:b + LANES, a:a + LANES] = turned.astype(BF16)
    mine = mine_ref[...].reshape(steps * rows, width)
    for j in range(0, width, TILE):
        cols = slice(j, j + TILE)
        middle[:, cols] = jnp.dot(mine, covariance[:, cols], preferred_element_type=F32).astype(BF16)
    copies = []
    for n in range(steps):
        rows_out[n] = nt(middle[n * rows:(n + 1) * rows, :], factor_ref[n]) + own_ref[n]
        copies.append(pltpu.make_async_copy(rows_out.at[n], out_ref.at[n], copied.at[n]))
        copies[-1].start()
    for copy in copies:
        copy.wait()


def finish(factors, own, mine, packed):
    steps, rows, width = own.shape
    vmem = pl.BlockSpec(memory_space=pltpu.VMEM)
    return pl.pallas_call(
        functools.partial(finish_kernel, len(packed)),
        in_specs=[vmem] * (3 + len(packed)),
        out_specs=pl.BlockSpec(memory_space=pl.ANY),
        scratch_shapes=[
            pltpu.VMEM((width, width), BF16),
            pltpu.VMEM((steps * rows, width), BF16),
            pltpu.VMEM((steps, rows, width), F32),
            pltpu.SemaphoreType.DMA((steps,)),
        ],
        out_shape=jax.ShapeDtypeStruct((steps, rows, width), F32),
        compiler_params=pltpu.CompilerParams(vmem_limit_bytes=26 * MIB),
        name="finish",
    )(factors, own, mine, *packed)


def ring_order(line, across):
    cycle = []
    for a in range(line):
        columns = list(range(1, across))
        cycle += [a * across + b for b in (columns if a % 2 == 0 else columns[::-1])]
    return cycle + [a * across for a in reversed(range(line))]


def pieces(steps):
    size = steps // 4
    return [(low, low + size) for low in reversed(range(0, steps, size))]


def local(gains, increments, terminal):
    count = lax.axis_size("tile")
    blocks = lax.axis_size("tm")
    line = math.gcd(count, LINE)
    steps = gains.shape[0]
    place = lax.axis_index("tile").astype(jnp.int32).reshape(1)
    block = lax.axis_index("tm").astype(jnp.int32).reshape(1)
    last = (block == blocks - 1).astype(jnp.int32)
    cycle = ring_order(line, count // line)

    def passed(array, way):
        return lax.ppermute(array, "tile", [(cycle[n], cycle[(n + way) % count]) for n in range(count)])

    ranges = pieces(steps)
    own = [
        *pack(place, block, gains, increments, terminal, count, ranges[:1]),
        *pack(place, block, gains, increments, None, count, ranges[1:2]),
        *pack(place, block, gains, increments, None, count, ranges[2:]),
    ]
    own[1], last = lax.optimization_barrier((own[1], last))
    rights = [count // 2 - turn % 2 for turn in range(len(own))]
    found = []
    for turn, array in enumerate(own):
        found.append({})
        for way, hops in ((1, rights[turn]), (-1, count - 1 - rights[turn])):
            source = array
            if turn > 1:
                before = found[turn - 1][way]
                gate = count // 2 - 1 if turn == 2 else len(before) - 3 - (way == 1)
                source, before[gate] = lax.optimization_barrier((source, before[gate]))
                for n in range(gate + 1, len(before)):
                    before[n] = passed(before[n - 1], way)
            found[turn][way] = [source]
            for _ in range(hops):
                found[turn][way].append(passed(found[turn][way][-1], way))
    ties = [
        [found[2][1][2], found[2][-1][2]],
        [found[2][1][3], found[2][-1][3]],
        [found[3][1][-2], found[3][-1][-2]],
    ]
    parts, _ = lax.optimization_barrier(
        (
            [own[0]] + found[0][1][1:] + found[0][-1][1:],
            [found[2][1][1], found[2][-1][1], found[1][1][-1], found[1][-1][-1]],
        )
    )
    tile = collect(place, cycle, rights[0], parts)
    ends = [
        lax.ppermute(tile, "tm", [(n, blocks - 1)]) if n < blocks - 1 else tile
        for n in range(gains.shape[2] // 2 // LANES + 1)
    ]
    state, half = None, None
    halves = []
    for turn, (low, high) in enumerate(ranges):
        parts = [own[turn]] + found[turn][1][1:] + found[turn][-1][1:]
        if turn < len(ties):
            parts, _ = lax.optimization_barrier((parts, ties[turn]))
            *state, kept, half = compose(
                last, place, cycle, rights[turn], parts, ends, state, half, low, high - low, steps
            )
        else:
            late_gains, kept, folded = chain(place, cycle, rights[turn], parts, half, high)
        halves.insert(0, kept)
    factors, mine = extend_factors(place, late_gains, *state)
    packed = []
    for turn in range(blocks - 1, 0, -1):
        if turn == 1:
            own = own_rows(place, lax.optimization_barrier((halves, before))[0], gains.shape[1])
            packed, own = lax.optimization_barrier((packed, own))
        before = hop(factors, halves[0], packed) if packed else folded
        packed.append(lax.ppermute(before, "tm", [(turn, turn - 1)]))
    return finish(factors, own, mine, packed)


def solution(mesh):
    return jax.shard_map(
        local,
        mesh=mesh,
        in_specs=(P("tm", "tile", None), P("tm", "tile", None), P("tile", None)),
        out_specs=P("tm", "tile", None),
        check_vma=False,
    )
```
